32 devices in a mesh: grp: 2 (over x), blk: 16 (over z, y, core).
Axes of the slice: x: 2, y: 2, z: 4, core: 2. Of those that a mesh axis runs over, the one named last changes fastest.
Arguments:
- grad_out: bfloat16 [64, 14336], P(('grp', 'blk')), parts along dimension 0, may hold values from -6 to 6
- activations: bfloat16 [64, 4096], P(('grp', 'blk')), parts along dimension 0, may hold values from -6 to 6
- basis_out: bfloat16 [14336, 14336], P(None, 'blk'), may hold values from -0.046875 to 0.046875
- basis_in: bfloat16 [4096, 4096], P(None, 'blk'), may hold values from -0.09375 to 0.09375
- eigenvalues: float32 [14336, 4096], P('blk'), may hold values from 0.02 to 0.5
- tile_order: int32 [32], replicated, may hold values from 0 to 31, each once
- block_map: int32 [16], replicated, may hold values from 0 to 15, each once
Outputs:
- precond_window: float32 [1536, 512], P(('grp', 'blk')), parts along dimension 0
The draws below stay inside these ranges and needn't reach their ends.
There are 2 independent parts, one for each index of `grp`. The reference program is written for one: setup_inputs(seed, part) draws one part's arguments, and reference() takes and returns one part's arrays. A program takes and returns all parts, laid end to end along the dimension named above; an argument that names none is the same for every part. Nothing has to cross between parts.
Inputs may be any that keep to these rules, and one draw needn't show every extreme that they name: tile_order is a permutation. block_map is a permutation; activations' rows s * 2 onward belong to token block block_map[s].
All inputs are finite; a program needn't handle non-finite values.
Results may differ from the reference program's by a relative error of at most 0.0055.
Values may be sent and summed in bfloat16 or wider, within the bound.
No kernel may reach another device: no remote copies, remote signals or barrier semaphores. Data moves between devices by JAX's collectives and lax.ppermute only.
A program may use at most 192 MiB of HBM per device.

```python
import math
import jax
import jax.numpy as jnp
from jax import lax

OUT = 14336
IN = 4096
CT = 128
TOK_DEV = 2
WR = 768
WC = 512
TOKENS = 32
N_BLK = 16


def steps_of(own_key, shape, split, smallest, top_value):
    gain, own = 1.0, jax.random.fold_in(own_key, 6)
    for axis_at, shards_of in split:
        steps = jnp.exp(jax.random.uniform(jax.random.fold_in(own, axis_at), (shards_of,), jnp.float32, smallest / len(split), top_value / len(split)))
        gain = gain * jnp.repeat(steps, shape[axis_at] // shards_of).reshape([-1 if axis == axis_at else 1 for axis in range(len(shape))])
    return gain


def gaussian(rng, extent, scale, limit, split=(), held_as=jnp.bfloat16):
    gain = steps_of(rng, extent, split, -0.22, 0.18) if split else 1.0
    result = jax.random.normal(rng, extent, jnp.float32) * scale * gain
    return jnp.minimum(jnp.maximum(result, -limit), limit).astype(held_as)


def setup_inputs(seed: int = 0, part: int = 0) -> dict:
    keys = jax.random.split(jax.random.key(seed), 8)
    part_keys = jax.random.split(jax.random.fold_in(keys[7], part), 8)
    grad_out = gaussian(part_keys[0], (TOKENS, OUT), 1.0, 6.0, ((0, 16),))
    activations = gaussian(part_keys[1], (TOKENS, IN), 1.0, 6.0, ((0, 16),))
    basis_out = gaussian(keys[2], (OUT, OUT), OUT ** -0.5, 0.046875, ((1, 16),))
    basis_in = gaussian(keys[3], (IN, IN), IN ** -0.5, 0.09375, ((1, 16),))
    eigenvalues = jnp.clip(jnp.exp(math.log(0.5) - 3.218876 * jax.random.uniform(keys[4], (OUT, IN), jnp.float32) ** steps_of(keys[4], (OUT, IN), ((0, 16),), -0.2, 0.2)), 0.02, 0.5)
    tile_order = jax.random.permutation(keys[5], IN // CT).astype(jnp.int32)
    block_map = jax.random.permutation(keys[6], N_BLK).astype(jnp.int32)
    return {"grad_out": grad_out, "activations": activations, "basis_out": basis_out, "basis_in": basis_in, "eigenvalues": eigenvalues, "tile_order": tile_order, "block_map": block_map}


def reference(grad_out, activations, basis_out, basis_in, eigenvalues, tile_order, block_map):
    rotated_out = jnp.dot(grad_out, basis_out, preferred_element_type=jnp.float32).astype(jnp.bfloat16)
    rotated_in = jnp.dot(activations, basis_in, preferred_element_type=jnp.float32).astype(jnp.bfloat16)
    aligned_out = jnp.take(rotated_out.reshape(N_BLK, TOK_DEV, OUT), block_map, axis=0).reshape(TOKENS, OUT)
    rotated_grad = lax.dot_general(aligned_out, rotated_in, (((0,), (0,)), ((), ())), preferred_element_type=jnp.float32) / TOKENS
    damped = jnp.take(eigenvalues.reshape(OUT, IN // CT, CT), tile_order, axis=1).reshape(OUT, IN)
    scaled = rotated_grad / damped
    window_rows = jnp.dot(basis_out[:WR].astype(jnp.float32), scaled, precision=lax.Precision.HIGHEST)
    return jnp.dot(window_rows, basis_in[:WC].astype(jnp.float32).T, precision=lax.Precision.HIGHEST)
```

```python
import functools

import jax
import jax.numpy as jnp
import numpy as np
from jax import lax
from jax.experimental import pallas as pl
from jax.experimental.pallas import tpu as pltpu
from jax.sharding import PartitionSpec as P

WR = 768
WC = 512
LANES = 128
MIB = 1 << 20


def ring_of(n):
    chips = n // 2
    return [*range(0, chips, 2), *range(chips - 1, 0, -2)]


def shift_pairs(n, by):
    ring = ring_of(n)
    return [
        (2 * ring[p] + c, 2 * ring[(p + by) % len(ring)] + c)
        for p in range(len(ring))
        for c in range(2)
    ]


def xor_pairs(n, key):
    return [(b, b ^ (2 * key)) for b in range(n)]


def core_pairs(n):
    return [(b, b ^ 1) for b in range(n)]


def ring_sources(n):
    ring = ring_of(n)
    table = np.zeros((n, n), np.int32)
    for b in range(n):
        place = ring.index(b // 2)
        for k in range(n // 2):
            chip = ring[(place - k) % len(ring)]
            table[b, k] = 2 * chip + b % 2
            table[b, n // 2 + k] = 2 * chip + 1 - b % 2
    return table


def xor_sources(n):
    table = np.zeros((n, n), np.int32)
    for b in range(n):
        for k in range(n // 2):
            table[b, k] = 2 * (b // 2 ^ k) + b % 2
            table[b, n // 2 + k] = 2 * (b // 2 ^ k) + 1 - b % 2
    return table


def place_of(table):
    return np.argsort(table, axis=1).astype(np.int32)


def ring_gather(x, n, far_right):
    chips = n // 2
    pieces = [None] * chips
    pieces[0] = x
    right, left = x, x
    for step in range(1, chips // 2 + 1):
        if step < chips // 2 or far_right:
            right = lax.ppermute(right, "blk", shift_pairs(n, 1))
            pieces[step] = right
        if step < chips // 2 or not far_right:
            left = lax.ppermute(left, "blk", shift_pairs(n, -1))
            pieces[chips - step] = left
    return pieces


def direct_gather(x, n):
    return [x] + [lax.ppermute(x, "blk", xor_pairs(n, k)) for k in range(1, n // 2)]


def rotate_in_kernel(lower, near_ref, far_ref, basis_ref, order_ref, message_ref):
    acts = jnp.concatenate([near_ref[...], far_ref[...]], axis=0)
    rotated = jnp.dot(acts, basis_ref[...], preferred_element_type=jnp.float32)
    ordered = jnp.dot(
        order_ref[...], rotated.astype(jnp.bfloat16), preferred_element_type=jnp.float32
    )
    half = message_ref.shape[0] - ordered.shape[0]
    message_ref[:half, :] = basis_ref[lower : lower + half, :]
    message_ref[half:, :] = ordered.astype(jnp.bfloat16)


def rotate_out_kernel(near_ref, far_ref, basis_ref, order_ref, out_ref, total):
    step = pl.program_id(0)

    @pl.when(step == 0)
    def _():
        total[...] = jnp.zeros_like(total)

    grads = jnp.concatenate([near_ref[...], far_ref[...]], axis=0)
    total[...] += jnp.dot(grads, basis_ref[...], preferred_element_type=jnp.float32)

    @pl.when(step == pl.num_programs(0) - 1)
    def _():
        aligned = jnp.dot(
            order_ref[...], total[...].astype(jnp.bfloat16), preferred_element_type=jnp.float32
        )
        out_ref[...] = aligned.T.astype(jnp.bfloat16)


def window_kernel(
    n,
    scale,
    tiles_ref,
    sources_ref,
    blocks_ref,
    aligned_ref,
    window_ref,
    eigen_ref,
    *refs,
):
    pieces = refs[: 2 * n]
    send_ref, keep_ref = refs[2 * n : 2 * n + 2]
    basis, rotated, damped, projected, result, piece_sem, eigen_sem = refs[2 * n + 2 :]
    width = basis.shape[2]
    half = basis.shape[1] // 2
    per_piece = width // LANES

    def eigen_copy(at):
        source = sources_ref[at // per_piece] * per_piece + at % per_piece
        column = pl.multiple_of(tiles_ref[source] * LANES, LANES)
        return pltpu.make_async_copy(
            eigen_ref.at[:, pl.ds(column, LANES)], damped.at[at], eigen_sem.at[at]
        )

    def piece_copies(at):
        upper, lower = pieces[2 * at], pieces[2 * at + 1]
        return (
            pltpu.make_async_copy(upper, basis.at[at, pl.ds(0, half)], piece_sem.at[at, 0]),
            pltpu.make_async_copy(
                lower.at[pl.ds(0, half)], basis.at[at, pl.ds(half, half)], piece_sem.at[at, 1]
            ),
            pltpu.make_async_copy(
                lower.at[pl.ds(half, rotated.shape[1])], rotated.at[at], piece_sem.at[at, 2]
            ),
        )

    for at in range(n):
        for copy in piece_copies(at):
            copy.start()
        for tile in range(per_piece):
            eigen_copy(at * per_piece + tile).start()
    projected[...] = jnp.zeros_like(projected)
    for at in range(n):
        for copy in piece_copies(at):
            copy.wait()

    @pl.loop(0, n)
    def _(at):
        grad = jnp.dot(aligned_ref[...], rotated[at], preferred_element_type=jnp.float32)
        parts = []
        for tile in range(per_piece):
            eigen_copy(at * per_piece + tile).wait()
            columns = grad[:, tile * LANES : (tile + 1) * LANES]
            parts.append((columns / damped[at * per_piece + tile]).astype(jnp.bfloat16))
        scaled = jnp.concatenate(parts, axis=1)
        projected[...] += lax.dot_general(
            scaled, basis[at], (((1,), (1,)), ((), ())), preferred_element_type=jnp.float32
        )

    result[...] = scale * jnp.dot(
        window_ref[...], projected[...].astype(jnp.bfloat16), preferred_element_type=jnp.float32
    )
    rows = keep_ref.shape[1]
    for k in range(n // 2):
        keep_ref[k] = result[pl.ds(pl.multiple_of(blocks_ref[k] * rows, rows), rows), :]
        other = result[pl.ds(pl.multiple_of(blocks_ref[n // 2 + k] * rows, rows), rows), :]
        send_ref[k] = other.astype(jnp.bfloat16)


def add_core_kernel(keep_ref, got_ref, own_ref, *out_refs):
    own_ref[...] = keep_ref[0] + got_ref[0].astype(jnp.float32)
    for k, out_ref in enumerate(out_refs, 1):
        out_ref[...] = (keep_ref[k] + got_ref[k].astype(jnp.float32)).astype(jnp.bfloat16)


def add_chips_kernel(own_ref, *refs):
    total = own_ref[...]
    for ref in refs[:-1]:
        total += ref[...].astype(jnp.float32)
    refs[-1][...] = total


VMEM = pl.BlockSpec(memory_space=pltpu.VMEM)
SMEM = pl.BlockSpec(memory_space=pltpu.SMEM)
ANY = pl.BlockSpec(memory_space=pl.ANY)


def one_hot(index):
    columns = lax.broadcasted_iota(jnp.int32, (index.shape[0], index.shape[0]), 1)
    return (index[:, None] == columns).astype(jnp.bfloat16)


def rows_of(blocks, tok_rows):
    return (blocks[:, None] * tok_rows + jnp.arange(tok_rows)[None, :]).reshape(-1)


def ring_body(n, grad_out, activations, basis_out, basis_in, eigenvalues, tile_order, block_map):
    tok_rows, full_out = grad_out.shape
    tile_width = basis_out.shape[1]
    full_in, in_width = basis_in.shape
    tokens = n * tok_rows
    half = WC // 2
    me = lax.axis_index("blk")
    pick = lambda table: lax.dynamic_index_in_dim(jnp.asarray(table), me, 0, keepdims=False)

    acts = jnp.concatenate(direct_gather(activations, n), axis=0)
    acts_far = lax.ppermute(acts, "blk", core_pairs(n))
    order_in = one_hot(rows_of(pick(place_of(xor_sources(n))), tok_rows))
    message = pl.pallas_call(
        functools.partial(rotate_in_kernel, half),
        out_shape=jax.ShapeDtypeStruct((half + tokens, in_width), jnp.bfloat16),
        in_specs=[VMEM] * 4,
        out_specs=VMEM,
        compiler_params=pltpu.CompilerParams(vmem_limit_bytes=16 * MIB),
        name="rotate_in",
    )(acts, acts_far, basis_in, order_in)

    grads = jnp.concatenate(ring_gather(grad_out, n, True), axis=0)
    grads_far = lax.ppermute(grads, "blk", core_pairs(n))
    order_out = one_hot(rows_of(jnp.take(pick(place_of(ring_sources(n))), block_map), tok_rows))
    depth = 1024
    aligned = pl.pallas_call(
        rotate_out_kernel,
        grid=(full_out // depth,),
        out_shape=jax.ShapeDtypeStruct((tile_width, tokens), jnp.bfloat16),
        in_specs=[
            pl.BlockSpec((tokens // 2, depth), lambda k: (0, k)),
            pl.BlockSpec((tokens // 2, depth), lambda k: (0, k)),
            pl.BlockSpec((depth, tile_width), lambda k: (k, 0)),
            pl.BlockSpec((tokens, tokens), lambda k: (0, 0)),
        ],
        out_specs=pl.BlockSpec((tile_width, tokens), lambda k: (0, 0)),
        scratch_shapes=[pltpu.VMEM((tokens, tile_width), jnp.float32)],
        compiler_params=pltpu.CompilerParams(vmem_limit_bytes=24 * MIB),
        cost_estimate=pl.CostEstimate(
            flops=2 * tokens * full_out * tile_width,
            bytes_accessed=2 * full_out * tile_width,
            transcendentals=0,
        ),
        name="rotate_out",
    )(grads, grads_far, basis_out, order_out)

    upper = ring_gather(basis_in[:half], n, True)
    lower = ring_gather(message, n, False)
    swap = lambda x: lax.ppermute(x, "blk", core_pairs(n))
    pieces = []
    for top, bottom in zip(upper, lower):
        pieces += [top, bottom]
    pieces += [swap(piece) for piece in pieces]

    rows = WR // n
    send, keep = pl.pallas_call(
        functools.partial(window_kernel, n, 1.0 / tokens),
        out_shape=(
            jax.ShapeDtypeStruct((n // 2, rows, WC), jnp.bfloat16),
            jax.ShapeDtypeStruct((n // 2, rows, WC), jnp.float32),
        ),
        grid=(1,),
        in_specs=[
            SMEM,
            SMEM,
            SMEM,
            pl.BlockSpec((tile_width, tokens), lambda i: (0, 0)),
            pl.BlockSpec((WR, tile_width), lambda i: (0, 0)),
        ]
        + [ANY] * (2 * n + 1),
        out_specs=(VMEM, VMEM),
        scratch_shapes=[
            pltpu.VMEM((n, WC, in_width), jnp.bfloat16),
            pltpu.VMEM((n, tokens, in_width), jnp.bfloat16),
            pltpu.VMEM((full_in // LANES, tile_width, LANES), jnp.float32),
            pltpu.VMEM((tile_width, WC), jnp.float32),
            pltpu.VMEM((WR, WC), jnp.float32),
            pltpu.SemaphoreType.DMA((n, 3)),
            pltpu.SemaphoreType.DMA((full_in // LANES,)),
        ],
        compiler_params=pltpu.CompilerParams(vmem_limit_bytes=48 * MIB),
        cost_estimate=pl.CostEstimate(
            flops=2 * tile_width * full_in * (WC + tokens) + 2 * WR * tile_width * WC,
            bytes_accessed=4 * tile_width * full_in + 2 * WC * full_in,
            transcendentals=0,
        ),
        name="window",
    )(
        tile_order,
        pick(ring_sources(n)),
        pick(xor_sources(n)),
        aligned,
        basis_out,
        eigenvalues,
        *pieces,
    )

    got = swap(send)
    block = jax.ShapeDtypeStruct((rows, WC), jnp.bfloat16)
    own, *parts = pl.pallas_call(
        add_core_kernel,
        out_shape=[jax.ShapeDtypeStruct((rows, WC), jnp.float32)] + [block] * (n // 2 - 1),
        in_specs=[VMEM, VMEM],
        out_specs=[VMEM] * (n // 2),
        name="add_core",
    )(keep, got)
    arrived = [lax.ppermute(x, "blk", xor_pairs(n, k)) for k, x in enumerate(parts, 1)]
    return pl.pallas_call(
        add_chips_kernel,
        out_shape=jax.ShapeDtypeStruct((rows, WC), jnp.float32),
        in_specs=[VMEM] * (n // 2),
        out_specs=VMEM,
        name="add_chips",
    )(own, *arrived)


def gather_body(grad_out, activations, basis_out, basis_in, eigenvalues, tile_order, block_map):
    n_blocks = lax.axis_size("blk")
    tile_width = basis_out.shape[1]
    tok_rows = grad_out.shape[0]
    full_in = eigenvalues.shape[1]
    tokens = n_blocks * tok_rows
    dot = functools.partial(jnp.dot, preferred_element_type=jnp.float32)
    in_rows = lax.all_gather(basis_in[:WC], "blk", axis=1, tiled=True)
    acts = lax.all_gather(activations, "blk", axis=0, tiled=True)
    in_tile = dot(acts, basis_in).astype(jnp.bfloat16)
    rotated_in = lax.all_gather(in_tile, "blk", axis=1, tiled=True)
    grads = lax.all_gather(grad_out, "blk", axis=0, tiled=True)
    rotated_out = dot(grads, basis_out).astype(jnp.bfloat16)
    aligned = jnp.take(
        rotated_out.reshape(n_blocks, tok_rows, tile_width), block_map, axis=0
    ).reshape(tokens, tile_width)
    grad_tile = dot(aligned.T, rotated_in) / tokens
    damped = jnp.take(
        eigenvalues.reshape(tile_width, full_in // LANES, LANES), tile_order, axis=1
    ).reshape(tile_width, full_in)
    scaled = (grad_tile / damped).astype(jnp.bfloat16)
    projected = dot(scaled, in_rows.T).astype(jnp.bfloat16)
    return lax.psum_scatter(
        dot(basis_out[:WR], projected), "blk", scatter_dimension=0, tiled=True
    )


def solution(mesh):
    n = mesh.shape["blk"]

    def body(*args):
        wide = args[3].shape[1] % LANES == 0 and args[2].shape[1] % LANES == 0
        if wide and WR % (16 * n) == 0:
            return ring_body(n, *args)
        return gather_body(*args)

    placed = (
        P(("grp", "blk"), None),
        P(("grp", "blk"), None),
        P(None, "blk"),
        P(None, "blk"),
        P("blk", None),
        P(),
        P(),
    )
    return jax.shard_map(
        body, mesh=mesh, in_specs=placed, out_specs=P(("grp", "blk"), None), check_vma=False
    )
```

```python
import functools

import jax
import jax.numpy as jnp
import numpy as np
from jax import lax
from jax.experimental import pallas as pl
from jax.experimental.pallas import tpu as pltpu
from jax.sharding import PartitionSpec as P

WR = 768
WC = 512
LANES = 128
MIB = 1 << 20


def ring_of(n):
    chips = n // 2
    return [*range(0, chips, 2), *range(chips - 1, 0, -2)]


def shift_pairs(n, by):
    ring = ring_of(n)
    return [
        (2 * ring[p] + c, 2 * ring[(p + by) % len(ring)] + c)
        for p in range(len(ring))
        for c in range(2)
    ]


def xor_pairs(n, key):
    return [(b, b ^ key) for b in range(n)]


def swap(x, n):
    return lax.ppermute(x, "blk", xor_pairs(n, 1))


def planes(n):
    return [list(range(c, n, 2)) for c in range(2)]


def ring_sources(n):
    ring = ring_of(n)
    table = np.zeros((n, n), np.int32)
    for b in range(n):
        place = ring.index(b // 2)
        for k in range(n // 2):
            chip = ring[(place - k) % len(ring)]
            table[b, k] = 2 * chip + b % 2
            table[b, n // 2 + k] = 2 * chip + 1 - b % 2
    return table


def plane_sources(n):
    return np.array([[2 * (k % (n // 2)) + (b + k // (n // 2)) % 2 for k in range(n)] for b in range(n)], np.int32)


def doubled_sources(n):
    keys = [0]
    step = n // 4
    while step:
        keys += [k ^ step for k in keys]
        step //= 2
    return np.array([[b ^ (2 * k + c) for c in range(2) for k in keys] for b in range(n)], np.int32)


def place_of(table):
    return np.argsort(table, axis=1).astype(np.int32)


def ring_gather(x, n):
    chips = n // 2
    pieces = [None] * chips
    pieces[0] = x
    right, left = x, x
    for step in range(1, chips // 2 + 1):
        right = lax.ppermute(right, "blk", shift_pairs(n, 1))
        pieces[step] = right
        if step < chips // 2:
            left = lax.ppermute(left, "blk", shift_pairs(n, -1))
            pieces[chips - step] = left
    return pieces


def doubling_gather(x, n):
    x = x[None]
    step = n // 2
    while step > 1:
        x = jnp.concatenate([x, lax.ppermute(x, "blk", xor_pairs(n, step))], axis=0)
        step //= 2
    return x


def plane_exchange(x, n):
    return lax.all_to_all(x, "blk", 0, 0, axis_index_groups=planes(n), tiled=True)


def plane_gather(x, n):
    return plane_exchange(jnp.broadcast_to(x[None], (n // 2, *x.shape)), n)


def rotate_in_kernel(near_ref, far_ref, basis_ref, order_ref, out_ref):
    acts = jnp.concatenate([near_ref[...], far_ref[...]], axis=0)
    rotated = jnp.dot(acts, basis_ref[...], preferred_element_type=jnp.float32)
    ordered = jnp.dot(
        order_ref[...], rotated.astype(jnp.bfloat16), preferred_element_type=jnp.float32
    )
    out_ref[...] = ordered.astype(jnp.bfloat16)


def rotate_out_kernel(near_ref, far_ref, basis_ref, order_ref, out_ref, total):
    step = pl.program_id(0)

    @pl.when(step == 0)
    def _():
        total[...] = jnp.zeros_like(total)

    grads = jnp.concatenate([near_ref[...], far_ref[...]], axis=0)
    total[...] += jnp.dot(grads, basis_ref[...], preferred_element_type=jnp.float32)

    @pl.when(step == pl.num_programs(0) - 1)
    def _():
        aligned = jnp.dot(
            order_ref[...], total[...].astype(jnp.bfloat16), preferred_element_type=jnp.float32
        )
        out_ref[...] = aligned.T.astype(jnp.bfloat16)


def scale_kernel(tiles_ref, me_ref, aligned_ref, near_ref, far_ref, *refs):
    out_ref = refs[-1]
    at = pl.program_id(0)
    mine = lax.rem(at, 2) == me_ref[0]
    rotated = jnp.where(mine, near_ref[at // 2], far_ref[at // 2])
    grad = jnp.dot(aligned_ref[...], rotated, preferred_element_type=jnp.float32)
    for tile, damped_ref in enumerate(refs[:-1]):
        lanes = slice(tile * LANES, (tile + 1) * LANES)
        damped = damped_ref[...]
        inverse = pl.reciprocal(damped, approx=True)
        inverse = inverse * (2.0 - damped * inverse)
        out_ref[:, lanes] = (grad[:, lanes] * inverse).astype(jnp.bfloat16)


def window_kernel(n, scale, sources_ref, blocks_ref, window_ref, scaled_ref, *refs):
    pieces = refs[:n]
    send_ref, keep_ref = refs[n : n + 2]
    basis, projected, result, sem = refs[n + 2 :]
    chips = n // 2
    width = basis.shape[2]

    def copy_of(at):
        return pltpu.make_async_copy(pieces[at], basis.at[at % chips, at // chips], sem.at[at])

    for at in range(n):
        copy_of(at).start()
    projected[...] = jnp.zeros_like(projected)
    for at in range(n):
        copy_of(at).wait()

    @pl.loop(0, chips)
    def _(at):
        total = projected[...]
        for other in range(2):
            source = sources_ref[other * chips + at]
            columns = pl.ds(pl.multiple_of(source * width, width), width)
            total += jnp.dot(
                scaled_ref[:, columns], basis[at, other], preferred_element_type=jnp.float32
            )
        projected[...] = total

    result[...] = scale * jnp.dot(
        window_ref[...], projected[...].astype(jnp.bfloat16), preferred_element_type=jnp.float32
    )
    rows = keep_ref.shape[1]
    for k in range(chips):
        keep_ref[k] = result[pl.ds(pl.multiple_of(blocks_ref[k] * rows, rows), rows), :]
        other = result[pl.ds(pl.multiple_of(blocks_ref[chips + k] * rows, rows), rows), :]
        send_ref[k] = other.astype(jnp.bfloat16)


def add_core_kernel(keep_ref, got_ref, out_ref):
    out_ref[...] = (keep_ref[...] + got_ref[...].astype(jnp.float32)).astype(jnp.bfloat16)


def add_chips_kernel(parts_ref, out_ref):
    out_ref[...] = jnp.sum(parts_ref[...].astype(jnp.float32), axis=0)


VMEM = pl.BlockSpec(memory_space=pltpu.VMEM)
SMEM = pl.BlockSpec(memory_space=pltpu.SMEM)
ANY = pl.BlockSpec(memory_space=pl.ANY)


def one_hot(index):
    columns = lax.broadcasted_iota(jnp.int32, (index.shape[0], index.shape[0]), 1)
    return (index[:, None] == columns).astype(jnp.bfloat16)


def rows_of(blocks, tok_rows):
    return (blocks[:, None] * tok_rows + jnp.arange(tok_rows)[None, :]).reshape(-1)


def ring_body(n, grad_out, activations, basis_out, basis_in, eigenvalues, tile_order, block_map):
    tok_rows, full_out = grad_out.shape
    tile_width = basis_out.shape[1]
    full_in, in_width = basis_in.shape
    tokens = n * tok_rows
    chips = n // 2
    me = lax.axis_index("blk")
    pick = lambda table: lax.dynamic_index_in_dim(jnp.asarray(table), me, 0, keepdims=False)

    acts = plane_gather(activations, n).reshape(tokens // 2, full_in)
    order_in = one_hot(rows_of(pick(place_of(plane_sources(n))), tok_rows))
    rotated = pl.pallas_call(
        rotate_in_kernel,
        out_shape=jax.ShapeDtypeStruct((tokens, in_width), jnp.bfloat16),
        in_specs=[VMEM] * 4,
        out_specs=VMEM,
        compiler_params=pltpu.CompilerParams(vmem_limit_bytes=16 * MIB),
        name="rotate_in",
    )(acts, swap(acts, n), basis_in, order_in)
    rotated = plane_gather(rotated, n)
    rotated_far = swap(rotated, n)

    grads = doubling_gather(grad_out, n).reshape(tokens // 2, full_out)
    order_out = one_hot(rows_of(jnp.take(pick(place_of(doubled_sources(n))), block_map), tok_rows))
    depth = 1024
    aligned = pl.pallas_call(
        rotate_out_kernel,
        grid=(full_out // depth,),
        out_shape=jax.ShapeDtypeStruct((tile_width, tokens), jnp.bfloat16),
        in_specs=[
            pl.BlockSpec((tokens // 2, depth), lambda k: (0, k)),
            pl.BlockSpec((tokens // 2, depth), lambda k: (0, k)),
            pl.BlockSpec((depth, tile_width), lambda k: (k, 0)),
            pl.BlockSpec((tokens, tokens), lambda k: (0, 0)),
        ],
        out_specs=pl.BlockSpec((tile_width, tokens), lambda k: (0, 0)),
        scratch_shapes=[pltpu.VMEM((tokens, tile_width), jnp.float32)],
        compiler_params=pltpu.CompilerParams(vmem_limit_bytes=44 * MIB),
        cost_estimate=pl.CostEstimate(
            flops=2 * tokens * full_out * tile_width,
            bytes_accessed=2 * full_out * tile_width,
            transcendentals=0,
        ),
        name="rotate_out",
    )(grads, swap(grads, n), basis_out, order_out)

    per_piece = in_width // LANES

    def eigen_spec(tile):
        return pl.BlockSpec(
            (tile_width, LANES), lambda j, tiles, core: (0, tiles[j * per_piece + tile])
        )

    whole = lambda *shape: pl.BlockSpec(shape, lambda j, tiles, core: (0,) * len(shape))
    scaled = pl.pallas_call(
        scale_kernel,
        out_shape=jax.ShapeDtypeStruct((tile_width, full_in), jnp.bfloat16),
        grid_spec=pltpu.PrefetchScalarGridSpec(
            num_scalar_prefetch=2,
            grid=(n,),
            in_specs=[
                whole(tile_width, tokens),
                whole(chips, tokens, in_width),
                whole(chips, tokens, in_width),
            ]
            + [eigen_spec(tile) for tile in range(per_piece)],
            out_specs=pl.BlockSpec((tile_width, in_width), lambda j, tiles, core: (0, j)),
        ),
        compiler_params=pltpu.CompilerParams(vmem_limit_bytes=48 * MIB),
        cost_estimate=pl.CostEstimate(
            flops=2 * tile_width * full_in * tokens,
            bytes_accessed=6 * tile_width * full_in,
            transcendentals=tile_width * full_in,
        ),
        name="scale",
    )(
        tile_order,
        lax.rem(me, 2).reshape(1),
        aligned,
        rotated,
        rotated_far,
        *[eigenvalues] * per_piece,
    )

    pieces = ring_gather(basis_in[:WC].T, n)
    pieces += [swap(piece, n) for piece in pieces]

    rows = WR // n
    send, keep = pl.pallas_call(
        functools.partial(window_kernel, n, 1.0 / tokens),
        out_shape=(
            jax.ShapeDtypeStruct((chips, rows, WC), jnp.bfloat16),
            jax.ShapeDtypeStruct((chips, rows, WC), jnp.float32),
        ),
        grid=(1,),
        in_specs=[
            SMEM,
            SMEM,
            pl.BlockSpec((WR, tile_width), lambda i: (0, 0)),
            pl.BlockSpec((tile_width, full_in), lambda i: (0, 0)),
        ]
        + [ANY] * n,
        out_specs=(VMEM, VMEM),
        scratch_shapes=[
            pltpu.VMEM((chips, 2, in_width, WC), jnp.bfloat16),
            pltpu.VMEM((tile_width, WC), jnp.float32),
            pltpu.VMEM((WR, WC), jnp.float32),
            pltpu.SemaphoreType.DMA((n,)),
        ],
        compiler_params=pltpu.CompilerParams(vmem_limit_bytes=40 * MIB),
        cost_estimate=pl.CostEstimate(
            flops=2 * tile_width * full_in * WC + 2 * WR * tile_width * WC,
            bytes_accessed=2 * tile_width * full_in + 2 * WC * full_in,
            transcendentals=0,
        ),
        name="window",
    )(pick(ring_sources(n)), pick(plane_sources(n)), basis_out, scaled, *pieces)

    summed = pl.pallas_call(
        add_core_kernel,
        out_shape=jax.ShapeDtypeStruct((chips, rows, WC), jnp.bfloat16),
        in_specs=[VMEM, VMEM],
        out_specs=VMEM,
        name="add_core",
    )(keep, swap(send, n))
    return pl.pallas_call(
        add_chips_kernel,
        out_shape=jax.ShapeDtypeStruct((rows, WC), jnp.float32),
        in_specs=[VMEM],
        out_specs=VMEM,
        name="add_chips",
    )(plane_exchange(summed, n))


def gather_body(grad_out, activations, basis_out, basis_in, eigenvalues, tile_order, block_map):
    n_blocks = lax.axis_size("blk")
    tile_width = basis_out.shape[1]
    tok_rows = grad_out.shape[0]
    full_in = eigenvalues.shape[1]
    tokens = n_blocks * tok_rows
    dot = functools.partial(jnp.dot, preferred_element_type=jnp.float32)
    in_rows = lax.all_gather(basis_in[:WC], "blk", axis=1, tiled=True)
    acts = lax.all_gather(activations, "blk", axis=0, tiled=True)
    in_tile = dot(acts, basis_in).astype(jnp.bfloat16)
    rotated_in = lax.all_gather(in_tile, "blk", axis=1, tiled=True)
    grads = lax.all_gather(grad_out, "blk", axis=0, tiled=True)
    rotated_out = dot(grads, basis_out).astype(jnp.bfloat16)
    aligned = jnp.take(
        rotated_out.reshape(n_blocks, tok_rows, tile_width), block_map, axis=0
    ).reshape(tokens, tile_width)
    grad_tile = dot(aligned.T, rotated_in) / tokens
    damped = jnp.take(
        eigenvalues.reshape(tile_width, full_in // LANES, LANES), tile_order, axis=1
    ).reshape(tile_width, full_in)
    scaled = (grad_tile / damped).astype(jnp.bfloat16)
    projected = dot(scaled, in_rows.T).astype(jnp.bfloat16)
    return lax.psum_scatter(
        dot(basis_out[:WR], projected), "blk", scatter_dimension=0, tiled=True
    )


def solution(mesh):
    n = mesh.shape["blk"]

    def body(*args):
        wide = args[3].shape[1] % LANES == 0 and args[2].shape[1] % LANES == 0
        if wide and WR % (16 * n) == 0:
            return ring_body(n, *args)
        return gather_body(*args)

    placed = (
        P(("grp", "blk"), None),
        P(("grp", "blk"), None),
        P(None, "blk"),
        P(None, "blk"),
        P("blk", None),
        P(),
        P(),
    )
    return jax.shard_map(
        body, mesh=mesh, in_specs=placed, out_specs=P(("grp", "blk"), None), check_vma=False
    )
```

```python
import functools

import jax
import jax.numpy as jnp
import numpy as np
from jax import lax
from jax.experimental import pallas as pl
from jax.experimental.pallas import tpu as pltpu
from jax.sharding import PartitionSpec as P

WR = 768
WC = 512
LANES = 128
MIB = 1 << 20


def ring_of(n):
    chips = n // 2
    return [*range(0, chips, 2), *range(chips - 1, 0, -2)]


def shift_pairs(n, by):
    ring = ring_of(n)
    return [
        (2 * ring[p] + c, 2 * ring[(p + by) % len(ring)] + c)
        for p in range(len(ring))
        for c in range(2)
    ]


def xor_pairs(n, key):
    return [(b, b ^ key) for b in range(n)]


def swap(x, n):
    return lax.ppermute(x, "blk", xor_pairs(n, 1))


def planes(n):
    return [list(range(c, n, 2)) for c in range(2)]


def ring_sources(n):
    ring = ring_of(n)
    table = np.zeros((n, n), np.int32)
    for b in range(n):
        place = ring.index(b // 2)
        for k in range(n // 2):
            chip = ring[(place - k) % len(ring)]
            table[b, k] = 2 * chip + b % 2
            table[b, n // 2 + k] = 2 * chip + 1 - b % 2
    return table


def plane_sources(n):
    return np.array([[2 * (k % (n // 2)) + (b + k // (n // 2)) % 2 for k in range(n)] for b in range(n)], np.int32)


def doubled_sources(n):
    keys = [0]
    step = n // 4
    while step:
        keys += [k ^ step for k in keys]
        step //= 2
    return np.array([[b ^ (2 * k + c) for c in range(2) for k in keys] for b in range(n)], np.int32)


def place_of(table):
    return np.argsort(table, axis=1).astype(np.int32)


def doubling_gather(x, n):
    x = x[None]
    step = n // 2
    while step > 1:
        x = jnp.concatenate([x, lax.ppermute(x, "blk", xor_pairs(n, step))], axis=0)
        step //= 2
    return x


def plane_exchange(x, n):
    return lax.all_to_all(x, "blk", 0, 0, axis_index_groups=planes(n), tiled=True)


def plane_gather(x, n):
    return plane_exchange(jnp.broadcast_to(x[None], (n // 2, *x.shape)), n)


def rotate_in_kernel(near_ref, far_ref, basis_ref, order_ref, out_ref):
    acts = jnp.concatenate([near_ref[...], far_ref[...]], axis=0)
    rotated = jnp.dot(acts, basis_ref[...], preferred_element_type=jnp.float32)
    ordered = jnp.dot(
        order_ref[...], rotated.astype(jnp.bfloat16), preferred_element_type=jnp.float32
    )
    out_ref[...] = ordered.astype(jnp.bfloat16)


def rotate_out_kernel(near_ref, far_ref, basis_ref, order_ref, out_ref, basis, total, sem):
    steps, depth = basis.shape[:2]

    def copy_of(step):
        rows = pl.ds(pl.multiple_of(step * depth, depth), depth)
        return pltpu.make_async_copy(basis_ref.at[rows], basis.at[step], sem.at[step])

    @pl.loop(0, steps)
    def _(step):
        copy_of(step).start()

    total[...] = jnp.zeros_like(total)

    @pl.loop(0, steps)
    def _(step):
        columns = pl.ds(pl.multiple_of(step * depth, depth), depth)
        grads = jnp.concatenate([near_ref[:, columns], far_ref[:, columns]], axis=0)
        copy_of(step).wait()
        total[...] += jnp.dot(grads, basis[step], preferred_element_type=jnp.float32)

    aligned = jnp.dot(
        order_ref[...], total[...].astype(jnp.bfloat16), preferred_element_type=jnp.float32
    )
    out_ref[...] = aligned.T.astype(jnp.bfloat16)


def scale_kernel(
    tiles_ref, me_ref, aligned_ref, near_ref, far_ref, eigen_ref, out_ref, damped, sem
):
    tiles = damped.shape[0]
    width = near_ref.shape[2]
    per_piece = width // LANES

    def copy_of(tile):
        columns = pl.ds(pl.multiple_of(tiles_ref[tile] * LANES, LANES), LANES)
        return pltpu.make_async_copy(eigen_ref.at[:, columns], damped.at[tile], sem.at[tile])

    @pl.loop(0, tiles)
    def _(tile):
        copy_of(tile).start()

    @pl.loop(0, tiles // per_piece)
    def _(at):
        mine = lax.rem(at, 2) == me_ref[0]
        rotated = jnp.where(mine, near_ref[at // 2], far_ref[at // 2])
        grad = jnp.dot(aligned_ref[...], rotated, preferred_element_type=jnp.float32)
        for part in range(per_piece):
            tile = at * per_piece + part
            copy_of(tile).wait()
            eigen = damped[tile]
            inverse = pl.reciprocal(eigen, approx=True)
            inverse = inverse * (2.0 - eigen * inverse)
            columns = pl.ds(pl.multiple_of(tile * LANES, LANES), LANES)
            scaled = grad[:, part * LANES : (part + 1) * LANES] * inverse
            out_ref[:, columns] = scaled.astype(jnp.bfloat16)


def window_kernel(n, scale, sources_ref, blocks_ref, window_ref, scaled_ref, *refs):
    pieces = refs[:n]
    send_ref, keep_ref = refs[n : n + 2]
    basis, projected, result, sem = refs[n + 2 :]
    chips = n // 2
    width = basis.shape[2]

    def copy_of(at):
        return pltpu.make_async_copy(pieces[at], basis.at[at % chips, at // chips], sem.at[at])

    for at in range(n):
        copy_of(at).start()
    projected[...] = jnp.zeros_like(projected)
    for at in range(n):
        copy_of(at).wait()

    @pl.loop(0, chips)
    def _(at):
        total = projected[...]
        for other in range(2):
            source = sources_ref[other * chips + at]
            columns = pl.ds(pl.multiple_of(source * width, width), width)
            total += jnp.dot(
                scaled_ref[:, columns], basis[at, other], preferred_element_type=jnp.float32
            )
        projected[...] = total

    result[...] = scale * jnp.dot(
        window_ref[...], projected[...].astype(jnp.bfloat16), preferred_element_type=jnp.float32
    )
    rows = keep_ref.shape[1]
    for k in range(chips):
        keep_ref[k] = result[pl.ds(pl.multiple_of(blocks_ref[k] * rows, rows), rows), :]
        other = result[pl.ds(pl.multiple_of(blocks_ref[chips + k] * rows, rows), rows), :]
        send_ref[k] = other.astype(jnp.bfloat16)


def add_core_kernel(keep_ref, got_ref, out_ref):
    out_ref[...] = (keep_ref[...] + got_ref[...].astype(jnp.float32)).astype(jnp.bfloat16)


def add_chips_kernel(parts_ref, out_ref):
    out_ref[...] = jnp.sum(parts_ref[...].astype(jnp.float32), axis=0)


VMEM = pl.BlockSpec(memory_space=pltpu.VMEM)
SMEM = pl.BlockSpec(memory_space=pltpu.SMEM)
ANY = pl.BlockSpec(memory_space=pl.ANY)


def one_hot(index):
    columns = lax.broadcasted_iota(jnp.int32, (index.shape[0], index.shape[0]), 1)
    return (index[:, None] == columns).astype(jnp.bfloat16)


def rows_of(blocks, tok_rows):
    return (blocks[:, None] * tok_rows + jnp.arange(tok_rows)[None, :]).reshape(-1)


def ring_body(n, grad_out, activations, basis_out, basis_in, eigenvalues, tile_order, block_map):
    tok_rows, full_out = grad_out.shape
    tile_width = basis_out.shape[1]
    full_in, in_width = basis_in.shape
    tokens = n * tok_rows
    chips = n // 2
    me = lax.axis_index("blk")
    pick = lambda table: lax.dynamic_index_in_dim(jnp.asarray(table), me, 0, keepdims=False)

    acts = plane_gather(activations, n).reshape(tokens // 2, full_in)
    order_in = one_hot(rows_of(pick(place_of(plane_sources(n))), tok_rows))
    rotated = pl.pallas_call(
        rotate_in_kernel,
        out_shape=jax.ShapeDtypeStruct((tokens, in_width), jnp.bfloat16),
        in_specs=[VMEM] * 4,
        out_specs=VMEM,
        compiler_params=pltpu.CompilerParams(vmem_limit_bytes=16 * MIB),
        name="rotate_in",
    )(acts, swap(acts, n), basis_in, order_in)
    rotated = plane_gather(rotated, n)

    own = basis_in[:WC].T
    right = [own]
    left = [own]
    early = max(chips // 2 - 2, 1)
    for _ in range(early):
        right.append(lax.ppermute(right[-1], "blk", shift_pairs(n, 1)))
        left.append(lax.ppermute(left[-1], "blk", shift_pairs(n, -1)))

    grads = doubling_gather(grad_out, n).reshape(tokens // 2, full_out)
    grads_far = swap(grads, n)
    order_out = one_hot(rows_of(jnp.take(pick(place_of(doubled_sources(n))), block_map), tok_rows))
    grads, grads_far, rotated, right[-1], left[-1] = lax.optimization_barrier(
        (grads, grads_far, rotated, right[-1], left[-1])
    )
    rotated_far = swap(rotated, n)
    for _ in range(early, chips // 2 - 1):
        right.append(lax.ppermute(right[-1], "blk", shift_pairs(n, 1)))
        left.append(lax.ppermute(left[-1], "blk", shift_pairs(n, -1)))
    depth = 1024
    aligned = pl.pallas_call(
        rotate_out_kernel,
        out_shape=jax.ShapeDtypeStruct((tile_width, tokens), jnp.bfloat16),
        in_specs=[VMEM, VMEM, ANY, VMEM],
        out_specs=VMEM,
        scratch_shapes=[
            pltpu.VMEM((full_out // depth, depth, tile_width), jnp.bfloat16),
            pltpu.VMEM((tokens, tile_width), jnp.float32),
            pltpu.SemaphoreType.DMA((full_out // depth,)),
        ],
        compiler_params=pltpu.CompilerParams(vmem_limit_bytes=40 * MIB),
        cost_estimate=pl.CostEstimate(
            flops=2 * tokens * full_out * tile_width,
            bytes_accessed=2 * full_out * tile_width,
            transcendentals=0,
        ),
        name="rotate_out",
    )(grads, grads_far, basis_out, order_out)

    aligned, right[-1], left[-1] = lax.optimization_barrier((aligned, right[-1], left[-1]))
    right.append(lax.ppermute(right[-1], "blk", shift_pairs(n, 1)))
    tiles = full_in // LANES
    scaled = pl.pallas_call(
        scale_kernel,
        out_shape=jax.ShapeDtypeStruct((tile_width, full_in), jnp.bfloat16),
        in_specs=[SMEM, SMEM, VMEM, VMEM, VMEM, ANY],
        out_specs=VMEM,
        scratch_shapes=[
            pltpu.VMEM((tiles, tile_width, LANES), jnp.float32),
            pltpu.SemaphoreType.DMA((tiles,)),
        ],
        compiler_params=pltpu.CompilerParams(vmem_limit_bytes=40 * MIB),
        cost_estimate=pl.CostEstimate(
            flops=2 * tile_width * full_in * tokens,
            bytes_accessed=6 * tile_width * full_in,
            transcendentals=tile_width * full_in,
        ),
        name="scale",
    )(tile_order, lax.rem(me, 2).reshape(1), aligned, rotated, rotated_far, eigenvalues)

    scaled, right[-1] = lax.optimization_barrier((scaled, right[-1]))
    pieces = right + left[:0:-1]
    pieces += [swap(piece, n) for piece in pieces]
    rows = WR // n
    send, keep = pl.pallas_call(
        functools.partial(window_kernel, n, 1.0 / tokens),
        out_shape=(
            jax.ShapeDtypeStruct((chips, rows, WC), jnp.bfloat16),
            jax.ShapeDtypeStruct((chips, rows, WC), jnp.float32),
        ),
        grid=(1,),
        in_specs=[
            SMEM,
            SMEM,
            pl.BlockSpec((WR, tile_width), lambda i: (0, 0)),
            VMEM,
        ]
        + [ANY] * n,
        out_specs=(VMEM, VMEM),
        scratch_shapes=[
            pltpu.VMEM((chips, 2, in_width, WC), jnp.bfloat16),
            pltpu.VMEM((tile_width, WC), jnp.float32),
            pltpu.VMEM((WR, WC), jnp.float32),
            pltpu.SemaphoreType.DMA((n,)),
        ],
        compiler_params=pltpu.CompilerParams(vmem_limit_bytes=36 * MIB),
        cost_estimate=pl.CostEstimate(
            flops=2 * tile_width * full_in * WC + 2 * WR * tile_width * WC,
            bytes_accessed=2 * tile_width * full_in + 2 * WC * full_in,
            transcendentals=0,
        ),
        name="window",
    )(pick(ring_sources(n)), pick(plane_sources(n)), basis_out, scaled, *pieces)

    summed = pl.pallas_call(
        add_core_kernel,
        out_shape=jax.ShapeDtypeStruct((chips, rows, WC), jnp.bfloat16),
        in_specs=[VMEM, VMEM],
        out_specs=VMEM,
        compiler_params=pltpu.CompilerParams(vmem_limit_bytes=8 * MIB),
        name="add_core",
    )(keep, swap(send, n))
    return pl.pallas_call(
        add_chips_kernel,
        out_shape=jax.ShapeDtypeStruct((rows, WC), jnp.float32),
        in_specs=[VMEM],
        out_specs=VMEM,
        compiler_params=pltpu.CompilerParams(vmem_limit_bytes=4 * MIB),
        name="add_chips",
    )(plane_exchange(summed, n))


def gather_body(grad_out, activations, basis_out, basis_in, eigenvalues, tile_order, block_map):
    n_blocks = lax.axis_size("blk")
    tile_width = basis_out.shape[1]
    tok_rows = grad_out.shape[0]
    full_in = eigenvalues.shape[1]
    tokens = n_blocks * tok_rows
    dot = functools.partial(jnp.dot, preferred_element_type=jnp.float32)
    in_rows = lax.all_gather(basis_in[:WC], "blk", axis=1, tiled=True)
    acts = lax.all_gather(activations, "blk", axis=0, tiled=True)
    in_tile = dot(acts, basis_in).astype(jnp.bfloat16)
    rotated_in = lax.all_gather(in_tile, "blk", axis=1, tiled=True)
    grads = lax.all_gather(grad_out, "blk", axis=0, tiled=True)
    rotated_out = dot(grads, basis_out).astype(jnp.bfloat16)
    aligned = jnp.take(
        rotated_out.reshape(n_blocks, tok_rows, tile_width), block_map, axis=0
    ).reshape(tokens, tile_width)
    grad_tile = dot(aligned.T, rotated_in) / tokens
    damped = jnp.take(
        eigenvalues.reshape(tile_width, full_in // LANES, LANES), tile_order, axis=1
    ).reshape(tile_width, full_in)
    scaled = (grad_tile / damped).astype(jnp.bfloat16)
    projected = dot(scaled, in_rows.T).astype(jnp.bfloat16)
    return lax.psum_scatter(
        dot(basis_out[:WR], projected), "blk", scatter_dimension=0, tiled=True
    )


def solution(mesh):
    n = mesh.shape["blk"]

    def body(*args):
        wide = args[3].shape[1] % LANES == 0 and args[2].shape[1] % LANES == 0
        if wide and WR % (16 * n) == 0:
            return ring_body(n, *args)
        return gather_body(*args)

    placed = (
        P(("grp", "blk"), None),
        P(("grp", "blk"), None),
        P(None, "blk"),
        P(None, "blk"),
        P("blk", None),
        P(),
        P(),
    )
    return jax.shard_map(
        body, mesh=mesh, in_specs=placed, out_specs=P(("grp", "blk"), None), check_vma=False
    )
```

```python
import functools

import jax
import jax.numpy as jnp
from jax import lax
from jax.experimental import pallas as pl
from jax.experimental.pallas import tpu as pltpu
from jax.sharding import PartitionSpec as P

WR = 768
WC = 512
LANES = 128
MIB = 1 << 20


def ring_of(n):
    chips = n // 2
    return [*range(0, chips, 2), *range(chips - 1, 0, -2)]


def shift_pairs(n, by):
    ring = ring_of(n)
    return [
        (2 * ring[p] + c, 2 * ring[(p + by) % len(ring)] + c)
        for p in range(len(ring))
        for c in range(2)
    ]


def ring_source(me, steps, other, chips):
    chip, core = me // 2, lax.rem(me, 2)
    place = jnp.where(lax.rem(chip, 2) == 0, chip // 2, chips - 1 - chip // 2)
    place = lax.rem(place + chips - steps, chips)
    chip = jnp.where(place < chips // 2, 2 * place, 2 * (chips - 1 - place) + 1)
    return 2 * chip + (core ^ other)


def xor_pairs(n, key):
    return [(b, b ^ key) for b in range(n)]


def swap(x, n):
    return lax.ppermute(x, "blk", xor_pairs(n, 1))


def plane_exchange(x, n):
    planes = [list(range(c, n, 2)) for c in range(2)]
    return lax.all_to_all(x, "blk", 0, 0, axis_index_groups=planes, tiled=True)


def bits_of(size):
    return size.bit_length() - 1


def held_tokens(me, tokens, tok_rows):
    row = lax.broadcasted_iota(jnp.int32, (tokens, tokens), 1)
    chips = tokens // tok_rows // 2
    place = (row >> bits_of(tok_rows)) & (chips - 1)
    chip = jnp.zeros_like(row)
    for bit in range(bits_of(chips)):
        chip |= ((place >> bit) & 1) << (bits_of(chips) - 1 - bit)
    other = row >> bits_of(tokens // 2)
    device = me ^ (2 * chip + other)
    return (device << bits_of(tok_rows)) + (row & (tok_rows - 1))


def reorder(wanted, held, rotated):
    order = jnp.where(wanted == held, 1.0, 0.0).astype(jnp.bfloat16)
    return jnp.dot(order, rotated.astype(jnp.bfloat16), preferred_element_type=jnp.float32)


def rotate_in_kernel(tok_rows, first, me_ref, near_ref, far_ref, basis_ref, out_ref, basis, sem):
    steps, depth = basis.shape[:2]
    tokens = out_ref.shape[1]

    def copy_of(step):
        return pltpu.make_async_copy(
            basis_ref.at[pl.ds(step * depth, depth)], basis.at[step], sem.at[step]
        )

    for step in range(steps):
        copy_of(step).start()
    rotated = jnp.zeros((tokens, basis.shape[2]), jnp.float32)
    for step in range(steps):
        columns = slice(first + step * depth, first + (step + 1) * depth)
        acts = jnp.concatenate([near_ref[:, columns], far_ref[:, columns]], axis=0)
        copy_of(step).wait()
        rotated += jnp.dot(acts, basis[step], preferred_element_type=jnp.float32)
    wanted = lax.broadcasted_iota(jnp.int32, (tokens, tokens), 0)
    held = held_tokens(me_ref[0], tokens, tok_rows)
    ordered = reorder(wanted, held, rotated).astype(jnp.bfloat16)
    for copy in range(out_ref.shape[0]):
        out_ref[copy] = ordered


def rotate_out_kernel(
    tok_rows, me_ref, map_ref, near_ref, far_ref, basis_ref, out_ref, basis, total, sem
):
    steps, depth = basis.shape[:2]
    tokens = total.shape[0]

    def copy_of(step):
        rows = pl.ds(pl.multiple_of(step * depth, depth), depth)
        return pltpu.make_async_copy(basis_ref.at[rows], basis.at[step], sem.at[step])

    @pl.loop(0, steps)
    def _(step):
        copy_of(step).start()

    total[...] = jnp.zeros_like(total)

    @pl.loop(0, steps)
    def _(step):
        columns = pl.ds(pl.multiple_of(step * depth, depth), depth)
        grads = jnp.concatenate([near_ref[:, columns], far_ref[:, columns]], axis=0)
        copy_of(step).wait()
        total[...] += jnp.dot(grads, basis[step], preferred_element_type=jnp.float32)

    row = lax.broadcasted_iota(jnp.int32, (tokens, tokens), 0)
    block = row >> bits_of(tok_rows)
    wanted = jnp.zeros_like(row)
    for stored in range(tokens // tok_rows):
        wanted = jnp.where(block == stored, map_ref[stored] * tok_rows, wanted)
    wanted += row & (tok_rows - 1)
    held = held_tokens(me_ref[0], tokens, tok_rows)
    out_ref[...] = reorder(wanted, held, total[...]).T.astype(jnp.bfloat16)


def scale_kernel(
    tiles_ref, me_ref, aligned_ref, near_ref, far_ref, eigen_ref, out_ref, damped, sem
):
    blocks, depth = damped.shape[:2]
    chips, _, width = near_ref.shape

    def copy_of(block):
        rows = pl.ds(pl.multiple_of(block * depth, depth), depth)
        return pltpu.make_async_copy(eigen_ref.at[rows], damped.at[block], sem.at[block])

    @pl.loop(0, blocks)
    def _(block):
        copy_of(block).start()

    odd = lax.rem(me_ref[0], 2) == 1

    @pl.loop(0, blocks)
    def _(block):
        rows = pl.ds(pl.multiple_of(block * depth, depth), depth)
        aligned = aligned_ref[rows, :]
        copy_of(block).wait()
        for at in range(2 * chips):
            mine = odd if at % 2 else jnp.logical_not(odd)
            rotated = jnp.where(mine, near_ref[at // 2], far_ref[at // 2])
            grad = jnp.dot(aligned, rotated, preferred_element_type=jnp.float32)
            for first in range(0, width, LANES):
                tile = (at * width + first) // LANES
                lanes = pl.ds(pl.multiple_of(tiles_ref[tile] * LANES, LANES), LANES)
                eigen = damped[block, :, lanes]
                inverse = pl.reciprocal(eigen, approx=True)
                inverse = inverse * (2.0 - eigen * inverse)
                scaled = grad[:, first : first + LANES] * inverse
                out_ref[rows, tile * LANES : (tile + 1) * LANES] = scaled.astype(jnp.bfloat16)


def window_kernel(n, begun, scale, me_ref, window_ref, scaled_ref, *refs):
    pieces = refs[:n]
    send_ref, keep_ref = refs[n : n + 2]
    basis, projected, result, sem = refs[n + 2 :]
    chips = n // 2
    width = basis.shape[2]
    me = me_ref[0]

    for other in range(2):
        for at, piece in zip(begun, pieces[other * chips : (other + 1) * chips]):
            pltpu.make_async_copy(piece, basis.at[at, other], sem.at[at, other]).start()
    projected[...] = jnp.zeros_like(projected)

    @pl.loop(0, chips)
    def _(at):
        total = projected[...]
        for other in range(2):
            source = ring_source(me, at, other, chips)
            columns = pl.ds(pl.multiple_of(source * width, width), width)
            place = basis.at[at, other]
            pltpu.make_async_copy(place, place, sem.at[at, other]).wait()
            total += jnp.dot(
                scaled_ref[:, columns], basis[at, other], preferred_element_type=jnp.float32
            )
        projected[...] = total

    result[...] = scale * jnp.dot(
        window_ref[...], projected[...].astype(jnp.bfloat16), preferred_element_type=jnp.float32
    )
    rows = keep_ref.shape[1]
    core = lax.rem(me, 2)
    for k in range(chips):
        mine = pl.ds(pl.multiple_of((2 * k + core) * rows, rows), rows)
        keep_ref[k] = result[mine, :]
        other = pl.ds(pl.multiple_of((2 * k + 1 - core) * rows, rows), rows)
        send_ref[k] = result[other, :].astype(jnp.bfloat16)


def add_core_kernel(keep_ref, got_ref, out_ref):
    out_ref[...] = (keep_ref[...] + got_ref[...].astype(jnp.float32)).astype(jnp.bfloat16)


def add_chips_kernel(parts_ref, out_ref):
    out_ref[...] = jnp.sum(parts_ref[...].astype(jnp.float32), axis=0)


VMEM = pl.BlockSpec(memory_space=pltpu.VMEM)
SMEM = pl.BlockSpec(memory_space=pltpu.SMEM)
ANY = pl.BlockSpec(memory_space=pl.ANY)


def after(first, *others):
    return lax.optimization_barrier((first, *others))


def ring_body(n, grad_out, activations, basis_out, basis_in, eigenvalues, tile_order, block_map):
    tok_rows, full_out = grad_out.shape
    tile_width = basis_out.shape[1]
    full_in, in_width = basis_in.shape
    tokens = n * tok_rows
    chips = n // 2
    me = lax.axis_index("blk").reshape(1)
    to_right = lambda x: lax.ppermute(x, "blk", shift_pairs(n, 1))
    to_left = lambda x: lax.ppermute(x, "blk", shift_pairs(n, -1))

    both = jnp.concatenate([grad_out, activations], axis=1)[None]
    own = basis_in[:WC].T
    right, left = [own], [own]
    steps = chips // 2
    key = n // 2
    while key > 1:
        got = lax.ppermute(both, "blk", xor_pairs(n, key))
        if key <= 4 and len(right) < steps - 1:
            right.append(to_right(right[-1]))
            left.append(to_left(left[-1]))
            got, right[-1], left[-1] = after(got, right[-1], left[-1])
        both = jnp.concatenate([both, got], axis=0)
        key //= 2
    while len(right) < steps - 1:
        right.append(to_right(right[-1]))
        left.append(to_left(left[-1]))
    both = both.reshape(tokens // 2, full_out + full_in)
    both_far = swap(both, n)

    parts = 4
    rotated = pl.pallas_call(
        functools.partial(rotate_in_kernel, tok_rows, full_out),
        out_shape=jax.ShapeDtypeStruct((chips, tokens, in_width), jnp.bfloat16),
        in_specs=[SMEM, VMEM, VMEM, ANY],
        out_specs=VMEM,
        scratch_shapes=[
            pltpu.VMEM((parts, full_in // parts, in_width), jnp.bfloat16),
            pltpu.SemaphoreType.DMA((parts,)),
        ],
        compiler_params=pltpu.CompilerParams(vmem_limit_bytes=16 * MIB),
        name="rotate_in",
    )(me, both, both_far, basis_in)
    near = right[:-1] + left[1:-1]
    far = [swap(piece, n) for piece in near]
    both, both_far, rotated, right[-1], left[-1], *far = after(
        both, both_far, rotated, right[-1], left[-1], *far
    )
    late = [right[-1], left[-1]]
    rotated = plane_exchange(rotated, n)
    while len(right) < steps:
        right.append(to_right(right[-1]))
        left.append(to_left(left[-1]))

    depth = 1024
    aligned = pl.pallas_call(
        functools.partial(rotate_out_kernel, tok_rows),
        out_shape=jax.ShapeDtypeStruct((tile_width, tokens), jnp.bfloat16),
        in_specs=[SMEM, SMEM, VMEM, VMEM, ANY],
        out_specs=VMEM,
        scratch_shapes=[
            pltpu.VMEM((full_out // depth, depth, tile_width), jnp.bfloat16),
            pltpu.VMEM((tokens, tile_width), jnp.float32),
            pltpu.SemaphoreType.DMA((full_out // depth,)),
        ],
        compiler_params=pltpu.CompilerParams(vmem_limit_bytes=40 * MIB),
        cost_estimate=pl.CostEstimate(
            flops=2 * tokens * full_out * tile_width,
            bytes_accessed=2 * full_out * tile_width,
            transcendentals=0,
        ),
        name="rotate_out",
    )(me, block_map, both, both_far, basis_out)

    aligned, rotated, right[-1], left[-1] = after(aligned, rotated, right[-1], left[-1])
    rotated_far = swap(rotated, n)
    near += late
    late = [swap(piece, n) for piece in late]
    aligned, rotated_far, *late = after(aligned, rotated_far, *late)
    far += late
    late = [right[-1], left[-1], to_right(right[-1])]
    blocks = 8
    scaled = pl.pallas_call(
        scale_kernel,
        out_shape=jax.ShapeDtypeStruct((tile_width, full_in), jnp.bfloat16),
        in_specs=[SMEM, SMEM, VMEM, VMEM, VMEM, ANY],
        out_specs=VMEM,
        scratch_shapes=[
            pltpu.VMEM((blocks, tile_width // blocks, full_in), jnp.float32),
            pltpu.SemaphoreType.DMA((blocks,)),
        ],
        compiler_params=pltpu.CompilerParams(vmem_limit_bytes=40 * MIB),
        cost_estimate=pl.CostEstimate(
            flops=2 * tile_width * full_in * tokens,
            bytes_accessed=6 * tile_width * full_in,
            transcendentals=tile_width * full_in,
        ),
        name="scale",
    )(tile_order, me, aligned, rotated, rotated_far, eigenvalues)

    scaled, *late = after(scaled, *late)
    near += late
    far += [swap(piece, n) for piece in late]
    begun = [*range(steps - 2), *range(chips - 1, chips - steps + 2, -1)]
    begun += [steps - 2, chips - steps + 2, steps - 1, chips - steps + 1, steps]

    rows = WR // n
    send, keep = pl.pallas_call(
        functools.partial(window_kernel, n, begun, 1.0 / tokens),
        out_shape=(
            jax.ShapeDtypeStruct((chips, rows, WC), jnp.bfloat16),
            jax.ShapeDtypeStruct((chips, rows, WC), jnp.float32),
        ),
        grid=(1,),
        in_specs=[SMEM, pl.BlockSpec((WR, tile_width), lambda i: (0, 0)), VMEM] + [ANY] * n,
        out_specs=(VMEM, VMEM),
        scratch_shapes=[
            pltpu.VMEM((chips, 2, in_width, WC), jnp.bfloat16),
            pltpu.VMEM((tile_width, WC), jnp.float32),
            pltpu.VMEM((WR, WC), jnp.float32),
            pltpu.SemaphoreType.DMA((chips, 2)),
        ],
        compiler_params=pltpu.CompilerParams(vmem_limit_bytes=36 * MIB),
        cost_estimate=pl.CostEstimate(
            flops=2 * tile_width * full_in * WC + 2 * WR * tile_width * WC,
            bytes_accessed=2 * tile_width * full_in + 2 * WC * full_in,
            transcendentals=0,
        ),
        name="window",
    )(me, basis_out, scaled, *near, *far)

    summed = pl.pallas_call(
        add_core_kernel,
        out_shape=jax.ShapeDtypeStruct((chips, rows, WC), jnp.bfloat16),
        in_specs=[VMEM, VMEM],
        out_specs=VMEM,
        compiler_params=pltpu.CompilerParams(vmem_limit_bytes=8 * MIB),
        name="add_core",
    )(keep, swap(send, n))
    return pl.pallas_call(
        add_chips_kernel,
        out_shape=jax.ShapeDtypeStruct((rows, WC), jnp.float32),
        in_specs=[VMEM],
        out_specs=VMEM,
        compiler_params=pltpu.CompilerParams(vmem_limit_bytes=4 * MIB),
        name="add_chips",
    )(plane_exchange(summed, n))


def gather_body(grad_out, activations, basis_out, basis_in, eigenvalues, tile_order, block_map):
    n_blocks = lax.axis_size("blk")
    tile_width = basis_out.shape[1]
    tok_rows = grad_out.shape[0]
    full_in = eigenvalues.shape[1]
    tokens = n_blocks * tok_rows
    dot = functools.partial(jnp.dot, preferred_element_type=jnp.float32)
    in_rows = lax.all_gather(basis_in[:WC], "blk", axis=1, tiled=True)
    acts = lax.all_gather(activations, "blk", axis=0, tiled=True)
    in_tile = dot(acts, basis_in).astype(jnp.bfloat16)
    rotated_in = lax.all_gather(in_tile, "blk", axis=1, tiled=True)
    grads = lax.all_gather(grad_out, "blk", axis=0, tiled=True)
    rotated_out = dot(grads, basis_out).astype(jnp.bfloat16)
    aligned = jnp.take(
        rotated_out.reshape(n_blocks, tok_rows, tile_width), block_map, axis=0
    ).reshape(tokens, tile_width)
    grad_tile = dot(aligned.T, rotated_in) / tokens
    damped = jnp.take(
        eigenvalues.reshape(tile_width, full_in // LANES, LANES), tile_order, axis=1
    ).reshape(tile_width, full_in)
    scaled = (grad_tile / damped).astype(jnp.bfloat16)
    projected = dot(scaled, in_rows.T).astype(jnp.bfloat16)
    return lax.psum_scatter(
        dot(basis_out[:WR], projected), "blk", scatter_dimension=0, tiled=True
    )


def solution(mesh):
    n = mesh.shape["blk"]

    def body(*args):
        wide = args[3].shape[1] % LANES == 0 and args[2].shape[1] % LANES == 0
        doubles = n & (n - 1) == 0 and args[0].shape[0] & (args[0].shape[0] - 1) == 0
        if wide and doubles and WR % (16 * n) == 0:
            return ring_body(n, *args)
        return gather_body(*args)

    placed = (
        P(("grp", "blk"), None),
        P(("grp", "blk"), None),
        P(None, "blk"),
        P(None, "blk"),
        P("blk", None),
        P(),
        P(),
    )
    return jax.shard_map(
        body, mesh=mesh, in_specs=placed, out_specs=P(("grp", "blk"), None), check_vma=False
    )
```

```python
import functools

import jax
import jax.numpy as jnp
from jax import lax
from jax.experimental import pallas as pl
from jax.experimental.pallas import tpu as pltpu
from jax.sharding import PartitionSpec as P

WR = 768
WC = 512
LANES = 128
MIB = 1 << 20


def ring_of(n):
    chips = n // 2
    return [*range(0, chips, 2), *range(chips - 1, 0, -2)]


def shift_pairs(n, by):
    ring = ring_of(n)
    return [
        (2 * ring[p] + c, 2 * ring[(p + by) % len(ring)] + c)
        for p in range(len(ring))
        for c in range(2)
    ]


def ring_source(me, steps, other, chips):
    chip, core = me // 2, lax.rem(me, 2)
    place = jnp.where(lax.rem(chip, 2) == 0, chip // 2, chips - 1 - chip // 2)
    place = lax.rem(place + chips - steps, chips)
    chip = jnp.where(place < chips // 2, 2 * place, 2 * (chips - 1 - place) + 1)
    return 2 * chip + (core ^ other)


def xor_pairs(n, key):
    return [(b, b ^ key) for b in range(n)]


def swap(x, n):
    return lax.ppermute(x, "blk", xor_pairs(n, 1))


def plane_exchange(x, n):
    planes = [list(range(c, n, 2)) for c in range(2)]
    return lax.all_to_all(x, "blk", 0, 0, axis_index_groups=planes, tiled=True)


def bits_of(size):
    return size.bit_length() - 1


def held_tokens(me, tokens, tok_rows):
    row = lax.broadcasted_iota(jnp.int32, (tokens, tokens), 1)
    chips = tokens // tok_rows // 2
    place = (row >> bits_of(tok_rows)) & (chips - 1)
    chip = jnp.zeros_like(row)
    for bit in range(bits_of(chips)):
        chip |= ((place >> bit) & 1) << (bits_of(chips) - 1 - bit)
    other = row >> bits_of(tokens // 2)
    device = me ^ (2 * chip + other)
    return (device << bits_of(tok_rows)) + (row & (tok_rows - 1))


def plane_tokens(me, tokens, tok_rows):
    row = lax.broadcasted_iota(jnp.int32, (tokens, tokens), 1)
    chips = tokens // tok_rows // 2
    chip = (row >> bits_of(tok_rows)) & (chips - 1)
    core = (me & 1) ^ (row >> bits_of(tokens // 2))
    return ((2 * chip + core) << bits_of(tok_rows)) + (row & (tok_rows - 1))


def reorder(wanted, held, rotated):
    order = jnp.where(wanted == held, 1.0, 0.0).astype(jnp.bfloat16)
    return jnp.dot(order, rotated.astype(jnp.bfloat16), preferred_element_type=jnp.float32)


def rotate_in_kernel(tok_rows, scalars_ref, near_ref, far_ref, basis_ref, out_ref):
    tokens = out_ref.shape[1]
    acts = jnp.concatenate([near_ref[...], far_ref[...]], axis=0)
    rotated = jnp.dot(acts, basis_ref[...], preferred_element_type=jnp.float32)
    wanted = lax.broadcasted_iota(jnp.int32, (tokens, tokens), 0)
    ordered = reorder(wanted, plane_tokens(scalars_ref[0], tokens, tok_rows), rotated)
    for copy in range(out_ref.shape[0]):
        out_ref[copy] = ordered.astype(jnp.bfloat16)


def rotate_out_kernel(
    tok_rows, map_at, scalars_ref, near_ref, far_ref, basis_ref, out_ref, basis, total, sem
):
    steps, depth = basis.shape[:2]
    tokens = total.shape[0]

    def copy_of(step):
        rows = pl.ds(pl.multiple_of(step * depth, depth), depth)
        return pltpu.make_async_copy(basis_ref.at[rows], basis.at[step], sem.at[step])

    @pl.loop(0, steps)
    def _(step):
        copy_of(step).start()

    total[...] = jnp.zeros_like(total)

    @pl.loop(0, steps)
    def _(step):
        columns = pl.ds(pl.multiple_of(step * depth, depth), depth)
        grads = jnp.concatenate([near_ref[:, columns], far_ref[:, columns]], axis=0)
        copy_of(step).wait()
        total[...] += jnp.dot(grads, basis[step], preferred_element_type=jnp.float32)

    row = lax.broadcasted_iota(jnp.int32, (tokens, tokens), 0)
    block = row >> bits_of(tok_rows)
    wanted = jnp.zeros_like(row)
    for stored in range(tokens // tok_rows):
        wanted = jnp.where(block == stored, scalars_ref[map_at + stored] * tok_rows, wanted)
    wanted += row & (tok_rows - 1)
    held = held_tokens(scalars_ref[0], tokens, tok_rows)
    out_ref[...] = reorder(wanted, held, total[...]).T.astype(jnp.bfloat16)


def scale_kernel(
    begun, tiles_at, scalars_ref, aligned_ref, near_ref, far_ref, eigen_ref, out_ref, damped, sem
):
    blocks, depth = damped.shape[:2]
    chips, _, width = near_ref.shape

    def copy_of(block):
        rows = pl.ds(pl.multiple_of(block * depth, depth), depth)
        return pltpu.make_async_copy(eigen_ref.at[rows], damped.at[block], sem.at[block])

    @pl.loop(0, blocks)
    def _(block):
        copy_of(block).start()

    @pl.loop(0, blocks)
    def _(block):
        rows = pl.ds(pl.multiple_of(block * depth, depth), depth)
        aligned = aligned_ref[rows, :]
        copy_of(block).wait()
        place = 0
        for steps in begun:
            for other, rotated_ref in enumerate((near_ref, far_ref)):
                source = ring_source(scalars_ref[0], steps, other, chips)
                grad = jnp.dot(
                    aligned, rotated_ref[source // 2], preferred_element_type=jnp.float32
                )
                for first in range(0, width, LANES):
                    tile = scalars_ref[tiles_at + (source * width + first) // LANES]
                    lanes = pl.ds(pl.multiple_of(tile * LANES, LANES), LANES)
                    eigen = damped[block, :, lanes]
                    inverse = pl.reciprocal(eigen, approx=True)
                    inverse = inverse * (2.0 - eigen * inverse)
                    scaled = grad[:, first : first + LANES] * inverse
                    out_ref[rows, place : place + LANES] = scaled.astype(jnp.bfloat16)
                    place += LANES


def project_kernel(cuts, scaled_ref, *refs):
    pieces = refs[:-3]
    out_ref, basis, sem = refs[-3:]
    width = pieces[0].shape[0]
    rows = out_ref.shape[0] // 2
    copies = [
        pltpu.make_async_copy(piece, basis.at[pl.ds(at * width, width)], sem.at[at])
        for at, piece in enumerate(pieces)
    ]
    for copy in copies:
        copy.start()
    for first, last in zip(cuts[:-1], cuts[1:]):
        for copy in copies[first:last]:
            copy.wait()
        deep = slice(first * width, last * width)

        @pl.loop(0, 2)
        def _(half):
            block = pl.ds(pl.multiple_of(half * rows, rows), rows)
            part = jnp.dot(
                scaled_ref[block, deep], basis[deep, :], preferred_element_type=jnp.float32
            )
            out_ref[block, :] = part if first == 0 else out_ref[block, :] + part


def window_kernel(scale, scalars_ref, window_ref, scaled_ref, projected_ref, *refs):
    pieces = refs[:-3]
    send_ref, keep_ref, result = refs[-3:]
    chips, rows, _ = keep_ref.shape
    width = pieces[0].shape[0]
    total = projected_ref[...]
    for at, piece in enumerate(pieces, scaled_ref.shape[1] // width - len(pieces)):
        total += jnp.dot(
            scaled_ref[:, at * width : (at + 1) * width],
            piece[...],
            preferred_element_type=jnp.float32,
        )
    result[...] = scale * jnp.dot(
        window_ref[...], total.astype(jnp.bfloat16), preferred_element_type=jnp.float32
    )
    core = lax.rem(scalars_ref[0], 2)
    for k in range(chips):
        mine = pl.ds(pl.multiple_of((2 * k + core) * rows, rows), rows)
        keep_ref[k] = result[mine, :]
        other = pl.ds(pl.multiple_of((2 * k + 1 - core) * rows, rows), rows)
        send_ref[k] = result[other, :].astype(jnp.bfloat16)


def add_core_kernel(keep_ref, got_ref, out_ref):
    out_ref[...] = (keep_ref[...] + got_ref[...].astype(jnp.float32)).astype(jnp.bfloat16)


def add_chips_kernel(parts_ref, out_ref):
    out_ref[...] = jnp.sum(parts_ref[...].astype(jnp.float32), axis=0)


VMEM = pl.BlockSpec(memory_space=pltpu.VMEM)
SMEM = pl.BlockSpec(memory_space=pltpu.SMEM)
ANY = pl.BlockSpec(memory_space=pl.ANY)


def after(first, *others):
    return lax.optimization_barrier((first, *others))


def ring_body(n, grad_out, activations, basis_out, basis_in, eigenvalues, tile_order, block_map):
    tok_rows, full_out = grad_out.shape
    tile_width = basis_out.shape[1]
    full_in, in_width = basis_in.shape
    tokens = n * tok_rows
    chips = n // 2
    me = lax.axis_index("blk").reshape(1)
    scalars = jnp.concatenate([me, tile_order, block_map])
    to_right = lambda x: lax.ppermute(x, "blk", shift_pairs(n, 1))
    to_left = lambda x: lax.ppermute(x, "blk", shift_pairs(n, -1))
    steps = chips // 2

    own = basis_in[:WC].T

    acts = jnp.broadcast_to(activations[None], (chips, *activations.shape))
    acts = plane_exchange(acts, n).reshape(tokens // 2, full_in)
    rotated = pl.pallas_call(
        functools.partial(rotate_in_kernel, tok_rows),
        out_shape=jax.ShapeDtypeStruct((chips, tokens, in_width), jnp.bfloat16),
        in_specs=[SMEM, VMEM, VMEM, VMEM],
        out_specs=VMEM,
        compiler_params=pltpu.CompilerParams(vmem_limit_bytes=8 * MIB),
        name="rotate_in",
    )(scalars, acts, swap(acts, n), basis_in)
    rotated = plane_exchange(rotated, n)
    rotated_far = swap(rotated, n)

    right, left = [own], [own]
    while len(right) < max(steps - 2, 2):
        right.append(to_right(right[-1]))
        left.append(to_left(left[-1]))

    grads = grad_out[None]
    key = n // 2
    while key > 1:
        got = lax.ppermute(grads, "blk", xor_pairs(n, key))
        if key == 2:
            got, rotated, rotated_far, right[-1], left[-1] = after(
                got, rotated, rotated_far, right[-1], left[-1]
            )
        grads = jnp.concatenate([grads, got], axis=0)
        key //= 2
    grads = grads.reshape(tokens // 2, full_out)
    grads_far = swap(grads, n)
    right.append(to_right(right[-1]))
    left.append(to_left(left[-1]))

    depth = 1024
    aligned = pl.pallas_call(
        functools.partial(rotate_out_kernel, tok_rows, 1 + full_in // LANES),
        out_shape=jax.ShapeDtypeStruct((tile_width, tokens), jnp.bfloat16),
        in_specs=[SMEM, VMEM, VMEM, ANY],
        out_specs=VMEM,
        scratch_shapes=[
            pltpu.VMEM((full_out // depth, depth, tile_width), jnp.bfloat16),
            pltpu.VMEM((tokens, tile_width), jnp.float32),
            pltpu.SemaphoreType.DMA((full_out // depth,)),
        ],
        compiler_params=pltpu.CompilerParams(vmem_limit_bytes=40 * MIB),
        cost_estimate=pl.CostEstimate(
            flops=2 * tokens * full_out * tile_width,
            bytes_accessed=2 * full_out * tile_width,
            transcendentals=0,
        ),
        name="rotate_out",
    )(scalars, grads, grads_far, basis_out)

    aligned, right[-1], left[-1] = after(aligned, right[-1], left[-1])
    right.append(to_right(right[-1]))
    left.append(to_left(left[-1]))
    begun = [0] + [at for step in range(1, steps) for at in (step, chips - step)] + [steps]
    blocks = 8
    scaled = pl.pallas_call(
        functools.partial(scale_kernel, begun, 1),
        out_shape=jax.ShapeDtypeStruct((tile_width, full_in), jnp.bfloat16),
        in_specs=[SMEM, VMEM, VMEM, VMEM, ANY],
        out_specs=VMEM,
        scratch_shapes=[
            pltpu.VMEM((blocks, tile_width // blocks, full_in), jnp.float32),
            pltpu.SemaphoreType.DMA((blocks,)),
        ],
        compiler_params=pltpu.CompilerParams(vmem_limit_bytes=40 * MIB),
        cost_estimate=pl.CostEstimate(
            flops=2 * tile_width * full_in * tokens,
            bytes_accessed=6 * tile_width * full_in,
            transcendentals=tile_width * full_in,
        ),
        name="scale",
    )(scalars, aligned, rotated, rotated_far, eigenvalues)

    scaled, right[-1], left[-1] = after(scaled, right[-1], left[-1])
    last = to_right(right[-1])
    pieces = []
    for at in begun[:-1]:
        near = right[at] if at < steps else left[chips - at]
        pieces += [near, swap(near, n)]
    projected = pl.pallas_call(
        functools.partial(project_kernel, (0, 6, len(pieces))),
        out_shape=jax.ShapeDtypeStruct((tile_width, WC), jnp.float32),
        in_specs=[VMEM] + [ANY] * len(pieces),
        out_specs=VMEM,
        scratch_shapes=[
            pltpu.VMEM((len(pieces) * in_width, WC), jnp.bfloat16),
            pltpu.SemaphoreType.DMA((len(pieces),)),
        ],
        compiler_params=pltpu.CompilerParams(vmem_limit_bytes=24 * MIB),
        cost_estimate=pl.CostEstimate(
            flops=2 * tile_width * full_in * WC,
            bytes_accessed=2 * tile_width * full_in + 2 * WC * full_in,
            transcendentals=0,
        ),
        name="project",
    )(scaled, *pieces)

    projected, last = after(projected, last)
    rows = WR // n
    send, keep = pl.pallas_call(
        functools.partial(window_kernel, 1.0 / tokens),
        out_shape=(
            jax.ShapeDtypeStruct((chips, rows, WC), jnp.bfloat16),
            jax.ShapeDtypeStruct((chips, rows, WC), jnp.float32),
        ),
        grid=(1,),
        in_specs=[SMEM, pl.BlockSpec((WR, tile_width), lambda i: (0, 0))] + [VMEM] * 4,
        out_specs=(VMEM, VMEM),
        scratch_shapes=[pltpu.VMEM((WR, WC), jnp.float32)],
        compiler_params=pltpu.CompilerParams(vmem_limit_bytes=36 * MIB),
        cost_estimate=pl.CostEstimate(
            flops=2 * WR * tile_width * WC,
            bytes_accessed=2 * WR * tile_width + 12 * WR * WC,
            transcendentals=0,
        ),
        name="window",
    )(scalars, basis_out, scaled, projected, last, swap(last, n))

    summed = pl.pallas_call(
        add_core_kernel,
        out_shape=jax.ShapeDtypeStruct((chips, rows, WC), jnp.bfloat16),
        in_specs=[VMEM, VMEM],
        out_specs=VMEM,
        compiler_params=pltpu.CompilerParams(vmem_limit_bytes=8 * MIB),
        name="add_core",
    )(keep, swap(send, n))
    return pl.pallas_call(
        add_chips_kernel,
        out_shape=jax.ShapeDtypeStruct((rows, WC), jnp.float32),
        in_specs=[VMEM],
        out_specs=VMEM,
        compiler_params=pltpu.CompilerParams(vmem_limit_bytes=4 * MIB),
        name="add_chips",
    )(plane_exchange(summed, n))


def gather_body(grad_out, activations, basis_out, basis_in, eigenvalues, tile_order, block_map):
    n_blocks = lax.axis_size("blk")
    tile_width = basis_out.shape[1]
    tok_rows = grad_out.shape[0]
    full_in = eigenvalues.shape[1]
    tokens = n_blocks * tok_rows
    dot = functools.partial(jnp.dot, preferred_element_type=jnp.float32)
    in_rows = lax.all_gather(basis_in[:WC], "blk", axis=1, tiled=True)
    acts = lax.all_gather(activations, "blk", axis=0, tiled=True)
    in_tile = dot(acts, basis_in).astype(jnp.bfloat16)
    rotated_in = lax.all_gather(in_tile, "blk", axis=1, tiled=True)
    grads = lax.all_gather(grad_out, "blk", axis=0, tiled=True)
    rotated_out = dot(grads, basis_out).astype(jnp.bfloat16)
    aligned = jnp.take(
        rotated_out.reshape(n_blocks, tok_rows, tile_width), block_map, axis=0
    ).reshape(tokens, tile_width)
    grad_tile = dot(aligned.T, rotated_in) / tokens
    damped = jnp.take(
        eigenvalues.reshape(tile_width, full_in // LANES, LANES), tile_order, axis=1
    ).reshape(tile_width, full_in)
    scaled = (grad_tile / damped).astype(jnp.bfloat16)
    projected = dot(scaled, in_rows.T).astype(jnp.bfloat16)
    return lax.psum_scatter(
        dot(basis_out[:WR], projected), "blk", scatter_dimension=0, tiled=True
    )


def solution(mesh):
    n = mesh.shape["blk"]

    def body(*args):
        wide = args[3].shape[1] % LANES == 0 and args[2].shape[1] % LANES == 0
        doubles = n & (n - 1) == 0 and args[0].shape[0] & (args[0].shape[0] - 1) == 0
        if wide and doubles and WR % (16 * n) == 0:
            return ring_body(n, *args)
        return gather_body(*args)

    placed = (
        P(("grp", "blk"), None),
        P(("grp", "blk"), None),
        P(None, "blk"),
        P(None, "blk"),
        P("blk", None),
        P(),
        P(),
    )
    return jax.shard_map(
        body, mesh=mesh, in_specs=placed, out_specs=P(("grp", "blk"), None), check_vma=False
    )
```

```python
import functools

import jax
import jax.numpy as jnp
from jax import lax
from jax.experimental import pallas as pl
from jax.experimental.pallas import tpu as pltpu
from jax.sharding import PartitionSpec as P

WR = 768
WC = 512
LANES = 128
MIB = 1 << 20


def ring_of(n):
    chips = n // 2
    return [*range(0, chips, 2), *range(chips - 1, 0, -2)]


def shift_pairs(n, by):
    ring = ring_of(n)
    return [
        (2 * ring[p] + c, 2 * ring[(p + by) % len(ring)] + c)
        for p in range(len(ring))
        for c in range(2)
    ]


def ring_source(me, steps, other, chips):
    chip, core = me // 2, lax.rem(me, 2)
    place = jnp.where(lax.rem(chip, 2) == 0, chip // 2, chips - 1 - chip // 2)
    place = lax.rem(place + chips - steps, chips)
    chip = jnp.where(place < chips // 2, 2 * place, 2 * (chips - 1 - place) + 1)
    return 2 * chip + (core ^ other)


def xor_pairs(n, key):
    return [(b, b ^ key) for b in range(n)]


def swap(x, n):
    return lax.ppermute(x, "blk", xor_pairs(n, 1))


def exchange(x, n, stride):
    groups = [list(range(first, n, stride)) for first in range(stride)]
    return lax.all_to_all(x, "blk", 0, 0, axis_index_groups=groups, tiled=True)


def bits_of(size):
    return size.bit_length() - 1


def held_tokens(me, tokens, tok_rows):
    row = lax.broadcasted_iota(jnp.int32, (tokens, tokens), 1)
    chips = tokens // tok_rows // 2
    place = (row >> bits_of(tok_rows)) & (chips - 1)
    chip = jnp.zeros_like(row)
    for bit in range(bits_of(chips)):
        chip |= ((place >> bit) & 1) << (bits_of(chips) - 1 - bit)
    other = row >> bits_of(tokens // 2)
    device = me ^ (2 * chip + other)
    return (device << bits_of(tok_rows)) + (row & (tok_rows - 1))


def reorder(wanted, held, rotated):
    order = jnp.where(wanted == held, 1.0, 0.0).astype(jnp.bfloat16)
    return jnp.dot(order, rotated.astype(jnp.bfloat16), preferred_element_type=jnp.float32)


def rotate_in_kernel(tok_rows, near_ref, far_ref, basis_ref, out_ref):
    tokens = out_ref.shape[1]
    acts = jnp.concatenate([near_ref[...], far_ref[...]], axis=0)
    rotated = jnp.dot(acts, basis_ref[...], preferred_element_type=jnp.float32)
    wanted = lax.broadcasted_iota(jnp.int32, (tokens, tokens), 0)
    held = held_tokens(lax.axis_index("blk"), tokens, tok_rows)
    ordered = reorder(wanted, held, rotated).astype(jnp.bfloat16)
    for copy in range(out_ref.shape[0]):
        out_ref[copy] = ordered


def rotate_out_kernel(
    tok_rows, near_ref, far_ref, basis_ref, map_ref, out_ref, basis, total, stored_map, sem
):
    steps, depth = basis.shape[:2]
    tokens = total.shape[0]

    def copy_of(step):
        rows = pl.ds(pl.multiple_of(step * depth, depth), depth)
        return pltpu.make_async_copy(basis_ref.at[rows], basis.at[step], sem.at[step])

    @pl.loop(0, steps)
    def _(step):
        copy_of(step).start()

    map_copy = pltpu.make_async_copy(map_ref, stored_map, sem.at[steps])
    map_copy.start()
    total[...] = jnp.zeros_like(total)

    @pl.loop(0, steps)
    def _(step):
        columns = pl.ds(pl.multiple_of(step * depth, depth), depth)
        grads = jnp.concatenate([near_ref[:, columns], far_ref[:, columns]], axis=0)
        copy_of(step).wait()
        total[...] += jnp.dot(grads, basis[step], preferred_element_type=jnp.float32)

    map_copy.wait()
    row = lax.broadcasted_iota(jnp.int32, (tokens, tokens), 0)
    block = row >> bits_of(tok_rows)
    wanted = jnp.zeros_like(row)
    for stored in range(tokens // tok_rows):
        wanted = jnp.where(block == stored, stored_map[stored] * tok_rows, wanted)
    wanted += row & (tok_rows - 1)
    held = held_tokens(lax.axis_index("blk"), tokens, tok_rows)
    out_ref[...] = reorder(wanted, held, total[...]).T.astype(jnp.bfloat16)


def scale_kernel(
    begun, aligned_ref, near_ref, far_ref, tiles_ref, eigen_ref, out_ref, damped, tiles, sem
):
    blocks, depth = damped.shape[:2]
    chips, _, width = near_ref.shape

    def copy_of(block):
        rows = pl.ds(pl.multiple_of(block * depth, depth), depth)
        return pltpu.make_async_copy(eigen_ref.at[rows], damped.at[block], sem.at[block])

    tiles_copy = pltpu.make_async_copy(tiles_ref, tiles, sem.at[blocks])
    tiles_copy.start()

    @pl.loop(0, blocks)
    def _(block):
        copy_of(block).start()

    tiles_copy.wait()
    me = lax.axis_index("blk")

    @pl.loop(0, blocks)
    def _(block):
        rows = pl.ds(pl.multiple_of(block * depth, depth), depth)
        aligned = aligned_ref[rows, :]
        copy_of(block).wait()
        place = 0
        for steps in begun:
            for other, rotated_ref in enumerate((near_ref, far_ref)):
                source = ring_source(me, steps, other, chips)
                grad = jnp.dot(
                    aligned, rotated_ref[source // 2], preferred_element_type=jnp.float32
                )
                for first in range(0, width, LANES):
                    tile = tiles[(source * width + first) // LANES]
                    lanes = pl.ds(pl.multiple_of(tile * LANES, LANES), LANES)
                    eigen = damped[block, :, lanes]
                    inverse = pl.reciprocal(eigen, approx=True)
                    inverse = inverse * (2.0 - eigen * inverse)
                    scaled = grad[:, first : first + LANES] * inverse
                    out_ref[rows, place : place + LANES] = scaled.astype(jnp.bfloat16)
                    place += LANES


def project_kernel(cuts, scaled_ref, basis_out_ref, *refs):
    pieces = refs[:-4]
    out_ref, window_ref, basis, sem = refs[-4:]
    width = pieces[0].shape[0]
    rows = out_ref.shape[0] // 2
    copies = [
        pltpu.make_async_copy(piece, basis.at[pl.ds(at * width, width)], sem.at[at])
        for at, piece in enumerate(pieces)
    ]
    window_copy = pltpu.make_async_copy(
        basis_out_ref.at[pl.ds(0, window_ref.shape[0])], window_ref, sem.at[len(pieces)]
    )
    window_copy.start()
    for copy in copies:
        copy.start()
    for first, last in zip(cuts[:-1], cuts[1:]):
        for copy in copies[first:last]:
            copy.wait()
        deep = slice(first * width, last * width)

        @pl.loop(0, 2)
        def _(half):
            block = pl.ds(pl.multiple_of(half * rows, rows), rows)
            part = jnp.dot(
                scaled_ref[block, deep], basis[deep, :], preferred_element_type=jnp.float32
            )
            out_ref[block, :] = part if first == 0 else out_ref[block, :] + part

    window_copy.wait()


def window_kernel(scale, window_ref, scaled_ref, projected_ref, *refs):
    pieces = refs[:-3]
    send_ref, keep_ref, result = refs[-3:]
    chips, rows, _ = keep_ref.shape
    width = pieces[0].shape[0]
    total = projected_ref[...]
    for at, piece in enumerate(pieces, scaled_ref.shape[1] // width - len(pieces)):
        total += jnp.dot(
            scaled_ref[:, at * width : (at + 1) * width],
            piece[...],
            preferred_element_type=jnp.float32,
        )
    result[...] = scale * jnp.dot(
        window_ref[...], total.astype(jnp.bfloat16), preferred_element_type=jnp.float32
    )
    core = lax.rem(lax.axis_index("blk"), 2)
    for k in range(chips):
        mine = pl.ds(pl.multiple_of((2 * k + core) * rows, rows), rows)
        keep_ref[k] = result[mine, :]
        other = pl.ds(pl.multiple_of((2 * k + 1 - core) * rows, rows), rows)
        send_ref[k] = result[other, :].astype(jnp.bfloat16)


def add_core_kernel(keep_ref, got_ref, mine_ref, send_ref):
    side = lax.rem(lax.axis_index("blk") // 2, 2)
    for pair in range(mine_ref.shape[0]):
        mine, other = 2 * pair + side, 2 * pair + 1 - side
        mine_ref[pair] = keep_ref[mine] + got_ref[mine].astype(jnp.float32)
        sent = keep_ref[other] + got_ref[other].astype(jnp.float32)
        send_ref[pair] = sent.astype(jnp.bfloat16)


def add_pair_kernel(mine_ref, got_ref, out_ref):
    out_ref[...] = (mine_ref[...] + got_ref[...].astype(jnp.float32)).astype(jnp.bfloat16)


def add_chips_kernel(parts_ref, out_ref):
    out_ref[...] = jnp.sum(parts_ref[...].astype(jnp.float32), axis=0)


VMEM = pl.BlockSpec(memory_space=pltpu.VMEM)
SMEM = pl.BlockSpec(memory_space=pltpu.SMEM)
ANY = pl.BlockSpec(memory_space=pl.ANY)


def after(first, *others):
    return lax.optimization_barrier((first, *others))


def ring_body(n, grad_out, activations, basis_out, basis_in, eigenvalues, tile_order, block_map):
    tok_rows, full_out = grad_out.shape
    tile_width = basis_out.shape[1]
    full_in, in_width = basis_in.shape
    tokens = n * tok_rows
    chips = n // 2
    to_right = lambda x: lax.ppermute(x, "blk", shift_pairs(n, 1))
    to_left = lambda x: lax.ppermute(x, "blk", shift_pairs(n, -1))
    steps = chips // 2

    own = basis_in[:WC].T

    both = jnp.concatenate([grad_out, activations], axis=1)[None]
    key = n // 2
    while key > 2:
        got = lax.ppermute(both, "blk", xor_pairs(n, key))
        key //= 2
        if key > 2:
            both = jnp.concatenate([both, got], axis=0)

    got, own = after(got, own)
    right, left = [own], [own]
    while len(right) < max(steps - 2, 2):
        right.append(to_right(right[-1]))
        left.append(to_left(left[-1]))

    acts = jnp.concatenate([both[..., full_out:], got[..., full_out:]], axis=0)
    grads = jnp.concatenate([both[..., :full_out], got[..., :full_out]], axis=0)
    got = lax.ppermute(acts, "blk", xor_pairs(n, 2))
    acts = jnp.concatenate([acts, got], axis=0).reshape(tokens // 2, full_in)
    rotated = pl.pallas_call(
        functools.partial(rotate_in_kernel, tok_rows),
        out_shape=jax.ShapeDtypeStruct((chips, tokens, in_width), jnp.bfloat16),
        in_specs=[VMEM, VMEM, VMEM],
        out_specs=VMEM,
        compiler_params=pltpu.CompilerParams(vmem_limit_bytes=8 * MIB),
        name="rotate_in",
    )(acts, swap(acts, n), basis_in)
    rotated = exchange(rotated, n, 2)
    got = lax.ppermute(grads, "blk", xor_pairs(n, 2))
    got, rotated, right[-1], left[-1] = after(got, rotated, right[-1], left[-1])
    rotated_far = swap(rotated, n)
    grads = jnp.concatenate([grads, got], axis=0).reshape(tokens // 2, full_out)
    grads_far = swap(grads, n)
    near = [right[0]] + [x for pair in zip(right[1:], left[1:]) for x in pair]
    far = [swap(piece, n) for piece in near]
    grads, grads_far, rotated_far, *far = after(grads, grads_far, rotated_far, *far)
    right.append(to_right(right[-1]))
    left.append(to_left(left[-1]))

    depth = 1024
    aligned = pl.pallas_call(
        functools.partial(rotate_out_kernel, tok_rows),
        out_shape=jax.ShapeDtypeStruct((tile_width, tokens), jnp.bfloat16),
        in_specs=[VMEM, VMEM, ANY, ANY],
        out_specs=VMEM,
        scratch_shapes=[
            pltpu.VMEM((full_out // depth, depth, tile_width), jnp.bfloat16),
            pltpu.VMEM((tokens, tile_width), jnp.float32),
            pltpu.SMEM(block_map.shape, jnp.int32),
            pltpu.SemaphoreType.DMA((full_out // depth + 1,)),
        ],
        compiler_params=pltpu.CompilerParams(vmem_limit_bytes=40 * MIB),
        cost_estimate=pl.CostEstimate(
            flops=2 * tokens * full_out * tile_width,
            bytes_accessed=2 * full_out * tile_width,
            transcendentals=0,
        ),
        name="rotate_out",
    )(grads, grads_far, basis_out, block_map)

    aligned, right[-1], left[-1] = after(aligned, right[-1], left[-1])
    right.append(to_right(right[-1]))
    left.append(to_left(left[-1]))
    begun = [0] + [at for step in range(1, steps) for at in (step, chips - step)] + [steps]
    blocks = 8
    scaled = pl.pallas_call(
        functools.partial(scale_kernel, begun),
        out_shape=jax.ShapeDtypeStruct((tile_width, full_in), jnp.bfloat16),
        in_specs=[VMEM, VMEM, VMEM, ANY, ANY],
        out_specs=VMEM,
        scratch_shapes=[
            pltpu.VMEM((blocks, tile_width // blocks, full_in), jnp.float32),
            pltpu.SMEM(tile_order.shape, jnp.int32),
            pltpu.SemaphoreType.DMA((blocks + 1,)),
        ],
        compiler_params=pltpu.CompilerParams(vmem_limit_bytes=40 * MIB),
        cost_estimate=pl.CostEstimate(
            flops=2 * tile_width * full_in * tokens,
            bytes_accessed=6 * tile_width * full_in,
            transcendentals=tile_width * full_in,
        ),
        name="scale",
    )(aligned, rotated, rotated_far, tile_order, eigenvalues)

    scaled, right[-1], left[-1] = after(scaled, right[-1], left[-1])
    last = to_right(right[-1])
    for at in begun[len(near) : -1]:
        near.append(right[at] if at < steps else left[chips - at])
        far.append(swap(near[-1], n))
    pieces = [piece for pair in zip(near, far) for piece in pair]
    projected, window = pl.pallas_call(
        functools.partial(project_kernel, (0, 6, len(pieces))),
        out_shape=(
            jax.ShapeDtypeStruct((tile_width, WC), jnp.float32),
            jax.ShapeDtypeStruct((WR, tile_width), jnp.bfloat16),
        ),
        in_specs=[VMEM] + [ANY] * (len(pieces) + 1),
        out_specs=(VMEM, VMEM),
        scratch_shapes=[
            pltpu.VMEM((len(pieces) * in_width, WC), jnp.bfloat16),
            pltpu.SemaphoreType.DMA((len(pieces) + 1,)),
        ],
        compiler_params=pltpu.CompilerParams(vmem_limit_bytes=24 * MIB),
        cost_estimate=pl.CostEstimate(
            flops=2 * tile_width * full_in * WC,
            bytes_accessed=2 * tile_width * full_in + 2 * WC * full_in,
            transcendentals=0,
        ),
        name="project",
    )(scaled, basis_out, *pieces)

    projected, last = after(projected, last)
    rows = WR // n
    send, keep = pl.pallas_call(
        functools.partial(window_kernel, 1.0 / tokens),
        out_shape=(
            jax.ShapeDtypeStruct((chips, rows, WC), jnp.bfloat16),
            jax.ShapeDtypeStruct((chips, rows, WC), jnp.float32),
        ),
        in_specs=[VMEM] * 5,
        out_specs=(VMEM, VMEM),
        scratch_shapes=[pltpu.VMEM((WR, WC), jnp.float32)],
        compiler_params=pltpu.CompilerParams(vmem_limit_bytes=24 * MIB),
        cost_estimate=pl.CostEstimate(
            flops=2 * WR * tile_width * WC,
            bytes_accessed=2 * WR * tile_width + 12 * WR * WC,
            transcendentals=0,
        ),
        name="window",
    )(window, scaled, projected, last, swap(last, n))

    small = pltpu.CompilerParams(vmem_limit_bytes=8 * MIB)
    half = (chips // 2, rows, WC)
    mine, send = pl.pallas_call(
        add_core_kernel,
        out_shape=(
            jax.ShapeDtypeStruct(half, jnp.float32),
            jax.ShapeDtypeStruct(half, jnp.bfloat16),
        ),
        in_specs=[VMEM, VMEM],
        out_specs=(VMEM, VMEM),
        compiler_params=small,
        name="add_core",
    )(keep, swap(send, n))
    got = lax.ppermute(send, "blk", xor_pairs(n, 2))
    summed = pl.pallas_call(
        add_pair_kernel,
        out_shape=jax.ShapeDtypeStruct(half, jnp.bfloat16),
        in_specs=[VMEM, VMEM],
        out_specs=VMEM,
        compiler_params=small,
        name="add_pair",
    )(mine, got)
    return pl.pallas_call(
        add_chips_kernel,
        out_shape=jax.ShapeDtypeStruct((rows, WC), jnp.float32),
        in_specs=[VMEM],
        out_specs=VMEM,
        compiler_params=small,
        name="add_chips",
    )(exchange(summed, n, 4))


def gather_body(grad_out, activations, basis_out, basis_in, eigenvalues, tile_order, block_map):
    n_blocks = lax.axis_size("blk")
    tile_width = basis_out.shape[1]
    tok_rows = grad_out.shape[0]
    full_in = eigenvalues.shape[1]
    tokens = n_blocks * tok_rows
    dot = functools.partial(jnp.dot, preferred_element_type=jnp.float32)
    in_rows = lax.all_gather(basis_in[:WC], "blk", axis=1, tiled=True)
    acts = lax.all_gather(activations, "blk", axis=0, tiled=True)
    in_tile = dot(acts, basis_in).astype(jnp.bfloat16)
    rotated_in = lax.all_gather(in_tile, "blk", axis=1, tiled=True)
    grads = lax.all_gather(grad_out, "blk", axis=0, tiled=True)
    rotated_out = dot(grads, basis_out).astype(jnp.bfloat16)
    aligned = jnp.take(
        rotated_out.reshape(n_blocks, tok_rows, tile_width), block_map, axis=0
    ).reshape(tokens, tile_width)
    grad_tile = dot(aligned.T, rotated_in) / tokens
    damped = jnp.take(
        eigenvalues.reshape(tile_width, full_in // LANES, LANES), tile_order, axis=1
    ).reshape(tile_width, full_in)
    scaled = (grad_tile / damped).astype(jnp.bfloat16)
    projected = dot(scaled, in_rows.T).astype(jnp.bfloat16)
    return lax.psum_scatter(
        dot(basis_out[:WR], projected), "blk", scatter_dimension=0, tiled=True
    )


def solution(mesh):
    n = mesh.shape["blk"]

    def body(*args):
        wide = args[3].shape[1] % LANES == 0 and args[2].shape[1] % LANES == 0
        doubles = n & (n - 1) == 0 and args[0].shape[0] & (args[0].shape[0] - 1) == 0
        if wide and doubles and WR % (16 * n) == 0:
            return ring_body(n, *args)
        return gather_body(*args)

    placed = (
        P(("grp", "blk"), None),
        P(("grp", "blk"), None),
        P(None, "blk"),
        P(None, "blk"),
        P("blk", None),
        P(),
        P(),
    )
    return jax.shard_map(
        body, mesh=mesh, in_specs=placed, out_specs=P(("grp", "blk"), None), check_vma=False
    )
```

```python
import functools

import jax
import jax.numpy as jnp
from jax import lax
from jax.experimental import pallas as pl
from jax.experimental.pallas import tpu as pltpu
from jax.sharding import PartitionSpec as P

WR = 768
WC = 512
LANES = 128
MIB = 1 << 20


def ring_of(n):
    chips = n // 2
    return [*range(0, chips, 2), *range(chips - 1, 0, -2)]


def shift_pairs(n, by):
    ring = ring_of(n)
    return [
        (2 * ring[p] + c, 2 * ring[(p + by) % len(ring)] + c)
        for p in range(len(ring))
        for c in range(2)
    ]


def ring_source(me, steps, other, chips):
    chip, core = me // 2, lax.rem(me, 2)
    place = jnp.where(lax.rem(chip, 2) == 0, chip // 2, chips - 1 - chip // 2)
    place = lax.rem(place + chips - steps, chips)
    chip = jnp.where(place < chips // 2, 2 * place, 2 * (chips - 1 - place) + 1)
    return 2 * chip + (core ^ other)


def xor_pairs(n, key):
    return [(b, b ^ key) for b in range(n)]


def swap(x, n):
    return lax.ppermute(x, "blk", xor_pairs(n, 1))


def exchange(x, n, stride):
    groups = [list(range(first, n, stride)) for first in range(stride)]
    return lax.all_to_all(x, "blk", 0, 0, axis_index_groups=groups, tiled=True)


def bits_of(size):
    return size.bit_length() - 1


def held_tokens(me, tokens, tok_rows):
    row = lax.broadcasted_iota(jnp.int32, (tokens, tokens), 1)
    chips = tokens // tok_rows // 2
    place = (row >> bits_of(tok_rows)) & (chips - 1)
    chip = jnp.zeros_like(row)
    for bit in range(bits_of(chips)):
        chip |= ((place >> bit) & 1) << (bits_of(chips) - 1 - bit)
    other = row >> bits_of(tokens // 2)
    device = me ^ (2 * chip + other)
    return (device << bits_of(tok_rows)) + (row & (tok_rows - 1))


def reorder(wanted, held, rotated):
    order = jnp.where(wanted == held, 1.0, 0.0).astype(jnp.bfloat16)
    return jnp.dot(order, rotated.astype(jnp.bfloat16), preferred_element_type=jnp.float32)


def rotate_in_kernel(tok_rows, near_ref, far_ref, basis_ref, out_ref):
    tokens = out_ref.shape[1]
    acts = jnp.concatenate([near_ref[...], far_ref[...]], axis=0)
    rotated = lax.dot_general(
        acts, basis_ref[...], (((1,), (1,)), ((), ())), preferred_element_type=jnp.float32
    )
    wanted = lax.broadcasted_iota(jnp.int32, (tokens, tokens), 0)
    held = held_tokens(lax.axis_index("blk"), tokens, tok_rows)
    ordered = reorder(wanted, held, rotated).astype(jnp.bfloat16)
    for copy in range(out_ref.shape[0]):
        out_ref[copy] = ordered


def rotate_out_kernel(
    tok_rows, near_ref, far_ref, basis_ref, map_ref, out_ref, basis, total, stored_map, sem
):
    steps, depth = basis.shape[:2]
    tokens = total.shape[0]

    def copy_of(step):
        rows = pl.ds(pl.multiple_of(step * depth, depth), depth)
        return pltpu.make_async_copy(basis_ref.at[rows], basis.at[step], sem.at[step])

    @pl.loop(0, steps)
    def _(step):
        copy_of(step).start()

    map_copy = pltpu.make_async_copy(map_ref, stored_map, sem.at[steps])
    map_copy.start()
    total[...] = jnp.zeros_like(total)

    @pl.loop(0, steps)
    def _(step):
        columns = pl.ds(pl.multiple_of(step * depth, depth), depth)
        grads = jnp.concatenate([near_ref[:, columns], far_ref[:, columns]], axis=0)
        copy_of(step).wait()
        total[...] += jnp.dot(grads, basis[step], preferred_element_type=jnp.float32)

    map_copy.wait()
    row = lax.broadcasted_iota(jnp.int32, (tokens, tokens), 0)
    block = row >> bits_of(tok_rows)
    wanted = jnp.zeros_like(row)
    for stored in range(tokens // tok_rows):
        wanted = jnp.where(block == stored, stored_map[stored] * tok_rows, wanted)
    wanted += row & (tok_rows - 1)
    held = held_tokens(lax.axis_index("blk"), tokens, tok_rows)
    out_ref[...] = reorder(wanted, held, total[...]).T.astype(jnp.bfloat16)


def scale_kernel(
    begun, aligned_ref, near_ref, far_ref, tiles_ref, eigen_ref, out_ref, damped, tiles, sem
):
    blocks, depth = damped.shape[:2]
    chips, _, width = near_ref.shape

    def copy_of(block):
        rows = pl.ds(pl.multiple_of(block * depth, depth), depth)
        return pltpu.make_async_copy(eigen_ref.at[rows], damped.at[block], sem.at[block])

    tiles_copy = pltpu.make_async_copy(tiles_ref, tiles, sem.at[blocks])
    tiles_copy.start()

    @pl.loop(0, blocks)
    def _(block):
        copy_of(block).start()

    tiles_copy.wait()
    me = lax.axis_index("blk")

    @pl.loop(0, blocks)
    def _(block):
        rows = pl.ds(pl.multiple_of(block * depth, depth), depth)
        aligned = aligned_ref[rows, :]
        copy_of(block).wait()
        place = 0
        for steps in begun:
            for other, rotated_ref in enumerate((near_ref, far_ref)):
                source = ring_source(me, steps, other, chips)
                grad = jnp.dot(
                    aligned, rotated_ref[source // 2], preferred_element_type=jnp.float32
                )
                for first in range(0, width, LANES):
                    tile = tiles[(source * width + first) // LANES]
                    lanes = pl.ds(pl.multiple_of(tile * LANES, LANES), LANES)
                    eigen = damped[block, :, lanes]
                    inverse = pl.reciprocal(eigen, approx=True)
                    inverse = inverse * (2.0 - eigen * inverse)
                    scaled = grad[:, first : first + LANES] * inverse
                    out_ref[rows, place : place + LANES] = scaled.astype(jnp.bfloat16)
                    place += LANES


def project_kernel(cuts, scaled_ref, basis_out_ref, *refs):
    pieces = refs[:-4]
    out_ref, window_ref, basis, sem = refs[-4:]
    width = pieces[0].shape[0]
    rows = out_ref.shape[0] // 2
    copies = [
        pltpu.make_async_copy(piece, basis.at[pl.ds(at * width, width)], sem.at[at])
        for at, piece in enumerate(pieces)
    ]
    window_copy = pltpu.make_async_copy(
        basis_out_ref.at[pl.ds(0, window_ref.shape[0])], window_ref, sem.at[len(pieces)]
    )
    window_copy.start()
    for copy in copies:
        copy.start()
    for first, last in zip(cuts[:-1], cuts[1:]):
        for copy in copies[first:last]:
            copy.wait()
        deep = slice(first * width, last * width)

        @pl.loop(0, 2)
        def _(half):
            block = pl.ds(pl.multiple_of(half * rows, rows), rows)
            part = jnp.dot(
                scaled_ref[block, deep], basis[deep, :], preferred_element_type=jnp.float32
            )
            out_ref[block, :] = part if first == 0 else out_ref[block, :] + part

    window_copy.wait()


def window_kernel(scale, window_ref, scaled_ref, projected_ref, *refs):
    pieces = refs[:-3]
    send_ref, keep_ref, result = refs[-3:]
    chips, rows, _ = keep_ref.shape
    width = pieces[0].shape[0]
    total = projected_ref[...]
    first = scaled_ref.shape[1] - width * len(pieces)
    basis = jnp.concatenate([piece[...] for piece in pieces], axis=0)
    total += jnp.dot(scaled_ref[:, first:], basis, preferred_element_type=jnp.float32)
    result[...] = scale * jnp.dot(
        window_ref[...], total.astype(jnp.bfloat16), preferred_element_type=jnp.float32
    )
    core = lax.rem(lax.axis_index("blk"), 2)
    for k in range(chips):
        mine = pl.ds(pl.multiple_of((2 * k + core) * rows, rows), rows)
        keep_ref[k] = result[mine, :]
        other = pl.ds(pl.multiple_of((2 * k + 1 - core) * rows, rows), rows)
        send_ref[k] = result[other, :].astype(jnp.bfloat16)


def add_core_kernel(keep_ref, got_ref, mine_ref, send_ref):
    side = lax.rem(lax.axis_index("blk") // 2, 2)
    for pair in range(mine_ref.shape[0]):
        mine, other = 2 * pair + side, 2 * pair + 1 - side
        mine_ref[pair] = keep_ref[mine] + got_ref[mine].astype(jnp.float32)
        sent = keep_ref[other] + got_ref[other].astype(jnp.float32)
        send_ref[pair] = sent.astype(jnp.bfloat16)


def add_pair_kernel(mine_ref, got_ref, own_ref, *send_refs):
    me = lax.axis_index("blk") // 4
    own_ref[...] = mine_ref[me] + got_ref[me].astype(jnp.float32)
    for key, send_ref in enumerate(send_refs, 1):
        other = me ^ key
        sent = mine_ref[other] + got_ref[other].astype(jnp.float32)
        send_ref[...] = sent.astype(jnp.bfloat16)


def add_chips_kernel(own_ref, *refs):
    total = own_ref[...]
    for ref in refs[:-1]:
        total += ref[...].astype(jnp.float32)
    refs[-1][...] = total


VMEM = pl.BlockSpec(memory_space=pltpu.VMEM)
SMEM = pl.BlockSpec(memory_space=pltpu.SMEM)
ANY = pl.BlockSpec(memory_space=pl.ANY)


def after(first, *others):
    return lax.optimization_barrier((first, *others))


def ring_body(n, grad_out, activations, basis_out, basis_in, eigenvalues, tile_order, block_map):
    tok_rows, full_out = grad_out.shape
    tile_width = basis_out.shape[1]
    full_in, in_width = basis_in.shape
    tokens = n * tok_rows
    chips = n // 2
    to_right = lambda x: lax.ppermute(x, "blk", shift_pairs(n, 1))
    to_left = lambda x: lax.ppermute(x, "blk", shift_pairs(n, -1))
    steps = chips // 2

    turned = basis_in.T
    own = basis_in[:WC].T

    right, left = [own, to_right(own)], [own, to_left(own)]

    both = jnp.concatenate([grad_out, activations], axis=1)[None]
    key = n // 2
    while key > 2:
        got = lax.ppermute(both, "blk", xor_pairs(n, key))
        key //= 2
        if key > 2:
            both = jnp.concatenate([both, got], axis=0)
    got, turned = after(got, turned)
    acts = jnp.concatenate([both[..., full_out:], got[..., full_out:]], axis=0)
    grads = jnp.concatenate([both[..., :full_out], got[..., :full_out]], axis=0)
    got = lax.ppermute(acts, "blk", xor_pairs(n, 2))
    got, right[-1], left[-1] = after(got, right[-1], left[-1])
    while len(right) < steps - 1:
        right.append(to_right(right[-1]))
        left.append(to_left(left[-1]))
    acts = jnp.concatenate([acts, got], axis=0).reshape(tokens // 2, full_in)
    rotated = pl.pallas_call(
        functools.partial(rotate_in_kernel, tok_rows),
        out_shape=jax.ShapeDtypeStruct((chips, tokens, in_width), jnp.bfloat16),
        in_specs=[VMEM, VMEM, VMEM],
        out_specs=VMEM,
        compiler_params=pltpu.CompilerParams(vmem_limit_bytes=8 * MIB),
        name="rotate_in",
    )(acts, swap(acts, n), turned)
    got = lax.ppermute(grads, "blk", xor_pairs(n, 2))
    got, rotated, right[-1], left[-1] = after(got, rotated, right[-1], left[-1])
    rotated = exchange(rotated, n, 2)
    grads = jnp.concatenate([grads, got], axis=0).reshape(tokens // 2, full_out)
    grads_far = swap(grads, n)
    right.append(to_right(right[-1]))
    left.append(to_left(left[-1]))

    depth = 1024
    aligned = pl.pallas_call(
        functools.partial(rotate_out_kernel, tok_rows),
        out_shape=jax.ShapeDtypeStruct((tile_width, tokens), jnp.bfloat16),
        in_specs=[VMEM, VMEM, ANY, ANY],
        out_specs=VMEM,
        scratch_shapes=[
            pltpu.VMEM((full_out // depth, depth, tile_width), jnp.bfloat16),
            pltpu.VMEM((tokens, tile_width), jnp.float32),
            pltpu.SMEM(block_map.shape, jnp.int32),
            pltpu.SemaphoreType.DMA((full_out // depth + 1,)),
        ],
        compiler_params=pltpu.CompilerParams(vmem_limit_bytes=40 * MIB),
        cost_estimate=pl.CostEstimate(
            flops=2 * tokens * full_out * tile_width,
            bytes_accessed=2 * full_out * tile_width,
            transcendentals=0,
        ),
        name="rotate_out",
    )(grads, grads_far, basis_out, block_map)

    aligned, rotated, right[-1], left[-1] = after(aligned, rotated, right[-1], left[-1])
    rotated_far = swap(rotated, n)
    cut = in_width // 2
    last = [to_right(right[-1][:cut]), to_left(left[-1][cut:])]
    begun = [0] + [at for step in range(1, steps) for at in (step, chips - step)] + [steps]
    blocks = 8
    scaled = pl.pallas_call(
        functools.partial(scale_kernel, begun),
        out_shape=jax.ShapeDtypeStruct((tile_width, full_in), jnp.bfloat16),
        in_specs=[VMEM, VMEM, VMEM, ANY, ANY],
        out_specs=VMEM,
        scratch_shapes=[
            pltpu.VMEM((blocks, tile_width // blocks, full_in), jnp.float32),
            pltpu.SMEM(tile_order.shape, jnp.int32),
            pltpu.SemaphoreType.DMA((blocks + 1,)),
        ],
        compiler_params=pltpu.CompilerParams(vmem_limit_bytes=40 * MIB),
        cost_estimate=pl.CostEstimate(
            flops=2 * tile_width * full_in * tokens,
            bytes_accessed=6 * tile_width * full_in,
            transcendentals=tile_width * full_in,
        ),
        name="scale",
    )(aligned, rotated, rotated_far, tile_order, eigenvalues)

    scaled, *last = after(scaled, *last)
    last += [swap(piece, n) for piece in last]
    near = [right[at] if at < steps else left[chips - at] for at in begun[:-1]]
    far = [swap(piece, n) for piece in near]
    pieces = [piece for pair in zip(near, far) for piece in pair]
    projected, window = pl.pallas_call(
        functools.partial(project_kernel, (0, 6, len(pieces))),
        out_shape=(
            jax.ShapeDtypeStruct((tile_width, WC), jnp.float32),
            jax.ShapeDtypeStruct((WR, tile_width), jnp.bfloat16),
        ),
        in_specs=[VMEM] + [ANY] * (len(pieces) + 1),
        out_specs=(VMEM, VMEM),
        scratch_shapes=[
            pltpu.VMEM((len(pieces) * in_width, WC), jnp.bfloat16),
            pltpu.SemaphoreType.DMA((len(pieces) + 1,)),
        ],
        compiler_params=pltpu.CompilerParams(vmem_limit_bytes=24 * MIB),
        cost_estimate=pl.CostEstimate(
            flops=2 * tile_width * full_in * WC,
            bytes_accessed=2 * tile_width * full_in + 2 * WC * full_in,
            transcendentals=0,
        ),
        name="project",
    )(scaled, basis_out, *pieces)

    rows = WR // n
    send, keep = pl.pallas_call(
        functools.partial(window_kernel, 1.0 / tokens),
        out_shape=(
            jax.ShapeDtypeStruct((chips, rows, WC), jnp.bfloat16),
            jax.ShapeDtypeStruct((chips, rows, WC), jnp.float32),
        ),
        in_specs=[VMEM] * 7,
        out_specs=(VMEM, VMEM),
        scratch_shapes=[pltpu.VMEM((WR, WC), jnp.float32)],
        compiler_params=pltpu.CompilerParams(vmem_limit_bytes=24 * MIB),
        cost_estimate=pl.CostEstimate(
            flops=2 * WR * tile_width * WC,
            bytes_accessed=2 * WR * tile_width + 12 * WR * WC,
            transcendentals=0,
        ),
        name="window",
    )(window, scaled, projected, *last)

    small = pltpu.CompilerParams(vmem_limit_bytes=8 * MIB)
    half = (chips // 2, rows, WC)
    mine, send = pl.pallas_call(
        add_core_kernel,
        out_shape=(
            jax.ShapeDtypeStruct(half, jnp.float32),
            jax.ShapeDtypeStruct(half, jnp.bfloat16),
        ),
        in_specs=[VMEM, VMEM],
        out_specs=(VMEM, VMEM),
        compiler_params=small,
        name="add_core",
    )(keep, swap(send, n))
    got = lax.ppermute(send, "blk", xor_pairs(n, 2))
    block = (rows, WC)
    own, *sends = pl.pallas_call(
        add_pair_kernel,
        out_shape=[jax.ShapeDtypeStruct(block, jnp.float32)]
        + [jax.ShapeDtypeStruct(block, jnp.bfloat16)] * (chips // 2 - 1),
        in_specs=[VMEM, VMEM],
        out_specs=[VMEM] * (chips // 2),
        compiler_params=small,
        name="add_pair",
    )(mine, got)
    arrived = [lax.ppermute(x, "blk", xor_pairs(n, 4 * k)) for k, x in enumerate(sends, 1)]
    return pl.pallas_call(
        add_chips_kernel,
        out_shape=jax.ShapeDtypeStruct(block, jnp.float32),
        in_specs=[VMEM] * (chips // 2),
        out_specs=VMEM,
        compiler_params=small,
        name="add_chips",
    )(own, *arrived)


def gather_body(grad_out, activations, basis_out, basis_in, eigenvalues, tile_order, block_map):
    n_blocks = lax.axis_size("blk")
    tile_width = basis_out.shape[1]
    tok_rows = grad_out.shape[0]
    full_in = eigenvalues.shape[1]
    tokens = n_blocks * tok_rows
    dot = functools.partial(jnp.dot, preferred_element_type=jnp.float32)
    in_rows = lax.all_gather(basis_in[:WC], "blk", axis=1, tiled=True)
    acts = lax.all_gather(activations, "blk", axis=0, tiled=True)
    in_tile = dot(acts, basis_in).astype(jnp.bfloat16)
    rotated_in = lax.all_gather(in_tile, "blk", axis=1, tiled=True)
    grads = lax.all_gather(grad_out, "blk", axis=0, tiled=True)
    rotated_out = dot(grads, basis_out).astype(jnp.bfloat16)
    aligned = jnp.take(
        rotated_out.reshape(n_blocks, tok_rows, tile_width), block_map, axis=0
    ).reshape(tokens, tile_width)
    grad_tile = dot(aligned.T, rotated_in) / tokens
    damped = jnp.take(
        eigenvalues.reshape(tile_width, full_in // LANES, LANES), tile_order, axis=1
    ).reshape(tile_width, full_in)
    scaled = (grad_tile / damped).astype(jnp.bfloat16)
    projected = dot(scaled, in_rows.T).astype(jnp.bfloat16)
    return lax.psum_scatter(
        dot(basis_out[:WR], projected), "blk", scatter_dimension=0, tiled=True
    )


def solution(mesh):
    n = mesh.shape["blk"]

    def body(*args):
        wide = args[3].shape[1] % LANES == 0 and args[2].shape[1] % LANES == 0
        doubles = n & (n - 1) == 0 and args[0].shape[0] & (args[0].shape[0] - 1) == 0
        if wide and doubles and WR % (16 * n) == 0:
            return ring_body(n, *args)
        return gather_body(*args)

    placed = (
        P(("grp", "blk"), None),
        P(("grp", "blk"), None),
        P(None, "blk"),
        P(None, "blk"),
        P("blk", None),
        P(),
        P(),
    )
    return jax.shard_map(
        body, mesh=mesh, in_specs=placed, out_specs=P(("grp", "blk"), None), check_vma=False
    )
```

```python
import functools

import jax
import jax.numpy as jnp
from jax import lax
from jax.experimental import pallas as pl
from jax.experimental.pallas import tpu as pltpu
from jax.sharding import PartitionSpec as P

WR = 768
WC = 512
LANES = 128
MIB = 1 << 20


def ring_of(n):
    chips = n // 2
    return [*range(0, chips, 2), *range(chips - 1, 0, -2)]


def shift_pairs(n, by):
    ring = ring_of(n)
    return [
        (2 * ring[p] + c, 2 * ring[(p + by) % len(ring)] + c)
        for p in range(len(ring))
        for c in range(2)
    ]


def ring_source(me, steps, other, chips):
    chip, core = me // 2, lax.rem(me, 2)
    place = jnp.where(lax.rem(chip, 2) == 0, chip // 2, chips - 1 - chip // 2)
    place = lax.rem(place + chips - steps, chips)
    chip = jnp.where(place < chips // 2, 2 * place, 2 * (chips - 1 - place) + 1)
    return 2 * chip + (core ^ other)


def xor_pairs(n, key):
    return [(b, b ^ key) for b in range(n)]


def swap(x, n):
    return lax.ppermute(x, "blk", xor_pairs(n, 1))


def exchange(x, n, stride):
    groups = [list(range(first, n, stride)) for first in range(stride)]
    return lax.all_to_all(x, "blk", 0, 0, axis_index_groups=groups, tiled=True)


def bits_of(size):
    return size.bit_length() - 1


def held_tokens(me, tokens, tok_rows):
    row = lax.broadcasted_iota(jnp.int32, (tokens, tokens), 1)
    pairs = tokens // tok_rows // 4
    place = row >> bits_of(tok_rows)
    chip = 2 * (place & (pairs - 1)) + ((place >> bits_of(pairs)) & 1)
    other = row >> bits_of(tokens // 2)
    device = me ^ (2 * chip + other)
    return (device << bits_of(tok_rows)) + (row & (tok_rows - 1))


def reorder(wanted, held, rotated):
    order = jnp.where(wanted == held, 1.0, 0.0).astype(jnp.bfloat16)
    return jnp.dot(order, rotated.astype(jnp.bfloat16), preferred_element_type=jnp.float32)


def part_kernel(*refs):
    grads_ref, acts_ref = refs[-2:]
    first = grads_ref.shape[2]
    for at, ref in enumerate(refs[:-2]):
        grads_ref[at] = ref[:, :first]
        acts_ref[at] = ref[:, first:]


def rotate_in_kernel(tok_rows, near_ref, far_ref, basis_ref, out_ref):
    tokens = out_ref.shape[1]
    acts = jnp.concatenate([near_ref[...], far_ref[...]], axis=0)
    rotated = lax.dot_general(
        acts, basis_ref[...], (((1,), (1,)), ((), ())), preferred_element_type=jnp.float32
    )
    wanted = lax.broadcasted_iota(jnp.int32, (tokens, tokens), 0)
    held = held_tokens(lax.axis_index("blk"), tokens, tok_rows)
    ordered = reorder(wanted, held, rotated).astype(jnp.bfloat16)
    for copy in range(out_ref.shape[0]):
        out_ref[copy] = ordered


def rotate_out_kernel(
    tok_rows, near_ref, far_ref, basis_ref, map_ref, out_ref, basis, total, stored_map, sem
):
    steps, depth = basis.shape[:2]
    tokens = total.shape[0]

    def copy_of(step):
        rows = pl.ds(pl.multiple_of(step * depth, depth), depth)
        return pltpu.make_async_copy(basis_ref.at[rows], basis.at[step], sem.at[step])

    @pl.loop(0, steps)
    def _(step):
        copy_of(step).start()

    map_copy = pltpu.make_async_copy(map_ref, stored_map, sem.at[steps])
    map_copy.start()
    total[...] = jnp.zeros_like(total)

    @pl.loop(0, steps)
    def _(step):
        columns = pl.ds(pl.multiple_of(step * depth, depth), depth)
        grads = jnp.concatenate([near_ref[:, columns], far_ref[:, columns]], axis=0)
        copy_of(step).wait()
        total[...] += jnp.dot(grads, basis[step], preferred_element_type=jnp.float32)

    map_copy.wait()
    row = lax.broadcasted_iota(jnp.int32, (tokens, tokens), 0)
    block = row >> bits_of(tok_rows)
    wanted = jnp.zeros_like(row)
    for stored in range(tokens // tok_rows):
        wanted = jnp.where(block == stored, stored_map[stored] * tok_rows, wanted)
    wanted += row & (tok_rows - 1)
    held = held_tokens(lax.axis_index("blk"), tokens, tok_rows)
    out_ref[...] = reorder(wanted, held, total[...]).T.astype(jnp.bfloat16)


def scale_kernel(
    begun, aligned_ref, near_ref, far_ref, tiles_ref, eigen_ref, out_ref, damped, tiles, sem
):
    blocks, depth = damped.shape[:2]
    chips, _, width = near_ref.shape

    def copy_of(block):
        rows = pl.ds(pl.multiple_of(block * depth, depth), depth)
        return pltpu.make_async_copy(eigen_ref.at[rows], damped.at[block], sem.at[block])

    tiles_copy = pltpu.make_async_copy(tiles_ref, tiles, sem.at[blocks])
    tiles_copy.start()

    @pl.loop(0, blocks)
    def _(block):
        copy_of(block).start()

    tiles_copy.wait()
    me = lax.axis_index("blk")

    @pl.loop(0, blocks)
    def _(block):
        rows = pl.ds(pl.multiple_of(block * depth, depth), depth)
        aligned = aligned_ref[rows, :]
        copy_of(block).wait()
        place = 0
        for steps in begun:
            for other, rotated_ref in enumerate((near_ref, far_ref)):
                source = ring_source(me, steps, other, chips)
                grad = jnp.dot(
                    aligned, rotated_ref[source // 2], preferred_element_type=jnp.float32
                )
                for first in range(0, width, LANES):
                    tile = tiles[(source * width + first) // LANES]
                    lanes = pl.ds(pl.multiple_of(tile * LANES, LANES), LANES)
                    eigen = damped[block, :, lanes]
                    inverse = pl.reciprocal(eigen, approx=True)
                    inverse = inverse * (2.0 - eigen * inverse)
                    scaled = grad[:, first : first + LANES] * inverse
                    out_ref[rows, place : place + LANES] = scaled.astype(jnp.bfloat16)
                    place += LANES


def project_kernel(cuts, scaled_ref, basis_out_ref, *refs):
    pieces = refs[:-4]
    out_ref, window_ref, basis, sem = refs[-4:]
    width = pieces[0].shape[0]
    rows = out_ref.shape[0] // 2
    copies = [
        pltpu.make_async_copy(piece, basis.at[pl.ds(at * width, width)], sem.at[at])
        for at, piece in enumerate(pieces)
    ]
    window_copy = pltpu.make_async_copy(
        basis_out_ref.at[pl.ds(0, window_ref.shape[0])], window_ref, sem.at[len(pieces)]
    )
    window_copy.start()
    for copy in copies:
        copy.start()
    for first, last in zip(cuts[:-1], cuts[1:]):
        for copy in copies[first:last]:
            copy.wait()
        deep = slice(first * width, last * width)

        @pl.loop(0, 2)
        def _(half):
            block = pl.ds(pl.multiple_of(half * rows, rows), rows)
            part = jnp.dot(
                scaled_ref[block, deep], basis[deep, :], preferred_element_type=jnp.float32
            )
            out_ref[block, :] = part if first == 0 else out_ref[block, :] + part

    window_copy.wait()


def window_kernel(scale, window_ref, scaled_ref, projected_ref, *refs):
    pieces = refs[:-3]
    send_ref, keep_ref, result = refs[-3:]
    chips, rows, _ = keep_ref.shape
    width = pieces[0].shape[0]
    total = projected_ref[...]
    first = scaled_ref.shape[1] - width * len(pieces)
    basis = jnp.concatenate([piece[...] for piece in pieces], axis=0)
    total += jnp.dot(scaled_ref[:, first:], basis, preferred_element_type=jnp.float32)
    result[...] = scale * jnp.dot(
        window_ref[...], total.astype(jnp.bfloat16), preferred_element_type=jnp.float32
    )
    core = lax.rem(lax.axis_index("blk"), 2)
    for k in range(chips):
        mine = pl.ds(pl.multiple_of((2 * k + core) * rows, rows), rows)
        keep_ref[k] = result[mine, :]
        other = pl.ds(pl.multiple_of((2 * k + 1 - core) * rows, rows), rows)
        send_ref[k] = result[other, :].astype(jnp.bfloat16)


def add_core_kernel(keep_ref, got_ref, pair_mine_ref, pair_send_ref, axis_mine_ref, *axis_refs):
    chip = lax.axis_index("blk") // 2
    side, place = lax.rem(chip, 2), chip // 2
    pairs, _, half = pair_mine_ref.shape
    first, last = slice(0, half), slice(half, 2 * half)

    def total(at, columns):
        return keep_ref[at, :, columns] + got_ref[at, :, columns].astype(jnp.float32)

    for pair in range(pairs):
        pair_mine_ref[pair] = total(2 * pair + side, first)
        pair_send_ref[pair] = total(2 * pair + 1 - side, first).astype(jnp.bfloat16)
    for other in range(2):
        axis_mine_ref[other] = total(2 * place + other, last)
        for key, axis_ref in enumerate(axis_refs, 1):
            axis_ref[other] = total(2 * (place ^ key) + other, last).astype(jnp.bfloat16)


def add_pair_kernel(mine_ref, got_ref, own_ref, *send_refs):
    place = lax.axis_index("blk") // 4
    for key, ref in enumerate((own_ref, *send_refs)):
        at = place ^ key
        ref[...] = (mine_ref[at] + got_ref[at].astype(jnp.float32)).astype(ref.dtype)


def add_axis_kernel(mine_ref, *refs):
    own_ref, send_ref = refs[-2:]
    side = lax.rem(lax.axis_index("blk") // 2, 2)
    for ref, at in ((own_ref, side), (send_ref, 1 - side)):
        total = mine_ref[at]
        for got_ref in refs[:-2]:
            total += got_ref[at].astype(jnp.float32)
        ref[...] = total.astype(ref.dtype)


def add_last_kernel(first_ref, last_ref, last_got_ref, *refs):
    half = first_ref.shape[1]
    total = first_ref[...]
    for ref in refs[:-1]:
        total += ref[...].astype(jnp.float32)
    refs[-1][:, :half] = total
    refs[-1][:, half:] = last_ref[...] + last_got_ref[...].astype(jnp.float32)


VMEM = pl.BlockSpec(memory_space=pltpu.VMEM)
SMEM = pl.BlockSpec(memory_space=pltpu.SMEM)
ANY = pl.BlockSpec(memory_space=pl.ANY)


def after(first, *others):
    return lax.optimization_barrier((first, *others))


def ring_body(n, grad_out, activations, basis_out, basis_in, eigenvalues, tile_order, block_map):
    tok_rows, full_out = grad_out.shape
    tile_width = basis_out.shape[1]
    full_in, in_width = basis_in.shape
    tokens = n * tok_rows
    chips = n // 2
    to_right = lambda x: lax.ppermute(x, "blk", shift_pairs(n, 1))
    to_left = lambda x: lax.ppermute(x, "blk", shift_pairs(n, -1))
    steps = chips // 2

    turned = basis_in.T
    own = basis_in[:WC].T

    pairs = chips // 2
    both = jnp.concatenate([grad_out, activations], axis=1)
    got = [lax.ppermute(both, "blk", xor_pairs(n, 4 * key)) for key in range(1, pairs)]
    both, turned, *got = after(both, turned, *got)
    grads, acts = pl.pallas_call(
        part_kernel,
        out_shape=(
            jax.ShapeDtypeStruct((pairs, tok_rows, full_out), jnp.bfloat16),
            jax.ShapeDtypeStruct((pairs, tok_rows, full_in), jnp.bfloat16),
        ),
        in_specs=[VMEM] * pairs,
        out_specs=(VMEM, VMEM),
        compiler_params=pltpu.CompilerParams(vmem_limit_bytes=8 * MIB),
        name="part",
    )(both, *got)
    acts_got = lax.ppermute(acts, "blk", xor_pairs(n, 2))
    grads_got = lax.ppermute(grads, "blk", xor_pairs(n, 2))

    acts_got, own = after(acts_got, own)
    right, left = [own], [own]
    while len(right) < steps - 2:
        right.append(to_right(right[-1]))
        left.append(to_left(left[-1]))

    acts = jnp.concatenate([acts, acts_got], axis=0).reshape(tokens // 2, full_in)
    rotated = pl.pallas_call(
        functools.partial(rotate_in_kernel, tok_rows),
        out_shape=jax.ShapeDtypeStruct((chips, tokens, in_width), jnp.bfloat16),
        in_specs=[VMEM, VMEM, VMEM],
        out_specs=VMEM,
        compiler_params=pltpu.CompilerParams(vmem_limit_bytes=8 * MIB),
        name="rotate_in",
    )(acts, swap(acts, n), turned)
    grads_got, rotated, right[-1], left[-1] = after(grads_got, rotated, right[-1], left[-1])
    rotated = exchange(rotated, n, 2)
    grads = jnp.concatenate([grads, grads_got], axis=0).reshape(tokens // 2, full_out)
    grads_far = swap(grads, n)
    near = [right[0], right[1], left[1]]
    far = [swap(piece, n) for piece in near]
    right.append(to_right(right[-1]))
    left.append(to_left(left[-1]))

    depth = 1024
    aligned = pl.pallas_call(
        functools.partial(rotate_out_kernel, tok_rows),
        out_shape=jax.ShapeDtypeStruct((tile_width, tokens), jnp.bfloat16),
        in_specs=[VMEM, VMEM, ANY, ANY],
        out_specs=VMEM,
        scratch_shapes=[
            pltpu.VMEM((full_out // depth, depth, tile_width), jnp.bfloat16),
            pltpu.VMEM((tokens, tile_width), jnp.float32),
            pltpu.SMEM(block_map.shape, jnp.int32),
            pltpu.SemaphoreType.DMA((full_out // depth + 1,)),
        ],
        compiler_params=pltpu.CompilerParams(vmem_limit_bytes=40 * MIB),
        cost_estimate=pl.CostEstimate(
            flops=2 * tokens * full_out * tile_width,
            bytes_accessed=2 * full_out * tile_width,
            transcendentals=0,
        ),
        name="rotate_out",
    )(grads, grads_far, basis_out, block_map)

    aligned, rotated, right[-1], left[-1], *far = after(
        aligned, rotated, right[-1], left[-1], *far
    )
    rotated_far = swap(rotated, n)
    near += [right[-1], left[-1]]
    far += [swap(right[-1], n), swap(left[-1], n)]
    right.append(to_right(right[-1]))
    left.append(to_left(left[-1]))
    begun = [0] + [at for step in range(1, steps) for at in (step, chips - step)] + [steps]
    blocks = 8
    scaled = pl.pallas_call(
        functools.partial(scale_kernel, begun),
        out_shape=jax.ShapeDtypeStruct((tile_width, full_in), jnp.bfloat16),
        in_specs=[VMEM, VMEM, VMEM, ANY, ANY],
        out_specs=VMEM,
        scratch_shapes=[
            pltpu.VMEM((blocks, tile_width // blocks, full_in), jnp.float32),
            pltpu.SMEM(tile_order.shape, jnp.int32),
            pltpu.SemaphoreType.DMA((blocks + 1,)),
        ],
        compiler_params=pltpu.CompilerParams(vmem_limit_bytes=40 * MIB),
        cost_estimate=pl.CostEstimate(
            flops=2 * tile_width * full_in * tokens,
            bytes_accessed=6 * tile_width * full_in,
            transcendentals=tile_width * full_in,
        ),
        name="scale",
    )(aligned, rotated, rotated_far, tile_order, eigenvalues)

    scaled, right[-1], left[-1], *far = after(scaled, right[-1], left[-1], *far)
    cut = in_width // 2
    last = [to_right(right[-1][:cut]), to_left(left[-1][cut:])]
    near += [right[-1], left[-1]]
    far += [swap(right[-1], n), swap(left[-1], n)]
    pieces = [piece for pair in zip(near, far) for piece in pair]
    projected, window = pl.pallas_call(
        functools.partial(project_kernel, (0, 6, len(pieces))),
        out_shape=(
            jax.ShapeDtypeStruct((tile_width, WC), jnp.float32),
            jax.ShapeDtypeStruct((WR, tile_width), jnp.bfloat16),
        ),
        in_specs=[VMEM] + [ANY] * (len(pieces) + 1),
        out_specs=(VMEM, VMEM),
        scratch_shapes=[
            pltpu.VMEM((len(pieces) * in_width, WC), jnp.bfloat16),
            pltpu.SemaphoreType.DMA((len(pieces) + 1,)),
        ],
        compiler_params=pltpu.CompilerParams(vmem_limit_bytes=24 * MIB),
        cost_estimate=pl.CostEstimate(
            flops=2 * tile_width * full_in * WC,
            bytes_accessed=2 * tile_width * full_in + 2 * WC * full_in,
            transcendentals=0,
        ),
        name="project",
    )(scaled, basis_out, *pieces)

    projected, *last = after(projected, *last)
    last += [swap(piece, n) for piece in last]
    rows = WR // n
    send, keep = pl.pallas_call(
        functools.partial(window_kernel, 1.0 / tokens),
        out_shape=(
            jax.ShapeDtypeStruct((chips, rows, WC), jnp.bfloat16),
            jax.ShapeDtypeStruct((chips, rows, WC), jnp.float32),
        ),
        in_specs=[VMEM] * 7,
        out_specs=(VMEM, VMEM),
        scratch_shapes=[pltpu.VMEM((WR, WC), jnp.float32)],
        compiler_params=pltpu.CompilerParams(vmem_limit_bytes=24 * MIB),
        cost_estimate=pl.CostEstimate(
            flops=2 * WR * tile_width * WC,
            bytes_accessed=2 * WR * tile_width + 12 * WR * WC,
            transcendentals=0,
        ),
        name="window",
    )(window, scaled, projected, *last)

    def add(kernel, shapes, *operands):
        return pl.pallas_call(
            kernel,
            out_shape=shapes,
            in_specs=[VMEM] * len(operands),
            out_specs=[VMEM] * len(shapes),
            compiler_params=pltpu.CompilerParams(vmem_limit_bytes=8 * MIB),
            name=kernel.__name__[:-7],
        )(*operands)

    exact = lambda *shape: jax.ShapeDtypeStruct((*shape, rows, WC // 2), jnp.float32)
    sent = lambda *shape: jax.ShapeDtypeStruct((*shape, rows, WC // 2), jnp.bfloat16)
    to_pair = lambda x: lax.ppermute(x, "blk", xor_pairs(n, 2))
    to_axis = lambda xs: [
        lax.ppermute(x, "blk", xor_pairs(n, 4 * key)) for key, x in enumerate(xs, 1)
    ]
    pair_mine, pair_send, axis_mine, *axis_sends = add(
        add_core_kernel,
        [exact(pairs), sent(pairs), exact(2)] + [sent(2)] * (pairs - 1),
        keep,
        swap(send, n),
    )
    first, *first_sends = add(
        add_pair_kernel, [exact()] + [sent()] * (pairs - 1), pair_mine, to_pair(pair_send)
    )
    last, last_send = add(
        add_axis_kernel, [exact(), sent()], axis_mine, *to_axis(axis_sends)
    )
    return add(
        add_last_kernel,
        [jax.ShapeDtypeStruct((rows, WC), jnp.float32)],
        first,
        last,
        to_pair(last_send),
        *to_axis(first_sends),
    )[0]


def gather_body(grad_out, activations, basis_out, basis_in, eigenvalues, tile_order, block_map):
    n_blocks = lax.axis_size("blk")
    tile_width = basis_out.shape[1]
    tok_rows = grad_out.shape[0]
    full_in = eigenvalues.shape[1]
    tokens = n_blocks * tok_rows
    dot = functools.partial(jnp.dot, preferred_element_type=jnp.float32)
    in_rows = lax.all_gather(basis_in[:WC], "blk", axis=1, tiled=True)
    acts = lax.all_gather(activations, "blk", axis=0, tiled=True)
    in_tile = dot(acts, basis_in).astype(jnp.bfloat16)
    rotated_in = lax.all_gather(in_tile, "blk", axis=1, tiled=True)
    grads = lax.all_gather(grad_out, "blk", axis=0, tiled=True)
    rotated_out = dot(grads, basis_out).astype(jnp.bfloat16)
    aligned = jnp.take(
        rotated_out.reshape(n_blocks, tok_rows, tile_width), block_map, axis=0
    ).reshape(tokens, tile_width)
    grad_tile = dot(aligned.T, rotated_in) / tokens
    damped = jnp.take(
        eigenvalues.reshape(tile_width, full_in // LANES, LANES), tile_order, axis=1
    ).reshape(tile_width, full_in)
    scaled = (grad_tile / damped).astype(jnp.bfloat16)
    projected = dot(scaled, in_rows.T).astype(jnp.bfloat16)
    return lax.psum_scatter(
        dot(basis_out[:WR], projected), "blk", scatter_dimension=0, tiled=True
    )


def solution(mesh):
    n = mesh.shape["blk"]

    def body(*args):
        wide = args[3].shape[1] % LANES == 0 and args[2].shape[1] % LANES == 0
        doubles = n & (n - 1) == 0 and args[0].shape[0] & (args[0].shape[0] - 1) == 0
        if wide and doubles and WR % (16 * n) == 0:
            return ring_body(n, *args)
        return gather_body(*args)

    placed = (
        P(("grp", "blk"), None),
        P(("grp", "blk"), None),
        P(None, "blk"),
        P(None, "blk"),
        P("blk", None),
        P(),
        P(),
    )
    return jax.shard_map(
        body, mesh=mesh, in_specs=placed, out_specs=P(("grp", "blk"), None), check_vma=False
    )
```

```python
import functools

import jax
import jax.numpy as jnp
from jax import lax
from jax.experimental import pallas as pl
from jax.experimental.pallas import tpu as pltpu
from jax.sharding import PartitionSpec as P

WR = 768
WC = 512
LANES = 128
MIB = 1 << 20


def ring_of(n):
    chips = n // 2
    return [*range(0, chips, 2), *range(chips - 1, 0, -2)]


def shift_pairs(n, by):
    ring = ring_of(n)
    return [
        (2 * ring[p] + c, 2 * ring[(p + by) % len(ring)] + c)
        for p in range(len(ring))
        for c in range(2)
    ]


def ring_source(me, steps, other, chips):
    chip, core = me // 2, lax.rem(me, 2)
    place = jnp.where(lax.rem(chip, 2) == 0, chip // 2, chips - 1 - chip // 2)
    place = lax.rem(place + chips - steps, chips)
    chip = jnp.where(place < chips // 2, 2 * place, 2 * (chips - 1 - place) + 1)
    return 2 * chip + (core ^ other)


def xor_pairs(n, key):
    return [(b, b ^ key) for b in range(n)]


def swap(x, n):
    return lax.ppermute(x, "blk", xor_pairs(n, 1))


def exchange(x, n, stride):
    groups = [list(range(first, n, stride)) for first in range(stride)]
    return lax.all_to_all(x, "blk", 0, 0, axis_index_groups=groups, tiled=True)


def bits_of(size):
    return size.bit_length() - 1


def held_tokens(me, tokens, tok_rows):
    row = lax.broadcasted_iota(jnp.int32, (tokens, tokens), 1)
    pairs = tokens // tok_rows // 4
    place = row >> bits_of(tok_rows)
    chip = 2 * (place & (pairs - 1)) + ((place >> bits_of(pairs)) & 1)
    other = row >> bits_of(tokens // 2)
    device = me ^ (2 * chip + other)
    return (device << bits_of(tok_rows)) + (row & (tok_rows - 1))


def reorder(wanted, held, rotated):
    order = jnp.where(wanted == held, 1.0, 0.0).astype(jnp.bfloat16)
    return jnp.dot(order, rotated.astype(jnp.bfloat16), preferred_element_type=jnp.float32)


def part_kernel(*refs):
    grads_ref, acts_ref = refs[-2:]
    first = grads_ref.shape[2]
    for at, ref in enumerate(refs[:-2]):
        grads_ref[at] = ref[0, :, :first]
        acts_ref[at] = ref[0, :, first:]


def rotate_in_kernel(tok_rows, near_ref, far_ref, basis_ref, out_ref):
    tokens = out_ref.shape[1]
    acts = jnp.concatenate([near_ref[...], far_ref[...]], axis=0)
    rotated = lax.dot_general(
        acts, basis_ref[...], (((1,), (1,)), ((), ())), preferred_element_type=jnp.float32
    )
    wanted = lax.broadcasted_iota(jnp.int32, (tokens, tokens), 0)
    held = held_tokens(lax.axis_index("blk"), tokens, tok_rows)
    ordered = reorder(wanted, held, rotated).astype(jnp.bfloat16)
    for copy in range(out_ref.shape[0]):
        out_ref[copy] = ordered


def hold_kernel(basis_ref, held_ref, sem):
    steps, depth = held_ref.shape[:2]
    copies = [
        pltpu.make_async_copy(
            basis_ref.at[pl.ds(step * depth, depth)], held_ref.at[step], sem.at[step]
        )
        for step in range(steps)
    ]
    for copy in copies:
        copy.start()
    for copy in copies:
        copy.wait()


def rotate_out_kernel(
    tok_rows,
    near_ref,
    far_ref,
    held_ref,
    basis_ref,
    map_ref,
    out_ref,
    basis,
    total,
    stored_map,
    sem,
):
    steps, depth = basis.shape[:2]
    ahead = held_ref.shape[0]
    tokens = total.shape[0]

    def copy_of(step):
        rows = pl.ds(pl.multiple_of((ahead + step) * depth, depth), depth)
        return pltpu.make_async_copy(basis_ref.at[rows], basis.at[step], sem.at[step])

    def grads_of(step):
        columns = pl.ds(pl.multiple_of(step * depth, depth), depth)
        return jnp.concatenate([near_ref[:, columns], far_ref[:, columns]], axis=0)

    @pl.loop(0, steps)
    def _(step):
        copy_of(step).start()

    map_copy = pltpu.make_async_copy(map_ref, stored_map, sem.at[steps])
    map_copy.start()
    total[...] = jnp.zeros_like(total)

    @pl.loop(0, ahead)
    def _(step):
        total[...] += jnp.dot(grads_of(step), held_ref[step], preferred_element_type=jnp.float32)

    @pl.loop(0, steps)
    def _(step):
        copy_of(step).wait()
        total[...] += jnp.dot(
            grads_of(ahead + step), basis[step], preferred_element_type=jnp.float32
        )

    map_copy.wait()
    row = lax.broadcasted_iota(jnp.int32, (tokens, tokens), 0)
    block = row >> bits_of(tok_rows)
    wanted = jnp.zeros_like(row)
    for stored in range(tokens // tok_rows):
        wanted = jnp.where(block == stored, stored_map[stored] * tok_rows, wanted)
    wanted += row & (tok_rows - 1)
    held = held_tokens(lax.axis_index("blk"), tokens, tok_rows)
    out_ref[...] = reorder(wanted, held, total[...]).T.astype(jnp.bfloat16)


def scale_kernel(
    begun, aligned_ref, near_ref, far_ref, tiles_ref, eigen_ref, out_ref, damped, tiles, sem
):
    blocks, depth = damped.shape[:2]
    chips, _, width = near_ref.shape

    def copy_of(block):
        rows = pl.ds(pl.multiple_of(block * depth, depth), depth)
        return pltpu.make_async_copy(eigen_ref.at[rows], damped.at[block], sem.at[block])

    tiles_copy = pltpu.make_async_copy(tiles_ref, tiles, sem.at[blocks])
    tiles_copy.start()

    @pl.loop(0, blocks)
    def _(block):
        copy_of(block).start()

    tiles_copy.wait()
    me = lax.axis_index("blk")

    @pl.loop(0, blocks)
    def _(block):
        rows = pl.ds(pl.multiple_of(block * depth, depth), depth)
        aligned = aligned_ref[rows, :]
        copy_of(block).wait()
        place = 0
        for steps in begun:
            for other, rotated_ref in enumerate((near_ref, far_ref)):
                source = ring_source(me, steps, other, chips)
                grad = jnp.dot(
                    aligned, rotated_ref[source // 2], preferred_element_type=jnp.float32
                )
                for first in range(0, width, LANES):
                    tile = tiles[(source * width + first) // LANES]
                    lanes = pl.ds(pl.multiple_of(tile * LANES, LANES), LANES)
                    eigen = damped[block, :, lanes]
                    inverse = pl.reciprocal(eigen, approx=True)
                    inverse = inverse * (2.0 - eigen * inverse)
                    scaled = grad[:, first : first + LANES] * inverse
                    out_ref[rows, place : place + LANES] = scaled.astype(jnp.bfloat16)
                    place += LANES


def project_kernel(cuts, scaled_ref, basis_out_ref, *refs):
    pieces = refs[:-4]
    out_ref, window_ref, basis, sem = refs[-4:]
    width = pieces[0].shape[0]
    rows = out_ref.shape[0] // 2
    copies = [
        pltpu.make_async_copy(piece, basis.at[pl.ds(at * width, width)], sem.at[at])
        for at, piece in enumerate(pieces)
    ]
    window_copy = pltpu.make_async_copy(
        basis_out_ref.at[pl.ds(0, window_ref.shape[0])], window_ref, sem.at[len(pieces)]
    )
    window_copy.start()
    for copy in copies:
        copy.start()
    for first, last in zip(cuts[:-1], cuts[1:]):
        for copy in copies[first:last]:
            copy.wait()
        deep = slice(first * width, last * width)

        @pl.loop(0, 2)
        def _(half):
            block = pl.ds(pl.multiple_of(half * rows, rows), rows)
            part = jnp.dot(
                scaled_ref[block, deep], basis[deep, :], preferred_element_type=jnp.float32
            )
            out_ref[block, :] = part if first == 0 else out_ref[block, :] + part

    window_copy.wait()


def window_kernel(scale, window_ref, scaled_ref, projected_ref, *refs):
    pieces = refs[:-3]
    send_ref, keep_ref, result = refs[-3:]
    chips, rows, _ = keep_ref.shape
    width = pieces[0].shape[0]
    total = projected_ref[...]
    first = scaled_ref.shape[1] - width * len(pieces)
    basis = jnp.concatenate([piece[...] for piece in pieces], axis=0)
    total += jnp.dot(scaled_ref[:, first:], basis, preferred_element_type=jnp.float32)
    result[...] = scale * jnp.dot(
        window_ref[...], total.astype(jnp.bfloat16), preferred_element_type=jnp.float32
    )
    core = lax.rem(lax.axis_index("blk"), 2)
    for k in range(chips):
        mine = pl.ds(pl.multiple_of((2 * k + core) * rows, rows), rows)
        keep_ref[k] = result[mine, :]
        other = pl.ds(pl.multiple_of((2 * k + 1 - core) * rows, rows), rows)
        send_ref[k] = result[other, :].astype(jnp.bfloat16)


def add_core_kernel(keys, keep_ref, got_ref, own_ref, *send_refs):
    chip = lax.axis_index("blk") // 2
    for key, ref in zip((0, *keys), (own_ref, *send_refs)):
        at = chip ^ key
        ref[...] = (keep_ref[at] + got_ref[at].astype(jnp.float32)).astype(ref.dtype)


def add_chips_kernel(own_ref, *refs):
    total = own_ref[...]
    for ref in refs[:-1]:
        total += ref[...].astype(jnp.float32)
    refs[-1][...] = total


VMEM = pl.BlockSpec(memory_space=pltpu.VMEM)
SMEM = pl.BlockSpec(memory_space=pltpu.SMEM)
ANY = pl.BlockSpec(memory_space=pl.ANY)


def after(first, *others):
    return lax.optimization_barrier((first, *others))


def ring_body(n, grad_out, activations, basis_out, basis_in, eigenvalues, tile_order, block_map):
    tok_rows, full_out = grad_out.shape
    tile_width = basis_out.shape[1]
    full_in, in_width = basis_in.shape
    tokens = n * tok_rows
    chips = n // 2
    to_right = lambda x: lax.ppermute(x, "blk", shift_pairs(n, 1))
    to_left = lambda x: lax.ppermute(x, "blk", shift_pairs(n, -1))
    steps = chips // 2

    turned = basis_in.T
    own = basis_in[:WC].T

    pairs = chips // 2
    both = jnp.concatenate([grad_out, activations], axis=1)[None]
    got = [lax.ppermute(both, "blk", xor_pairs(n, 4 * key)) for key in range(1, pairs)]
    both, turned, *got = after(both, turned, *got)
    grads, acts = pl.pallas_call(
        part_kernel,
        out_shape=(
            jax.ShapeDtypeStruct((pairs, tok_rows, full_out), jnp.bfloat16),
            jax.ShapeDtypeStruct((pairs, tok_rows, full_in), jnp.bfloat16),
        ),
        in_specs=[VMEM] * pairs,
        out_specs=(VMEM, VMEM),
        compiler_params=pltpu.CompilerParams(vmem_limit_bytes=8 * MIB),
        name="part",
    )(both, *got)
    acts, grads, own = after(acts, grads, own)
    acts_got = lax.ppermute(acts, "blk", xor_pairs(n, 2))
    grads_got = lax.ppermute(grads, "blk", xor_pairs(n, 2))
    right, left = [own, to_right(own)], [own, to_left(own)]

    depth, ahead = 1024, 4
    held = pl.pallas_call(
        hold_kernel,
        out_shape=jax.ShapeDtypeStruct((ahead, depth, tile_width), jnp.bfloat16),
        in_specs=[ANY],
        out_specs=VMEM,
        scratch_shapes=[pltpu.SemaphoreType.DMA((ahead,))],
        compiler_params=pltpu.CompilerParams(vmem_limit_bytes=40 * MIB),
        cost_estimate=pl.CostEstimate(
            flops=0, bytes_accessed=4 * ahead * depth * tile_width, transcendentals=0
        ),
        name="hold",
    )(basis_out)

    acts = jnp.concatenate([acts, acts_got], axis=0).reshape(tokens // 2, full_in)
    rotated = pl.pallas_call(
        functools.partial(rotate_in_kernel, tok_rows),
        out_shape=jax.ShapeDtypeStruct((chips, tokens, in_width), jnp.bfloat16),
        in_specs=[VMEM, VMEM, VMEM],
        out_specs=VMEM,
        compiler_params=pltpu.CompilerParams(vmem_limit_bytes=8 * MIB),
        name="rotate_in",
    )(acts, swap(acts, n), turned)
    grads_got, rotated, held, own_far, right[-1], left[-1] = after(
        grads_got, rotated, held, swap(own, n), right[-1], left[-1]
    )
    rotated = exchange(rotated, n, 2)
    near = [right[0], right[1], left[1]]
    while len(right) < steps - 1:
        right.append(to_right(right[-1]))
        left.append(to_left(left[-1]))
    grads = jnp.concatenate([grads, grads_got], axis=0).reshape(tokens // 2, full_out)
    grads_far = swap(grads, n)
    far = [swap(piece, n) for piece in near[1:]]
    grads, grads_far, right[-1], left[-1], *far = after(
        grads, grads_far, right[-1], left[-1], *far
    )
    near += [right[-1], left[-1]]
    far = [own_far, *far, swap(right[-1], n), swap(left[-1], n)]
    right.append(to_right(right[-1]))
    left.append(to_left(left[-1]))

    aligned = pl.pallas_call(
        functools.partial(rotate_out_kernel, tok_rows),
        out_shape=jax.ShapeDtypeStruct((tile_width, tokens), jnp.bfloat16),
        in_specs=[VMEM, VMEM, VMEM, ANY, ANY],
        out_specs=VMEM,
        scratch_shapes=[
            pltpu.VMEM((full_out // depth - ahead, depth, tile_width), jnp.bfloat16),
            pltpu.VMEM((tokens, tile_width), jnp.float32),
            pltpu.SMEM(block_map.shape, jnp.int32),
            pltpu.SemaphoreType.DMA((full_out // depth - ahead + 1,)),
        ],
        compiler_params=pltpu.CompilerParams(vmem_limit_bytes=40 * MIB),
        cost_estimate=pl.CostEstimate(
            flops=2 * tokens * full_out * tile_width,
            bytes_accessed=2 * full_out * tile_width,
            transcendentals=0,
        ),
        name="rotate_out",
    )(grads, grads_far, held, basis_out, block_map)

    aligned, rotated, right[-1], left[-1], *far = after(
        aligned, rotated, right[-1], left[-1], *far
    )
    rotated_far = swap(rotated, n)
    cut = in_width // 2
    last = [to_right(right[-1][:cut]), to_left(left[-1][cut:])]
    near += [right[-1], left[-1]]
    far += [swap(piece, n) for piece in near[len(far) :]]
    begun = [0] + [at for step in range(1, steps) for at in (step, chips - step)] + [steps]
    blocks = 8
    scaled = pl.pallas_call(
        functools.partial(scale_kernel, begun),
        out_shape=jax.ShapeDtypeStruct((tile_width, full_in), jnp.bfloat16),
        in_specs=[VMEM, VMEM, VMEM, ANY, ANY],
        out_specs=VMEM,
        scratch_shapes=[
            pltpu.VMEM((blocks, tile_width // blocks, full_in), jnp.float32),
            pltpu.SMEM(tile_order.shape, jnp.int32),
            pltpu.SemaphoreType.DMA((blocks + 1,)),
        ],
        compiler_params=pltpu.CompilerParams(vmem_limit_bytes=40 * MIB),
        cost_estimate=pl.CostEstimate(
            flops=2 * tile_width * full_in * tokens,
            bytes_accessed=6 * tile_width * full_in,
            transcendentals=tile_width * full_in,
        ),
        name="scale",
    )(aligned, rotated, rotated_far, tile_order, eigenvalues)

    scaled, *last = after(scaled, *last, *far[-2:])
    far[-2:] = last[2:]
    last = last[:2]
    last += [swap(piece, n) for piece in last]
    pieces = [piece for pair in zip(near, far) for piece in pair]
    projected, window = pl.pallas_call(
        functools.partial(project_kernel, (0, 6, len(pieces))),
        out_shape=(
            jax.ShapeDtypeStruct((tile_width, WC), jnp.float32),
            jax.ShapeDtypeStruct((WR, tile_width), jnp.bfloat16),
        ),
        in_specs=[VMEM] + [ANY] * (len(pieces) + 1),
        out_specs=(VMEM, VMEM),
        scratch_shapes=[
            pltpu.VMEM((len(pieces) * in_width, WC), jnp.bfloat16),
            pltpu.SemaphoreType.DMA((len(pieces) + 1,)),
        ],
        compiler_params=pltpu.CompilerParams(vmem_limit_bytes=24 * MIB),
        cost_estimate=pl.CostEstimate(
            flops=2 * tile_width * full_in * WC,
            bytes_accessed=2 * tile_width * full_in + 2 * WC * full_in,
            transcendentals=0,
        ),
        name="project",
    )(scaled, basis_out, *pieces)

    rows = WR // n
    send, keep = pl.pallas_call(
        functools.partial(window_kernel, 1.0 / tokens),
        out_shape=(
            jax.ShapeDtypeStruct((chips, rows, WC), jnp.bfloat16),
            jax.ShapeDtypeStruct((chips, rows, WC), jnp.float32),
        ),
        in_specs=[VMEM] * 7,
        out_specs=(VMEM, VMEM),
        scratch_shapes=[pltpu.VMEM((WR, WC), jnp.float32)],
        compiler_params=pltpu.CompilerParams(vmem_limit_bytes=24 * MIB),
        cost_estimate=pl.CostEstimate(
            flops=2 * WR * tile_width * WC,
            bytes_accessed=2 * WR * tile_width + 12 * WR * WC,
            transcendentals=0,
        ),
        name="window",
    )(window, scaled, projected, *last)

    keys = sorted(range(1, chips), key=lambda key: -(key & -2))
    small = pltpu.CompilerParams(vmem_limit_bytes=8 * MIB)
    own, *sends = pl.pallas_call(
        functools.partial(add_core_kernel, keys),
        out_shape=[jax.ShapeDtypeStruct((rows, WC), jnp.float32)]
        + [jax.ShapeDtypeStruct((rows, WC), jnp.bfloat16)] * len(keys),
        in_specs=[VMEM, VMEM],
        out_specs=[VMEM] * chips,
        compiler_params=small,
        name="add_core",
    )(keep, swap(send, n))
    arrived = [lax.ppermute(x, "blk", xor_pairs(n, 2 * key)) for key, x in zip(keys, sends)]
    return pl.pallas_call(
        add_chips_kernel,
        out_shape=jax.ShapeDtypeStruct((rows, WC), jnp.float32),
        in_specs=[VMEM] * chips,
        out_specs=VMEM,
        compiler_params=small,
        name="add_chips",
    )(own, *arrived)


def gather_body(grad_out, activations, basis_out, basis_in, eigenvalues, tile_order, block_map):
    n_blocks = lax.axis_size("blk")
    tile_width = basis_out.shape[1]
    tok_rows = grad_out.shape[0]
    full_in = eigenvalues.shape[1]
    tokens = n_blocks * tok_rows
    dot = functools.partial(jnp.dot, preferred_element_type=jnp.float32)
    in_rows = lax.all_gather(basis_in[:WC], "blk", axis=1, tiled=True)
    acts = lax.all_gather(activations, "blk", axis=0, tiled=True)
    in_tile = dot(acts, basis_in).astype(jnp.bfloat16)
    rotated_in = lax.all_gather(in_tile, "blk", axis=1, tiled=True)
    grads = lax.all_gather(grad_out, "blk", axis=0, tiled=True)
    rotated_out = dot(grads, basis_out).astype(jnp.bfloat16)
    aligned = jnp.take(
        rotated_out.reshape(n_blocks, tok_rows, tile_width), block_map, axis=0
    ).reshape(tokens, tile_width)
    grad_tile = dot(aligned.T, rotated_in) / tokens
    damped = jnp.take(
        eigenvalues.reshape(tile_width, full_in // LANES, LANES), tile_order, axis=1
    ).reshape(tile_width, full_in)
    scaled = (grad_tile / damped).astype(jnp.bfloat16)
    projected = dot(scaled, in_rows.T).astype(jnp.bfloat16)
    return lax.psum_scatter(
        dot(basis_out[:WR], projected), "blk", scatter_dimension=0, tiled=True
    )


def solution(mesh):
    n = mesh.shape["blk"]

    def body(*args):
        wide = args[3].shape[1] % LANES == 0 and args[2].shape[1] % LANES == 0
        doubles = n & (n - 1) == 0 and args[0].shape[0] & (args[0].shape[0] - 1) == 0
        if wide and doubles and WR % (16 * n) == 0:
            return ring_body(n, *args)
        return gather_body(*args)

    placed = (
        P(("grp", "blk"), None),
        P(("grp", "blk"), None),
        P(None, "blk"),
        P(None, "blk"),
        P("blk", None),
        P(),
        P(),
    )
    return jax.shard_map(
        body, mesh=mesh, in_specs=placed, out_specs=P(("grp", "blk"), None), check_vma=False
    )
```

```python
import functools

import jax
import jax.numpy as jnp
from jax import lax
from jax.experimental import pallas as pl
from jax.experimental.pallas import tpu as pltpu
from jax.sharding import PartitionSpec as P

WR = 768
WC = 512
LANES = 128
MIB = 1 << 20


def xor_pairs(n, key):
    return [(b, b ^ key) for b in range(n)]


def swap(x, n):
    return lax.ppermute(x, "blk", xor_pairs(n, 1))


def exchange(x, n, stride):
    groups = [list(range(first, n, stride)) for first in range(stride)]
    return lax.all_to_all(x, "blk", 0, 0, axis_index_groups=groups, tiled=True)


def bits_of(size):
    return size.bit_length() - 1


def held_tokens(me, tokens, tok_rows):
    row = lax.broadcasted_iota(jnp.int32, (tokens, tokens), 1)
    pairs = tokens // tok_rows // 4
    place = row >> bits_of(tok_rows)
    chip = 2 * (place & (pairs - 1)) + ((place >> bits_of(pairs)) & 1)
    other = row >> bits_of(tokens // 2)
    device = me ^ (2 * chip + other)
    return (device << bits_of(tok_rows)) + (row & (tok_rows - 1))


def reorder(wanted, held, rotated):
    order = jnp.where(wanted == held, 1.0, 0.0).astype(jnp.bfloat16)
    return jnp.dot(order, rotated.astype(jnp.bfloat16), preferred_element_type=jnp.float32)


def part_kernel(*refs):
    grads_ref, acts_ref = refs[-2:]
    first = grads_ref.shape[2]
    for at, ref in enumerate(refs[:-2]):
        grads_ref[at] = ref[0, :, :first]
        acts_ref[at] = ref[0, :, first:]


def rotate_in_kernel(tok_rows, near_ref, far_ref, basis_ref, out_ref):
    tokens = out_ref.shape[1]
    acts = jnp.concatenate([near_ref[...], far_ref[...]], axis=0)
    rotated = jnp.dot(acts, basis_ref[...], preferred_element_type=jnp.float32)
    wanted = lax.broadcasted_iota(jnp.int32, (tokens, tokens), 0)
    held = held_tokens(lax.axis_index("blk"), tokens, tok_rows)
    ordered = reorder(wanted, held, rotated).astype(jnp.bfloat16)
    for copy in range(out_ref.shape[0]):
        out_ref[copy] = ordered


def rotate_out_kernel(
    tok_rows, near_ref, far_ref, basis_ref, map_ref, out_ref, basis, total, stored_map, sem
):
    steps, depth = basis.shape[:2]
    tokens = total.shape[0]

    def copy_of(step):
        rows = pl.ds(pl.multiple_of(step * depth, depth), depth)
        return pltpu.make_async_copy(basis_ref.at[rows], basis.at[step], sem.at[step])

    @pl.loop(0, steps)
    def _(step):
        copy_of(step).start()

    map_copy = pltpu.make_async_copy(map_ref, stored_map, sem.at[steps])
    map_copy.start()
    total[...] = jnp.zeros_like(total)

    @pl.loop(0, steps)
    def _(step):
        columns = pl.ds(pl.multiple_of(step * depth, depth), depth)
        grads = jnp.concatenate([near_ref[:, columns], far_ref[:, columns]], axis=0)
        copy_of(step).wait()
        total[...] += jnp.dot(grads, basis[step], preferred_element_type=jnp.float32)

    map_copy.wait()
    row = lax.broadcasted_iota(jnp.int32, (tokens, tokens), 0)
    block = row >> bits_of(tok_rows)
    wanted = jnp.zeros_like(row)
    for stored in range(tokens // tok_rows):
        wanted = jnp.where(block == stored, stored_map[stored] * tok_rows, wanted)
    wanted += row & (tok_rows - 1)
    held = held_tokens(lax.axis_index("blk"), tokens, tok_rows)
    out_ref[...] = reorder(wanted, held, total[...]).T.astype(jnp.bfloat16)


def scale_kernel(
    groups, aligned_ref, near_ref, far_ref, tiles_ref, eigen_ref, out_ref, damped, tiles, sem
):
    blocks, depth = damped.shape[:2]
    chips, _, width = near_ref.shape
    share = width // groups

    def copy_of(block):
        rows = pl.ds(pl.multiple_of(block * depth, depth), depth)
        return pltpu.make_async_copy(eigen_ref.at[rows], damped.at[block], sem.at[block])

    tiles_copy = pltpu.make_async_copy(tiles_ref, tiles, sem.at[blocks])
    tiles_copy.start()

    @pl.loop(0, blocks)
    def _(block):
        copy_of(block).start()

    tiles_copy.wait()
    odd = lax.rem(lax.axis_index("blk"), 2) == 1

    @pl.loop(0, blocks)
    def _(block):
        rows = pl.ds(pl.multiple_of(block * depth, depth), depth)
        aligned = aligned_ref[rows, :]
        copy_of(block).wait()
        for source in range(2 * chips):
            mine = odd if source % 2 else jnp.logical_not(odd)
            rotated = jnp.where(mine, near_ref[source // 2], far_ref[source // 2])
            grad = jnp.dot(aligned, rotated, preferred_element_type=jnp.float32)
            for first in range(0, width, LANES):
                tile = tiles[(source * width + first) // LANES]
                lanes = pl.ds(pl.multiple_of(tile * LANES, LANES), LANES)
                eigen = damped[block, :, lanes]
                inverse = pl.reciprocal(eigen, approx=True)
                inverse = inverse * (2.0 - eigen * inverse)
                scaled = grad[:, first : first + LANES] * inverse
                place = (first // share * 2 * chips + source) * share + first % share
                out_ref[rows, place : place + LANES] = scaled.astype(jnp.bfloat16)


def window_kernel(scale, basis_out_ref, scaled_ref, basis_ref, *refs):
    send_ref, keep_ref, basis, window, projected, result, sem = refs
    chips, rows, _ = keep_ref.shape
    parts, deep = basis.shape[:2]
    window_copy = pltpu.make_async_copy(
        basis_out_ref.at[pl.ds(0, window.shape[0])], window, sem.at[parts]
    )
    copies = [
        pltpu.make_async_copy(basis_ref.at[pl.ds(part * deep, deep)], basis.at[part], sem.at[part])
        for part in range(parts)
    ]
    for copy in copies:
        copy.start()
    window_copy.start()
    half = projected.shape[0] // 2
    for part in range(parts):
        copies[part].wait()
        columns = slice(part * deep, (part + 1) * deep)

        @pl.loop(0, 2)
        def _(at):
            block = pl.ds(pl.multiple_of(at * half, half), half)
            total = jnp.dot(
                scaled_ref[block, columns], basis[part], preferred_element_type=jnp.float32
            )
            projected[block, :] = total if part == 0 else projected[block, :] + total

    window_copy.wait()
    result[...] = scale * jnp.dot(
        window[...], projected[...].astype(jnp.bfloat16), preferred_element_type=jnp.float32
    )
    core = lax.rem(lax.axis_index("blk"), 2)
    for k in range(chips):
        mine = pl.ds(pl.multiple_of((2 * k + core) * rows, rows), rows)
        keep_ref[k] = result[mine, :]
        other = pl.ds(pl.multiple_of((2 * k + 1 - core) * rows, rows), rows)
        send_ref[k] = result[other, :].astype(jnp.bfloat16)


def add_core_kernel(keys, keep_ref, got_ref, own_ref, *send_refs):
    chip = lax.axis_index("blk") // 2
    for key, ref in zip((0, *keys), (own_ref, *send_refs)):
        at = chip ^ key
        ref[...] = (keep_ref[at] + got_ref[at].astype(jnp.float32)).astype(ref.dtype)


def add_chips_kernel(own_ref, *refs):
    total = own_ref[...]
    for ref in refs[:-1]:
        total += ref[...].astype(jnp.float32)
    refs[-1][...] = total


VMEM = pl.BlockSpec(memory_space=pltpu.VMEM)
SMEM = pl.BlockSpec(memory_space=pltpu.SMEM)
ANY = pl.BlockSpec(memory_space=pl.ANY)


def after(first, *others):
    return lax.optimization_barrier((first, *others))


def ring_body(n, grad_out, activations, basis_out, basis_in, eigenvalues, tile_order, block_map):
    tok_rows, full_out = grad_out.shape
    tile_width = basis_out.shape[1]
    full_in, in_width = basis_in.shape
    tokens = n * tok_rows
    chips = n // 2
    groups = lax.axis_size("grp")

    share = in_width // groups
    own = lax.dynamic_slice(basis_in, (0, lax.axis_index("grp") * share), (WC, share)).T
    first_rows = lax.all_gather(own, ("grp", "blk"), axis=0, tiled=True)

    pairs = chips // 2
    both = jnp.concatenate([grad_out, activations], axis=1)[None]
    got = [lax.ppermute(both, "blk", xor_pairs(n, 4 * key)) for key in range(1, pairs)]
    grads, acts = pl.pallas_call(
        part_kernel,
        out_shape=(
            jax.ShapeDtypeStruct((pairs, tok_rows, full_out), jnp.bfloat16),
            jax.ShapeDtypeStruct((pairs, tok_rows, full_in), jnp.bfloat16),
        ),
        in_specs=[VMEM] * pairs,
        out_specs=(VMEM, VMEM),
        compiler_params=pltpu.CompilerParams(vmem_limit_bytes=8 * MIB),
        name="part",
    )(both, *got)
    acts_got = lax.ppermute(acts, "blk", xor_pairs(n, 2))
    grads_got = lax.ppermute(grads, "blk", xor_pairs(n, 2))

    acts = jnp.concatenate([acts, acts_got], axis=0).reshape(tokens // 2, full_in)
    rotated = pl.pallas_call(
        functools.partial(rotate_in_kernel, tok_rows),
        out_shape=jax.ShapeDtypeStruct((chips, tokens, in_width), jnp.bfloat16),
        in_specs=[VMEM, VMEM, VMEM],
        out_specs=VMEM,
        compiler_params=pltpu.CompilerParams(vmem_limit_bytes=8 * MIB),
        name="rotate_in",
    )(acts, swap(acts, n), basis_in)
    grads_got, rotated = after(grads_got, rotated)
    rotated = exchange(rotated, n, 2)
    grads = jnp.concatenate([grads, grads_got], axis=0).reshape(tokens // 2, full_out)
    grads_far = swap(grads, n)

    depth = 1024
    aligned = pl.pallas_call(
        functools.partial(rotate_out_kernel, tok_rows),
        out_shape=jax.ShapeDtypeStruct((tile_width, tokens), jnp.bfloat16),
        in_specs=[VMEM, VMEM, ANY, ANY],
        out_specs=VMEM,
        scratch_shapes=[
            pltpu.VMEM((full_out // depth, depth, tile_width), jnp.bfloat16),
            pltpu.VMEM((tokens, tile_width), jnp.float32),
            pltpu.SMEM(block_map.shape, jnp.int32),
            pltpu.SemaphoreType.DMA((full_out // depth + 1,)),
        ],
        compiler_params=pltpu.CompilerParams(vmem_limit_bytes=40 * MIB),
        cost_estimate=pl.CostEstimate(
            flops=2 * tokens * full_out * tile_width,
            bytes_accessed=2 * full_out * tile_width,
            transcendentals=0,
        ),
        name="rotate_out",
    )(grads, grads_far, basis_out, block_map)

    rotated_far = swap(rotated, n)
    blocks = 8
    scaled = pl.pallas_call(
        functools.partial(scale_kernel, groups),
        out_shape=jax.ShapeDtypeStruct((tile_width, full_in), jnp.bfloat16),
        in_specs=[VMEM, VMEM, VMEM, ANY, ANY],
        out_specs=VMEM,
        scratch_shapes=[
            pltpu.VMEM((blocks, tile_width // blocks, full_in), jnp.float32),
            pltpu.SMEM(tile_order.shape, jnp.int32),
            pltpu.SemaphoreType.DMA((blocks + 1,)),
        ],
        compiler_params=pltpu.CompilerParams(vmem_limit_bytes=40 * MIB),
        cost_estimate=pl.CostEstimate(
            flops=2 * tile_width * full_in * tokens,
            bytes_accessed=6 * tile_width * full_in,
            transcendentals=tile_width * full_in,
        ),
        name="scale",
    )(aligned, rotated, rotated_far, tile_order, eigenvalues)

    rows = WR // n
    parts = 4
    send, keep = pl.pallas_call(
        functools.partial(window_kernel, 1.0 / tokens),
        out_shape=(
            jax.ShapeDtypeStruct((chips, rows, WC), jnp.bfloat16),
            jax.ShapeDtypeStruct((chips, rows, WC), jnp.float32),
        ),
        in_specs=[ANY, VMEM, ANY],
        out_specs=(VMEM, VMEM),
        scratch_shapes=[
            pltpu.VMEM((parts, full_in // parts, WC), jnp.bfloat16),
            pltpu.VMEM((WR, tile_width), jnp.bfloat16),
            pltpu.VMEM((tile_width, WC), jnp.float32),
            pltpu.VMEM((WR, WC), jnp.float32),
            pltpu.SemaphoreType.DMA((parts + 1,)),
        ],
        compiler_params=pltpu.CompilerParams(vmem_limit_bytes=52 * MIB),
        cost_estimate=pl.CostEstimate(
            flops=2 * tile_width * full_in * WC + 2 * WR * tile_width * WC,
            bytes_accessed=2 * tile_width * full_in + 2 * WC * full_in,
            transcendentals=0,
        ),
        name="window",
    )(basis_out, scaled, first_rows)

    keys = sorted(range(1, chips), key=lambda key: -(key & -2))
    small = pltpu.CompilerParams(vmem_limit_bytes=8 * MIB)
    own, *sends = pl.pallas_call(
        functools.partial(add_core_kernel, keys),
        out_shape=[jax.ShapeDtypeStruct((rows, WC), jnp.float32)]
        + [jax.ShapeDtypeStruct((rows, WC), jnp.bfloat16)] * len(keys),
        in_specs=[VMEM, VMEM],
        out_specs=[VMEM] * chips,
        compiler_params=small,
        name="add_core",
    )(keep, swap(send, n))
    arrived = [lax.ppermute(x, "blk", xor_pairs(n, 2 * key)) for key, x in zip(keys, sends)]
    return pl.pallas_call(
        add_chips_kernel,
        out_shape=jax.ShapeDtypeStruct((rows, WC), jnp.float32),
        in_specs=[VMEM] * chips,
        out_specs=VMEM,
        compiler_params=small,
        name="add_chips",
    )(own, *arrived)


def gather_body(grad_out, activations, basis_out, basis_in, eigenvalues, tile_order, block_map):
    n_blocks = lax.axis_size("blk")
    tile_width = basis_out.shape[1]
    tok_rows = grad_out.shape[0]
    full_in = eigenvalues.shape[1]
    tokens = n_blocks * tok_rows
    dot = functools.partial(jnp.dot, preferred_element_type=jnp.float32)
    in_rows = lax.all_gather(basis_in[:WC], "blk", axis=1, tiled=True)
    acts = lax.all_gather(activations, "blk", axis=0, tiled=True)
    in_tile = dot(acts, basis_in).astype(jnp.bfloat16)
    rotated_in = lax.all_gather(in_tile, "blk", axis=1, tiled=True)
    grads = lax.all_gather(grad_out, "blk", axis=0, tiled=True)
    rotated_out = dot(grads, basis_out).astype(jnp.bfloat16)
    aligned = jnp.take(
        rotated_out.reshape(n_blocks, tok_rows, tile_width), block_map, axis=0
    ).reshape(tokens, tile_width)
    grad_tile = dot(aligned.T, rotated_in) / tokens
    damped = jnp.take(
        eigenvalues.reshape(tile_width, full_in // LANES, LANES), tile_order, axis=1
    ).reshape(tile_width, full_in)
    scaled = (grad_tile / damped).astype(jnp.bfloat16)
    projected = dot(scaled, in_rows.T).astype(jnp.bfloat16)
    return lax.psum_scatter(
        dot(basis_out[:WR], projected), "blk", scatter_dimension=0, tiled=True
    )


def solution(mesh):
    n = mesh.shape["blk"]

    def body(*args):
        wide = args[3].shape[1] % LANES == 0 and args[2].shape[1] % LANES == 0
        doubles = n & (n - 1) == 0 and args[0].shape[0] & (args[0].shape[0] - 1) == 0
        if wide and doubles and WR % (16 * n) == 0:
            return ring_body(n, *args)
        return gather_body(*args)

    placed = (
        P(("grp", "blk"), None),
        P(("grp", "blk"), None),
        P(None, "blk"),
        P(None, "blk"),
        P("blk", None),
        P(),
        P(),
    )
    return jax.shard_map(
        body, mesh=mesh, in_specs=placed, out_specs=P(("grp", "blk"), None), check_vma=False
    )
```

```python
import functools

import jax
import jax.numpy as jnp
from jax import lax
from jax.experimental import pallas as pl
from jax.experimental.pallas import tpu as pltpu
from jax.sharding import PartitionSpec as P

WR = 768
WC = 512
LANES = 128
MIB = 1 << 20


def ring_of(n):
    chips = n // 2
    return [*range(0, chips, 2), *range(chips - 1, 0, -2)]


def shift_pairs(n, by):
    ring = ring_of(n)
    return [
        (2 * ring[p] + c, 2 * ring[(p + by) % len(ring)] + c)
        for p in range(len(ring))
        for c in range(2)
    ]


def ring_source(me, steps, other, chips):
    chip, core = me // 2, lax.rem(me, 2)
    place = jnp.where(lax.rem(chip, 2) == 0, chip // 2, chips - 1 - chip // 2)
    place = lax.rem(place + chips - steps, chips)
    chip = jnp.where(place < chips // 2, 2 * place, 2 * (chips - 1 - place) + 1)
    return 2 * chip + (core ^ other)


def xor_pairs(n, key):
    return [(b, b ^ key) for b in range(n)]


def swap(x, n):
    return lax.ppermute(x, "blk", xor_pairs(n, 1))


def exchange(x, n, stride):
    groups = [list(range(first, n, stride)) for first in range(stride)]
    return lax.all_to_all(x, "blk", 0, 0, axis_index_groups=groups, tiled=True)


def bits_of(size):
    return size.bit_length() - 1


def held_tokens(me, tokens, tok_rows):
    row = lax.broadcasted_iota(jnp.int32, (tokens, tokens), 1)
    pairs = tokens // tok_rows // 4
    place = row >> bits_of(tok_rows)
    chip = 2 * (place & (pairs - 1)) + ((place >> bits_of(pairs)) & 1)
    other = row >> bits_of(tokens // 2)
    device = me ^ (2 * chip + other)
    return (device << bits_of(tok_rows)) + (row & (tok_rows - 1))


def reorder(wanted, held, rotated):
    order = jnp.where(wanted == held, 1.0, 0.0).astype(jnp.bfloat16)
    return jnp.dot(order, rotated.astype(jnp.bfloat16), preferred_element_type=jnp.float32)


def part_kernel(*refs):
    grads_ref, acts_ref = refs[-2:]
    first = grads_ref.shape[2]
    for at, ref in enumerate(refs[:-2]):
        grads_ref[at] = ref[0, :, :first]
        acts_ref[at] = ref[0, :, first:]


def rotate_in_kernel(tok_rows, near_ref, far_ref, basis_ref, out_ref):
    tokens = out_ref.shape[1]
    acts = jnp.concatenate([near_ref[...], far_ref[...]], axis=0)
    rotated = jnp.dot(acts, basis_ref[...], preferred_element_type=jnp.float32)
    wanted = lax.broadcasted_iota(jnp.int32, (tokens, tokens), 0)
    held = held_tokens(lax.axis_index("blk"), tokens, tok_rows)
    ordered = reorder(wanted, held, rotated).astype(jnp.bfloat16)
    for copy in range(out_ref.shape[0]):
        out_ref[copy] = ordered


def rotate_out_kernel(
    tok_rows,
    near_ref,
    far_ref,
    basis_ref,
    map_ref,
    out_ref,
    basis,
    total,
    stored_map,
    sem,
):
    steps, depth = basis.shape[:2]
    tokens = total.shape[0]

    def copy_of(step):
        rows = pl.ds(pl.multiple_of(step * depth, depth), depth)
        return pltpu.make_async_copy(basis_ref.at[rows], basis.at[step], sem.at[step])

    def grads_of(step):
        columns = pl.ds(pl.multiple_of(step * depth, depth), depth)
        return jnp.concatenate([near_ref[:, columns], far_ref[:, columns]], axis=0)

    @pl.loop(0, steps)
    def _(step):
        copy_of(step).start()

    map_copy = pltpu.make_async_copy(map_ref, stored_map, sem.at[steps])
    map_copy.start()
    total[...] = jnp.zeros_like(total)

    @pl.loop(0, steps)
    def _(step):
        copy_of(step).wait()
        total[...] += jnp.dot(grads_of(step), basis[step], preferred_element_type=jnp.float32)

    map_copy.wait()
    row = lax.broadcasted_iota(jnp.int32, (tokens, tokens), 0)
    block = row >> bits_of(tok_rows)
    wanted = jnp.zeros_like(row)
    for stored in range(tokens // tok_rows):
        wanted = jnp.where(block == stored, stored_map[stored] * tok_rows, wanted)
    wanted += row & (tok_rows - 1)
    held = held_tokens(lax.axis_index("blk"), tokens, tok_rows)
    out_ref[...] = reorder(wanted, held, total[...]).T.astype(jnp.bfloat16)


def scale_kernel(
    begun, aligned_ref, near_ref, far_ref, tiles_ref, eigen_ref, out_ref, damped, tiles, sem
):
    blocks, depth = damped.shape[:2]
    chips, _, width = near_ref.shape

    def copy_of(block):
        rows = pl.ds(pl.multiple_of(block * depth, depth), depth)
        return pltpu.make_async_copy(eigen_ref.at[rows], damped.at[block], sem.at[block])

    tiles_copy = pltpu.make_async_copy(tiles_ref, tiles, sem.at[blocks])
    tiles_copy.start()

    @pl.loop(0, blocks)
    def _(block):
        copy_of(block).start()

    tiles_copy.wait()
    me = lax.axis_index("blk")

    @pl.loop(0, blocks)
    def _(block):
        rows = pl.ds(pl.multiple_of(block * depth, depth), depth)
        aligned = aligned_ref[rows, :]
        copy_of(block).wait()
        place = 0
        for steps in begun:
            for other, rotated_ref in enumerate((near_ref, far_ref)):
                source = ring_source(me, steps, other, chips)
                grad = jnp.dot(
                    aligned, rotated_ref[source // 2], preferred_element_type=jnp.float32
                )
                for first in range(0, width, LANES):
                    tile = tiles[(source * width + first) // LANES]
                    lanes = pl.ds(pl.multiple_of(tile * LANES, LANES), LANES)
                    eigen = damped[block, :, lanes]
                    inverse = pl.reciprocal(eigen, approx=True)
                    inverse = inverse * (2.0 - eigen * inverse)
                    scaled = grad[:, first : first + LANES] * inverse
                    out_ref[rows, place : place + LANES] = scaled.astype(jnp.bfloat16)
                    place += LANES


def project_kernel(cuts, scaled_ref, basis_out_ref, *refs):
    pieces = refs[:-4]
    out_ref, window_ref, basis, sem = refs[-4:]
    width = pieces[0].shape[0]
    rows = out_ref.shape[0] // 2
    copies = [
        pltpu.make_async_copy(piece, basis.at[pl.ds(at * width, width)], sem.at[at])
        for at, piece in enumerate(pieces)
    ]
    window_copy = pltpu.make_async_copy(
        basis_out_ref.at[pl.ds(0, window_ref.shape[0])], window_ref, sem.at[len(pieces)]
    )
    window_copy.start()
    for copy in copies:
        copy.start()
    for first, last in zip(cuts[:-1], cuts[1:]):
        for copy in copies[first:last]:
            copy.wait()
        deep = slice(first * width, last * width)

        @pl.loop(0, 2)
        def _(half):
            block = pl.ds(pl.multiple_of(half * rows, rows), rows)
            part = jnp.dot(
                scaled_ref[block, deep], basis[deep, :], preferred_element_type=jnp.float32
            )
            out_ref[block, :] = part if first == 0 else out_ref[block, :] + part

    window_copy.wait()


def window_kernel(scale, window_ref, scaled_ref, projected_ref, *refs):
    pieces = refs[:-3]
    send_ref, keep_ref, result = refs[-3:]
    chips, rows, _ = keep_ref.shape
    width = pieces[0].shape[0]
    total = projected_ref[...]
    first = scaled_ref.shape[1] - width * len(pieces)
    basis = jnp.concatenate([piece[...] for piece in pieces], axis=0)
    total += jnp.dot(scaled_ref[:, first:], basis, preferred_element_type=jnp.float32)
    result[...] = scale * jnp.dot(
        window_ref[...], total.astype(jnp.bfloat16), preferred_element_type=jnp.float32
    )
    core = lax.rem(lax.axis_index("blk"), 2)
    for k in range(chips):
        mine = pl.ds(pl.multiple_of((2 * k + core) * rows, rows), rows)
        keep_ref[k] = result[mine, :]
        other = pl.ds(pl.multiple_of((2 * k + 1 - core) * rows, rows), rows)
        send_ref[k] = result[other, :].astype(jnp.bfloat16)


def add_core_kernel(keys, keep_ref, got_ref, own_ref, *send_refs):
    chip = lax.axis_index("blk") // 2
    for key, ref in zip((0, *keys), (own_ref, *send_refs)):
        at = chip ^ key
        ref[...] = (keep_ref[at] + got_ref[at].astype(jnp.float32)).astype(ref.dtype)


def add_chips_kernel(own_ref, *refs):
    total = own_ref[...]
    for ref in refs[:-1]:
        total += ref[...].astype(jnp.float32)
    refs[-1][...] = total


VMEM = pl.BlockSpec(memory_space=pltpu.VMEM)
SMEM = pl.BlockSpec(memory_space=pltpu.SMEM)
ANY = pl.BlockSpec(memory_space=pl.ANY)
CHEAP = pl.CostEstimate(flops=1, bytes_accessed=1, transcendentals=0)


def after(first, *others):
    return lax.optimization_barrier((first, *others))


def ring_body(n, grad_out, activations, basis_out, basis_in, eigenvalues, tile_order, block_map):
    tok_rows, full_out = grad_out.shape
    tile_width = basis_out.shape[1]
    full_in, in_width = basis_in.shape
    tokens = n * tok_rows
    chips = n // 2
    to_right = lambda x: lax.ppermute(x, "blk", shift_pairs(n, 1))
    to_left = lambda x: lax.ppermute(x, "blk", shift_pairs(n, -1))
    steps = chips // 2

    own = basis_in[:WC].T

    pairs = chips // 2
    both = jnp.concatenate([grad_out, activations], axis=1)[None]
    got = [lax.ppermute(both, "blk", xor_pairs(n, 4 * key)) for key in range(1, pairs)]
    both, own, *got = after(both, own, *got)
    grads, acts = pl.pallas_call(
        part_kernel,
        out_shape=(
            jax.ShapeDtypeStruct((pairs, tok_rows, full_out), jnp.bfloat16),
            jax.ShapeDtypeStruct((pairs, tok_rows, full_in), jnp.bfloat16),
        ),
        in_specs=[VMEM] * pairs,
        out_specs=(VMEM, VMEM),
        compiler_params=pltpu.CompilerParams(vmem_limit_bytes=8 * MIB),
        name="part",
    )(both, *got)
    acts, grads, own = after(acts, grads, own)
    acts_got = lax.ppermute(acts, "blk", xor_pairs(n, 2))
    grads_got = lax.ppermute(grads, "blk", xor_pairs(n, 2))
    right, left = [own, to_right(own)], [own, to_left(own)]

    acts = jnp.concatenate([acts, acts_got], axis=0).reshape(tokens // 2, full_in)
    rotated = pl.pallas_call(
        functools.partial(rotate_in_kernel, tok_rows),
        out_shape=jax.ShapeDtypeStruct((chips, tokens, in_width), jnp.bfloat16),
        in_specs=[VMEM, VMEM, VMEM],
        out_specs=VMEM,
        compiler_params=pltpu.CompilerParams(vmem_limit_bytes=8 * MIB),
        cost_estimate=CHEAP,
        name="rotate_in",
    )(acts, swap(acts, n), basis_in)
    grads_got, rotated, own_far, right[-1], left[-1] = after(
        grads_got, rotated, swap(own, n), right[-1], left[-1]
    )
    rotated = exchange(rotated, n, 2)
    near = [right[0], right[1], left[1]]
    while len(right) < steps - 1:
        right.append(to_right(right[-1]))
        left.append(to_left(left[-1]))
    grads = jnp.concatenate([grads, grads_got], axis=0).reshape(tokens // 2, full_out)
    grads_far = swap(grads, n)
    far = [swap(piece, n) for piece in near[1:]]
    grads, grads_far, right[-1], left[-1], *far = after(
        grads, grads_far, right[-1], left[-1], *far
    )
    near += [right[-1], left[-1]]
    far = [own_far, *far, swap(right[-1], n), swap(left[-1], n)]
    right.append(to_right(right[-1]))
    left.append(to_left(left[-1]))

    depth = 1024
    aligned = pl.pallas_call(
        functools.partial(rotate_out_kernel, tok_rows),
        out_shape=jax.ShapeDtypeStruct((tile_width, tokens), jnp.bfloat16),
        in_specs=[VMEM, VMEM, ANY, ANY],
        out_specs=VMEM,
        scratch_shapes=[
            pltpu.VMEM((full_out // depth, depth, tile_width), jnp.bfloat16),
            pltpu.VMEM((tokens, tile_width), jnp.float32),
            pltpu.SMEM(block_map.shape, jnp.int32),
            pltpu.SemaphoreType.DMA((full_out // depth + 1,)),
        ],
        compiler_params=pltpu.CompilerParams(vmem_limit_bytes=40 * MIB),
        cost_estimate=CHEAP,
        name="rotate_out",
    )(grads, grads_far, basis_out, block_map)

    aligned, rotated, right[-1], left[-1], *far = after(
        aligned, rotated, right[-1], left[-1], *far
    )
    rotated_far = swap(rotated, n)
    cut = in_width // 2
    last = [to_right(right[-1][:cut]), to_left(left[-1][cut:])]
    near += [right[-1], left[-1]]
    far += [swap(piece, n) for piece in near[len(far) :]]
    begun = [0] + [at for step in range(1, steps) for at in (step, chips - step)] + [steps]
    blocks = 8
    scaled = pl.pallas_call(
        functools.partial(scale_kernel, begun),
        out_shape=jax.ShapeDtypeStruct((tile_width, full_in), jnp.bfloat16),
        in_specs=[VMEM, VMEM, VMEM, ANY, ANY],
        out_specs=VMEM,
        scratch_shapes=[
            pltpu.VMEM((blocks, tile_width // blocks, full_in), jnp.float32),
            pltpu.SMEM(tile_order.shape, jnp.int32),
            pltpu.SemaphoreType.DMA((blocks + 1,)),
        ],
        compiler_params=pltpu.CompilerParams(vmem_limit_bytes=40 * MIB),
        cost_estimate=CHEAP,
        name="scale",
    )(aligned, rotated, rotated_far, tile_order, eigenvalues)

    scaled, *last = after(scaled, *last, *far[-2:])
    far[-2:] = last[2:]
    last = last[:2]
    last += [swap(piece, n) for piece in last]
    pieces = [piece for pair in zip(near, far) for piece in pair]
    projected, window = pl.pallas_call(
        functools.partial(project_kernel, (0, 6, len(pieces))),
        out_shape=(
            jax.ShapeDtypeStruct((tile_width, WC), jnp.float32),
            jax.ShapeDtypeStruct((WR, tile_width), jnp.bfloat16),
        ),
        in_specs=[VMEM] + [ANY] * (len(pieces) + 1),
        out_specs=(VMEM, VMEM),
        scratch_shapes=[
            pltpu.VMEM((len(pieces) * in_width, WC), jnp.bfloat16),
            pltpu.SemaphoreType.DMA((len(pieces) + 1,)),
        ],
        compiler_params=pltpu.CompilerParams(vmem_limit_bytes=24 * MIB),
        cost_estimate=CHEAP,
        name="project",
    )(scaled, basis_out, *pieces)

    rows = WR // n
    send, keep = pl.pallas_call(
        functools.partial(window_kernel, 1.0 / tokens),
        out_shape=(
            jax.ShapeDtypeStruct((chips, rows, WC), jnp.bfloat16),
            jax.ShapeDtypeStruct((chips, rows, WC), jnp.float32),
        ),
        in_specs=[VMEM] * 7,
        out_specs=(VMEM, VMEM),
        scratch_shapes=[pltpu.VMEM((WR, WC), jnp.float32)],
        compiler_params=pltpu.CompilerParams(vmem_limit_bytes=24 * MIB),
        cost_estimate=CHEAP,
        name="window",
    )(window, scaled, projected, *last)

    keys = sorted(range(1, chips), key=lambda key: -(key & -2))
    small = pltpu.CompilerParams(vmem_limit_bytes=8 * MIB)
    own, *sends = pl.pallas_call(
        functools.partial(add_core_kernel, keys),
        out_shape=[jax.ShapeDtypeStruct((rows, WC), jnp.float32)]
        + [jax.ShapeDtypeStruct((rows, WC), jnp.bfloat16)] * len(keys),
        in_specs=[VMEM, VMEM],
        out_specs=[VMEM] * chips,
        compiler_params=small,
        name="add_core",
    )(keep, swap(send, n))
    arrived = [lax.ppermute(x, "blk", xor_pairs(n, 2 * key)) for key, x in zip(keys, sends)]
    return pl.pallas_call(
        add_chips_kernel,
        out_shape=jax.ShapeDtypeStruct((rows, WC), jnp.float32),
        in_specs=[VMEM] * chips,
        out_specs=VMEM,
        compiler_params=small,
        name="add_chips",
    )(own, *arrived)


def gather_body(grad_out, activations, basis_out, basis_in, eigenvalues, tile_order, block_map):
    n_blocks = lax.axis_size("blk")
    tile_width = basis_out.shape[1]
    tok_rows = grad_out.shape[0]
    full_in = eigenvalues.shape[1]
    tokens = n_blocks * tok_rows
    dot = functools.partial(jnp.dot, preferred_element_type=jnp.float32)
    in_rows = lax.all_gather(basis_in[:WC], "blk", axis=1, tiled=True)
    acts = lax.all_gather(activations, "blk", axis=0, tiled=True)
    in_tile = dot(acts, basis_in).astype(jnp.bfloat16)
    rotated_in = lax.all_gather(in_tile, "blk", axis=1, tiled=True)
    grads = lax.all_gather(grad_out, "blk", axis=0, tiled=True)
    rotated_out = dot(grads, basis_out).astype(jnp.bfloat16)
    aligned = jnp.take(
        rotated_out.reshape(n_blocks, tok_rows, tile_width), block_map, axis=0
    ).reshape(tokens, tile_width)
    grad_tile = dot(aligned.T, rotated_in) / tokens
    damped = jnp.take(
        eigenvalues.reshape(tile_width, full_in // LANES, LANES), tile_order, axis=1
    ).reshape(tile_width, full_in)
    scaled = (grad_tile / damped).astype(jnp.bfloat16)
    projected = dot(scaled, in_rows.T).astype(jnp.bfloat16)
    return lax.psum_scatter(
        dot(basis_out[:WR], projected), "blk", scatter_dimension=0, tiled=True
    )


def solution(mesh):
    n = mesh.shape["blk"]

    def body(*args):
        wide = args[3].shape[1] % LANES == 0 and args[2].shape[1] % LANES == 0
        doubles = n & (n - 1) == 0 and args[0].shape[0] & (args[0].shape[0] - 1) == 0
        if wide and doubles and WR % (16 * n) == 0:
            return ring_body(n, *args)
        return gather_body(*args)

    placed = (
        P(("grp", "blk"), None),
        P(("grp", "blk"), None),
        P(None, "blk"),
        P(None, "blk"),
        P("blk", None),
        P(),
        P(),
    )
    return jax.shard_map(
        body, mesh=mesh, in_specs=placed, out_specs=P(("grp", "blk"), None), check_vma=False
    )
```

```python
import functools

import jax
import jax.numpy as jnp
from jax import lax
from jax.experimental import pallas as pl
from jax.experimental.pallas import tpu as pltpu
from jax.sharding import PartitionSpec as P

WR = 768
WC = 512
LANES = 128
MIB = 1 << 20


def ring_of(n):
    chips = n // 2
    return [*range(0, chips, 2), *range(chips - 1, 0, -2)]


def shift_pairs(n, by):
    ring = ring_of(n)
    return [
        (2 * ring[p] + c, 2 * ring[(p + by) % len(ring)] + c)
        for p in range(len(ring))
        for c in range(2)
    ]


def ring_source(me, steps, other, chips):
    chip, core = me // 2, lax.rem(me, 2)
    place = jnp.where(lax.rem(chip, 2) == 0, chip // 2, chips - 1 - chip // 2)
    place = lax.rem(place + chips - steps, chips)
    chip = jnp.where(place < chips // 2, 2 * place, 2 * (chips - 1 - place) + 1)
    return 2 * chip + (core ^ other)


def xor_pairs(n, key):
    return [(b, b ^ key) for b in range(n)]


def swap(x, n):
    return lax.ppermute(x, "blk", xor_pairs(n, 1))


def exchange(x, n, stride):
    groups = [list(range(first, n, stride)) for first in range(stride)]
    return lax.all_to_all(x, "blk", 0, 0, axis_index_groups=groups, tiled=True)


def bits_of(size):
    return size.bit_length() - 1


def held_tokens(me, tokens, tok_rows):
    row = lax.broadcasted_iota(jnp.int32, (tokens, tokens), 1)
    pairs = tokens // tok_rows // 4
    place = row >> bits_of(tok_rows)
    chip = 2 * (place & (pairs - 1)) + ((place >> bits_of(pairs)) & 1)
    other = row >> bits_of(tokens // 2)
    device = me ^ (2 * chip + other)
    return (device << bits_of(tok_rows)) + (row & (tok_rows - 1))


def reorder(wanted, held, rotated):
    order = jnp.where(wanted == held, 1.0, 0.0).astype(jnp.bfloat16)
    return jnp.dot(order, rotated.astype(jnp.bfloat16), preferred_element_type=jnp.float32)


def part_kernel(*refs):
    grads_ref, acts_ref = refs[-2:]
    first = grads_ref.shape[2]
    for at, ref in enumerate(refs[:-2]):
        grads_ref[at] = ref[0, :, :first]
        acts_ref[at] = ref[0, :, first:]


def rotate_in_kernel(tok_rows, near_ref, far_ref, basis_ref, out_ref):
    tokens = out_ref.shape[1]
    acts = jnp.concatenate([near_ref[...], far_ref[...]], axis=0)
    rotated = jnp.dot(acts, basis_ref[...], preferred_element_type=jnp.float32)
    wanted = lax.broadcasted_iota(jnp.int32, (tokens, tokens), 0)
    held = held_tokens(lax.axis_index("blk"), tokens, tok_rows)
    ordered = reorder(wanted, held, rotated).astype(jnp.bfloat16)
    for copy in range(out_ref.shape[0]):
        out_ref[copy] = ordered


def rotate_part(first, near_ref, far_ref, basis_ref, basis, total, sem):
    steps, depth = basis.shape[:2]

    def copy_of(step):
        rows = pl.ds(pl.multiple_of((first + step) * depth, depth), depth)
        return pltpu.make_async_copy(basis_ref.at[rows], basis.at[step], sem.at[step])

    @pl.loop(0, steps)
    def _(step):
        copy_of(step).start()

    @pl.loop(0, steps)
    def _(step):
        columns = pl.ds(pl.multiple_of((first + step) * depth, depth), depth)
        grads = jnp.concatenate([near_ref[:, columns], far_ref[:, columns]], axis=0)
        copy_of(step).wait()
        total[...] += jnp.dot(grads, basis[step], preferred_element_type=jnp.float32)


def rotate_first_kernel(near_ref, far_ref, basis_ref, out_ref, basis, sem):
    out_ref[...] = jnp.zeros_like(out_ref)
    rotate_part(0, near_ref, far_ref, basis_ref, basis, out_ref, sem)


def rotate_last_kernel(
    tok_rows,
    first,
    near_ref,
    far_ref,
    basis_ref,
    map_ref,
    start_ref,
    out_ref,
    basis,
    total,
    stored_map,
    sem,
):
    tokens = total.shape[0]
    map_copy = pltpu.make_async_copy(map_ref, stored_map, sem.at[basis.shape[0]])
    map_copy.start()
    total[...] = start_ref[...]
    rotate_part(first, near_ref, far_ref, basis_ref, basis, total, sem)
    map_copy.wait()
    row = lax.broadcasted_iota(jnp.int32, (tokens, tokens), 0)
    block = row >> bits_of(tok_rows)
    wanted = jnp.zeros_like(row)
    for stored in range(tokens // tok_rows):
        wanted = jnp.where(block == stored, stored_map[stored] * tok_rows, wanted)
    wanted += row & (tok_rows - 1)
    held = held_tokens(lax.axis_index("blk"), tokens, tok_rows)
    out_ref[...] = reorder(wanted, held, total[...]).T.astype(jnp.bfloat16)


def scale_kernel(
    begun, aligned_ref, near_ref, far_ref, tiles_ref, eigen_ref, out_ref, damped, tiles, sem
):
    blocks, depth = damped.shape[:2]
    chips, _, width = near_ref.shape

    def copy_of(block):
        rows = pl.ds(pl.multiple_of(block * depth, depth), depth)
        return pltpu.make_async_copy(eigen_ref.at[rows], damped.at[block], sem.at[block])

    tiles_copy = pltpu.make_async_copy(tiles_ref, tiles, sem.at[blocks])
    tiles_copy.start()

    @pl.loop(0, blocks)
    def _(block):
        copy_of(block).start()

    tiles_copy.wait()
    me = lax.axis_index("blk")

    @pl.loop(0, blocks)
    def _(block):
        rows = pl.ds(pl.multiple_of(block * depth, depth), depth)
        aligned = aligned_ref[rows, :]
        copy_of(block).wait()
        place = 0
        for steps in begun:
            for other, rotated_ref in enumerate((near_ref, far_ref)):
                source = ring_source(me, steps, other, chips)
                grad = jnp.dot(
                    aligned, rotated_ref[source // 2], preferred_element_type=jnp.float32
                )
                for first in range(0, width, LANES):
                    tile = tiles[(source * width + first) // LANES]
                    lanes = pl.ds(pl.multiple_of(tile * LANES, LANES), LANES)
                    eigen = damped[block, :, lanes]
                    inverse = pl.reciprocal(eigen, approx=True)
                    inverse = inverse * (2.0 - eigen * inverse)
                    scaled = grad[:, first : first + LANES] * inverse
                    out_ref[rows, place : place + LANES] = scaled.astype(jnp.bfloat16)
                    place += LANES


def project_kernel(cuts, scaled_ref, basis_out_ref, *refs):
    pieces = refs[:-4]
    out_ref, window_ref, basis, sem = refs[-4:]
    width = pieces[0].shape[0]
    rows = out_ref.shape[0] // 2
    copies = [
        pltpu.make_async_copy(piece, basis.at[pl.ds(at * width, width)], sem.at[at])
        for at, piece in enumerate(pieces)
    ]
    window_copy = pltpu.make_async_copy(
        basis_out_ref.at[pl.ds(0, window_ref.shape[0])], window_ref, sem.at[len(pieces)]
    )
    window_copy.start()
    for copy in copies:
        copy.start()
    for first, last in zip(cuts[:-1], cuts[1:]):
        for copy in copies[first:last]:
            copy.wait()
        deep = slice(first * width, last * width)

        @pl.loop(0, 2)
        def _(half):
            block = pl.ds(pl.multiple_of(half * rows, rows), rows)
            part = jnp.dot(
                scaled_ref[block, deep], basis[deep, :], preferred_element_type=jnp.float32
            )
            out_ref[block, :] = part if first == 0 else out_ref[block, :] + part

    window_copy.wait()


def window_kernel(scale, window_ref, scaled_ref, projected_ref, *refs):
    pieces = refs[:-3]
    send_ref, keep_ref, result = refs[-3:]
    chips, rows, _ = keep_ref.shape
    width = pieces[0].shape[0]
    total = projected_ref[...]
    first = scaled_ref.shape[1] - width * len(pieces)
    basis = jnp.concatenate([piece[...] for piece in pieces], axis=0)
    total += jnp.dot(scaled_ref[:, first:], basis, preferred_element_type=jnp.float32)
    result[...] = scale * jnp.dot(
        window_ref[...], total.astype(jnp.bfloat16), preferred_element_type=jnp.float32
    )
    core = lax.rem(lax.axis_index("blk"), 2)
    for k in range(chips):
        mine = pl.ds(pl.multiple_of((2 * k + core) * rows, rows), rows)
        keep_ref[k] = result[mine, :]
        other = pl.ds(pl.multiple_of((2 * k + 1 - core) * rows, rows), rows)
        send_ref[k] = result[other, :].astype(jnp.bfloat16)


def add_core_kernel(keys, keep_ref, got_ref, own_ref, *send_refs):
    chip = lax.axis_index("blk") // 2
    for key, ref in zip((0, *keys), (own_ref, *send_refs)):
        at = chip ^ key
        ref[...] = (keep_ref[at] + got_ref[at].astype(jnp.float32)).astype(ref.dtype)


def add_chips_kernel(own_ref, *refs):
    total = own_ref[...]
    for ref in refs[:-1]:
        total += ref[...].astype(jnp.float32)
    refs[-1][...] = total


VMEM = pl.BlockSpec(memory_space=pltpu.VMEM)
SMEM = pl.BlockSpec(memory_space=pltpu.SMEM)
ANY = pl.BlockSpec(memory_space=pl.ANY)
CHEAP = pl.CostEstimate(flops=1, bytes_accessed=1, transcendentals=0)


def after(first, *others):
    return lax.optimization_barrier((first, *others))


def ring_body(n, grad_out, activations, basis_out, basis_in, eigenvalues, tile_order, block_map):
    tok_rows, full_out = grad_out.shape
    tile_width = basis_out.shape[1]
    full_in, in_width = basis_in.shape
    tokens = n * tok_rows
    chips = n // 2
    to_right = lambda x: lax.ppermute(x, "blk", shift_pairs(n, 1))
    to_left = lambda x: lax.ppermute(x, "blk", shift_pairs(n, -1))
    steps = chips // 2

    own = basis_in[:WC].T

    pairs = chips // 2
    both = jnp.concatenate([grad_out, activations], axis=1)[None]
    got = [lax.ppermute(both, "blk", xor_pairs(n, 4 * key)) for key in range(1, pairs)]
    both, own, *got = after(both, own, *got)
    grads, acts = pl.pallas_call(
        part_kernel,
        out_shape=(
            jax.ShapeDtypeStruct((pairs, tok_rows, full_out), jnp.bfloat16),
            jax.ShapeDtypeStruct((pairs, tok_rows, full_in), jnp.bfloat16),
        ),
        in_specs=[VMEM] * pairs,
        out_specs=(VMEM, VMEM),
        compiler_params=pltpu.CompilerParams(vmem_limit_bytes=8 * MIB),
        name="part",
    )(both, *got)
    acts, grads, own = after(acts, grads, own)
    acts_got = lax.ppermute(acts, "blk", xor_pairs(n, 2))
    grads_got = lax.ppermute(grads, "blk", xor_pairs(n, 2))
    right, left = [own, to_right(own)], [own, to_left(own)]

    acts = jnp.concatenate([acts, acts_got], axis=0).reshape(tokens // 2, full_in)
    rotated = pl.pallas_call(
        functools.partial(rotate_in_kernel, tok_rows),
        out_shape=jax.ShapeDtypeStruct((chips, tokens, in_width), jnp.bfloat16),
        in_specs=[VMEM, VMEM, VMEM],
        out_specs=VMEM,
        compiler_params=pltpu.CompilerParams(vmem_limit_bytes=8 * MIB),
        cost_estimate=CHEAP,
        name="rotate_in",
    )(acts, swap(acts, n), basis_in)
    own_far = swap(own, n)
    grads_got, right[-1], left[-1], own_far, _ = after(
        grads_got, right[-1], left[-1], own_far, rotated
    )
    rotated = exchange(rotated, n, 2)
    near = [right[0], right[1], left[1]]
    while len(right) < steps - 1:
        right.append(to_right(right[-1]))
        left.append(to_left(left[-1]))
    grads = jnp.concatenate([grads, grads_got], axis=0).reshape(tokens // 2, full_out)
    grads_far = swap(grads, n)
    far = [swap(piece, n) for piece in near[1:]]
    grads, grads_far, *far = after(grads, grads_far, *far)
    far = [own_far, *far]

    depth = 1024
    cuts = (0, full_out // depth // 2, full_out // depth)
    rotate = lambda kernel, count, scratch, shape, dtype, *operands: pl.pallas_call(
        kernel,
        out_shape=jax.ShapeDtypeStruct(shape, dtype),
        in_specs=[VMEM, VMEM, ANY, ANY, VMEM][: len(operands)],
        out_specs=VMEM,
        scratch_shapes=[pltpu.VMEM((count, depth, tile_width), jnp.bfloat16)]
        + scratch
        + [pltpu.SemaphoreType.DMA((count + 1,))],
        compiler_params=pltpu.CompilerParams(vmem_limit_bytes=40 * MIB),
        cost_estimate=CHEAP,
        name=kernel.func.__name__[:-7],
    )(*operands)
    start = rotate(
        functools.partial(rotate_first_kernel),
        cuts[1],
        [],
        (tokens, tile_width),
        jnp.float32,
        grads,
        grads_far,
        basis_out,
    )
    start, grads, rotated, right[-1], left[-1] = after(
        start, grads, rotated, right[-1], left[-1]
    )
    rotated_far = swap(rotated, n)
    near += [right[-1], left[-1]]
    far += [swap(right[-1], n), swap(left[-1], n)]
    right.append(to_right(right[-1]))
    left.append(to_left(left[-1]))
    aligned = rotate(
        functools.partial(rotate_last_kernel, tok_rows, cuts[1]),
        cuts[2] - cuts[1],
        [
            pltpu.VMEM((tokens, tile_width), jnp.float32),
            pltpu.SMEM(block_map.shape, jnp.int32),
        ],
        (tile_width, tokens),
        jnp.bfloat16,
        grads,
        grads_far,
        basis_out,
        block_map,
        start,
    )

    aligned, rotated_far, right[-1], left[-1], *far = after(
        aligned, rotated_far, right[-1], left[-1], *far
    )
    cut = in_width // 2
    last = [to_right(right[-1][:cut]), to_left(left[-1][cut:])]
    near += [right[-1], left[-1]]
    far += [swap(piece, n) for piece in near[len(far) :]]
    begun = [0] + [at for step in range(1, steps) for at in (step, chips - step)] + [steps]
    blocks = 8
    scaled = pl.pallas_call(
        functools.partial(scale_kernel, begun),
        out_shape=jax.ShapeDtypeStruct((tile_width, full_in), jnp.bfloat16),
        in_specs=[VMEM, VMEM, VMEM, ANY, ANY],
        out_specs=VMEM,
        scratch_shapes=[
            pltpu.VMEM((blocks, tile_width // blocks, full_in), jnp.float32),
            pltpu.SMEM(tile_order.shape, jnp.int32),
            pltpu.SemaphoreType.DMA((blocks + 1,)),
        ],
        compiler_params=pltpu.CompilerParams(vmem_limit_bytes=40 * MIB),
        cost_estimate=CHEAP,
        name="scale",
    )(aligned, rotated, rotated_far, tile_order, eigenvalues)

    scaled, *last = after(scaled, *last, *far[-2:])
    far[-2:] = last[2:]
    last = last[:2]
    last += [swap(piece, n) for piece in last]
    pieces = [piece for pair in zip(near, far) for piece in pair]
    projected, window = pl.pallas_call(
        functools.partial(project_kernel, (0, 6, len(pieces))),
        out_shape=(
            jax.ShapeDtypeStruct((tile_width, WC), jnp.float32),
            jax.ShapeDtypeStruct((WR, tile_width), jnp.bfloat16),
        ),
        in_specs=[VMEM] + [ANY] * (len(pieces) + 1),
        out_specs=(VMEM, VMEM),
        scratch_shapes=[
            pltpu.VMEM((len(pieces) * in_width, WC), jnp.bfloat16),
            pltpu.SemaphoreType.DMA((len(pieces) + 1,)),
        ],
        compiler_params=pltpu.CompilerParams(vmem_limit_bytes=24 * MIB),
        cost_estimate=CHEAP,
        name="project",
    )(scaled, basis_out, *pieces)

    rows = WR // n
    send, keep = pl.pallas_call(
        functools.partial(window_kernel, 1.0 / tokens),
        out_shape=(
            jax.ShapeDtypeStruct((chips, rows, WC), jnp.bfloat16),
            jax.ShapeDtypeStruct((chips, rows, WC), jnp.float32),
        ),
        in_specs=[VMEM] * 7,
        out_specs=(VMEM, VMEM),
        scratch_shapes=[pltpu.VMEM((WR, WC), jnp.float32)],
        compiler_params=pltpu.CompilerParams(vmem_limit_bytes=24 * MIB),
        cost_estimate=CHEAP,
        name="window",
    )(window, scaled, projected, *last)

    keys = sorted(range(1, chips), key=lambda key: -(key & -2))
    small = pltpu.CompilerParams(vmem_limit_bytes=8 * MIB)
    own, *sends = pl.pallas_call(
        functools.partial(add_core_kernel, keys),
        out_shape=[jax.ShapeDtypeStruct((rows, WC), jnp.float32)]
        + [jax.ShapeDtypeStruct((rows, WC), jnp.bfloat16)] * len(keys),
        in_specs=[VMEM, VMEM],
        out_specs=[VMEM] * chips,
        compiler_params=small,
        name="add_core",
    )(keep, swap(send, n))
    arrived = [lax.ppermute(x, "blk", xor_pairs(n, 2 * key)) for key, x in zip(keys, sends)]
    return pl.pallas_call(
        add_chips_kernel,
        out_shape=jax.ShapeDtypeStruct((rows, WC), jnp.float32),
        in_specs=[VMEM] * chips,
        out_specs=VMEM,
        compiler_params=small,
        name="add_chips",
    )(own, *arrived)


def gather_body(grad_out, activations, basis_out, basis_in, eigenvalues, tile_order, block_map):
    n_blocks = lax.axis_size("blk")
    tile_width = basis_out.shape[1]
    tok_rows = grad_out.shape[0]
    full_in = eigenvalues.shape[1]
    tokens = n_blocks * tok_rows
    dot = functools.partial(jnp.dot, preferred_element_type=jnp.float32)
    in_rows = lax.all_gather(basis_in[:WC], "blk", axis=1, tiled=True)
    acts = lax.all_gather(activations, "blk", axis=0, tiled=True)
    in_tile = dot(acts, basis_in).astype(jnp.bfloat16)
    rotated_in = lax.all_gather(in_tile, "blk", axis=1, tiled=True)
    grads = lax.all_gather(grad_out, "blk", axis=0, tiled=True)
    rotated_out = dot(grads, basis_out).astype(jnp.bfloat16)
    aligned = jnp.take(
        rotated_out.reshape(n_blocks, tok_rows, tile_width), block_map, axis=0
    ).reshape(tokens, tile_width)
    grad_tile = dot(aligned.T, rotated_in) / tokens
    damped = jnp.take(
        eigenvalues.reshape(tile_width, full_in // LANES, LANES), tile_order, axis=1
    ).reshape(tile_width, full_in)
    scaled = (grad_tile / damped).astype(jnp.bfloat16)
    projected = dot(scaled, in_rows.T).astype(jnp.bfloat16)
    return lax.psum_scatter(
        dot(basis_out[:WR], projected), "blk", scatter_dimension=0, tiled=True
    )


def solution(mesh):
    n = mesh.shape["blk"]

    def body(*args):
        wide = args[3].shape[1] % LANES == 0 and args[2].shape[1] % LANES == 0
        doubles = n & (n - 1) == 0 and args[0].shape[0] & (args[0].shape[0] - 1) == 0
        if wide and doubles and WR % (16 * n) == 0:
            return ring_body(n, *args)
        return gather_body(*args)

    placed = (
        P(("grp", "blk"), None),
        P(("grp", "blk"), None),
        P(None, "blk"),
        P(None, "blk"),
        P("blk", None),
        P(),
        P(),
    )
    return jax.shard_map(
        body, mesh=mesh, in_specs=placed, out_specs=P(("grp", "blk"), None), check_vma=False
    )
```

```python
import functools

import jax
import jax.numpy as jnp
from jax import lax
from jax.experimental import pallas as pl
from jax.experimental.pallas import tpu as pltpu
from jax.sharding import PartitionSpec as P

WR = 768
WC = 512
LANES = 128
MIB = 1 << 20


def ring_of(n):
    chips = n // 2
    return [*range(0, chips, 2), *range(chips - 1, 0, -2)]


def shift_pairs(n, by):
    ring = ring_of(n)
    return [
        (2 * ring[p] + c, 2 * ring[(p + by) % len(ring)] + c)
        for p in range(len(ring))
        for c in range(2)
    ]


def ring_source(me, steps, other, chips):
    chip, core = me // 2, lax.rem(me, 2)
    place = jnp.where(lax.rem(chip, 2) == 0, chip // 2, chips - 1 - chip // 2)
    place = lax.rem(place + chips - steps, chips)
    chip = jnp.where(place < chips // 2, 2 * place, 2 * (chips - 1 - place) + 1)
    return 2 * chip + (core ^ other)


def xor_pairs(n, key):
    return [(b, b ^ key) for b in range(n)]


def swap(x, n):
    return lax.ppermute(x, "blk", xor_pairs(n, 1))


def bits_of(size):
    return size.bit_length() - 1


def held_tokens(me, tokens, tok_rows):
    row = lax.broadcasted_iota(jnp.int32, (tokens, tokens), 1)
    pairs = tokens // tok_rows // 4
    place = row >> bits_of(tok_rows)
    chip = 2 * (place & (pairs - 1)) + ((place >> bits_of(pairs)) & 1)
    other = row >> bits_of(tokens // 2)
    device = me ^ (2 * chip + other)
    return (device << bits_of(tok_rows)) + (row & (tok_rows - 1))


def reorder(wanted, held, rotated):
    order = jnp.where(wanted == held, 1.0, 0.0).astype(jnp.bfloat16)
    return jnp.dot(order, rotated.astype(jnp.bfloat16), preferred_element_type=jnp.float32)


def part_kernel(*refs):
    grads_ref, acts_ref = refs[-2:]
    first = grads_ref.shape[2]
    for at, ref in enumerate(refs[:-2]):
        grads_ref[at] = ref[0, :, :first]
        acts_ref[at] = ref[0, :, first:]


def rotate_in_kernel(tok_rows, near_ref, far_ref, basis_ref, out_ref):
    tokens = out_ref.shape[0]
    depth = near_ref.shape[2]
    acts = jnp.concatenate([ref[...].reshape(-1, depth) for ref in (near_ref, far_ref)], axis=0)
    rotated = jnp.dot(acts, basis_ref[...], preferred_element_type=jnp.float32)
    wanted = lax.broadcasted_iota(jnp.int32, (tokens, tokens), 0)
    held = held_tokens(lax.axis_index("blk"), tokens, tok_rows)
    out_ref[...] = reorder(wanted, held, rotated).astype(jnp.bfloat16)


def stack_kernel(first_ref, last_ref, out_ref):
    half = first_ref.shape[0]
    out_ref[:half] = first_ref[...]
    out_ref[half:] = last_ref[...]


def hold_kernel(basis_ref, held_ref, sem):
    steps, depth = held_ref.shape[:2]
    copies = [
        pltpu.make_async_copy(
            basis_ref.at[pl.ds(step * depth, depth)], held_ref.at[step], sem.at[step]
        )
        for step in range(steps)
    ]
    for copy in copies:
        copy.start()
    for copy in copies:
        copy.wait()


def rotate_part(first, near_ref, far_ref, held_ref, basis_ref, basis, total, sem):
    steps, depth = basis.shape[:2]
    held = 0 if held_ref is None else held_ref.shape[0]

    def copy_of(step):
        rows = pl.ds(pl.multiple_of((first + held + step) * depth, depth), depth)
        return pltpu.make_async_copy(basis_ref.at[rows], basis.at[step], sem.at[step])

    def grads_of(step):
        columns = pl.ds(pl.multiple_of((first + step) * depth, depth), depth)
        rows = [ref[:, :, columns].reshape(-1, depth) for ref in (near_ref, far_ref)]
        return jnp.concatenate(rows, axis=0)

    @pl.loop(0, steps)
    def _(step):
        copy_of(step).start()

    if held:

        @pl.loop(0, held)
        def _(step):
            part = jnp.dot(grads_of(step), held_ref[step], preferred_element_type=jnp.float32)
            total[...] += part

    @pl.loop(0, steps)
    def _(step):
        grads = grads_of(held + step)
        copy_of(step).wait()
        total[...] += jnp.dot(grads, basis[step], preferred_element_type=jnp.float32)


def rotate_first_kernel(near_ref, far_ref, held_ref, basis_ref, out_ref, basis, sem):
    out_ref[...] = jnp.zeros_like(out_ref)
    rotate_part(0, near_ref, far_ref, held_ref, basis_ref, basis, out_ref, sem)


def rotate_last_kernel(
    tok_rows,
    first,
    near_ref,
    far_ref,
    basis_ref,
    map_ref,
    start_ref,
    out_ref,
    basis,
    total,
    stored_map,
    sem,
):
    tokens = total.shape[0]
    map_copy = pltpu.make_async_copy(map_ref, stored_map, sem.at[basis.shape[0]])
    map_copy.start()
    total[...] = start_ref[...]
    rotate_part(first, near_ref, far_ref, None, basis_ref, basis, total, sem)
    map_copy.wait()
    row = lax.broadcasted_iota(jnp.int32, (tokens, tokens), 0)
    block = row >> bits_of(tok_rows)
    wanted = jnp.zeros_like(row)
    for stored in range(tokens // tok_rows):
        wanted = jnp.where(block == stored, stored_map[stored] * tok_rows, wanted)
    wanted += row & (tok_rows - 1)
    held = held_tokens(lax.axis_index("blk"), tokens, tok_rows)
    out_ref[...] = reorder(wanted, held, total[...]).T.astype(jnp.bfloat16)


def scale_kernel(
    begun, aligned_ref, *refs
):
    rotated_refs, (tiles_ref, eigen_ref, out_ref, damped, tiles, sem) = refs[:4], refs[4:]
    blocks, depth = damped.shape[:2]
    pairs, _, width = rotated_refs[0].shape
    chips = 2 * pairs

    def copy_of(block):
        rows = pl.ds(pl.multiple_of(block * depth, depth), depth)
        return pltpu.make_async_copy(eigen_ref.at[rows], damped.at[block], sem.at[block])

    tiles_copy = pltpu.make_async_copy(tiles_ref, tiles, sem.at[blocks])
    tiles_copy.start()

    @pl.loop(0, blocks)
    def _(block):
        copy_of(block).start()

    tiles_copy.wait()
    me = lax.axis_index("blk")

    @pl.loop(0, blocks)
    def _(block):
        rows = pl.ds(pl.multiple_of(block * depth, depth), depth)
        aligned = aligned_ref[rows, :]
        copy_of(block).wait()
        place = 0
        for steps in begun:
            for other in range(2):
                source = ring_source(me, steps, other, chips)
                key = (source ^ me) // 2
                same, paired = (ref[key // 2] for ref in rotated_refs[2 * other : 2 * other + 2])
                rotated = jnp.where(lax.rem(key, 2) == 0, same, paired)
                grad = jnp.dot(aligned, rotated, preferred_element_type=jnp.float32)
                for first in range(0, width, LANES):
                    tile = tiles[(source * width + first) // LANES]
                    lanes = pl.ds(pl.multiple_of(tile * LANES, LANES), LANES)
                    eigen = damped[block, :, lanes]
                    inverse = pl.reciprocal(eigen, approx=True)
                    inverse = inverse * (2.0 - eigen * inverse)
                    scaled = grad[:, first : first + LANES] * inverse
                    out_ref[rows, place : place + LANES] = scaled.astype(jnp.bfloat16)
                    place += LANES


def project_kernel(cuts, scaled_ref, basis_out_ref, *refs):
    pieces = refs[:-4]
    out_ref, window_ref, basis, sem = refs[-4:]
    width = pieces[0].shape[0]
    rows = out_ref.shape[0] // 2
    copies = [
        pltpu.make_async_copy(piece, basis.at[pl.ds(at * width, width)], sem.at[at])
        for at, piece in enumerate(pieces)
    ]
    window_copy = pltpu.make_async_copy(
        basis_out_ref.at[pl.ds(0, window_ref.shape[0])], window_ref, sem.at[len(pieces)]
    )
    window_copy.start()
    for copy in copies:
        copy.start()
    for first, last in zip(cuts[:-1], cuts[1:]):
        for copy in copies[first:last]:
            copy.wait()
        deep = slice(first * width, last * width)

        @pl.loop(0, 2)
        def _(half):
            block = pl.ds(pl.multiple_of(half * rows, rows), rows)
            part = jnp.dot(
                scaled_ref[block, deep], basis[deep, :], preferred_element_type=jnp.float32
            )
            out_ref[block, :] = part if first == 0 else out_ref[block, :] + part

    window_copy.wait()


def window_kernel(scale, window_ref, scaled_ref, projected_ref, *refs):
    pieces = refs[:-3]
    send_ref, keep_ref, result = refs[-3:]
    chips, rows, _ = keep_ref.shape
    width = pieces[0].shape[0]
    total = projected_ref[...]
    first = scaled_ref.shape[1] - width * len(pieces)
    basis = jnp.concatenate([piece[...] for piece in pieces], axis=0)
    total += jnp.dot(scaled_ref[:, first:], basis, preferred_element_type=jnp.float32)
    result[...] = scale * jnp.dot(
        window_ref[...], total.astype(jnp.bfloat16), preferred_element_type=jnp.float32
    )
    core = lax.rem(lax.axis_index("blk"), 2)
    for k in range(chips):
        mine = pl.ds(pl.multiple_of((2 * k + core) * rows, rows), rows)
        keep_ref[k] = result[mine, :]
        other = pl.ds(pl.multiple_of((2 * k + 1 - core) * rows, rows), rows)
        send_ref[k] = result[other, :].astype(jnp.bfloat16)


def add_core_kernel(keys, keep_ref, got_ref, own_ref, *send_refs):
    chip = lax.axis_index("blk") // 2
    for key, ref in zip((0, *keys), (own_ref, *send_refs)):
        at = chip ^ key
        ref[...] = (keep_ref[at] + got_ref[at].astype(jnp.float32)).astype(ref.dtype)


def add_chips_kernel(own_ref, *refs):
    total = own_ref[...]
    for ref in refs[:-1]:
        total += ref[...].astype(jnp.float32)
    refs[-1][...] = total


VMEM = pl.BlockSpec(memory_space=pltpu.VMEM)
SMEM = pl.BlockSpec(memory_space=pltpu.SMEM)
ANY = pl.BlockSpec(memory_space=pl.ANY)
CHEAP = pl.CostEstimate(flops=1, bytes_accessed=1, transcendentals=0)


def after(first, *others):
    return lax.optimization_barrier((first, *others))


def ring_body(n, grad_out, activations, basis_out, basis_in, eigenvalues, tile_order, block_map):
    tok_rows, full_out = grad_out.shape
    tile_width = basis_out.shape[1]
    full_in, in_width = basis_in.shape
    tokens = n * tok_rows
    chips = n // 2
    to_right = lambda x: lax.ppermute(x, "blk", shift_pairs(n, 1))
    to_left = lambda x: lax.ppermute(x, "blk", shift_pairs(n, -1))
    steps = chips // 2

    own = basis_in[:WC].T

    pairs = chips // 2
    both = jnp.concatenate([grad_out, activations], axis=1)[None]
    got = [lax.ppermute(both, "blk", xor_pairs(n, 4 * key)) for key in range(1, pairs)]
    depth, ahead, later = 1024, 4, 5
    held = pl.pallas_call(
        hold_kernel,
        out_shape=jax.ShapeDtypeStruct((ahead, depth, tile_width), jnp.bfloat16),
        in_specs=[ANY],
        out_specs=VMEM,
        scratch_shapes=[pltpu.SemaphoreType.DMA((ahead,))],
        compiler_params=pltpu.CompilerParams(vmem_limit_bytes=40 * MIB),
        cost_estimate=CHEAP,
        name="hold",
    )(basis_out)

    both, own, held, *got = after(both, own, held, *got)
    grads, acts = pl.pallas_call(
        part_kernel,
        out_shape=(
            jax.ShapeDtypeStruct((pairs, tok_rows, full_out), jnp.bfloat16),
            jax.ShapeDtypeStruct((pairs, tok_rows, full_in), jnp.bfloat16),
        ),
        in_specs=[VMEM] * pairs,
        out_specs=(VMEM, VMEM),
        compiler_params=pltpu.CompilerParams(vmem_limit_bytes=8 * MIB),
        name="part",
    )(both, *got)
    acts, grads, own = after(acts, grads, own)
    acts_got = lax.ppermute(acts, "blk", xor_pairs(n, 2))
    grads_got = lax.ppermute(grads, "blk", xor_pairs(n, 2))
    right, left = [own, to_right(own)], [own, to_left(own)]

    acts = jnp.concatenate([acts, acts_got], axis=0)
    rotated = pl.pallas_call(
        functools.partial(rotate_in_kernel, tok_rows),
        out_shape=jax.ShapeDtypeStruct((tokens, in_width), jnp.bfloat16),
        in_specs=[VMEM, VMEM, VMEM],
        out_specs=VMEM,
        compiler_params=pltpu.CompilerParams(vmem_limit_bytes=8 * MIB),
        cost_estimate=CHEAP,
        name="rotate_in",
    )(acts, swap(acts, n), basis_in)

    def doubled(x, key):
        return pl.pallas_call(
            stack_kernel,
            out_shape=jax.ShapeDtypeStruct((2 * x.shape[0], *x.shape[1:]), x.dtype),
            in_specs=[VMEM, VMEM],
            out_specs=VMEM,
            compiler_params=pltpu.CompilerParams(vmem_limit_bytes=8 * MIB),
            cost_estimate=CHEAP,
            name="stack",
        )(x, lax.ppermute(x, "blk", xor_pairs(n, key)))

    rotated = doubled(rotated[None], 4)
    grads_got, rotated, right[-1], left[-1] = after(grads_got, rotated, right[-1], left[-1])
    key = 8
    while key < n:
        rotated = doubled(rotated, key)
        key *= 2
    near = [right[0], right[1], left[1]]
    while len(right) < steps - 1:
        right.append(to_right(right[-1]))
        left.append(to_left(left[-1]))
    grads = jnp.concatenate([grads, grads_got], axis=0)
    grads_far = swap(grads, n)
    far = [swap(piece, n) for piece in near]
    grads, grads_far, rotated, *far = after(grads, grads_far, rotated, *far)
    rotated = [rotated, lax.ppermute(rotated, "blk", xor_pairs(n, 2))]

    rotate = lambda kernel, count, scratch, shape, dtype, *operands: pl.pallas_call(
        kernel,
        out_shape=jax.ShapeDtypeStruct(shape, dtype),
        in_specs=[ANY if x is basis_out or x is block_map else VMEM for x in operands],
        out_specs=VMEM,
        scratch_shapes=[pltpu.VMEM((count, depth, tile_width), jnp.bfloat16)]
        + scratch
        + [pltpu.SemaphoreType.DMA((count + 1,))],
        compiler_params=pltpu.CompilerParams(vmem_limit_bytes=40 * MIB),
        cost_estimate=CHEAP,
        name=kernel.func.__name__[:-7],
    )(*operands)
    start = rotate(
        functools.partial(rotate_first_kernel),
        full_out // depth - ahead - later,
        [],
        (tokens, tile_width),
        jnp.float32,
        grads,
        grads_far,
        held,
        basis_out,
    )
    start, grads, right[-1], left[-1], *rotated = after(
        start, grads, right[-1], left[-1], *rotated
    )
    rotated += [swap(x, n) for x in rotated]
    near += [right[-1], left[-1]]
    far += [swap(right[-1], n), swap(left[-1], n)]
    right.append(to_right(right[-1]))
    left.append(to_left(left[-1]))
    aligned = rotate(
        functools.partial(rotate_last_kernel, tok_rows, full_out // depth - later),
        later,
        [
            pltpu.VMEM((tokens, tile_width), jnp.float32),
            pltpu.SMEM(block_map.shape, jnp.int32),
        ],
        (tile_width, tokens),
        jnp.bfloat16,
        grads,
        grads_far,
        basis_out,
        block_map,
        start,
    )

    aligned, right[-1], left[-1], *both = after(aligned, right[-1], left[-1], *rotated, *far)
    rotated, far = both[:4], both[4:]
    cut = in_width // 2
    last = [to_right(right[-1][:cut]), to_left(left[-1][cut:])]
    near += [right[-1], left[-1]]
    far += [swap(piece, n) for piece in near[len(far) :]]
    begun = [0] + [at for step in range(1, steps) for at in (step, chips - step)] + [steps]
    blocks = 8
    scaled = pl.pallas_call(
        functools.partial(scale_kernel, begun),
        out_shape=jax.ShapeDtypeStruct((tile_width, full_in), jnp.bfloat16),
        in_specs=[VMEM] * 5 + [ANY] * 2,
        out_specs=VMEM,
        scratch_shapes=[
            pltpu.VMEM((blocks, tile_width // blocks, full_in), jnp.float32),
            pltpu.SMEM(tile_order.shape, jnp.int32),
            pltpu.SemaphoreType.DMA((blocks + 1,)),
        ],
        compiler_params=pltpu.CompilerParams(vmem_limit_bytes=40 * MIB),
        cost_estimate=CHEAP,
        name="scale",
    )(aligned, *rotated, tile_order, eigenvalues)

    scaled, *last = after(scaled, *last, *far[-2:])
    far[-2:] = last[2:]
    last = last[:2]
    last += [swap(piece, n) for piece in last]
    pieces = [piece for pair in zip(near, far) for piece in pair]
    projected, window = pl.pallas_call(
        functools.partial(project_kernel, (0, 6, len(pieces))),
        out_shape=(
            jax.ShapeDtypeStruct((tile_width, WC), jnp.float32),
            jax.ShapeDtypeStruct((WR, tile_width), jnp.bfloat16),
        ),
        in_specs=[VMEM] + [ANY] * (len(pieces) + 1),
        out_specs=(VMEM, VMEM),
        scratch_shapes=[
            pltpu.VMEM((len(pieces) * in_width, WC), jnp.bfloat16),
            pltpu.SemaphoreType.DMA((len(pieces) + 1,)),
        ],
        compiler_params=pltpu.CompilerParams(vmem_limit_bytes=24 * MIB),
        cost_estimate=CHEAP,
        name="project",
    )(scaled, basis_out, *pieces)

    rows = WR // n
    send, keep = pl.pallas_call(
        functools.partial(window_kernel, 1.0 / tokens),
        out_shape=(
            jax.ShapeDtypeStruct((chips, rows, WC), jnp.bfloat16),
            jax.ShapeDtypeStruct((chips, rows, WC), jnp.float32),
        ),
        in_specs=[VMEM] * 7,
        out_specs=(VMEM, VMEM),
        scratch_shapes=[pltpu.VMEM((WR, WC), jnp.float32)],
        compiler_params=pltpu.CompilerParams(vmem_limit_bytes=24 * MIB),
        cost_estimate=CHEAP,
        name="window",
    )(window, scaled, projected, *last)

    keys = sorted(range(1, chips), key=lambda key: -(key & -2))
    small = pltpu.CompilerParams(vmem_limit_bytes=8 * MIB)
    own, *sends = pl.pallas_call(
        functools.partial(add_core_kernel, keys),
        out_shape=[jax.ShapeDtypeStruct((rows, WC), jnp.float32)]
        + [jax.ShapeDtypeStruct((rows, WC), jnp.bfloat16)] * len(keys),
        in_specs=[VMEM, VMEM],
        out_specs=[VMEM] * chips,
        compiler_params=small,
        name="add_core",
    )(keep, swap(send, n))
    arrived = [lax.ppermute(x, "blk", xor_pairs(n, 2 * key)) for key, x in zip(keys, sends)]
    return pl.pallas_call(
        add_chips_kernel,
        out_shape=jax.ShapeDtypeStruct((rows, WC), jnp.float32),
        in_specs=[VMEM] * chips,
        out_specs=VMEM,
        compiler_params=small,
        name="add_chips",
    )(own, *arrived)


def gather_body(grad_out, activations, basis_out, basis_in, eigenvalues, tile_order, block_map):
    n_blocks = lax.axis_size("blk")
    tile_width = basis_out.shape[1]
    tok_rows = grad_out.shape[0]
    full_in = eigenvalues.shape[1]
    tokens = n_blocks * tok_rows
    dot = functools.partial(jnp.dot, preferred_element_type=jnp.float32)
    in_rows = lax.all_gather(basis_in[:WC], "blk", axis=1, tiled=True)
    acts = lax.all_gather(activations, "blk", axis=0, tiled=True)
    in_tile = dot(acts, basis_in).astype(jnp.bfloat16)
    rotated_in = lax.all_gather(in_tile, "blk", axis=1, tiled=True)
    grads = lax.all_gather(grad_out, "blk", axis=0, tiled=True)
    rotated_out = dot(grads, basis_out).astype(jnp.bfloat16)
    aligned = jnp.take(
        rotated_out.reshape(n_blocks, tok_rows, tile_width), block_map, axis=0
    ).reshape(tokens, tile_width)
    grad_tile = dot(aligned.T, rotated_in) / tokens
    damped = jnp.take(
        eigenvalues.reshape(tile_width, full_in // LANES, LANES), tile_order, axis=1
    ).reshape(tile_width, full_in)
    scaled = (grad_tile / damped).astype(jnp.bfloat16)
    projected = dot(scaled, in_rows.T).astype(jnp.bfloat16)
    return lax.psum_scatter(
        dot(basis_out[:WR], projected), "blk", scatter_dimension=0, tiled=True
    )


def solution(mesh):
    n = mesh.shape["blk"]

    def body(*args):
        wide = args[3].shape[1] % LANES == 0 and args[2].shape[1] % LANES == 0
        doubles = n & (n - 1) == 0 and args[0].shape[0] & (args[0].shape[0] - 1) == 0
        if wide and doubles and WR % (16 * n) == 0:
            return ring_body(n, *args)
        return gather_body(*args)

    placed = (
        P(("grp", "blk"), None),
        P(("grp", "blk"), None),
        P(None, "blk"),
        P(None, "blk"),
        P("blk", None),
        P(),
        P(),
    )
    return jax.shard_map(
        body, mesh=mesh, in_specs=placed, out_specs=P(("grp", "blk"), None), check_vma=False
    )
```

```python
import functools

import jax
import jax.numpy as jnp
from jax import lax
from jax.experimental import pallas as pl
from jax.experimental.pallas import tpu as pltpu
from jax.sharding import PartitionSpec as P

WR = 768
WC = 512
LANES = 128
MIB = 1 << 20


def ring_of(n):
    chips = n // 2
    return [*range(0, chips, 2), *range(chips - 1, 0, -2)]


def shift_pairs(n, by):
    ring = ring_of(n)
    return [
        (2 * ring[p] + c, 2 * ring[(p + by) % len(ring)] + c)
        for p in range(len(ring))
        for c in range(2)
    ]


def ring_source(me, steps, other, chips):
    chip, core = me // 2, lax.rem(me, 2)
    place = jnp.where(lax.rem(chip, 2) == 0, chip // 2, chips - 1 - chip // 2)
    place = lax.rem(place + chips - steps, chips)
    chip = jnp.where(place < chips // 2, 2 * place, 2 * (chips - 1 - place) + 1)
    return 2 * chip + (core ^ other)


def xor_pairs(n, key):
    return [(b, b ^ key) for b in range(n)]


def swap(x, n):
    return lax.ppermute(x, "blk", xor_pairs(n, 1))


def bits_of(size):
    return size.bit_length() - 1


def held_tokens(me, tokens, tok_rows):
    row = lax.broadcasted_iota(jnp.int32, (tokens, tokens), 1)
    pairs = tokens // tok_rows // 4
    place = row >> bits_of(tok_rows)
    chip = 2 * (place & (pairs - 1)) + ((place >> bits_of(pairs)) & 1)
    other = row >> bits_of(tokens // 2)
    device = me ^ (2 * chip + other)
    return (device << bits_of(tok_rows)) + (row & (tok_rows - 1))


def reorder(wanted, held, rotated):
    order = jnp.where(wanted == held, 1.0, 0.0).astype(jnp.bfloat16)
    return jnp.dot(order, rotated.astype(jnp.bfloat16), preferred_element_type=jnp.float32)


def part_kernel(*refs):
    grads_ref, acts_ref = refs[-2:]
    first = grads_ref.shape[2]
    for at, ref in enumerate(refs[:-2]):
        grads_ref[at] = ref[0, :, :first]
        acts_ref[at] = ref[0, :, first:]


def rotate_in_kernel(tok_rows, near_ref, far_ref, basis_ref, out_ref):
    tokens = out_ref.shape[0]
    depth = near_ref.shape[2]
    acts = jnp.concatenate([ref[...].reshape(-1, depth) for ref in (near_ref, far_ref)], axis=0)
    rotated = jnp.dot(acts, basis_ref[...], preferred_element_type=jnp.float32)
    wanted = lax.broadcasted_iota(jnp.int32, (tokens, tokens), 0)
    held = held_tokens(lax.axis_index("blk"), tokens, tok_rows)
    out_ref[...] = reorder(wanted, held, rotated).astype(jnp.bfloat16)


def stack_kernel(first_ref, last_ref, out_ref):
    half = first_ref.shape[0]
    out_ref[:half] = first_ref[...]
    out_ref[half:] = last_ref[...]


def rotate_part(first, near_ref, far_ref, basis_ref, basis, total, sem):
    steps, depth = basis.shape[:2]

    def copy_of(step):
        rows = pl.ds(pl.multiple_of((first + step) * depth, depth), depth)
        return pltpu.make_async_copy(basis_ref.at[rows], basis.at[step], sem.at[step])

    @pl.loop(0, steps)
    def _(step):
        copy_of(step).start()

    @pl.loop(0, steps)
    def _(step):
        columns = pl.ds(pl.multiple_of((first + step) * depth, depth), depth)
        rows = [ref[:, :, columns].reshape(-1, depth) for ref in (near_ref, far_ref)]
        grads = jnp.concatenate(rows, axis=0)
        copy_of(step).wait()
        total[...] += jnp.dot(grads, basis[step], preferred_element_type=jnp.float32)


def rotate_first_kernel(near_ref, far_ref, basis_ref, out_ref, basis, sem):
    out_ref[...] = jnp.zeros_like(out_ref)
    rotate_part(0, near_ref, far_ref, basis_ref, basis, out_ref, sem)


def rotate_last_kernel(
    tok_rows,
    first,
    near_ref,
    far_ref,
    basis_ref,
    map_ref,
    start_ref,
    out_ref,
    basis,
    total,
    stored_map,
    sem,
):
    tokens = total.shape[0]
    map_copy = pltpu.make_async_copy(map_ref, stored_map, sem.at[basis.shape[0]])
    map_copy.start()
    total[...] = start_ref[...]
    rotate_part(first, near_ref, far_ref, basis_ref, basis, total, sem)
    map_copy.wait()
    row = lax.broadcasted_iota(jnp.int32, (tokens, tokens), 0)
    block = row >> bits_of(tok_rows)
    wanted = jnp.zeros_like(row)
    for stored in range(tokens // tok_rows):
        wanted = jnp.where(block == stored, stored_map[stored] * tok_rows, wanted)
    wanted += row & (tok_rows - 1)
    held = held_tokens(lax.axis_index("blk"), tokens, tok_rows)
    out_ref[...] = reorder(wanted, held, total[...]).T.astype(jnp.bfloat16)


def scale_kernel(
    begun, aligned_ref, near_ref, far_ref, tiles_ref, eigen_ref, out_ref, damped, tiles, sem
):
    blocks, depth = damped.shape[:2]
    chips, _, width = near_ref.shape

    def copy_of(block):
        rows = pl.ds(pl.multiple_of(block * depth, depth), depth)
        return pltpu.make_async_copy(eigen_ref.at[rows], damped.at[block], sem.at[block])

    tiles_copy = pltpu.make_async_copy(tiles_ref, tiles, sem.at[blocks])
    tiles_copy.start()

    @pl.loop(0, blocks)
    def _(block):
        copy_of(block).start()

    tiles_copy.wait()
    me = lax.axis_index("blk")

    @pl.loop(0, blocks)
    def _(block):
        rows = pl.ds(pl.multiple_of(block * depth, depth), depth)
        aligned = aligned_ref[rows, :]
        copy_of(block).wait()
        place = 0
        for steps in begun:
            for other, rotated_ref in enumerate((near_ref, far_ref)):
                source = ring_source(me, steps, other, chips)
                key = (source ^ me) // 2
                rotated = rotated_ref[lax.rem(key, 2) * (chips // 2) + key // 2]
                grad = jnp.dot(aligned, rotated, preferred_element_type=jnp.float32)
                for first in range(0, width, LANES):
                    tile = tiles[(source * width + first) // LANES]
                    lanes = pl.ds(pl.multiple_of(tile * LANES, LANES), LANES)
                    eigen = damped[block, :, lanes]
                    inverse = pl.reciprocal(eigen, approx=True)
                    inverse = inverse * (2.0 - eigen * inverse)
                    scaled = grad[:, first : first + LANES] * inverse
                    out_ref[rows, place : place + LANES] = scaled.astype(jnp.bfloat16)
                    place += LANES


def project_kernel(cuts, scaled_ref, basis_out_ref, *refs):
    pieces = refs[:-4]
    out_ref, window_ref, basis, sem = refs[-4:]
    width = pieces[0].shape[0]
    rows = out_ref.shape[0] // 2
    copies = [
        pltpu.make_async_copy(piece, basis.at[pl.ds(at * width, width)], sem.at[at])
        for at, piece in enumerate(pieces)
    ]
    window_copy = pltpu.make_async_copy(
        basis_out_ref.at[pl.ds(0, window_ref.shape[0])], window_ref, sem.at[len(pieces)]
    )
    window_copy.start()
    for copy in copies:
        copy.start()
    for first, last in zip(cuts[:-1], cuts[1:]):
        for copy in copies[first:last]:
            copy.wait()
        deep = slice(first * width, last * width)

        @pl.loop(0, 2)
        def _(half):
            block = pl.ds(pl.multiple_of(half * rows, rows), rows)
            part = jnp.dot(
                scaled_ref[block, deep], basis[deep, :], preferred_element_type=jnp.float32
            )
            out_ref[block, :] = part if first == 0 else out_ref[block, :] + part

    window_copy.wait()


def window_kernel(scale, window_ref, scaled_ref, projected_ref, *refs):
    pieces = refs[:-3]
    send_ref, keep_ref, result = refs[-3:]
    chips, rows, _ = keep_ref.shape
    width = pieces[0].shape[0]
    total = projected_ref[...]
    first = scaled_ref.shape[1] - width * len(pieces)
    basis = jnp.concatenate([piece[...] for piece in pieces], axis=0)
    total += jnp.dot(scaled_ref[:, first:], basis, preferred_element_type=jnp.float32)
    result[...] = scale * jnp.dot(
        window_ref[...], total.astype(jnp.bfloat16), preferred_element_type=jnp.float32
    )
    core = lax.rem(lax.axis_index("blk"), 2)
    for k in range(chips):
        mine = pl.ds(pl.multiple_of((2 * k + core) * rows, rows), rows)
        keep_ref[k] = result[mine, :]
        other = pl.ds(pl.multiple_of((2 * k + 1 - core) * rows, rows), rows)
        send_ref[k] = result[other, :].astype(jnp.bfloat16)


def add_core_kernel(keys, keep_ref, got_ref, own_ref, *send_refs):
    chip = lax.axis_index("blk") // 2
    for key, ref in zip((0, *keys), (own_ref, *send_refs)):
        at = chip ^ key
        ref[...] = (keep_ref[at] + got_ref[at].astype(jnp.float32)).astype(ref.dtype)


def add_chips_kernel(own_ref, *refs):
    total = own_ref[...]
    for ref in refs[:-1]:
        total += ref[...].astype(jnp.float32)
    refs[-1][...] = total


VMEM = pl.BlockSpec(memory_space=pltpu.VMEM)
SMEM = pl.BlockSpec(memory_space=pltpu.SMEM)
ANY = pl.BlockSpec(memory_space=pl.ANY)
CHEAP = pl.CostEstimate(flops=1, bytes_accessed=1, transcendentals=0)


def after(first, *others):
    return lax.optimization_barrier((first, *others))


def ring_body(n, grad_out, activations, basis_out, basis_in, eigenvalues, tile_order, block_map):
    tok_rows, full_out = grad_out.shape
    tile_width = basis_out.shape[1]
    full_in, in_width = basis_in.shape
    tokens = n * tok_rows
    chips = n // 2
    to_right = lambda x: lax.ppermute(x, "blk", shift_pairs(n, 1))
    to_left = lambda x: lax.ppermute(x, "blk", shift_pairs(n, -1))
    steps = chips // 2

    own = basis_in[:WC].T

    pairs = chips // 2
    both = jnp.concatenate([grad_out, activations], axis=1)[None]
    got = [lax.ppermute(both, "blk", xor_pairs(n, 4 * key)) for key in range(1, pairs)]
    both, own, *got = after(both, own, *got)
    depth, later = 1024, 7
    grads, acts = pl.pallas_call(
        part_kernel,
        out_shape=(
            jax.ShapeDtypeStruct((pairs, tok_rows, full_out), jnp.bfloat16),
            jax.ShapeDtypeStruct((pairs, tok_rows, full_in), jnp.bfloat16),
        ),
        in_specs=[VMEM] * pairs,
        out_specs=(VMEM, VMEM),
        compiler_params=pltpu.CompilerParams(vmem_limit_bytes=8 * MIB),
        name="part",
    )(both, *got)
    acts, grads, own = after(acts, grads, own)
    acts_got = lax.ppermute(acts, "blk", xor_pairs(n, 2))
    grads_got = lax.ppermute(grads, "blk", xor_pairs(n, 2))
    right, left = [own, to_right(own)], [own, to_left(own)]

    acts = jnp.concatenate([acts, acts_got], axis=0)
    rotated = pl.pallas_call(
        functools.partial(rotate_in_kernel, tok_rows),
        out_shape=jax.ShapeDtypeStruct((tokens, in_width), jnp.bfloat16),
        in_specs=[VMEM, VMEM, VMEM],
        out_specs=VMEM,
        compiler_params=pltpu.CompilerParams(vmem_limit_bytes=8 * MIB),
        cost_estimate=CHEAP,
        name="rotate_in",
    )(acts, swap(acts, n), basis_in)

    def doubled(x, key):
        return pl.pallas_call(
            stack_kernel,
            out_shape=jax.ShapeDtypeStruct((2 * x.shape[0], *x.shape[1:]), x.dtype),
            in_specs=[VMEM, VMEM],
            out_specs=VMEM,
            compiler_params=pltpu.CompilerParams(vmem_limit_bytes=8 * MIB),
            cost_estimate=CHEAP,
            name="stack",
        )(x, lax.ppermute(x, "blk", xor_pairs(n, key)))

    own_far = swap(own, n)
    grads_got, rotated, right[-1], left[-1], own_far = after(
        grads_got, rotated, right[-1], left[-1], own_far
    )
    rotated = doubled(rotated[None], 4)
    near = [right[0], right[1], left[1]]
    while len(right) < steps - 1:
        right.append(to_right(right[-1]))
        left.append(to_left(left[-1]))
    grads = jnp.concatenate([grads, grads_got], axis=0)
    grads_far = swap(grads, n)
    far = [swap(piece, n) for piece in near[1:]]
    grads, grads_far, rotated, *far = after(grads, grads_far, rotated, *far)
    far = [own_far, *far]
    key = 8
    while key < n:
        rotated = doubled(rotated, key)
        key *= 2

    rotate = lambda kernel, count, scratch, shape, dtype, *operands: pl.pallas_call(
        kernel,
        out_shape=jax.ShapeDtypeStruct(shape, dtype),
        in_specs=[ANY if x is basis_out or x is block_map else VMEM for x in operands],
        out_specs=VMEM,
        scratch_shapes=[pltpu.VMEM((count, depth, tile_width), jnp.bfloat16)]
        + scratch
        + [pltpu.SemaphoreType.DMA((count + 1,))],
        compiler_params=pltpu.CompilerParams(vmem_limit_bytes=40 * MIB),
        cost_estimate=CHEAP,
        name=kernel.func.__name__[:-7],
    )(*operands)
    start = rotate(
        functools.partial(rotate_first_kernel),
        full_out // depth - later,
        [],
        (tokens, tile_width),
        jnp.float32,
        grads,
        grads_far,
        basis_out,
    )
    start, grads, right[-1], left[-1], rotated = after(
        start, grads, right[-1], left[-1], rotated
    )
    rotated = doubled(rotated, 2)
    near += [right[-1], left[-1]]
    far += [swap(right[-1], n), swap(left[-1], n)]
    right.append(to_right(right[-1]))
    left.append(to_left(left[-1]))
    aligned = rotate(
        functools.partial(rotate_last_kernel, tok_rows, full_out // depth - later),
        later,
        [
            pltpu.VMEM((tokens, tile_width), jnp.float32),
            pltpu.SMEM(block_map.shape, jnp.int32),
        ],
        (tile_width, tokens),
        jnp.bfloat16,
        grads,
        grads_far,
        basis_out,
        block_map,
        start,
    )

    aligned, right[-1], left[-1], rotated, *far = after(
        aligned, right[-1], left[-1], rotated, *far
    )
    cut = in_width // 2
    last = [to_right(right[-1][:cut]), to_left(left[-1][cut:])]
    near += [right[-1], left[-1]]
    far += [swap(piece, n) for piece in near[len(far) :]]
    begun = [0] + [at for step in range(1, steps) for at in (step, chips - step)] + [steps]
    blocks = 8
    scaled = pl.pallas_call(
        functools.partial(scale_kernel, begun),
        out_shape=jax.ShapeDtypeStruct((tile_width, full_in), jnp.bfloat16),
        in_specs=[VMEM] * 3 + [ANY] * 2,
        out_specs=VMEM,
        scratch_shapes=[
            pltpu.VMEM((blocks, tile_width // blocks, full_in), jnp.float32),
            pltpu.SMEM(tile_order.shape, jnp.int32),
            pltpu.SemaphoreType.DMA((blocks + 1,)),
        ],
        compiler_params=pltpu.CompilerParams(vmem_limit_bytes=40 * MIB),
        cost_estimate=CHEAP,
        name="scale",
    )(aligned, rotated, swap(rotated, n), tile_order, eigenvalues)

    scaled, *last = after(scaled, *last, *far[-2:])
    far[-2:] = last[2:]
    last = last[:2]
    last += [swap(piece, n) for piece in last]
    pieces = [piece for pair in zip(near, far) for piece in pair]
    projected, window = pl.pallas_call(
        functools.partial(project_kernel, (0, 6, len(pieces))),
        out_shape=(
            jax.ShapeDtypeStruct((tile_width, WC), jnp.float32),
            jax.ShapeDtypeStruct((WR, tile_width), jnp.bfloat16),
        ),
        in_specs=[VMEM] + [ANY] * (len(pieces) + 1),
        out_specs=(VMEM, VMEM),
        scratch_shapes=[
            pltpu.VMEM((len(pieces) * in_width, WC), jnp.bfloat16),
            pltpu.SemaphoreType.DMA((len(pieces) + 1,)),
        ],
        compiler_params=pltpu.CompilerParams(vmem_limit_bytes=24 * MIB),
        cost_estimate=CHEAP,
        name="project",
    )(scaled, basis_out, *pieces)

    rows = WR // n
    send, keep = pl.pallas_call(
        functools.partial(window_kernel, 1.0 / tokens),
        out_shape=(
            jax.ShapeDtypeStruct((chips, rows, WC), jnp.bfloat16),
            jax.ShapeDtypeStruct((chips, rows, WC), jnp.float32),
        ),
        in_specs=[VMEM] * 7,
        out_specs=(VMEM, VMEM),
        scratch_shapes=[pltpu.VMEM((WR, WC), jnp.float32)],
        compiler_params=pltpu.CompilerParams(vmem_limit_bytes=24 * MIB),
        cost_estimate=CHEAP,
        name="window",
    )(window, scaled, projected, *last)

    keys = sorted(range(1, chips), key=lambda key: -(key & -2))
    small = pltpu.CompilerParams(vmem_limit_bytes=8 * MIB)
    own, *sends = pl.pallas_call(
        functools.partial(add_core_kernel, keys),
        out_shape=[jax.ShapeDtypeStruct((rows, WC), jnp.float32)]
        + [jax.ShapeDtypeStruct((rows, WC), jnp.bfloat16)] * len(keys),
        in_specs=[VMEM, VMEM],
        out_specs=[VMEM] * chips,
        compiler_params=small,
        name="add_core",
    )(keep, swap(send, n))
    arrived = [lax.ppermute(x, "blk", xor_pairs(n, 2 * key)) for key, x in zip(keys, sends)]
    return pl.pallas_call(
        add_chips_kernel,
        out_shape=jax.ShapeDtypeStruct((rows, WC), jnp.float32),
        in_specs=[VMEM] * chips,
        out_specs=VMEM,
        compiler_params=small,
        name="add_chips",
    )(own, *arrived)


def gather_body(grad_out, activations, basis_out, basis_in, eigenvalues, tile_order, block_map):
    n_blocks = lax.axis_size("blk")
    tile_width = basis_out.shape[1]
    tok_rows = grad_out.shape[0]
    full_in = eigenvalues.shape[1]
    tokens = n_blocks * tok_rows
    dot = functools.partial(jnp.dot, preferred_element_type=jnp.float32)
    in_rows = lax.all_gather(basis_in[:WC], "blk", axis=1, tiled=True)
    acts = lax.all_gather(activations, "blk", axis=0, tiled=True)
    in_tile = dot(acts, basis_in).astype(jnp.bfloat16)
    rotated_in = lax.all_gather(in_tile, "blk", axis=1, tiled=True)
    grads = lax.all_gather(grad_out, "blk", axis=0, tiled=True)
    rotated_out = dot(grads, basis_out).astype(jnp.bfloat16)
    aligned = jnp.take(
        rotated_out.reshape(n_blocks, tok_rows, tile_width), block_map, axis=0
    ).reshape(tokens, tile_width)
    grad_tile = dot(aligned.T, rotated_in) / tokens
    damped = jnp.take(
        eigenvalues.reshape(tile_width, full_in // LANES, LANES), tile_order, axis=1
    ).reshape(tile_width, full_in)
    scaled = (grad_tile / damped).astype(jnp.bfloat16)
    projected = dot(scaled, in_rows.T).astype(jnp.bfloat16)
    return lax.psum_scatter(
        dot(basis_out[:WR], projected), "blk", scatter_dimension=0, tiled=True
    )


def solution(mesh):
    n = mesh.shape["blk"]

    def body(*args):
        wide = args[3].shape[1] % LANES == 0 and args[2].shape[1] % LANES == 0
        doubles = n & (n - 1) == 0 and args[0].shape[0] & (args[0].shape[0] - 1) == 0
        if wide and doubles and WR % (16 * n) == 0:
            return ring_body(n, *args)
        return gather_body(*args)

    placed = (
        P(("grp", "blk"), None),
        P(("grp", "blk"), None),
        P(None, "blk"),
        P(None, "blk"),
        P("blk", None),
        P(),
        P(),
    )
    return jax.shard_map(
        body, mesh=mesh, in_specs=placed, out_specs=P(("grp", "blk"), None), check_vma=False
    )
```

```python
import functools

import jax
import jax.numpy as jnp
from jax import lax
from jax.experimental import pallas as pl
from jax.experimental.pallas import tpu as pltpu
from jax.sharding import PartitionSpec as P

WR = 768
WC = 512
LANES = 128
MIB = 1 << 20


def ring_of(n):
    chips = n // 2
    return [*range(0, chips, 2), *range(chips - 1, 0, -2)]


def shift_pairs(n, by):
    ring = ring_of(n)
    return [
        (2 * ring[p] + c, 2 * ring[(p + by) % len(ring)] + c)
        for p in range(len(ring))
        for c in range(2)
    ]


def ring_source(me, steps, other, chips):
    chip, core = me // 2, lax.rem(me, 2)
    place = jnp.where(lax.rem(chip, 2) == 0, chip // 2, chips - 1 - chip // 2)
    place = lax.rem(place + chips - steps, chips)
    chip = jnp.where(place < chips // 2, 2 * place, 2 * (chips - 1 - place) + 1)
    return 2 * chip + (core ^ other)


def xor_pairs(n, key):
    return [(b, b ^ key) for b in range(n)]


def swap(x, n):
    return lax.ppermute(x, "blk", xor_pairs(n, 1))


def bits_of(size):
    return size.bit_length() - 1


def held_tokens(me, tokens, tok_rows):
    row = lax.broadcasted_iota(jnp.int32, (tokens, tokens), 1)
    pairs = tokens // tok_rows // 4
    place = row >> bits_of(tok_rows)
    chip = 2 * (place & (pairs - 1)) + ((place >> bits_of(pairs)) & 1)
    other = row >> bits_of(tokens // 2)
    device = me ^ (2 * chip + other)
    return (device << bits_of(tok_rows)) + (row & (tok_rows - 1))


def reorder(wanted, held, rotated):
    order = jnp.where(wanted == held, 1.0, 0.0).astype(jnp.bfloat16)
    return jnp.dot(order, rotated.astype(jnp.bfloat16), preferred_element_type=jnp.float32)


def part_kernel(*refs):
    grads_ref, acts_ref = refs[-2:]
    first = grads_ref.shape[2]
    for at, ref in enumerate(refs[:-2]):
        grads_ref[at] = ref[0, :, :first]
        acts_ref[at] = ref[0, :, first:]


def rotate_in_kernel(tok_rows, near_ref, far_ref, basis_ref, out_ref):
    tokens = out_ref.shape[0]
    depth = near_ref.shape[2]
    acts = jnp.concatenate([ref[...].reshape(-1, depth) for ref in (near_ref, far_ref)], axis=0)
    rotated = jnp.dot(acts, basis_ref[...], preferred_element_type=jnp.float32)
    wanted = lax.broadcasted_iota(jnp.int32, (tokens, tokens), 0)
    held = held_tokens(lax.axis_index("blk"), tokens, tok_rows)
    out_ref[...] = reorder(wanted, held, rotated).astype(jnp.bfloat16)


def stack_kernel(first_ref, last_ref, out_ref):
    half = first_ref.shape[0]
    out_ref[:half] = first_ref[...]
    out_ref[half:] = last_ref[...]


def rotate_part(first, near_ref, far_ref, basis_ref, basis, total, sem):
    steps, depth = basis.shape[:2]

    def copy_of(step):
        rows = pl.ds(pl.multiple_of((first + step) * depth, depth), depth)
        return pltpu.make_async_copy(basis_ref.at[rows], basis.at[step], sem.at[step])

    @pl.loop(0, steps)
    def _(step):
        copy_of(step).start()

    @pl.loop(0, steps)
    def _(step):
        columns = pl.ds(pl.multiple_of((first + step) * depth, depth), depth)
        rows = [ref[:, :, columns].reshape(-1, depth) for ref in (near_ref, far_ref)]
        grads = jnp.concatenate(rows, axis=0)
        copy_of(step).wait()
        total[...] += jnp.dot(grads, basis[step], preferred_element_type=jnp.float32)


def rotate_first_kernel(near_ref, far_ref, basis_ref, out_ref, basis, sem):
    out_ref[...] = jnp.zeros_like(out_ref)
    rotate_part(0, near_ref, far_ref, basis_ref, basis, out_ref, sem)


def rotate_last_kernel(
    tok_rows,
    first,
    near_ref,
    far_ref,
    basis_ref,
    map_ref,
    start_ref,
    out_ref,
    basis,
    total,
    stored_map,
    sem,
):
    tokens = total.shape[0]
    map_copy = pltpu.make_async_copy(map_ref, stored_map, sem.at[basis.shape[0]])
    map_copy.start()
    total[...] = start_ref[...]
    rotate_part(first, near_ref, far_ref, basis_ref, basis, total, sem)
    map_copy.wait()
    row = lax.broadcasted_iota(jnp.int32, (tokens, tokens), 0)
    block = row >> bits_of(tok_rows)
    wanted = jnp.zeros_like(row)
    for stored in range(tokens // tok_rows):
        wanted = jnp.where(block == stored, stored_map[stored] * tok_rows, wanted)
    wanted += row & (tok_rows - 1)
    held = held_tokens(lax.axis_index("blk"), tokens, tok_rows)
    out_ref[...] = reorder(wanted, held, total[...]).T.astype(jnp.bfloat16)


def scale_kernel(
    begun, aligned_ref, near_ref, far_ref, tiles_ref, eigen_ref, out_ref, damped, tiles, sem
):
    blocks, depth = damped.shape[:2]
    chips, _, width = near_ref.shape

    def copy_of(block):
        rows = pl.ds(pl.multiple_of(block * depth, depth), depth)
        return pltpu.make_async_copy(eigen_ref.at[rows], damped.at[block], sem.at[block])

    tiles_copy = pltpu.make_async_copy(tiles_ref, tiles, sem.at[blocks])
    tiles_copy.start()

    @pl.loop(0, blocks)
    def _(block):
        copy_of(block).start()

    tiles_copy.wait()
    me = lax.axis_index("blk")

    @pl.loop(0, blocks)
    def _(block):
        rows = pl.ds(pl.multiple_of(block * depth, depth), depth)
        aligned = aligned_ref[rows, :]
        copy_of(block).wait()
        place = 0
        for steps in begun:
            for other, rotated_ref in enumerate((near_ref, far_ref)):
                source = ring_source(me, steps, other, chips)
                key = (source ^ me) // 2
                rotated = rotated_ref[lax.rem(key, 2) * (chips // 2) + key // 2]
                grad = jnp.dot(aligned, rotated, preferred_element_type=jnp.float32)
                for first in range(0, width, LANES):
                    tile = tiles[(source * width + first) // LANES]
                    lanes = pl.ds(pl.multiple_of(tile * LANES, LANES), LANES)
                    eigen = damped[block, :, lanes]
                    inverse = pl.reciprocal(eigen, approx=True)
                    inverse = inverse * (2.0 - eigen * inverse)
                    scaled = grad[:, first : first + LANES] * inverse
                    out_ref[rows, place : place + LANES] = scaled.astype(jnp.bfloat16)
                    place += LANES


def project_kernel(cuts, scaled_ref, basis_out_ref, *refs):
    pieces = refs[:-4]
    out_ref, window_ref, basis, sem = refs[-4:]
    width = pieces[0].shape[0]
    rows = out_ref.shape[0] // 2
    copies = [
        pltpu.make_async_copy(piece, basis.at[pl.ds(at * width, width)], sem.at[at])
        for at, piece in enumerate(pieces)
    ]
    window_copy = pltpu.make_async_copy(
        basis_out_ref.at[pl.ds(0, window_ref.shape[0])], window_ref, sem.at[len(pieces)]
    )
    window_copy.start()
    for copy in copies:
        copy.start()
    for first, last in zip(cuts[:-1], cuts[1:]):
        for copy in copies[first:last]:
            copy.wait()
        deep = slice(first * width, last * width)

        @pl.loop(0, 2)
        def _(half):
            block = pl.ds(pl.multiple_of(half * rows, rows), rows)
            part = jnp.dot(
                scaled_ref[block, deep], basis[deep, :], preferred_element_type=jnp.float32
            )
            out_ref[block, :] = part if first == 0 else out_ref[block, :] + part

    window_copy.wait()


def window_kernel(scale, window_ref, scaled_ref, projected_ref, *refs):
    pieces = refs[:-3]
    send_ref, keep_ref, result = refs[-3:]
    chips, rows, _ = keep_ref.shape
    width = pieces[0].shape[0]
    total = projected_ref[...]
    first = scaled_ref.shape[1] - width * len(pieces)
    basis = jnp.concatenate([piece[...] for piece in pieces], axis=0)
    total += jnp.dot(scaled_ref[:, first:], basis, preferred_element_type=jnp.float32)
    result[...] = scale * jnp.dot(
        window_ref[...], total.astype(jnp.bfloat16), preferred_element_type=jnp.float32
    )
    core = lax.rem(lax.axis_index("blk"), 2)
    for k in range(chips):
        mine = pl.ds(pl.multiple_of((2 * k + core) * rows, rows), rows)
        keep_ref[k] = result[mine, :]
        other = pl.ds(pl.multiple_of((2 * k + 1 - core) * rows, rows), rows)
        send_ref[k] = result[other, :].astype(jnp.bfloat16)


def add_core_kernel(keys, keep_ref, got_ref, own_ref, *send_refs):
    chip = lax.axis_index("blk") // 2
    for key, ref in zip((0, *keys), (own_ref, *send_refs)):
        at = chip ^ key
        ref[...] = (keep_ref[at] + got_ref[at].astype(jnp.float32)).astype(ref.dtype)


def add_chips_kernel(own_ref, *refs):
    total = own_ref[...]
    for ref in refs[:-1]:
        total += ref[...].astype(jnp.float32)
    refs[-1][...] = total


VMEM = pl.BlockSpec(memory_space=pltpu.VMEM)
SMEM = pl.BlockSpec(memory_space=pltpu.SMEM)
ANY = pl.BlockSpec(memory_space=pl.ANY)
CHEAP = pl.CostEstimate(flops=1, bytes_accessed=1, transcendentals=0)


def after(first, *others):
    return lax.optimization_barrier((first, *others))


def ring_body(n, grad_out, activations, basis_out, basis_in, eigenvalues, tile_order, block_map):
    tok_rows, full_out = grad_out.shape
    tile_width = basis_out.shape[1]
    full_in, in_width = basis_in.shape
    tokens = n * tok_rows
    chips = n // 2
    to_right = lambda x: lax.ppermute(x, "blk", shift_pairs(n, 1))
    to_left = lambda x: lax.ppermute(x, "blk", shift_pairs(n, -1))
    steps = chips // 2

    own = basis_in[:WC].T

    pairs = chips // 2
    both = jnp.concatenate([grad_out, activations], axis=1)[None]
    got = [lax.ppermute(both, "blk", xor_pairs(n, 4 * key)) for key in range(1, pairs)]
    both, own, *got = after(both, own, *got)
    depth, later = 1024, 7
    grads, acts = pl.pallas_call(
        part_kernel,
        out_shape=(
            jax.ShapeDtypeStruct((pairs, tok_rows, full_out), jnp.bfloat16),
            jax.ShapeDtypeStruct((pairs, tok_rows, full_in), jnp.bfloat16),
        ),
        in_specs=[VMEM] * pairs,
        out_specs=(VMEM, VMEM),
        compiler_params=pltpu.CompilerParams(vmem_limit_bytes=8 * MIB),
        name="part",
    )(both, *got)
    acts, grads, own = after(acts, grads, own)
    acts_got = lax.ppermute(acts, "blk", xor_pairs(n, 2))
    grads_got = lax.ppermute(grads, "blk", xor_pairs(n, 2))
    acts = jnp.concatenate([acts, acts_got], axis=0)
    rotated = pl.pallas_call(
        functools.partial(rotate_in_kernel, tok_rows),
        out_shape=jax.ShapeDtypeStruct((tokens, in_width), jnp.bfloat16),
        in_specs=[VMEM, VMEM, VMEM],
        out_specs=VMEM,
        compiler_params=pltpu.CompilerParams(vmem_limit_bytes=8 * MIB),
        cost_estimate=CHEAP,
        name="rotate_in",
    )(acts, swap(acts, n), basis_in)

    def doubled(x, key):
        return pl.pallas_call(
            stack_kernel,
            out_shape=jax.ShapeDtypeStruct((2 * x.shape[0], *x.shape[1:]), x.dtype),
            in_specs=[VMEM, VMEM],
            out_specs=VMEM,
            compiler_params=pltpu.CompilerParams(vmem_limit_bytes=8 * MIB),
            cost_estimate=CHEAP,
            name="stack",
        )(x, lax.ppermute(x, "blk", xor_pairs(n, key)))

    rotated, own = after(rotated, own)
    right, left = [own, to_right(own)], [own, to_left(own)]
    grads_got, rotated = after(grads_got, rotated)
    rotated = doubled(rotated[None], 4)
    grads = jnp.concatenate([grads, grads_got], axis=0)
    grads_far = swap(grads, n)
    grads, grads_far, rotated = after(grads, grads_far, rotated)
    far = [swap(own, n)]
    key = 8
    while key < n:
        rotated = doubled(rotated, key)
        key *= 2

    rotate = lambda kernel, count, scratch, shape, dtype, *operands: pl.pallas_call(
        kernel,
        out_shape=jax.ShapeDtypeStruct(shape, dtype),
        in_specs=[ANY if x is basis_out or x is block_map else VMEM for x in operands],
        out_specs=VMEM,
        scratch_shapes=[pltpu.VMEM((count, depth, tile_width), jnp.bfloat16)]
        + scratch
        + [pltpu.SemaphoreType.DMA((count + 1,))],
        compiler_params=pltpu.CompilerParams(vmem_limit_bytes=40 * MIB),
        cost_estimate=CHEAP,
        name=kernel.func.__name__[:-7],
    )(*operands)
    start = rotate(
        functools.partial(rotate_first_kernel),
        full_out // depth - later,
        [],
        (tokens, tile_width),
        jnp.float32,
        grads,
        grads_far,
        basis_out,
    )
    start, grads, right[-1], left[-1], rotated, *far = after(
        start, grads, right[-1], left[-1], rotated, *far
    )
    rotated = doubled(rotated, 2)
    far += [swap(right[-1], n), swap(left[-1], n)]
    right.append(to_right(right[-1]))
    left.append(to_left(left[-1]))
    aligned = rotate(
        functools.partial(rotate_last_kernel, tok_rows, full_out // depth - later),
        later,
        [
            pltpu.VMEM((tokens, tile_width), jnp.float32),
            pltpu.SMEM(block_map.shape, jnp.int32),
        ],
        (tile_width, tokens),
        jnp.bfloat16,
        grads,
        grads_far,
        basis_out,
        block_map,
        start,
    )

    aligned, right[-1], left[-1], rotated, *far = after(
        aligned, right[-1], left[-1], rotated, *far
    )
    far += [swap(right[-1], n), swap(left[-1], n)]
    right.append(to_right(right[-1]))
    left.append(to_left(left[-1]))
    begun = [0] + [at for step in range(1, steps) for at in (step, chips - step)] + [steps]
    blocks = 8
    scaled = pl.pallas_call(
        functools.partial(scale_kernel, begun),
        out_shape=jax.ShapeDtypeStruct((tile_width, full_in), jnp.bfloat16),
        in_specs=[VMEM] * 3 + [ANY] * 2,
        out_specs=VMEM,
        scratch_shapes=[
            pltpu.VMEM((blocks, tile_width // blocks, full_in), jnp.float32),
            pltpu.SMEM(tile_order.shape, jnp.int32),
            pltpu.SemaphoreType.DMA((blocks + 1,)),
        ],
        compiler_params=pltpu.CompilerParams(vmem_limit_bytes=40 * MIB),
        cost_estimate=CHEAP,
        name="scale",
    )(aligned, rotated, swap(rotated, n), tile_order, eigenvalues)

    scaled, right[-1], left[-1], *far = after(scaled, right[-1], left[-1], *far)
    cut = in_width // 2
    last = [to_right(right[-1][:cut]), to_left(left[-1][cut:])]
    near = [right[at] if at < steps else left[chips - at] for at in begun[:-1]]
    far += [swap(piece, n) for piece in near[len(far) :]]
    pieces = [piece for pair in zip(near, far) for piece in pair]
    projected, window = pl.pallas_call(
        functools.partial(project_kernel, (0, 6, len(pieces))),
        out_shape=(
            jax.ShapeDtypeStruct((tile_width, WC), jnp.float32),
            jax.ShapeDtypeStruct((WR, tile_width), jnp.bfloat16),
        ),
        in_specs=[VMEM] + [ANY] * (len(pieces) + 1),
        out_specs=(VMEM, VMEM),
        scratch_shapes=[
            pltpu.VMEM((len(pieces) * in_width, WC), jnp.bfloat16),
            pltpu.SemaphoreType.DMA((len(pieces) + 1,)),
        ],
        compiler_params=pltpu.CompilerParams(vmem_limit_bytes=24 * MIB),
        cost_estimate=CHEAP,
        name="project",
    )(scaled, basis_out, *pieces)

    projected, *last = after(projected, *last)
    last += [swap(piece, n) for piece in last]
    rows = WR // n
    send, keep = pl.pallas_call(
        functools.partial(window_kernel, 1.0 / tokens),
        out_shape=(
            jax.ShapeDtypeStruct((chips, rows, WC), jnp.bfloat16),
            jax.ShapeDtypeStruct((chips, rows, WC), jnp.float32),
        ),
        in_specs=[VMEM] * 7,
        out_specs=(VMEM, VMEM),
        scratch_shapes=[pltpu.VMEM((WR, WC), jnp.float32)],
        compiler_params=pltpu.CompilerParams(vmem_limit_bytes=24 * MIB),
        cost_estimate=CHEAP,
        name="window",
    )(window, scaled, projected, *last)

    keys = sorted(range(1, chips), key=lambda key: -(key & -2))
    small = pltpu.CompilerParams(vmem_limit_bytes=8 * MIB)
    own, *sends = pl.pallas_call(
        functools.partial(add_core_kernel, keys),
        out_shape=[jax.ShapeDtypeStruct((rows, WC), jnp.float32)]
        + [jax.ShapeDtypeStruct((rows, WC), jnp.bfloat16)] * len(keys),
        in_specs=[VMEM, VMEM],
        out_specs=[VMEM] * chips,
        compiler_params=small,
        name="add_core",
    )(keep, swap(send, n))
    arrived = [lax.ppermute(x, "blk", xor_pairs(n, 2 * key)) for key, x in zip(keys, sends)]
    return pl.pallas_call(
        add_chips_kernel,
        out_shape=jax.ShapeDtypeStruct((rows, WC), jnp.float32),
        in_specs=[VMEM] * chips,
        out_specs=VMEM,
        compiler_params=small,
        name="add_chips",
    )(own, *arrived)


def gather_body(grad_out, activations, basis_out, basis_in, eigenvalues, tile_order, block_map):
    n_blocks = lax.axis_size("blk")
    tile_width = basis_out.shape[1]
    tok_rows = grad_out.shape[0]
    full_in = eigenvalues.shape[1]
    tokens = n_blocks * tok_rows
    dot = functools.partial(jnp.dot, preferred_element_type=jnp.float32)
    in_rows = lax.all_gather(basis_in[:WC], "blk", axis=1, tiled=True)
    acts = lax.all_gather(activations, "blk", axis=0, tiled=True)
    in_tile = dot(acts, basis_in).astype(jnp.bfloat16)
    rotated_in = lax.all_gather(in_tile, "blk", axis=1, tiled=True)
    grads = lax.all_gather(grad_out, "blk", axis=0, tiled=True)
    rotated_out = dot(grads, basis_out).astype(jnp.bfloat16)
    aligned = jnp.take(
        rotated_out.reshape(n_blocks, tok_rows, tile_width), block_map, axis=0
    ).reshape(tokens, tile_width)
    grad_tile = dot(aligned.T, rotated_in) / tokens
    damped = jnp.take(
        eigenvalues.reshape(tile_width, full_in // LANES, LANES), tile_order, axis=1
    ).reshape(tile_width, full_in)
    scaled = (grad_tile / damped).astype(jnp.bfloat16)
    projected = dot(scaled, in_rows.T).astype(jnp.bfloat16)
    return lax.psum_scatter(
        dot(basis_out[:WR], projected), "blk", scatter_dimension=0, tiled=True
    )


def solution(mesh):
    n = mesh.shape["blk"]

    def body(*args):
        wide = args[3].shape[1] % LANES == 0 and args[2].shape[1] % LANES == 0
        doubles = n & (n - 1) == 0 and args[0].shape[0] & (args[0].shape[0] - 1) == 0
        if wide and doubles and WR % (16 * n) == 0:
            return ring_body(n, *args)
        return gather_body(*args)

    placed = (
        P(("grp", "blk"), None),
        P(("grp", "blk"), None),
        P(None, "blk"),
        P(None, "blk"),
        P("blk", None),
        P(),
        P(),
    )
    return jax.shard_map(
        body, mesh=mesh, in_specs=placed, out_specs=P(("grp", "blk"), None), check_vma=False
    )
```

```python
import functools

import jax
import jax.numpy as jnp
from jax import lax
from jax.experimental import pallas as pl
from jax.experimental.pallas import tpu as pltpu
from jax.sharding import PartitionSpec as P

WR = 768
WC = 512
LANES = 128
MIB = 1 << 20


def ring_of(n):
    chips = n // 2
    return [*range(0, chips, 2), *range(chips - 1, 0, -2)]


def shift_pairs(n, by):
    ring = ring_of(n)
    return [
        (2 * ring[p] + c, 2 * ring[(p + by) % len(ring)] + c)
        for p in range(len(ring))
        for c in range(2)
    ]


def ring_source(me, steps, other, chips):
    chip, core = me // 2, lax.rem(me, 2)
    place = jnp.where(lax.rem(chip, 2) == 0, chip // 2, chips - 1 - chip // 2)
    place = lax.rem(place + chips - steps, chips)
    chip = jnp.where(place < chips // 2, 2 * place, 2 * (chips - 1 - place) + 1)
    return 2 * chip + (core ^ other)


def xor_pairs(n, key):
    return [(b, b ^ key) for b in range(n)]


def swap(x, n):
    return lax.ppermute(x, "blk", xor_pairs(n, 1))


def bits_of(size):
    return size.bit_length() - 1


def held_tokens(me, tokens, tok_rows):
    row = lax.broadcasted_iota(jnp.int32, (tokens, tokens), 1)
    pairs = tokens // tok_rows // 4
    place = row >> bits_of(tok_rows)
    chip = 2 * (place & (pairs - 1)) + ((place >> bits_of(pairs)) & 1)
    other = row >> bits_of(tokens // 2)
    device = me ^ (2 * chip + other)
    return (device << bits_of(tok_rows)) + (row & (tok_rows - 1))


def reorder(wanted, held, rotated):
    order = jnp.where(wanted == held, 1.0, 0.0).astype(jnp.bfloat16)
    return jnp.dot(order, rotated.astype(jnp.bfloat16), preferred_element_type=jnp.float32)


def part_kernel(*refs):
    grads_ref, acts_ref = refs[-2:]
    first = grads_ref.shape[2]
    for at, ref in enumerate(refs[:-2]):
        grads_ref[at] = ref[0, :, :first]
        acts_ref[at] = ref[0, :, first:]


def rotate_in_kernel(tok_rows, near_ref, far_ref, basis_ref, out_ref):
    tokens = out_ref.shape[0]
    depth = near_ref.shape[2]
    acts = jnp.concatenate([ref[...].reshape(-1, depth) for ref in (near_ref, far_ref)], axis=0)
    rotated = jnp.dot(acts, basis_ref[...], preferred_element_type=jnp.float32)
    wanted = lax.broadcasted_iota(jnp.int32, (tokens, tokens), 0)
    held = held_tokens(lax.axis_index("blk"), tokens, tok_rows)
    out_ref[...] = reorder(wanted, held, rotated).astype(jnp.bfloat16)


def stack_kernel(first_ref, last_ref, out_ref):
    half = first_ref.shape[0]
    out_ref[:half] = first_ref[...]
    out_ref[half:] = last_ref[...]


def rotate_part(first, near_ref, far_ref, basis_ref, basis, total, sem):
    steps, depth = basis.shape[:2]

    def copy_of(step):
        rows = pl.ds(pl.multiple_of((first + step) * depth, depth), depth)
        return pltpu.make_async_copy(basis_ref.at[rows], basis.at[step], sem.at[step])

    @pl.loop(0, steps)
    def _(step):
        copy_of(step).start()

    @pl.loop(0, steps)
    def _(step):
        columns = pl.ds(pl.multiple_of((first + step) * depth, depth), depth)
        rows = [ref[:, :, columns].reshape(-1, depth) for ref in (near_ref, far_ref)]
        grads = jnp.concatenate(rows, axis=0)
        copy_of(step).wait()
        total[...] += jnp.dot(grads, basis[step], preferred_element_type=jnp.float32)


def rotate_first_kernel(near_ref, far_ref, basis_ref, out_ref, basis, sem):
    out_ref[...] = jnp.zeros_like(out_ref)
    rotate_part(0, near_ref, far_ref, basis_ref, basis, out_ref, sem)


def rotate_last_kernel(
    tok_rows,
    first,
    near_ref,
    far_ref,
    basis_ref,
    map_ref,
    start_ref,
    out_ref,
    basis,
    total,
    stored_map,
    sem,
):
    tokens = total.shape[0]
    map_copy = pltpu.make_async_copy(map_ref, stored_map, sem.at[basis.shape[0]])
    map_copy.start()
    total[...] = start_ref[...]
    rotate_part(first, near_ref, far_ref, basis_ref, basis, total, sem)
    map_copy.wait()
    row = lax.broadcasted_iota(jnp.int32, (tokens, tokens), 0)
    block = row >> bits_of(tok_rows)
    wanted = jnp.zeros_like(row)
    for stored in range(tokens // tok_rows):
        wanted = jnp.where(block == stored, stored_map[stored] * tok_rows, wanted)
    wanted += row & (tok_rows - 1)
    held = held_tokens(lax.axis_index("blk"), tokens, tok_rows)
    out_ref[...] = reorder(wanted, held, total[...]).T.astype(jnp.bfloat16)


def scale_kernel(
    begun, aligned_ref, near_ref, far_ref, tiles_ref, eigen_ref, out_ref, damped, tiles, sem
):
    blocks, depth = damped.shape[:2]
    chips, _, width = near_ref.shape

    def copy_of(block):
        rows = pl.ds(pl.multiple_of(block * depth, depth), depth)
        return pltpu.make_async_copy(eigen_ref.at[rows], damped.at[block], sem.at[block])

    tiles_copy = pltpu.make_async_copy(tiles_ref, tiles, sem.at[blocks])
    tiles_copy.start()

    @pl.loop(0, blocks)
    def _(block):
        copy_of(block).start()

    tiles_copy.wait()
    me = lax.axis_index("blk")

    @pl.loop(0, blocks)
    def _(block):
        rows = pl.ds(pl.multiple_of(block * depth, depth), depth)
        aligned = aligned_ref[rows, :]
        copy_of(block).wait()
        place = 0
        for steps in begun:
            for other, rotated_ref in enumerate((near_ref, far_ref)):
                source = ring_source(me, steps, other, chips)
                key = (source ^ me) // 2
                rotated = rotated_ref[lax.rem(key, 2) * (chips // 2) + key // 2]
                grad = jnp.dot(aligned, rotated, preferred_element_type=jnp.float32)
                for first in range(0, width, LANES):
                    tile = tiles[(source * width + first) // LANES]
                    lanes = pl.ds(pl.multiple_of(tile * LANES, LANES), LANES)
                    eigen = damped[block, :, lanes]
                    inverse = pl.reciprocal(eigen, approx=True)
                    inverse = inverse * (2.0 - eigen * inverse)
                    scaled = grad[:, first : first + LANES] * inverse
                    out_ref[rows, place : place + LANES] = scaled.astype(jnp.bfloat16)
                    place += LANES


def project_kernel(cuts, scaled_ref, basis_out_ref, *refs):
    pieces = refs[:-4]
    out_ref, window_ref, basis, sem = refs[-4:]
    width = pieces[0].shape[0]
    rows = out_ref.shape[0] // 2
    copies = [
        pltpu.make_async_copy(piece, basis.at[pl.ds(at * width, width)], sem.at[at])
        for at, piece in enumerate(pieces)
    ]
    window_copy = pltpu.make_async_copy(
        basis_out_ref.at[pl.ds(0, window_ref.shape[0])], window_ref, sem.at[len(pieces)]
    )
    window_copy.start()
    for copy in copies:
        copy.start()
    for first, last in zip(cuts[:-1], cuts[1:]):
        for copy in copies[first:last]:
            copy.wait()
        deep = slice(first * width, last * width)

        @pl.loop(0, 2)
        def _(half):
            block = pl.ds(pl.multiple_of(half * rows, rows), rows)
            part = jnp.dot(
                scaled_ref[block, deep], basis[deep, :], preferred_element_type=jnp.float32
            )
            out_ref[block, :] = part if first == 0 else out_ref[block, :] + part

    window_copy.wait()


def window_kernel(scale, window_ref, scaled_ref, projected_ref, *refs):
    pieces = refs[:-3]
    send_ref, keep_ref, result = refs[-3:]
    chips, rows, _ = keep_ref.shape
    width = pieces[0].shape[0]
    total = projected_ref[...]
    first = scaled_ref.shape[1] - width * len(pieces)
    basis = jnp.concatenate([piece[...] for piece in pieces], axis=0)
    total += jnp.dot(scaled_ref[:, first:], basis, preferred_element_type=jnp.float32)
    result[...] = scale * jnp.dot(
        window_ref[...], total.astype(jnp.bfloat16), preferred_element_type=jnp.float32
    )
    core = lax.rem(lax.axis_index("blk"), 2)
    for k in range(chips):
        mine = pl.ds(pl.multiple_of((2 * k + core) * rows, rows), rows)
        keep_ref[k] = result[mine, :]
        other = pl.ds(pl.multiple_of((2 * k + 1 - core) * rows, rows), rows)
        send_ref[k] = result[other, :].astype(jnp.bfloat16)


def add_core_kernel(keys, keep_ref, got_ref, own_ref, *send_refs):
    chip = lax.axis_index("blk") // 2
    for key, ref in zip((0, *keys), (own_ref, *send_refs)):
        at = chip ^ key
        ref[...] = (keep_ref[at] + got_ref[at].astype(jnp.float32)).astype(ref.dtype)


def add_chips_kernel(own_ref, *refs):
    total = own_ref[...]
    for ref in refs[:-1]:
        total += ref[...].astype(jnp.float32)
    refs[-1][...] = total


VMEM = pl.BlockSpec(memory_space=pltpu.VMEM)
SMEM = pl.BlockSpec(memory_space=pltpu.SMEM)
ANY = pl.BlockSpec(memory_space=pl.ANY)
CHEAP = pl.CostEstimate(flops=1, bytes_accessed=1, transcendentals=0)


def after(first, *others):
    return lax.optimization_barrier((first, *others))


def ring_body(n, grad_out, activations, basis_out, basis_in, eigenvalues, tile_order, block_map):
    tok_rows, full_out = grad_out.shape
    tile_width = basis_out.shape[1]
    full_in, in_width = basis_in.shape
    tokens = n * tok_rows
    chips = n // 2
    to_right = lambda x: lax.ppermute(x, "blk", shift_pairs(n, 1))
    to_left = lambda x: lax.ppermute(x, "blk", shift_pairs(n, -1))
    steps = chips // 2

    own = basis_in[:WC].T

    pairs = chips // 2
    both = jnp.concatenate([grad_out, activations], axis=1)[None]
    got = [lax.ppermute(both, "blk", xor_pairs(n, 4 * key)) for key in range(1, pairs)]
    both, own, *got = after(both, own, *got)
    depth, later = 1024, 7
    grads, acts = pl.pallas_call(
        part_kernel,
        out_shape=(
            jax.ShapeDtypeStruct((pairs, tok_rows, full_out), jnp.bfloat16),
            jax.ShapeDtypeStruct((pairs, tok_rows, full_in), jnp.bfloat16),
        ),
        in_specs=[VMEM] * pairs,
        out_specs=(VMEM, VMEM),
        compiler_params=pltpu.CompilerParams(vmem_limit_bytes=8 * MIB),
        name="part",
    )(both, *got)
    acts, grads, own = after(acts, grads, own)
    acts_got = lax.ppermute(acts, "blk", xor_pairs(n, 2))
    grads_got = lax.ppermute(grads, "blk", xor_pairs(n, 2))
    acts = jnp.concatenate([acts, acts_got], axis=0)
    rotated = pl.pallas_call(
        functools.partial(rotate_in_kernel, tok_rows),
        out_shape=jax.ShapeDtypeStruct((tokens, in_width), jnp.bfloat16),
        in_specs=[VMEM, VMEM, VMEM],
        out_specs=VMEM,
        compiler_params=pltpu.CompilerParams(vmem_limit_bytes=8 * MIB),
        cost_estimate=CHEAP,
        name="rotate_in",
    )(acts, swap(acts, n), basis_in)

    def doubled(x, key):
        return pl.pallas_call(
            stack_kernel,
            out_shape=jax.ShapeDtypeStruct((2 * x.shape[0], *x.shape[1:]), x.dtype),
            in_specs=[VMEM, VMEM],
            out_specs=VMEM,
            compiler_params=pltpu.CompilerParams(vmem_limit_bytes=8 * MIB),
            cost_estimate=CHEAP,
            name="stack",
        )(x, lax.ppermute(x, "blk", xor_pairs(n, key)))

    grads_got, rotated = after(grads_got, rotated)
    rotated, own = after(doubled(rotated[None], 4), own)
    right, left = [own, to_right(own)], [own, to_left(own)]
    grads = jnp.concatenate([grads, grads_got], axis=0)
    grads_far = swap(grads, n)
    grads, grads_far, rotated = after(grads, grads_far, rotated)
    far = [swap(own, n)]
    key = 8
    while key < n:
        rotated = doubled(rotated, key)
        key *= 2

    rotate = lambda kernel, count, scratch, shape, dtype, *operands: pl.pallas_call(
        kernel,
        out_shape=jax.ShapeDtypeStruct(shape, dtype),
        in_specs=[ANY if x is basis_out or x is block_map else VMEM for x in operands],
        out_specs=VMEM,
        scratch_shapes=[pltpu.VMEM((count, depth, tile_width), jnp.bfloat16)]
        + scratch
        + [pltpu.SemaphoreType.DMA((count + 1,))],
        compiler_params=pltpu.CompilerParams(vmem_limit_bytes=40 * MIB),
        cost_estimate=CHEAP,
        name=kernel.func.__name__[:-7],
    )(*operands)
    start = rotate(
        functools.partial(rotate_first_kernel),
        full_out // depth - later,
        [],
        (tokens, tile_width),
        jnp.float32,
        grads,
        grads_far,
        basis_out,
    )
    start, grads, right[-1], left[-1], rotated, *far = after(
        start, grads, right[-1], left[-1], rotated, *far
    )
    rotated = doubled(rotated, 2)
    far += [swap(right[-1], n), swap(left[-1], n)]
    right.append(to_right(right[-1]))
    left.append(to_left(left[-1]))
    aligned = rotate(
        functools.partial(rotate_last_kernel, tok_rows, full_out // depth - later),
        later,
        [
            pltpu.VMEM((tokens, tile_width), jnp.float32),
            pltpu.SMEM(block_map.shape, jnp.int32),
        ],
        (tile_width, tokens),
        jnp.bfloat16,
        grads,
        grads_far,
        basis_out,
        block_map,
        start,
    )

    aligned, right[-1], left[-1], rotated, *far = after(
        aligned, right[-1], left[-1], rotated, *far
    )
    far += [swap(right[-1], n), swap(left[-1], n)]
    right.append(to_right(right[-1]))
    left.append(to_left(left[-1]))
    begun = [0] + [at for step in range(1, steps) for at in (step, chips - step)] + [steps]
    blocks = 8
    scaled = pl.pallas_call(
        functools.partial(scale_kernel, begun),
        out_shape=jax.ShapeDtypeStruct((tile_width, full_in), jnp.bfloat16),
        in_specs=[VMEM] * 3 + [ANY] * 2,
        out_specs=VMEM,
        scratch_shapes=[
            pltpu.VMEM((blocks, tile_width // blocks, full_in), jnp.float32),
            pltpu.SMEM(tile_order.shape, jnp.int32),
            pltpu.SemaphoreType.DMA((blocks + 1,)),
        ],
        compiler_params=pltpu.CompilerParams(vmem_limit_bytes=40 * MIB),
        cost_estimate=CHEAP,
        name="scale",
    )(aligned, rotated, swap(rotated, n), tile_order, eigenvalues)

    scaled, right[-1], left[-1], *far = after(scaled, right[-1], left[-1], *far)
    cut = in_width // 2
    last = [to_right(right[-1][:cut]), to_left(left[-1][cut:])]
    near = [right[at] if at < steps else left[chips - at] for at in begun[:-1]]
    far += [swap(piece, n) for piece in near[len(far) :]]
    pieces = [piece for pair in zip(near, far) for piece in pair]
    projected, window = pl.pallas_call(
        functools.partial(project_kernel, (0, 6, len(pieces))),
        out_shape=(
            jax.ShapeDtypeStruct((tile_width, WC), jnp.float32),
            jax.ShapeDtypeStruct((WR, tile_width), jnp.bfloat16),
        ),
        in_specs=[VMEM] + [ANY] * (len(pieces) + 1),
        out_specs=(VMEM, VMEM),
        scratch_shapes=[
            pltpu.VMEM((len(pieces) * in_width, WC), jnp.bfloat16),
            pltpu.SemaphoreType.DMA((len(pieces) + 1,)),
        ],
        compiler_params=pltpu.CompilerParams(vmem_limit_bytes=24 * MIB),
        cost_estimate=CHEAP,
        name="project",
    )(scaled, basis_out, *pieces)

    projected, *last = after(projected, *last)
    last += [swap(piece, n) for piece in last]
    rows = WR // n
    send, keep = pl.pallas_call(
        functools.partial(window_kernel, 1.0 / tokens),
        out_shape=(
            jax.ShapeDtypeStruct((chips, rows, WC), jnp.bfloat16),
            jax.ShapeDtypeStruct((chips, rows, WC), jnp.float32),
        ),
        in_specs=[VMEM] * 7,
        out_specs=(VMEM, VMEM),
        scratch_shapes=[pltpu.VMEM((WR, WC), jnp.float32)],
        compiler_params=pltpu.CompilerParams(vmem_limit_bytes=24 * MIB),
        cost_estimate=CHEAP,
        name="window",
    )(window, scaled, projected, *last)

    keys = sorted(range(1, chips), key=lambda key: -(key & -2))
    small = pltpu.CompilerParams(vmem_limit_bytes=8 * MIB)
    own, *sends = pl.pallas_call(
        functools.partial(add_core_kernel, keys),
        out_shape=[jax.ShapeDtypeStruct((rows, WC), jnp.float32)]
        + [jax.ShapeDtypeStruct((rows, WC), jnp.bfloat16)] * len(keys),
        in_specs=[VMEM, VMEM],
        out_specs=[VMEM] * chips,
        compiler_params=small,
        name="add_core",
    )(keep, swap(send, n))
    arrived = [lax.ppermute(x, "blk", xor_pairs(n, 2 * key)) for key, x in zip(keys, sends)]
    return pl.pallas_call(
        add_chips_kernel,
        out_shape=jax.ShapeDtypeStruct((rows, WC), jnp.float32),
        in_specs=[VMEM] * chips,
        out_specs=VMEM,
        compiler_params=small,
        name="add_chips",
    )(own, *arrived)


def gather_body(grad_out, activations, basis_out, basis_in, eigenvalues, tile_order, block_map):
    n_blocks = lax.axis_size("blk")
    tile_width = basis_out.shape[1]
    tok_rows = grad_out.shape[0]
    full_in = eigenvalues.shape[1]
    tokens = n_blocks * tok_rows
    dot = functools.partial(jnp.dot, preferred_element_type=jnp.float32)
    in_rows = lax.all_gather(basis_in[:WC], "blk", axis=1, tiled=True)
    acts = lax.all_gather(activations, "blk", axis=0, tiled=True)
    in_tile = dot(acts, basis_in).astype(jnp.bfloat16)
    rotated_in = lax.all_gather(in_tile, "blk", axis=1, tiled=True)
    grads = lax.all_gather(grad_out, "blk", axis=0, tiled=True)
    rotated_out = dot(grads, basis_out).astype(jnp.bfloat16)
    aligned = jnp.take(
        rotated_out.reshape(n_blocks, tok_rows, tile_width), block_map, axis=0
    ).reshape(tokens, tile_width)
    grad_tile = dot(aligned.T, rotated_in) / tokens
    damped = jnp.take(
        eigenvalues.reshape(tile_width, full_in // LANES, LANES), tile_order, axis=1
    ).reshape(tile_width, full_in)
    scaled = (grad_tile / damped).astype(jnp.bfloat16)
    projected = dot(scaled, in_rows.T).astype(jnp.bfloat16)
    return lax.psum_scatter(
        dot(basis_out[:WR], projected), "blk", scatter_dimension=0, tiled=True
    )


def solution(mesh):
    n = mesh.shape["blk"]

    def body(*args):
        wide = args[3].shape[1] % LANES == 0 and args[2].shape[1] % LANES == 0
        doubles = n & (n - 1) == 0 and args[0].shape[0] & (args[0].shape[0] - 1) == 0
        if wide and doubles and WR % (16 * n) == 0:
            return ring_body(n, *args)
        return gather_body(*args)

    placed = (
        P(("grp", "blk"), None),
        P(("grp", "blk"), None),
        P(None, "blk"),
        P(None, "blk"),
        P("blk", None),
        P(),
        P(),
    )
    return jax.shard_map(
        body, mesh=mesh, in_specs=placed, out_specs=P(("grp", "blk"), None), check_vma=False
    )
```

```python
import functools

import jax
import jax.numpy as jnp
from jax import lax
from jax.experimental import pallas as pl
from jax.experimental.pallas import tpu as pltpu
from jax.sharding import PartitionSpec as P

WR = 768
WC = 512
LANES = 128
MIB = 1 << 20


def ring_of(n):
    chips = n // 2
    return [*range(0, chips, 2), *range(chips - 1, 0, -2)]


def shift_pairs(n, by):
    ring = ring_of(n)
    return [
        (2 * ring[p] + c, 2 * ring[(p + by) % len(ring)] + c)
        for p in range(len(ring))
        for c in range(2)
    ]


def ring_source(me, steps, other, chips):
    chip, core = me // 2, lax.rem(me, 2)
    place = jnp.where(lax.rem(chip, 2) == 0, chip // 2, chips - 1 - chip // 2)
    place = lax.rem(place + chips - steps, chips)
    chip = jnp.where(place < chips // 2, 2 * place, 2 * (chips - 1 - place) + 1)
    return 2 * chip + (core ^ other)


def xor_pairs(n, key):
    return [(b, b ^ key) for b in range(n)]


def swap(x, n):
    return lax.ppermute(x, "blk", xor_pairs(n, 1))


def bits_of(size):
    return size.bit_length() - 1


def held_tokens(me, tokens, tok_rows):
    row = lax.broadcasted_iota(jnp.int32, (tokens, tokens), 1)
    pairs = tokens // tok_rows // 4
    place = row >> bits_of(tok_rows)
    chip = 2 * (place & (pairs - 1)) + ((place >> bits_of(pairs)) & 1)
    other = row >> bits_of(tokens // 2)
    device = me ^ (2 * chip + other)
    return (device << bits_of(tok_rows)) + (row & (tok_rows - 1))


def reorder(wanted, held, rotated):
    order = jnp.where(wanted == held, 1.0, 0.0).astype(jnp.bfloat16)
    return jnp.dot(order, rotated.astype(jnp.bfloat16), preferred_element_type=jnp.float32)


def lay_kernel(*refs):
    for at, ref in enumerate(refs[:-1]):
        refs[-1][at] = ref[...]


def rotate_in_kernel(tok_rows, near_ref, far_ref, basis_ref, out_ref):
    tokens = out_ref.shape[0]
    depth = near_ref.shape[2]
    acts = jnp.concatenate([ref[...].reshape(-1, depth) for ref in (near_ref, far_ref)], axis=0)
    rotated = jnp.dot(acts, basis_ref[...], preferred_element_type=jnp.float32)
    wanted = lax.broadcasted_iota(jnp.int32, (tokens, tokens), 0)
    held = held_tokens(lax.axis_index("blk"), tokens, tok_rows)
    out_ref[...] = reorder(wanted, held, rotated).astype(jnp.bfloat16)


def stack_kernel(first_ref, last_ref, out_ref):
    half = first_ref.shape[0]
    out_ref[:half] = first_ref[...]
    out_ref[half:] = last_ref[...]


def rotate_part(first, near_ref, far_ref, basis_ref, basis, total, sem):
    steps, depth = basis.shape[:2]

    def copy_of(step):
        rows = pl.ds(pl.multiple_of((first + step) * depth, depth), depth)
        return pltpu.make_async_copy(basis_ref.at[rows], basis.at[step], sem.at[step])

    @pl.loop(0, steps)
    def _(step):
        copy_of(step).start()

    @pl.loop(0, steps)
    def _(step):
        columns = pl.ds(pl.multiple_of((first + step) * depth, depth), depth)
        rows = [ref[:, :, columns].reshape(-1, depth) for ref in (near_ref, far_ref)]
        grads = jnp.concatenate(rows, axis=0)
        copy_of(step).wait()
        total[...] += jnp.dot(grads, basis[step], preferred_element_type=jnp.float32)


def rotate_first_kernel(near_ref, far_ref, basis_ref, out_ref, basis, sem):
    out_ref[...] = jnp.zeros_like(out_ref)
    rotate_part(0, near_ref, far_ref, basis_ref, basis, out_ref, sem)


def rotate_last_kernel(
    tok_rows,
    first,
    near_ref,
    far_ref,
    basis_ref,
    map_ref,
    start_ref,
    out_ref,
    basis,
    total,
    stored_map,
    sem,
):
    tokens = total.shape[0]
    map_copy = pltpu.make_async_copy(map_ref, stored_map, sem.at[basis.shape[0]])
    map_copy.start()
    total[...] = start_ref[...]
    rotate_part(first, near_ref, far_ref, basis_ref, basis, total, sem)
    map_copy.wait()
    row = lax.broadcasted_iota(jnp.int32, (tokens, tokens), 0)
    block = row >> bits_of(tok_rows)
    wanted = jnp.zeros_like(row)
    for stored in range(tokens // tok_rows):
        wanted = jnp.where(block == stored, stored_map[stored] * tok_rows, wanted)
    wanted += row & (tok_rows - 1)
    held = held_tokens(lax.axis_index("blk"), tokens, tok_rows)
    out_ref[...] = reorder(wanted, held, total[...]).T.astype(jnp.bfloat16)


def scale_kernel(
    begun, aligned_ref, near_ref, far_ref, tiles_ref, eigen_ref, out_ref, damped, tiles, sem
):
    blocks, depth = damped.shape[:2]
    chips, _, width = near_ref.shape

    def copy_of(block):
        rows = pl.ds(pl.multiple_of(block * depth, depth), depth)
        return pltpu.make_async_copy(eigen_ref.at[rows], damped.at[block], sem.at[block])

    tiles_copy = pltpu.make_async_copy(tiles_ref, tiles, sem.at[blocks])
    tiles_copy.start()

    @pl.loop(0, blocks)
    def _(block):
        copy_of(block).start()

    tiles_copy.wait()
    me = lax.axis_index("blk")

    @pl.loop(0, blocks)
    def _(block):
        rows = pl.ds(pl.multiple_of(block * depth, depth), depth)
        aligned = aligned_ref[rows, :]
        copy_of(block).wait()
        place = 0
        for steps in begun:
            for other, rotated_ref in enumerate((near_ref, far_ref)):
                source = ring_source(me, steps, other, chips)
                key = (source ^ me) // 2
                rotated = rotated_ref[lax.rem(key, 2) * (chips // 2) + key // 2]
                grad = jnp.dot(aligned, rotated, preferred_element_type=jnp.float32)
                for first in range(0, width, LANES):
                    tile = tiles[(source * width + first) // LANES]
                    lanes = pl.ds(pl.multiple_of(tile * LANES, LANES), LANES)
                    eigen = damped[block, :, lanes]
                    inverse = pl.reciprocal(eigen, approx=True)
                    inverse = inverse * (2.0 - eigen * inverse)
                    scaled = grad[:, first : first + LANES] * inverse
                    out_ref[rows, place : place + LANES] = scaled.astype(jnp.bfloat16)
                    place += LANES


def project_kernel(cuts, scaled_ref, basis_out_ref, *refs):
    pieces = refs[:-4]
    out_ref, window_ref, basis, sem = refs[-4:]
    width = pieces[0].shape[0]
    rows = out_ref.shape[0] // 2
    copies = [
        pltpu.make_async_copy(piece, basis.at[pl.ds(at * width, width)], sem.at[at])
        for at, piece in enumerate(pieces)
    ]
    window_copy = pltpu.make_async_copy(
        basis_out_ref.at[pl.ds(0, window_ref.shape[0])], window_ref, sem.at[len(pieces)]
    )
    window_copy.start()
    for copy in copies:
        copy.start()
    for first, last in zip(cuts[:-1], cuts[1:]):
        for copy in copies[first:last]:
            copy.wait()
        deep = slice(first * width, last * width)

        @pl.loop(0, 2)
        def _(half):
            block = pl.ds(pl.multiple_of(half * rows, rows), rows)
            part = jnp.dot(
                scaled_ref[block, deep], basis[deep, :], preferred_element_type=jnp.float32
            )
            out_ref[block, :] = part if first == 0 else out_ref[block, :] + part

    window_copy.wait()


def window_kernel(scale, window_ref, scaled_ref, projected_ref, *refs):
    pieces = refs[:-3]
    send_ref, keep_ref, result = refs[-3:]
    chips, rows, _ = keep_ref.shape
    width = pieces[0].shape[0]
    total = projected_ref[...]
    first = scaled_ref.shape[1] - width * len(pieces)
    basis = jnp.concatenate([piece[...] for piece in pieces], axis=0)
    total += jnp.dot(scaled_ref[:, first:], basis, preferred_element_type=jnp.float32)
    result[...] = scale * jnp.dot(
        window_ref[...], total.astype(jnp.bfloat16), preferred_element_type=jnp.float32
    )
    core = lax.rem(lax.axis_index("blk"), 2)
    for k in range(chips):
        mine = pl.ds(pl.multiple_of((2 * k + core) * rows, rows), rows)
        keep_ref[k] = result[mine, :]
        other = pl.ds(pl.multiple_of((2 * k + 1 - core) * rows, rows), rows)
        send_ref[k] = result[other, :].astype(jnp.bfloat16)


def add_core_kernel(keys, keep_ref, got_ref, own_ref, *send_refs):
    chip = lax.axis_index("blk") // 2
    for key, ref in zip((0, *keys), (own_ref, *send_refs)):
        at = chip ^ key
        ref[...] = (keep_ref[at] + got_ref[at].astype(jnp.float32)).astype(ref.dtype)


def add_chips_kernel(own_ref, *refs):
    total = own_ref[...]
    for ref in refs[:-1]:
        total += ref[...].astype(jnp.float32)
    refs[-1][...] = total


VMEM = pl.BlockSpec(memory_space=pltpu.VMEM)
SMEM = pl.BlockSpec(memory_space=pltpu.SMEM)
ANY = pl.BlockSpec(memory_space=pl.ANY)
CHEAP = pl.CostEstimate(flops=1, bytes_accessed=1, transcendentals=0)


def after(first, *others):
    return lax.optimization_barrier((first, *others))


def ring_body(n, grad_out, activations, basis_out, basis_in, eigenvalues, tile_order, block_map):
    tok_rows, full_out = grad_out.shape
    tile_width = basis_out.shape[1]
    full_in, in_width = basis_in.shape
    tokens = n * tok_rows
    chips = n // 2
    to_right = lambda x: lax.ppermute(x, "blk", shift_pairs(n, 1))
    to_left = lambda x: lax.ppermute(x, "blk", shift_pairs(n, -1))
    steps = chips // 2

    own = basis_in[:WC].T

    pairs = chips // 2

    def along(x):
        return [x] + [lax.ppermute(x, "blk", xor_pairs(n, 4 * key)) for key in range(1, pairs)]

    def lay(blocks):
        return pl.pallas_call(
            lay_kernel,
            out_shape=jax.ShapeDtypeStruct((pairs, *blocks[0].shape), jnp.bfloat16),
            in_specs=[VMEM] * pairs,
            out_specs=VMEM,
            compiler_params=pltpu.CompilerParams(vmem_limit_bytes=8 * MIB),
            cost_estimate=CHEAP,
            name="lay",
        )(*blocks)

    acts = lay(along(activations))
    acts_got = lax.ppermute(acts, "blk", xor_pairs(n, 2))
    acts_got, *grads = after(acts_got, *along(grad_out))
    grads = lay(grads)
    grads_got = lax.ppermute(grads, "blk", xor_pairs(n, 2))
    depth, later = 1024, 7
    acts = jnp.concatenate([acts, acts_got], axis=0)
    rotated = pl.pallas_call(
        functools.partial(rotate_in_kernel, tok_rows),
        out_shape=jax.ShapeDtypeStruct((tokens, in_width), jnp.bfloat16),
        in_specs=[VMEM, VMEM, VMEM],
        out_specs=VMEM,
        compiler_params=pltpu.CompilerParams(vmem_limit_bytes=8 * MIB),
        cost_estimate=CHEAP,
        name="rotate_in",
    )(acts, swap(acts, n), basis_in)

    def stack(x, got):
        return pl.pallas_call(
            stack_kernel,
            out_shape=jax.ShapeDtypeStruct((2 * x.shape[0], *x.shape[1:]), x.dtype),
            in_specs=[VMEM, VMEM],
            out_specs=VMEM,
            compiler_params=pltpu.CompilerParams(vmem_limit_bytes=8 * MIB),
            cost_estimate=CHEAP,
            name="stack",
        )(x, got)

    rotated = rotated[None]
    key = 4
    while key < n:
        rotated = stack(rotated, lax.ppermute(rotated, "blk", xor_pairs(n, key)))
        key *= 2
    grads_got, rotated, own = after(grads_got, rotated, own)
    right, left = [own, to_right(own)], [own, to_left(own)]
    grads = jnp.concatenate([grads, grads_got], axis=0)
    grads_far = swap(grads, n)
    far = [swap(own, n)]
    rotated_got = lax.ppermute(rotated, "blk", xor_pairs(n, 2))

    rotate = lambda kernel, count, scratch, shape, dtype, *operands: pl.pallas_call(
        kernel,
        out_shape=jax.ShapeDtypeStruct(shape, dtype),
        in_specs=[ANY if x is basis_out or x is block_map else VMEM for x in operands],
        out_specs=VMEM,
        scratch_shapes=[pltpu.VMEM((count, depth, tile_width), jnp.bfloat16)]
        + scratch
        + [pltpu.SemaphoreType.DMA((count + 1,))],
        compiler_params=pltpu.CompilerParams(vmem_limit_bytes=40 * MIB),
        cost_estimate=CHEAP,
        name=kernel.func.__name__[:-7],
    )(*operands)
    start = rotate(
        functools.partial(rotate_first_kernel),
        full_out // depth - later,
        [],
        (tokens, tile_width),
        jnp.float32,
        grads,
        grads_far,
        basis_out,
    )
    start, grads, right[-1], left[-1], rotated_got, *far = after(
        start, grads, right[-1], left[-1], rotated_got, *far
    )
    rotated = stack(rotated, rotated_got)
    rotated_far = swap(rotated, n)
    far += [swap(right[-1], n), swap(left[-1], n)]
    right.append(to_right(right[-1]))
    left.append(to_left(left[-1]))
    aligned = rotate(
        functools.partial(rotate_last_kernel, tok_rows, full_out // depth - later),
        later,
        [
            pltpu.VMEM((tokens, tile_width), jnp.float32),
            pltpu.SMEM(block_map.shape, jnp.int32),
        ],
        (tile_width, tokens),
        jnp.bfloat16,
        grads,
        grads_far,
        basis_out,
        block_map,
        start,
    )

    aligned, right[-1], left[-1], rotated_far, *far = after(
        aligned, right[-1], left[-1], rotated_far, *far
    )
    far += [swap(right[-1], n), swap(left[-1], n)]
    right.append(to_right(right[-1]))
    left.append(to_left(left[-1]))
    begun = [0] + [at for step in range(1, steps) for at in (step, chips - step)] + [steps]
    blocks = 8
    scaled = pl.pallas_call(
        functools.partial(scale_kernel, begun),
        out_shape=jax.ShapeDtypeStruct((tile_width, full_in), jnp.bfloat16),
        in_specs=[VMEM] * 3 + [ANY] * 2,
        out_specs=VMEM,
        scratch_shapes=[
            pltpu.VMEM((blocks, tile_width // blocks, full_in), jnp.float32),
            pltpu.SMEM(tile_order.shape, jnp.int32),
            pltpu.SemaphoreType.DMA((blocks + 1,)),
        ],
        compiler_params=pltpu.CompilerParams(vmem_limit_bytes=40 * MIB),
        cost_estimate=CHEAP,
        name="scale",
    )(aligned, rotated, rotated_far, tile_order, eigenvalues)

    scaled, right[-1], left[-1], *far = after(scaled, right[-1], left[-1], *far)
    cut = in_width // 2
    last = [to_right(right[-1][:cut]), to_left(left[-1][cut:])]
    near = [right[at] if at < steps else left[chips - at] for at in begun[:-1]]
    far += [swap(piece, n) for piece in near[len(far) :]]
    pieces = [piece for pair in zip(near, far) for piece in pair]
    projected, window = pl.pallas_call(
        functools.partial(project_kernel, (0, 6, len(pieces))),
        out_shape=(
            jax.ShapeDtypeStruct((tile_width, WC), jnp.float32),
            jax.ShapeDtypeStruct((WR, tile_width), jnp.bfloat16),
        ),
        in_specs=[VMEM] + [ANY] * (len(pieces) + 1),
        out_specs=(VMEM, VMEM),
        scratch_shapes=[
            pltpu.VMEM((len(pieces) * in_width, WC), jnp.bfloat16),
            pltpu.SemaphoreType.DMA((len(pieces) + 1,)),
        ],
        compiler_params=pltpu.CompilerParams(vmem_limit_bytes=24 * MIB),
        cost_estimate=CHEAP,
        name="project",
    )(scaled, basis_out, *pieces)

    projected, *last = after(projected, *last)
    last += [swap(piece, n) for piece in last]
    rows = WR // n
    send, keep = pl.pallas_call(
        functools.partial(window_kernel, 1.0 / tokens),
        out_shape=(
            jax.ShapeDtypeStruct((chips, rows, WC), jnp.bfloat16),
            jax.ShapeDtypeStruct((chips, rows, WC), jnp.float32),
        ),
        in_specs=[VMEM] * 7,
        out_specs=(VMEM, VMEM),
        scratch_shapes=[pltpu.VMEM((WR, WC), jnp.float32)],
        compiler_params=pltpu.CompilerParams(vmem_limit_bytes=24 * MIB),
        cost_estimate=CHEAP,
        name="window",
    )(window, scaled, projected, *last)

    keys = sorted(range(1, chips), key=lambda key: -(key & -2))
    small = pltpu.CompilerParams(vmem_limit_bytes=8 * MIB)
    own, *sends = pl.pallas_call(
        functools.partial(add_core_kernel, keys),
        out_shape=[jax.ShapeDtypeStruct((rows, WC), jnp.float32)]
        + [jax.ShapeDtypeStruct((rows, WC), jnp.bfloat16)] * len(keys),
        in_specs=[VMEM, VMEM],
        out_specs=[VMEM] * chips,
        compiler_params=small,
        name="add_core",
    )(keep, swap(send, n))
    arrived = [lax.ppermute(x, "blk", xor_pairs(n, 2 * key)) for key, x in zip(keys, sends)]
    return pl.pallas_call(
        add_chips_kernel,
        out_shape=jax.ShapeDtypeStruct((rows, WC), jnp.float32),
        in_specs=[VMEM] * chips,
        out_specs=VMEM,
        compiler_params=small,
        name="add_chips",
    )(own, *arrived)


def gather_body(grad_out, activations, basis_out, basis_in, eigenvalues, tile_order, block_map):
    n_blocks = lax.axis_size("blk")
    tile_width = basis_out.shape[1]
    tok_rows = grad_out.shape[0]
    full_in = eigenvalues.shape[1]
    tokens = n_blocks * tok_rows
    dot = functools.partial(jnp.dot, preferred_element_type=jnp.float32)
    in_rows = lax.all_gather(basis_in[:WC], "blk", axis=1, tiled=True)
    acts = lax.all_gather(activations, "blk", axis=0, tiled=True)
    in_tile = dot(acts, basis_in).astype(jnp.bfloat16)
    rotated_in = lax.all_gather(in_tile, "blk", axis=1, tiled=True)
    grads = lax.all_gather(grad_out, "blk", axis=0, tiled=True)
    rotated_out = dot(grads, basis_out).astype(jnp.bfloat16)
    aligned = jnp.take(
        rotated_out.reshape(n_blocks, tok_rows, tile_width), block_map, axis=0
    ).reshape(tokens, tile_width)
    grad_tile = dot(aligned.T, rotated_in) / tokens
    damped = jnp.take(
        eigenvalues.reshape(tile_width, full_in // LANES, LANES), tile_order, axis=1
    ).reshape(tile_width, full_in)
    scaled = (grad_tile / damped).astype(jnp.bfloat16)
    projected = dot(scaled, in_rows.T).astype(jnp.bfloat16)
    return lax.psum_scatter(
        dot(basis_out[:WR], projected), "blk", scatter_dimension=0, tiled=True
    )


def solution(mesh):
    n = mesh.shape["blk"]

    def body(*args):
        wide = args[3].shape[1] % LANES == 0 and args[2].shape[1] % LANES == 0
        doubles = n & (n - 1) == 0 and args[0].shape[0] & (args[0].shape[0] - 1) == 0
        if wide and doubles and WR % (16 * n) == 0:
            return ring_body(n, *args)
        return gather_body(*args)

    placed = (
        P(("grp", "blk"), None),
        P(("grp", "blk"), None),
        P(None, "blk"),
        P(None, "blk"),
        P("blk", None),
        P(),
        P(),
    )
    return jax.shard_map(
        body, mesh=mesh, in_specs=placed, out_specs=P(("grp", "blk"), None), check_vma=False
    )
```

```python
import functools

import jax
import jax.numpy as jnp
from jax import lax
from jax.experimental import pallas as pl
from jax.experimental.pallas import tpu as pltpu
from jax.sharding import PartitionSpec as P

WR = 768
WC = 512
LANES = 128
MIB = 1 << 20


def ring_of(n):
    chips = n // 2
    return [*range(0, chips, 2), *range(chips - 1, 0, -2)]


def shift_pairs(n, by):
    ring = ring_of(n)
    return [
        (2 * ring[p] + c, 2 * ring[(p + by) % len(ring)] + c)
        for p in range(len(ring))
        for c in range(2)
    ]


def ring_source(me, steps, other, chips):
    chip, core = me // 2, lax.rem(me, 2)
    place = jnp.where(lax.rem(chip, 2) == 0, chip // 2, chips - 1 - chip // 2)
    place = lax.rem(place + chips - steps, chips)
    chip = jnp.where(place < chips // 2, 2 * place, 2 * (chips - 1 - place) + 1)
    return 2 * chip + (core ^ other)


def xor_pairs(n, key):
    return [(b, b ^ key) for b in range(n)]


def swap(x, n):
    return lax.ppermute(x, "blk", xor_pairs(n, 1))


def bits_of(size):
    return size.bit_length() - 1


def held_tokens(me, tokens, tok_rows):
    row = lax.broadcasted_iota(jnp.int32, (tokens, tokens), 1)
    pairs = tokens // tok_rows // 4
    place = row >> bits_of(tok_rows)
    chip = 2 * (place & (pairs - 1)) + ((place >> bits_of(pairs)) & 1)
    other = row >> bits_of(tokens // 2)
    device = me ^ (2 * chip + other)
    return (device << bits_of(tok_rows)) + (row & (tok_rows - 1))


def reorder(wanted, held, rotated):
    order = jnp.where(wanted == held, 1.0, 0.0).astype(jnp.bfloat16)
    return jnp.dot(order, rotated.astype(jnp.bfloat16), preferred_element_type=jnp.float32)


def part_kernel(*refs):
    grads_ref, acts_ref = refs[-2:]
    first = grads_ref.shape[2]
    for at, ref in enumerate(refs[:-2]):
        grads_ref[at] = ref[0, :, :first]
        acts_ref[at] = ref[0, :, first:]


def rotate_in_kernel(tok_rows, near_ref, far_ref, basis_ref, out_ref):
    tokens = out_ref.shape[0]
    depth = near_ref.shape[2]
    acts = jnp.concatenate([ref[...].reshape(-1, depth) for ref in (near_ref, far_ref)], axis=0)
    rotated = jnp.dot(acts, basis_ref[...], preferred_element_type=jnp.float32)
    wanted = lax.broadcasted_iota(jnp.int32, (tokens, tokens), 0)
    held = held_tokens(lax.axis_index("blk"), tokens, tok_rows)
    out_ref[...] = reorder(wanted, held, rotated).astype(jnp.bfloat16)


def keep_kernel(basis_ref, kept_ref):
    kept_ref[...] = basis_ref[...]


def lay_kernel(*refs):
    for at, ref in enumerate(refs[:-1]):
        refs[-1][at] = ref[...]


def stack_kernel(first_ref, last_ref, out_ref):
    half = first_ref.shape[0]
    out_ref[:half] = first_ref[...]
    out_ref[half:] = last_ref[...]


def rotate_part(first, near_ref, far_ref, basis_ref, basis, total, sem):
    steps, depth = basis.shape[:2]

    def copy_of(step):
        rows = pl.ds(pl.multiple_of((first + step) * depth, depth), depth)
        return pltpu.make_async_copy(basis_ref.at[rows], basis.at[step], sem.at[step])

    @pl.loop(0, steps)
    def _(step):
        copy_of(step).start()

    @pl.loop(0, steps)
    def _(step):
        columns = pl.ds(pl.multiple_of((first + step) * depth, depth), depth)
        rows = [ref[:, :, columns].reshape(-1, depth) for ref in (near_ref, far_ref)]
        grads = jnp.concatenate(rows, axis=0)
        copy_of(step).wait()
        total[...] += jnp.dot(grads, basis[step], preferred_element_type=jnp.float32)


def rotate_first_kernel(near_ref, far_ref, basis_ref, out_ref, basis, sem):
    out_ref[...] = jnp.zeros_like(out_ref)
    rotate_part(0, near_ref, far_ref, basis_ref, basis, out_ref, sem)


def rotate_last_kernel(
    tok_rows,
    first,
    near_ref,
    far_ref,
    basis_ref,
    map_ref,
    start_ref,
    out_ref,
    basis,
    total,
    stored_map,
    sem,
):
    tokens = total.shape[0]
    map_copy = pltpu.make_async_copy(map_ref, stored_map, sem.at[basis.shape[0]])
    map_copy.start()
    total[...] = start_ref[...]
    rotate_part(first, near_ref, far_ref, basis_ref, basis, total, sem)
    map_copy.wait()
    row = lax.broadcasted_iota(jnp.int32, (tokens, tokens), 0)
    block = row >> bits_of(tok_rows)
    wanted = jnp.zeros_like(row)
    for stored in range(tokens // tok_rows):
        wanted = jnp.where(block == stored, stored_map[stored] * tok_rows, wanted)
    wanted += row & (tok_rows - 1)
    held = held_tokens(lax.axis_index("blk"), tokens, tok_rows)
    out_ref[...] = reorder(wanted, held, total[...]).T.astype(jnp.bfloat16)


def scale_kernel(
    begun,
    aligned_ref,
    near_ref,
    far_ref,
    tiles_ref,
    eigen_ref,
    out_ref,
    damped,
    tiles,
    lanes,
    rotated,
    sem,
):
    blocks, depth = damped.shape[:2]
    chips, _, width = near_ref.shape
    per_piece = width // LANES

    def copy_of(block):
        rows = pl.ds(pl.multiple_of(block * depth, depth), depth)
        return pltpu.make_async_copy(eigen_ref.at[rows], damped.at[block], sem.at[block])

    tiles_copy = pltpu.make_async_copy(tiles_ref, tiles, sem.at[blocks])
    tiles_copy.start()

    @pl.loop(0, blocks)
    def _(block):
        copy_of(block).start()

    tiles_copy.wait()
    me = lax.axis_index("blk")
    for at, steps in enumerate(begun):
        for other, rotated_ref in enumerate((near_ref, far_ref)):
            source = ring_source(me, steps, other, chips)
            key = (source ^ me) // 2
            piece = 2 * at + other
            rotated[piece] = rotated_ref[lax.rem(key, 2) * (chips // 2) + key // 2]
            for part in range(per_piece):
                lanes[piece * per_piece + part] = tiles[source * per_piece + part] * LANES

    @pl.loop(0, blocks)
    def _(block):
        rows = pl.ds(pl.multiple_of(block * depth, depth), depth)
        aligned = aligned_ref[rows, :]
        copy_of(block).wait()
        for piece in range(2 * chips):
            grad = jnp.dot(aligned, rotated[piece], preferred_element_type=jnp.float32)
            for part in range(per_piece):
                tile = piece * per_piece + part
                eigen = damped[block, :, pl.ds(pl.multiple_of(lanes[tile], LANES), LANES)]
                inverse = pl.reciprocal(eigen, approx=True)
                inverse = inverse * (2.0 - eigen * inverse)
                scaled = grad[:, part * LANES : (part + 1) * LANES] * inverse
                out_ref[rows, tile * LANES : (tile + 1) * LANES] = scaled.astype(jnp.bfloat16)


def project_kernel(cuts, scaled_ref, basis_out_ref, *refs):
    pieces = refs[:-4]
    out_ref, window_ref, basis, sem = refs[-4:]
    width = pieces[0].shape[0]
    rows = out_ref.shape[0] // 2
    copies = [
        pltpu.make_async_copy(piece, basis.at[pl.ds(at * width, width)], sem.at[at])
        for at, piece in enumerate(pieces)
    ]
    window_copy = pltpu.make_async_copy(
        basis_out_ref.at[pl.ds(0, window_ref.shape[0])], window_ref, sem.at[len(pieces)]
    )
    window_copy.start()
    for copy in copies:
        copy.start()
    for first, last in zip(cuts[:-1], cuts[1:]):
        for copy in copies[first:last]:
            copy.wait()
        deep = slice(first * width, last * width)

        @pl.loop(0, 2)
        def _(half):
            block = pl.ds(pl.multiple_of(half * rows, rows), rows)
            part = jnp.dot(
                scaled_ref[block, deep], basis[deep, :], preferred_element_type=jnp.float32
            )
            out_ref[block, :] = part if first == 0 else out_ref[block, :] + part

    window_copy.wait()


def window_kernel(scale, window_ref, scaled_ref, projected_ref, *refs):
    pieces = refs[:-3]
    send_ref, keep_ref, result = refs[-3:]
    chips, rows, _ = keep_ref.shape
    width = pieces[0].shape[0]
    total = projected_ref[...]
    first = scaled_ref.shape[1] - width * len(pieces)
    basis = jnp.concatenate([piece[...] for piece in pieces], axis=0)
    total += jnp.dot(scaled_ref[:, first:], basis, preferred_element_type=jnp.float32)
    result[...] = scale * jnp.dot(
        window_ref[...], total.astype(jnp.bfloat16), preferred_element_type=jnp.float32
    )
    core = lax.rem(lax.axis_index("blk"), 2)
    for k in range(chips):
        mine = pl.ds(pl.multiple_of((2 * k + core) * rows, rows), rows)
        keep_ref[k] = result[mine, :]
        other = pl.ds(pl.multiple_of((2 * k + 1 - core) * rows, rows), rows)
        send_ref[k] = result[other, :].astype(jnp.bfloat16)


def add_core_kernel(keys, keep_ref, got_ref, own_ref, *send_refs):
    chip = lax.axis_index("blk") // 2
    for key, ref in zip((0, *keys), (own_ref, *send_refs)):
        at = chip ^ key
        ref[...] = (keep_ref[at] + got_ref[at].astype(jnp.float32)).astype(ref.dtype)


def add_chips_kernel(own_ref, *refs):
    total = own_ref[...]
    for ref in refs[:-1]:
        total += ref[...].astype(jnp.float32)
    refs[-1][...] = total


VMEM = pl.BlockSpec(memory_space=pltpu.VMEM)
SMEM = pl.BlockSpec(memory_space=pltpu.SMEM)
ANY = pl.BlockSpec(memory_space=pl.ANY)
CHEAP = pl.CostEstimate(flops=1, bytes_accessed=1, transcendentals=0)


def after(first, *others):
    return lax.optimization_barrier((first, *others))


def ring_body(n, grad_out, activations, basis_out, basis_in, eigenvalues, tile_order, block_map):
    tok_rows, full_out = grad_out.shape
    tile_width = basis_out.shape[1]
    full_in, in_width = basis_in.shape
    tokens = n * tok_rows
    chips = n // 2
    to_right = lambda x: lax.ppermute(x, "blk", shift_pairs(n, 1))
    to_left = lambda x: lax.ppermute(x, "blk", shift_pairs(n, -1))
    steps = chips // 2

    own = basis_in[:WC].T

    pairs = chips // 2
    both = jnp.concatenate([grad_out, activations], axis=1)[None]
    got = [lax.ppermute(both, "blk", xor_pairs(n, 4 * key)) for key in range(1, pairs)]
    kept = pl.pallas_call(
        keep_kernel,
        out_shape=jax.ShapeDtypeStruct(basis_in.shape, jnp.bfloat16),
        in_specs=[VMEM],
        out_specs=VMEM,
        compiler_params=pltpu.CompilerParams(vmem_limit_bytes=8 * MIB),
        cost_estimate=CHEAP,
        name="keep",
    )(basis_in)
    both, own, kept, *got = after(both, own, kept, *got)
    depth, later = 1024, 7
    grads, acts = pl.pallas_call(
        part_kernel,
        out_shape=(
            jax.ShapeDtypeStruct((pairs, tok_rows, full_out), jnp.bfloat16),
            jax.ShapeDtypeStruct((pairs, tok_rows, full_in), jnp.bfloat16),
        ),
        in_specs=[VMEM] * pairs,
        out_specs=(VMEM, VMEM),
        compiler_params=pltpu.CompilerParams(vmem_limit_bytes=8 * MIB),
        name="part",
    )(both, *got)
    acts, grads, own = after(acts, grads, own)
    acts_got = lax.ppermute(acts, "blk", xor_pairs(n, 2))
    grads_got = lax.ppermute(grads, "blk", xor_pairs(n, 2))
    acts = jnp.concatenate([acts, acts_got], axis=0)
    rotated = pl.pallas_call(
        functools.partial(rotate_in_kernel, tok_rows),
        out_shape=jax.ShapeDtypeStruct((tokens, in_width), jnp.bfloat16),
        in_specs=[VMEM, VMEM, VMEM],
        out_specs=VMEM,
        compiler_params=pltpu.CompilerParams(vmem_limit_bytes=8 * MIB),
        cost_estimate=CHEAP,
        name="rotate_in",
    )(acts, swap(acts, n), kept)

    def lay(kernel, shape, *blocks):
        return pl.pallas_call(
            kernel,
            out_shape=jax.ShapeDtypeStruct(shape, jnp.bfloat16),
            in_specs=[VMEM] * len(blocks),
            out_specs=VMEM,
            compiler_params=pltpu.CompilerParams(vmem_limit_bytes=8 * MIB),
            cost_estimate=CHEAP,
            name=kernel.__name__[:-7],
        )(*blocks)

    grads_got, _ = after(grads_got, rotated)
    blocks = [rotated] + [
        lax.ppermute(rotated, "blk", xor_pairs(n, 4 * key)) for key in range(1, pairs)
    ]
    rotated = lay(lay_kernel, (pairs, tokens, in_width), *blocks)
    rotated, own = after(rotated, own)
    right, left = [own, to_right(own)], [own, to_left(own)]
    grads = jnp.concatenate([grads, grads_got], axis=0)
    grads_far = swap(grads, n)
    far = [swap(own, n)]
    rotated_got = lax.ppermute(rotated, "blk", xor_pairs(n, 2))

    rotate = lambda kernel, count, scratch, shape, dtype, *operands: pl.pallas_call(
        kernel,
        out_shape=jax.ShapeDtypeStruct(shape, dtype),
        in_specs=[ANY if x is basis_out or x is block_map else VMEM for x in operands],
        out_specs=VMEM,
        scratch_shapes=[pltpu.VMEM((count, depth, tile_width), jnp.bfloat16)]
        + scratch
        + [pltpu.SemaphoreType.DMA((count + 1,))],
        compiler_params=pltpu.CompilerParams(vmem_limit_bytes=40 * MIB),
        cost_estimate=CHEAP,
        name=kernel.func.__name__[:-7],
    )(*operands)
    start = rotate(
        functools.partial(rotate_first_kernel),
        full_out // depth - later,
        [],
        (tokens, tile_width),
        jnp.float32,
        grads,
        grads_far,
        basis_out,
    )
    start, grads, right[-1], left[-1], rotated_got, *far = after(
        start, grads, right[-1], left[-1], rotated_got, *far
    )
    rotated = lay(stack_kernel, (chips, tokens, in_width), rotated, rotated_got)
    rotated_far = swap(rotated, n)
    far += [swap(right[-1], n), swap(left[-1], n)]
    right.append(to_right(right[-1]))
    left.append(to_left(left[-1]))
    aligned = rotate(
        functools.partial(rotate_last_kernel, tok_rows, full_out // depth - later),
        later,
        [
            pltpu.VMEM((tokens, tile_width), jnp.float32),
            pltpu.SMEM(block_map.shape, jnp.int32),
        ],
        (tile_width, tokens),
        jnp.bfloat16,
        grads,
        grads_far,
        basis_out,
        block_map,
        start,
    )

    aligned, right[-1], left[-1], rotated_far, *far = after(
        aligned, right[-1], left[-1], rotated_far, *far
    )
    far += [swap(right[-1], n), swap(left[-1], n)]
    right.append(to_right(right[-1]))
    left.append(to_left(left[-1]))
    begun = [0] + [at for step in range(1, steps) for at in (step, chips - step)] + [steps]
    blocks = 8
    scaled = pl.pallas_call(
        functools.partial(scale_kernel, begun),
        out_shape=jax.ShapeDtypeStruct((tile_width, full_in), jnp.bfloat16),
        in_specs=[VMEM] * 3 + [ANY] * 2,
        out_specs=VMEM,
        scratch_shapes=[
            pltpu.VMEM((blocks, tile_width // blocks, full_in), jnp.float32),
            pltpu.SMEM(tile_order.shape, jnp.int32),
            pltpu.SMEM(tile_order.shape, jnp.int32),
            pltpu.VMEM((n, tokens, in_width), jnp.bfloat16),
            pltpu.SemaphoreType.DMA((blocks + 1,)),
        ],
        compiler_params=pltpu.CompilerParams(vmem_limit_bytes=40 * MIB),
        cost_estimate=CHEAP,
        name="scale",
    )(aligned, rotated, rotated_far, tile_order, eigenvalues)

    scaled, right[-1], left[-1], *far = after(scaled, right[-1], left[-1], *far)
    cut = in_width // 2
    last = [to_right(right[-1][:cut]), to_left(left[-1][cut:])]
    near = [right[at] if at < steps else left[chips - at] for at in begun[:-1]]
    far += [swap(piece, n) for piece in near[len(far) :]]
    pieces = [piece for pair in zip(near, far) for piece in pair]
    projected, window = pl.pallas_call(
        functools.partial(project_kernel, (0, 6, len(pieces))),
        out_shape=(
            jax.ShapeDtypeStruct((tile_width, WC), jnp.float32),
            jax.ShapeDtypeStruct((WR, tile_width), jnp.bfloat16),
        ),
        in_specs=[VMEM] + [ANY] * (len(pieces) + 1),
        out_specs=(VMEM, VMEM),
        scratch_shapes=[
            pltpu.VMEM((len(pieces) * in_width, WC), jnp.bfloat16),
            pltpu.SemaphoreType.DMA((len(pieces) + 1,)),
        ],
        compiler_params=pltpu.CompilerParams(vmem_limit_bytes=24 * MIB),
        cost_estimate=CHEAP,
        name="project",
    )(scaled, basis_out, *pieces)

    projected, *last = after(projected, *last)
    last += [swap(piece, n) for piece in last]
    rows = WR // n
    send, keep = pl.pallas_call(
        functools.partial(window_kernel, 1.0 / tokens),
        out_shape=(
            jax.ShapeDtypeStruct((chips, rows, WC), jnp.bfloat16),
            jax.ShapeDtypeStruct((chips, rows, WC), jnp.float32),
        ),
        in_specs=[VMEM] * 7,
        out_specs=(VMEM, VMEM),
        scratch_shapes=[pltpu.VMEM((WR, WC), jnp.float32)],
        compiler_params=pltpu.CompilerParams(vmem_limit_bytes=24 * MIB),
        cost_estimate=CHEAP,
        name="window",
    )(window, scaled, projected, *last)

    keys = sorted(range(1, chips), key=lambda key: -(key & -2))
    small = pltpu.CompilerParams(vmem_limit_bytes=8 * MIB)
    own, *sends = pl.pallas_call(
        functools.partial(add_core_kernel, keys),
        out_shape=[jax.ShapeDtypeStruct((rows, WC), jnp.float32)]
        + [jax.ShapeDtypeStruct((rows, WC), jnp.bfloat16)] * len(keys),
        in_specs=[VMEM, VMEM],
        out_specs=[VMEM] * chips,
        compiler_params=small,
        name="add_core",
    )(keep, swap(send, n))
    arrived = [lax.ppermute(x, "blk", xor_pairs(n, 2 * key)) for key, x in zip(keys, sends)]
    return pl.pallas_call(
        add_chips_kernel,
        out_shape=jax.ShapeDtypeStruct((rows, WC), jnp.float32),
        in_specs=[VMEM] * chips,
        out_specs=VMEM,
        compiler_params=small,
        name="add_chips",
    )(own, *arrived)


def gather_body(grad_out, activations, basis_out, basis_in, eigenvalues, tile_order, block_map):
    n_blocks = lax.axis_size("blk")
    tile_width = basis_out.shape[1]
    tok_rows = grad_out.shape[0]
    full_in = eigenvalues.shape[1]
    tokens = n_blocks * tok_rows
    dot = functools.partial(jnp.dot, preferred_element_type=jnp.float32)
    in_rows = lax.all_gather(basis_in[:WC], "blk", axis=1, tiled=True)
    acts = lax.all_gather(activations, "blk", axis=0, tiled=True)
    in_tile = dot(acts, basis_in).astype(jnp.bfloat16)
    rotated_in = lax.all_gather(in_tile, "blk", axis=1, tiled=True)
    grads = lax.all_gather(grad_out, "blk", axis=0, tiled=True)
    rotated_out = dot(grads, basis_out).astype(jnp.bfloat16)
    aligned = jnp.take(
        rotated_out.reshape(n_blocks, tok_rows, tile_width), block_map, axis=0
    ).reshape(tokens, tile_width)
    grad_tile = dot(aligned.T, rotated_in) / tokens
    damped = jnp.take(
        eigenvalues.reshape(tile_width, full_in // LANES, LANES), tile_order, axis=1
    ).reshape(tile_width, full_in)
    scaled = (grad_tile / damped).astype(jnp.bfloat16)
    projected = dot(scaled, in_rows.T).astype(jnp.bfloat16)
    return lax.psum_scatter(
        dot(basis_out[:WR], projected), "blk", scatter_dimension=0, tiled=True
    )


def solution(mesh):
    n = mesh.shape["blk"]

    def body(*args):
        wide = args[3].shape[1] % LANES == 0 and args[2].shape[1] % LANES == 0
        doubles = n & (n - 1) == 0 and args[0].shape[0] & (args[0].shape[0] - 1) == 0
        if wide and doubles and WR % (16 * n) == 0:
            return ring_body(n, *args)
        return gather_body(*args)

    placed = (
        P(("grp", "blk"), None),
        P(("grp", "blk"), None),
        P(None, "blk"),
        P(None, "blk"),
        P("blk", None),
        P(),
        P(),
    )
    return jax.shard_map(
        body, mesh=mesh, in_specs=placed, out_specs=P(("grp", "blk"), None), check_vma=False
    )
```

```python
import functools

import jax
import jax.numpy as jnp
from jax import lax
from jax.experimental import pallas as pl
from jax.experimental.pallas import tpu as pltpu
from jax.sharding import PartitionSpec as P

WR = 768
WC = 512
LANES = 128
MIB = 1 << 20


def ring_of(n):
    chips = n // 2
    return [*range(0, chips, 2), *range(chips - 1, 0, -2)]


def shift_pairs(n, by):
    ring = ring_of(n)
    return [
        (2 * ring[p] + c, 2 * ring[(p + by) % len(ring)] + c)
        for p in range(len(ring))
        for c in range(2)
    ]


def ring_source(me, steps, other, chips):
    chip, core = me // 2, lax.rem(me, 2)
    place = jnp.where(lax.rem(chip, 2) == 0, chip // 2, chips - 1 - chip // 2)
    place = lax.rem(place + chips - steps, chips)
    chip = jnp.where(place < chips // 2, 2 * place, 2 * (chips - 1 - place) + 1)
    return 2 * chip + (core ^ other)


def xor_pairs(n, key):
    return [(b, b ^ key) for b in range(n)]


def exchange(x, n, stride):
    groups = [list(range(first, n, stride)) for first in range(stride)]
    return lax.all_to_all(x, "blk", 0, 0, axis_index_groups=groups, tiled=True)


def swap(x, n):
    return lax.ppermute(x, "blk", xor_pairs(n, 1))


def bits_of(size):
    return size.bit_length() - 1


def held_tokens(me, tokens, tok_rows):
    row = lax.broadcasted_iota(jnp.int32, (tokens, tokens), 1)
    pairs = tokens // tok_rows // 4
    place = row >> bits_of(tok_rows)
    chip = 2 * (place & (pairs - 1)) + ((place >> bits_of(pairs)) & 1)
    other = row >> bits_of(tokens // 2)
    device = me ^ (2 * chip + other)
    return (device << bits_of(tok_rows)) + (row & (tok_rows - 1))


def reorder(wanted, held, rotated):
    order = jnp.where(wanted == held, 1.0, 0.0).astype(jnp.bfloat16)
    return jnp.dot(order, rotated.astype(jnp.bfloat16), preferred_element_type=jnp.float32)


def part_kernel(*refs):
    grads_ref, acts_ref = refs[-2:]
    first = grads_ref.shape[2]
    for at, ref in enumerate(refs[:-2]):
        grads_ref[at] = ref[0, :, :first]
        acts_ref[at] = ref[0, :, first:]


def rotate_in_kernel(tok_rows, near_ref, far_ref, basis_ref, out_ref):
    tokens = out_ref.shape[1]
    depth = near_ref.shape[2]
    acts = jnp.concatenate([ref[...].reshape(-1, depth) for ref in (near_ref, far_ref)], axis=0)
    rotated = jnp.dot(acts, basis_ref[...], preferred_element_type=jnp.float32)
    wanted = lax.broadcasted_iota(jnp.int32, (tokens, tokens), 0)
    held = held_tokens(lax.axis_index("blk"), tokens, tok_rows)
    ordered = reorder(wanted, held, rotated).astype(jnp.bfloat16)
    for copy in range(out_ref.shape[0]):
        out_ref[copy] = ordered


def keep_kernel(basis_ref, kept_ref):
    kept_ref[...] = basis_ref[...]


def rotate_part(first, near_ref, far_ref, basis_ref, basis, total, sem):
    steps, depth = basis.shape[:2]

    def copy_of(step):
        rows = pl.ds(pl.multiple_of((first + step) * depth, depth), depth)
        return pltpu.make_async_copy(basis_ref.at[rows], basis.at[step], sem.at[step])

    @pl.loop(0, steps)
    def _(step):
        copy_of(step).start()

    @pl.loop(0, steps)
    def _(step):
        columns = pl.ds(pl.multiple_of((first + step) * depth, depth), depth)
        rows = [ref[:, :, columns].reshape(-1, depth) for ref in (near_ref, far_ref)]
        grads = jnp.concatenate(rows, axis=0)
        copy_of(step).wait()
        total[...] += jnp.dot(grads, basis[step], preferred_element_type=jnp.float32)


def rotate_first_kernel(near_ref, far_ref, basis_ref, out_ref, basis, sem):
    out_ref[...] = jnp.zeros_like(out_ref)
    rotate_part(0, near_ref, far_ref, basis_ref, basis, out_ref, sem)


def rotate_last_kernel(
    tok_rows,
    first,
    near_ref,
    far_ref,
    basis_ref,
    map_ref,
    start_ref,
    out_ref,
    basis,
    total,
    stored_map,
    sem,
):
    tokens = total.shape[0]
    map_copy = pltpu.make_async_copy(map_ref, stored_map, sem.at[basis.shape[0]])
    map_copy.start()
    total[...] = start_ref[...]
    rotate_part(first, near_ref, far_ref, basis_ref, basis, total, sem)
    map_copy.wait()
    row = lax.broadcasted_iota(jnp.int32, (tokens, tokens), 0)
    block = row >> bits_of(tok_rows)
    wanted = jnp.zeros_like(row)
    for stored in range(tokens // tok_rows):
        wanted = jnp.where(block == stored, stored_map[stored] * tok_rows, wanted)
    wanted += row & (tok_rows - 1)
    held = held_tokens(lax.axis_index("blk"), tokens, tok_rows)
    out_ref[...] = reorder(wanted, held, total[...]).T.astype(jnp.bfloat16)


def scale_kernel(
    begun,
    aligned_ref,
    near_ref,
    far_ref,
    tiles_ref,
    eigen_ref,
    out_ref,
    damped,
    tiles,
    lanes,
    rotated,
    sem,
):
    blocks, depth = damped.shape[:2]
    chips, _, width = near_ref.shape
    per_piece = width // LANES

    def copy_of(block):
        rows = pl.ds(pl.multiple_of(block * depth, depth), depth)
        return pltpu.make_async_copy(eigen_ref.at[rows], damped.at[block], sem.at[block])

    tiles_copy = pltpu.make_async_copy(tiles_ref, tiles, sem.at[blocks])
    tiles_copy.start()

    @pl.loop(0, blocks)
    def _(block):
        copy_of(block).start()

    tiles_copy.wait()
    me = lax.axis_index("blk")
    for at, steps in enumerate(begun):
        for other, rotated_ref in enumerate((near_ref, far_ref)):
            source = ring_source(me, steps, other, chips)
            piece = 2 * at + other
            rotated[piece] = rotated_ref[source // 2]
            for part in range(per_piece):
                lanes[piece * per_piece + part] = tiles[source * per_piece + part] * LANES

    @pl.loop(0, blocks)
    def _(block):
        rows = pl.ds(pl.multiple_of(block * depth, depth), depth)
        aligned = aligned_ref[rows, :]
        copy_of(block).wait()
        for piece in range(2 * chips):
            grad = jnp.dot(aligned, rotated[piece], preferred_element_type=jnp.float32)
            for part in range(per_piece):
                tile = piece * per_piece + part
                eigen = damped[block, :, pl.ds(pl.multiple_of(lanes[tile], LANES), LANES)]
                inverse = pl.reciprocal(eigen, approx=True)
                inverse = inverse * (2.0 - eigen * inverse)
                scaled = grad[:, part * LANES : (part + 1) * LANES] * inverse
                out_ref[rows, tile * LANES : (tile + 1) * LANES] = scaled.astype(jnp.bfloat16)


def project_kernel(cuts, scaled_ref, basis_out_ref, *refs):
    pieces = refs[:-4]
    out_ref, window_ref, basis, sem = refs[-4:]
    width = pieces[0].shape[0]
    rows = out_ref.shape[0] // 2
    copies = [
        pltpu.make_async_copy(piece, basis.at[pl.ds(at * width, width)], sem.at[at])
        for at, piece in enumerate(pieces)
    ]
    window_copy = pltpu.make_async_copy(
        basis_out_ref.at[pl.ds(0, window_ref.shape[0])], window_ref, sem.at[len(pieces)]
    )
    window_copy.start()
    for copy in copies:
        copy.start()
    for first, last in zip(cuts[:-1], cuts[1:]):
        for copy in copies[first:last]:
            copy.wait()
        deep = slice(first * width, last * width)

        @pl.loop(0, 2)
        def _(half):
            block = pl.ds(pl.multiple_of(half * rows, rows), rows)
            part = jnp.dot(
                scaled_ref[block, deep], basis[deep, :], preferred_element_type=jnp.float32
            )
            out_ref[block, :] = part if first == 0 else out_ref[block, :] + part

    window_copy.wait()


def window_kernel(scale, window_ref, scaled_ref, projected_ref, *refs):
    pieces = refs[:-3]
    send_ref, keep_ref, result = refs[-3:]
    chips, rows, _ = keep_ref.shape
    width = pieces[0].shape[0]
    total = projected_ref[...]
    first = scaled_ref.shape[1] - width * len(pieces)
    basis = jnp.concatenate([piece[...] for piece in pieces], axis=0)
    total += jnp.dot(scaled_ref[:, first:], basis, preferred_element_type=jnp.float32)
    result[...] = scale * jnp.dot(
        window_ref[...], total.astype(jnp.bfloat16), preferred_element_type=jnp.float32
    )
    core = lax.rem(lax.axis_index("blk"), 2)
    for k in range(chips):
        mine = pl.ds(pl.multiple_of((2 * k + core) * rows, rows), rows)
        keep_ref[k] = result[mine, :]
        other = pl.ds(pl.multiple_of((2 * k + 1 - core) * rows, rows), rows)
        send_ref[k] = result[other, :].astype(jnp.bfloat16)


def add_core_kernel(keys, keep_ref, got_ref, own_ref, *send_refs):
    chip = lax.axis_index("blk") // 2
    for key, ref in zip((0, *keys), (own_ref, *send_refs)):
        at = chip ^ key
        ref[...] = (keep_ref[at] + got_ref[at].astype(jnp.float32)).astype(ref.dtype)


def add_chips_kernel(own_ref, *refs):
    total = own_ref[...]
    for ref in refs[:-1]:
        total += ref[...].astype(jnp.float32)
    refs[-1][...] = total


VMEM = pl.BlockSpec(memory_space=pltpu.VMEM)
SMEM = pl.BlockSpec(memory_space=pltpu.SMEM)
ANY = pl.BlockSpec(memory_space=pl.ANY)
CHEAP = pl.CostEstimate(flops=1, bytes_accessed=1, transcendentals=0)


def after(first, *others):
    return lax.optimization_barrier((first, *others))


def ring_body(n, grad_out, activations, basis_out, basis_in, eigenvalues, tile_order, block_map):
    tok_rows, full_out = grad_out.shape
    tile_width = basis_out.shape[1]
    full_in, in_width = basis_in.shape
    tokens = n * tok_rows
    chips = n // 2
    to_right = lambda x: lax.ppermute(x, "blk", shift_pairs(n, 1))
    to_left = lambda x: lax.ppermute(x, "blk", shift_pairs(n, -1))
    steps = chips // 2

    own = basis_in[:WC].T

    pairs = chips // 2
    both = jnp.concatenate([grad_out, activations], axis=1)[None]
    got = [lax.ppermute(both, "blk", xor_pairs(n, 4 * key)) for key in range(1, pairs)]
    kept = pl.pallas_call(
        keep_kernel,
        out_shape=jax.ShapeDtypeStruct(basis_in.shape, jnp.bfloat16),
        in_specs=[VMEM],
        out_specs=VMEM,
        compiler_params=pltpu.CompilerParams(vmem_limit_bytes=8 * MIB),
        cost_estimate=CHEAP,
        name="keep",
    )(basis_in)
    both, own, kept, *got = after(both, own, kept, *got)
    depth, later = 1024, 7
    grads, acts = pl.pallas_call(
        part_kernel,
        out_shape=(
            jax.ShapeDtypeStruct((pairs, tok_rows, full_out), jnp.bfloat16),
            jax.ShapeDtypeStruct((pairs, tok_rows, full_in), jnp.bfloat16),
        ),
        in_specs=[VMEM] * pairs,
        out_specs=(VMEM, VMEM),
        compiler_params=pltpu.CompilerParams(vmem_limit_bytes=8 * MIB),
        name="part",
    )(both, *got)
    acts, grads, own = after(acts, grads, own)
    acts_got = lax.ppermute(acts, "blk", xor_pairs(n, 2))
    grads_got = lax.ppermute(grads, "blk", xor_pairs(n, 2))
    acts = jnp.concatenate([acts, acts_got], axis=0)
    rotated = pl.pallas_call(
        functools.partial(rotate_in_kernel, tok_rows),
        out_shape=jax.ShapeDtypeStruct((chips, tokens, in_width), jnp.bfloat16),
        in_specs=[VMEM, VMEM, VMEM],
        out_specs=VMEM,
        compiler_params=pltpu.CompilerParams(vmem_limit_bytes=8 * MIB),
        cost_estimate=CHEAP,
        name="rotate_in",
    )(acts, swap(acts, n), kept)

    grads_got, own, _ = after(grads_got, own, rotated)
    rotated = exchange(rotated, n, 2)
    right, left = [own, to_right(own)], [own, to_left(own)]
    grads = jnp.concatenate([grads, grads_got], axis=0)
    grads_far = swap(grads, n)
    far = [swap(own, n)]

    rotate = lambda kernel, count, scratch, shape, dtype, *operands: pl.pallas_call(
        kernel,
        out_shape=jax.ShapeDtypeStruct(shape, dtype),
        in_specs=[ANY if x is basis_out or x is block_map else VMEM for x in operands],
        out_specs=VMEM,
        scratch_shapes=[pltpu.VMEM((count, depth, tile_width), jnp.bfloat16)]
        + scratch
        + [pltpu.SemaphoreType.DMA((count + 1,))],
        compiler_params=pltpu.CompilerParams(vmem_limit_bytes=40 * MIB),
        cost_estimate=CHEAP,
        name=kernel.func.__name__[:-7],
    )(*operands)
    start = rotate(
        functools.partial(rotate_first_kernel),
        full_out // depth - later,
        [],
        (tokens, tile_width),
        jnp.float32,
        grads,
        grads_far,
        basis_out,
    )
    start, grads, right[-1], left[-1], rotated, *far = after(
        start, grads, right[-1], left[-1], rotated, *far
    )
    rotated_far = swap(rotated, n)
    far += [swap(right[-1], n), swap(left[-1], n)]
    right.append(to_right(right[-1]))
    left.append(to_left(left[-1]))
    aligned = rotate(
        functools.partial(rotate_last_kernel, tok_rows, full_out // depth - later),
        later,
        [
            pltpu.VMEM((tokens, tile_width), jnp.float32),
            pltpu.SMEM(block_map.shape, jnp.int32),
        ],
        (tile_width, tokens),
        jnp.bfloat16,
        grads,
        grads_far,
        basis_out,
        block_map,
        start,
    )

    aligned, right[-1], left[-1], rotated_far, *far = after(
        aligned, right[-1], left[-1], rotated_far, *far
    )
    far += [swap(right[-1], n), swap(left[-1], n)]
    right.append(to_right(right[-1]))
    left.append(to_left(left[-1]))
    begun = [0] + [at for step in range(1, steps) for at in (step, chips - step)] + [steps]
    blocks = 8
    scaled = pl.pallas_call(
        functools.partial(scale_kernel, begun),
        out_shape=jax.ShapeDtypeStruct((tile_width, full_in), jnp.bfloat16),
        in_specs=[VMEM] * 3 + [ANY] * 2,
        out_specs=VMEM,
        scratch_shapes=[
            pltpu.VMEM((blocks, tile_width // blocks, full_in), jnp.float32),
            pltpu.SMEM(tile_order.shape, jnp.int32),
            pltpu.SMEM(tile_order.shape, jnp.int32),
            pltpu.VMEM((n, tokens, in_width), jnp.bfloat16),
            pltpu.SemaphoreType.DMA((blocks + 1,)),
        ],
        compiler_params=pltpu.CompilerParams(vmem_limit_bytes=40 * MIB),
        cost_estimate=CHEAP,
        name="scale",
    )(aligned, rotated, rotated_far, tile_order, eigenvalues)

    scaled, right[-1], left[-1], *far = after(scaled, right[-1], left[-1], *far)
    cut = in_width // 2
    last = [to_right(right[-1][:cut]), to_left(left[-1][cut:])]
    near = [right[at] if at < steps else left[chips - at] for at in begun[:-1]]
    far += [swap(piece, n) for piece in near[len(far) :]]
    pieces = [piece for pair in zip(near, far) for piece in pair]
    projected, window = pl.pallas_call(
        functools.partial(project_kernel, (0, 6, len(pieces))),
        out_shape=(
            jax.ShapeDtypeStruct((tile_width, WC), jnp.float32),
            jax.ShapeDtypeStruct((WR, tile_width), jnp.bfloat16),
        ),
        in_specs=[VMEM] + [ANY] * (len(pieces) + 1),
        out_specs=(VMEM, VMEM),
        scratch_shapes=[
            pltpu.VMEM((len(pieces) * in_width, WC), jnp.bfloat16),
            pltpu.SemaphoreType.DMA((len(pieces) + 1,)),
        ],
        compiler_params=pltpu.CompilerParams(vmem_limit_bytes=24 * MIB),
        cost_estimate=CHEAP,
        name="project",
    )(scaled, basis_out, *pieces)

    projected, *last = after(projected, *last)
    last += [swap(piece, n) for piece in last]
    rows = WR // n
    send, keep = pl.pallas_call(
        functools.partial(window_kernel, 1.0 / tokens),
        out_shape=(
            jax.ShapeDtypeStruct((chips, rows, WC), jnp.bfloat16),
            jax.ShapeDtypeStruct((chips, rows, WC), jnp.float32),
        ),
        in_specs=[VMEM] * 7,
        out_specs=(VMEM, VMEM),
        scratch_shapes=[pltpu.VMEM((WR, WC), jnp.float32)],
        compiler_params=pltpu.CompilerParams(vmem_limit_bytes=24 * MIB),
        cost_estimate=CHEAP,
        name="window",
    )(window, scaled, projected, *last)

    keys = sorted(range(1, chips), key=lambda key: -(key & -2))
    small = pltpu.CompilerParams(vmem_limit_bytes=8 * MIB)
    own, *sends = pl.pallas_call(
        functools.partial(add_core_kernel, keys),
        out_shape=[jax.ShapeDtypeStruct((rows, WC), jnp.float32)]
        + [jax.ShapeDtypeStruct((rows, WC), jnp.bfloat16)] * len(keys),
        in_specs=[VMEM, VMEM],
        out_specs=[VMEM] * chips,
        compiler_params=small,
        name="add_core",
    )(keep, swap(send, n))
    arrived = [lax.ppermute(x, "blk", xor_pairs(n, 2 * key)) for key, x in zip(keys, sends)]
    return pl.pallas_call(
        add_chips_kernel,
        out_shape=jax.ShapeDtypeStruct((rows, WC), jnp.float32),
        in_specs=[VMEM] * chips,
        out_specs=VMEM,
        compiler_params=small,
        name="add_chips",
    )(own, *arrived)


def gather_body(grad_out, activations, basis_out, basis_in, eigenvalues, tile_order, block_map):
    n_blocks = lax.axis_size("blk")
    tile_width = basis_out.shape[1]
    tok_rows = grad_out.shape[0]
    full_in = eigenvalues.shape[1]
    tokens = n_blocks * tok_rows
    dot = functools.partial(jnp.dot, preferred_element_type=jnp.float32)
    in_rows = lax.all_gather(basis_in[:WC], "blk", axis=1, tiled=True)
    acts = lax.all_gather(activations, "blk", axis=0, tiled=True)
    in_tile = dot(acts, basis_in).astype(jnp.bfloat16)
    rotated_in = lax.all_gather(in_tile, "blk", axis=1, tiled=True)
    grads = lax.all_gather(grad_out, "blk", axis=0, tiled=True)
    rotated_out = dot(grads, basis_out).astype(jnp.bfloat16)
    aligned = jnp.take(
        rotated_out.reshape(n_blocks, tok_rows, tile_width), block_map, axis=0
    ).reshape(tokens, tile_width)
    grad_tile = dot(aligned.T, rotated_in) / tokens
    damped = jnp.take(
        eigenvalues.reshape(tile_width, full_in // LANES, LANES), tile_order, axis=1
    ).reshape(tile_width, full_in)
    scaled = (grad_tile / damped).astype(jnp.bfloat16)
    projected = dot(scaled, in_rows.T).astype(jnp.bfloat16)
    return lax.psum_scatter(
        dot(basis_out[:WR], projected), "blk", scatter_dimension=0, tiled=True
    )


def solution(mesh):
    n = mesh.shape["blk"]

    def body(*args):
        wide = args[3].shape[1] % LANES == 0 and args[2].shape[1] % LANES == 0
        doubles = n & (n - 1) == 0 and args[0].shape[0] & (args[0].shape[0] - 1) == 0
        if wide and doubles and WR % (16 * n) == 0:
            return ring_body(n, *args)
        return gather_body(*args)

    placed = (
        P(("grp", "blk"), None),
        P(("grp", "blk"), None),
        P(None, "blk"),
        P(None, "blk"),
        P("blk", None),
        P(),
        P(),
    )
    return jax.shard_map(
        body, mesh=mesh, in_specs=placed, out_specs=P(("grp", "blk"), None), check_vma=False
    )
```

```python
import functools

import jax
import jax.numpy as jnp
from jax import lax
from jax.experimental import pallas as pl
from jax.experimental.pallas import tpu as pltpu
from jax.sharding import PartitionSpec as P

WR = 768
WC = 512
LANES = 128
MIB = 1 << 20


def ring_of(n):
    chips = n // 2
    return [*range(0, chips, 2), *range(chips - 1, 0, -2)]


def shift_pairs(n, by):
    ring = ring_of(n)
    return [
        (2 * ring[p] + c, 2 * ring[(p + by) % len(ring)] + c)
        for p in range(len(ring))
        for c in range(2)
    ]


def ring_source(me, steps, other, chips):
    chip, core = me // 2, lax.rem(me, 2)
    place = jnp.where(lax.rem(chip, 2) == 0, chip // 2, chips - 1 - chip // 2)
    place = lax.rem(place + chips - steps, chips)
    chip = jnp.where(place < chips // 2, 2 * place, 2 * (chips - 1 - place) + 1)
    return 2 * chip + (core ^ other)


def xor_pairs(n, key):
    return [(b, b ^ key) for b in range(n)]


def exchange(x, n, stride):
    groups = [list(range(first, n, stride)) for first in range(stride)]
    return lax.all_to_all(x, "blk", 0, 0, axis_index_groups=groups, tiled=True)


def swap(x, n):
    return lax.ppermute(x, "blk", xor_pairs(n, 1))


def bits_of(size):
    return size.bit_length() - 1


def held_tokens(me, tokens, tok_rows):
    row = lax.broadcasted_iota(jnp.int32, (tokens, tokens), 1)
    pairs = tokens // tok_rows // 4
    place = row >> bits_of(tok_rows)
    chip = 2 * (place & (pairs - 1)) + ((place >> bits_of(pairs)) & 1)
    other = row >> bits_of(tokens // 2)
    device = me ^ (2 * chip + other)
    return (device << bits_of(tok_rows)) + (row & (tok_rows - 1))


def reorder(wanted, held, rotated):
    order = jnp.where(wanted == held, 1.0, 0.0).astype(jnp.bfloat16)
    return jnp.dot(order, rotated.astype(jnp.bfloat16), preferred_element_type=jnp.float32)


def part_kernel(*refs):
    grads_ref, acts_ref = refs[-2:]
    first = grads_ref.shape[2]
    for at, ref in enumerate(refs[:-2]):
        grads_ref[at] = ref[0, :, :first]
        acts_ref[at] = ref[0, :, first:]


def rotate_in_kernel(tok_rows, near_ref, far_ref, basis_ref, out_ref):
    tokens = out_ref.shape[1]
    depth = near_ref.shape[2]
    acts = jnp.concatenate([ref[...].reshape(-1, depth) for ref in (near_ref, far_ref)], axis=0)
    rotated = jnp.dot(acts, basis_ref[...], preferred_element_type=jnp.float32)
    wanted = lax.broadcasted_iota(jnp.int32, (tokens, tokens), 0)
    held = held_tokens(lax.axis_index("blk"), tokens, tok_rows)
    ordered = reorder(wanted, held, rotated).astype(jnp.bfloat16)
    for copy in range(out_ref.shape[0]):
        out_ref[copy] = ordered


def keep_kernel(basis_ref, kept_ref):
    kept_ref[...] = basis_ref[...]


def rotate_part(first, near_ref, far_ref, basis_ref, basis, total, sem):
    steps, depth = basis.shape[:2]

    def copy_of(step):
        rows = pl.ds(pl.multiple_of((first + step) * depth, depth), depth)
        return pltpu.make_async_copy(basis_ref.at[rows], basis.at[step], sem.at[step])

    @pl.loop(0, steps)
    def _(step):
        copy_of(step).start()

    @pl.loop(0, steps)
    def _(step):
        columns = pl.ds(pl.multiple_of((first + step) * depth, depth), depth)
        rows = [ref[:, :, columns].reshape(-1, depth) for ref in (near_ref, far_ref)]
        grads = jnp.concatenate(rows, axis=0)
        copy_of(step).wait()
        total[...] += jnp.dot(grads, basis[step], preferred_element_type=jnp.float32)


def rotate_first_kernel(near_ref, far_ref, basis_ref, out_ref, basis, sem):
    out_ref[...] = jnp.zeros_like(out_ref)
    rotate_part(0, near_ref, far_ref, basis_ref, basis, out_ref, sem)


def rotate_last_kernel(
    tok_rows,
    first,
    near_ref,
    far_ref,
    basis_ref,
    map_ref,
    start_ref,
    out_ref,
    basis,
    total,
    stored_map,
    sem,
):
    tokens = total.shape[0]
    map_copy = pltpu.make_async_copy(map_ref, stored_map, sem.at[basis.shape[0]])
    map_copy.start()
    total[...] = start_ref[...]
    rotate_part(first, near_ref, far_ref, basis_ref, basis, total, sem)
    map_copy.wait()
    row = lax.broadcasted_iota(jnp.int32, (tokens, tokens), 0)
    block = row >> bits_of(tok_rows)
    wanted = jnp.zeros_like(row)
    for stored in range(tokens // tok_rows):
        wanted = jnp.where(block == stored, stored_map[stored] * tok_rows, wanted)
    wanted += row & (tok_rows - 1)
    held = held_tokens(lax.axis_index("blk"), tokens, tok_rows)
    out_ref[...] = reorder(wanted, held, total[...]).T.astype(jnp.bfloat16)


def scale_kernel(
    begun,
    aligned_ref,
    near_ref,
    far_ref,
    tiles_ref,
    eigen_ref,
    out_ref,
    damped,
    tiles,
    lanes,
    rotated,
    sem,
):
    blocks, depth = damped.shape[:2]
    chips, _, width = near_ref.shape
    per_piece = width // LANES

    def copy_of(block):
        rows = pl.ds(pl.multiple_of(block * depth, depth), depth)
        return pltpu.make_async_copy(eigen_ref.at[rows], damped.at[block], sem.at[block])

    tiles_copy = pltpu.make_async_copy(tiles_ref, tiles, sem.at[blocks])
    tiles_copy.start()

    @pl.loop(0, blocks)
    def _(block):
        copy_of(block).start()

    tiles_copy.wait()
    me = lax.axis_index("blk")
    for at, steps in enumerate(begun):
        for other, rotated_ref in enumerate((near_ref, far_ref)):
            source = ring_source(me, steps, other, chips)
            piece = 2 * at + other
            rotated[piece] = rotated_ref[source // 2]
            for part in range(per_piece):
                lanes[piece * per_piece + part] = tiles[source * per_piece + part] * LANES

    @pl.loop(0, blocks)
    def _(block):
        rows = pl.ds(pl.multiple_of(block * depth, depth), depth)
        aligned = aligned_ref[rows, :]
        copy_of(block).wait()
        for piece in range(2 * chips):
            grad = jnp.dot(aligned, rotated[piece], preferred_element_type=jnp.float32)
            for part in range(per_piece):
                tile = piece * per_piece + part
                eigen = damped[block, :, pl.ds(pl.multiple_of(lanes[tile], LANES), LANES)]
                inverse = pl.reciprocal(eigen, approx=True)
                inverse = inverse * (2.0 - eigen * inverse)
                scaled = grad[:, part * LANES : (part + 1) * LANES] * inverse
                out_ref[rows, tile * LANES : (tile + 1) * LANES] = scaled.astype(jnp.bfloat16)


def project_kernel(cuts, scaled_ref, basis_out_ref, *refs):
    pieces = refs[:-4]
    out_ref, window_ref, basis, sem = refs[-4:]
    width = pieces[0].shape[0]
    copies = [
        pltpu.make_async_copy(piece, basis.at[pl.ds(at * width, width)], sem.at[at])
        for at, piece in enumerate(pieces)
    ]
    window_copy = pltpu.make_async_copy(
        basis_out_ref.at[pl.ds(0, window_ref.shape[0])], window_ref, sem.at[len(pieces)]
    )
    window_copy.start()
    for copy in copies:
        copy.start()
    for first, last in zip(cuts[:-1], cuts[1:]):
        for copy in copies[first:last]:
            copy.wait()
        deep = slice(first * width, last * width)
        part = jnp.dot(scaled_ref[:, deep], basis[deep, :], preferred_element_type=jnp.float32)
        out_ref[...] = part if first == 0 else out_ref[...] + part

    window_copy.wait()


def window_kernel(scale, window_ref, scaled_ref, projected_ref, *refs):
    pieces = refs[:-3]
    send_ref, keep_ref, result = refs[-3:]
    chips, rows, _ = keep_ref.shape
    width = pieces[0].shape[0]
    total = projected_ref[...]
    first = scaled_ref.shape[1] - width * len(pieces)
    basis = jnp.concatenate([piece[...] for piece in pieces], axis=0)
    total += jnp.dot(scaled_ref[:, first:], basis, preferred_element_type=jnp.float32)
    result[...] = scale * jnp.dot(
        window_ref[...], total.astype(jnp.bfloat16), preferred_element_type=jnp.float32
    )
    core = lax.rem(lax.axis_index("blk"), 2)
    for k in range(chips):
        mine = pl.ds(pl.multiple_of((2 * k + core) * rows, rows), rows)
        keep_ref[k] = result[mine, :]
        other = pl.ds(pl.multiple_of((2 * k + 1 - core) * rows, rows), rows)
        send_ref[k] = result[other, :].astype(jnp.bfloat16)


def add_core_kernel(keys, keep_ref, got_ref, own_ref, *send_refs):
    chip = lax.axis_index("blk") // 2
    for key, ref in zip((0, *keys), (own_ref, *send_refs)):
        at = chip ^ key
        ref[...] = (keep_ref[at] + got_ref[at].astype(jnp.float32)).astype(ref.dtype)


def add_chips_kernel(own_ref, *refs):
    total = own_ref[...]
    for ref in refs[:-1]:
        total += ref[...].astype(jnp.float32)
    refs[-1][...] = total


VMEM = pl.BlockSpec(memory_space=pltpu.VMEM)
SMEM = pl.BlockSpec(memory_space=pltpu.SMEM)
ANY = pl.BlockSpec(memory_space=pl.ANY)
CHEAP = pl.CostEstimate(flops=1, bytes_accessed=1, transcendentals=0)


def after(first, *others):
    return lax.optimization_barrier((first, *others))


def ring_body(n, grad_out, activations, basis_out, basis_in, eigenvalues, tile_order, block_map):
    tok_rows, full_out = grad_out.shape
    tile_width = basis_out.shape[1]
    full_in, in_width = basis_in.shape
    tokens = n * tok_rows
    chips = n // 2
    to_right = lambda x: lax.ppermute(x, "blk", shift_pairs(n, 1))
    to_left = lambda x: lax.ppermute(x, "blk", shift_pairs(n, -1))
    steps = chips // 2

    own = basis_in[:WC].T

    pairs = chips // 2
    both = jnp.concatenate([grad_out, activations], axis=1)[None]
    got = [lax.ppermute(both, "blk", xor_pairs(n, 4 * key)) for key in range(1, pairs)]
    kept = pl.pallas_call(
        keep_kernel,
        out_shape=jax.ShapeDtypeStruct(basis_in.shape, jnp.bfloat16),
        in_specs=[VMEM],
        out_specs=VMEM,
        compiler_params=pltpu.CompilerParams(vmem_limit_bytes=8 * MIB),
        cost_estimate=CHEAP,
        name="keep",
    )(basis_in)
    both, own, kept, *got = after(both, own, kept, *got)
    depth, later = 512, 14
    grads, acts = pl.pallas_call(
        part_kernel,
        out_shape=(
            jax.ShapeDtypeStruct((pairs, tok_rows, full_out), jnp.bfloat16),
            jax.ShapeDtypeStruct((pairs, tok_rows, full_in), jnp.bfloat16),
        ),
        in_specs=[VMEM] * pairs,
        out_specs=(VMEM, VMEM),
        compiler_params=pltpu.CompilerParams(vmem_limit_bytes=8 * MIB),
        name="part",
    )(both, *got)
    acts, grads, own = after(acts, grads, own)
    acts_got = lax.ppermute(acts, "blk", xor_pairs(n, 2))
    grads_got = lax.ppermute(grads, "blk", xor_pairs(n, 2))
    acts = jnp.concatenate([acts, acts_got], axis=0)
    rotated = pl.pallas_call(
        functools.partial(rotate_in_kernel, tok_rows),
        out_shape=jax.ShapeDtypeStruct((chips, tokens, in_width), jnp.bfloat16),
        in_specs=[VMEM, VMEM, VMEM],
        out_specs=VMEM,
        compiler_params=pltpu.CompilerParams(vmem_limit_bytes=8 * MIB),
        cost_estimate=CHEAP,
        name="rotate_in",
    )(acts, swap(acts, n), kept)

    grads_got, own, _ = after(grads_got, own, rotated)
    rotated = exchange(rotated, n, 2)
    right, left = [own, to_right(own)], [own, to_left(own)]
    grads = jnp.concatenate([grads, grads_got], axis=0)
    grads_far = swap(grads, n)
    far = [swap(own, n)]

    rotate = lambda kernel, count, scratch, shape, dtype, *operands: pl.pallas_call(
        kernel,
        out_shape=jax.ShapeDtypeStruct(shape, dtype),
        in_specs=[ANY if x is basis_out or x is block_map else VMEM for x in operands],
        out_specs=VMEM,
        scratch_shapes=[pltpu.VMEM((count, depth, tile_width), jnp.bfloat16)]
        + scratch
        + [pltpu.SemaphoreType.DMA((count + 1,))],
        compiler_params=pltpu.CompilerParams(vmem_limit_bytes=40 * MIB),
        cost_estimate=CHEAP,
        name=kernel.func.__name__[:-7],
    )(*operands)
    start = rotate(
        functools.partial(rotate_first_kernel),
        full_out // depth - later,
        [],
        (tokens, tile_width),
        jnp.float32,
        grads,
        grads_far,
        basis_out,
    )
    start, right[-1], left[-1], *far = after(start, right[-1], left[-1], *far)
    far += [swap(right[-1], n), swap(left[-1], n)]
    right.append(to_right(right[-1]))
    left.append(to_left(left[-1]))
    start, grads, rotated = after(start, grads, rotated)
    rotated_far = swap(rotated, n)
    aligned = rotate(
        functools.partial(rotate_last_kernel, tok_rows, full_out // depth - later),
        later,
        [
            pltpu.VMEM((tokens, tile_width), jnp.float32),
            pltpu.SMEM(block_map.shape, jnp.int32),
        ],
        (tile_width, tokens),
        jnp.bfloat16,
        grads,
        grads_far,
        basis_out,
        block_map,
        start,
    )

    aligned, right[-1], left[-1], rotated_far, *far = after(
        aligned, right[-1], left[-1], rotated_far, *far
    )
    far += [swap(right[-1], n), swap(left[-1], n)]
    right.append(to_right(right[-1]))
    left.append(to_left(left[-1]))
    begun = [0] + [at for step in range(1, steps) for at in (step, chips - step)] + [steps]
    blocks = 14
    scaled = pl.pallas_call(
        functools.partial(scale_kernel, begun),
        out_shape=jax.ShapeDtypeStruct((tile_width, full_in), jnp.bfloat16),
        in_specs=[VMEM] * 3 + [ANY] * 2,
        out_specs=VMEM,
        scratch_shapes=[
            pltpu.VMEM((blocks, tile_width // blocks, full_in), jnp.float32),
            pltpu.SMEM(tile_order.shape, jnp.int32),
            pltpu.SMEM(tile_order.shape, jnp.int32),
            pltpu.VMEM((n, tokens, in_width), jnp.bfloat16),
            pltpu.SemaphoreType.DMA((blocks + 1,)),
        ],
        compiler_params=pltpu.CompilerParams(vmem_limit_bytes=40 * MIB),
        cost_estimate=CHEAP,
        name="scale",
    )(aligned, rotated, rotated_far, tile_order, eigenvalues)

    scaled, right[-1], left[-1], *far = after(scaled, right[-1], left[-1], *far)
    cut = in_width // 2
    last = [to_right(right[-1][:cut]), to_left(left[-1][cut:])]
    near = [right[at] if at < steps else left[chips - at] for at in begun[:-1]]
    far += [swap(piece, n) for piece in near[len(far) :]]
    pieces = [piece for pair in zip(near, far) for piece in pair]
    projected, window = pl.pallas_call(
        functools.partial(project_kernel, (0, 6, len(pieces))),
        out_shape=(
            jax.ShapeDtypeStruct((tile_width, WC), jnp.float32),
            jax.ShapeDtypeStruct((WR, tile_width), jnp.bfloat16),
        ),
        in_specs=[VMEM] + [ANY] * (len(pieces) + 1),
        out_specs=(VMEM, VMEM),
        scratch_shapes=[
            pltpu.VMEM((len(pieces) * in_width, WC), jnp.bfloat16),
            pltpu.SemaphoreType.DMA((len(pieces) + 1,)),
        ],
        compiler_params=pltpu.CompilerParams(vmem_limit_bytes=24 * MIB),
        cost_estimate=CHEAP,
        name="project",
    )(scaled, basis_out, *pieces)

    projected, *last = after(projected, *last)
    last += [swap(piece, n) for piece in last]
    rows = WR // n
    send, keep = pl.pallas_call(
        functools.partial(window_kernel, 1.0 / tokens),
        out_shape=(
            jax.ShapeDtypeStruct((chips, rows, WC), jnp.bfloat16),
            jax.ShapeDtypeStruct((chips, rows, WC), jnp.float32),
        ),
        in_specs=[VMEM] * 7,
        out_specs=(VMEM, VMEM),
        scratch_shapes=[pltpu.VMEM((WR, WC), jnp.float32)],
        compiler_params=pltpu.CompilerParams(vmem_limit_bytes=24 * MIB),
        cost_estimate=CHEAP,
        name="window",
    )(window, scaled, projected, *last)

    keys = sorted(range(1, chips), key=lambda key: -(key & -2))
    small = pltpu.CompilerParams(vmem_limit_bytes=8 * MIB)
    own, *sends = pl.pallas_call(
        functools.partial(add_core_kernel, keys),
        out_shape=[jax.ShapeDtypeStruct((rows, WC), jnp.float32)]
        + [jax.ShapeDtypeStruct((rows, WC), jnp.bfloat16)] * len(keys),
        in_specs=[VMEM, VMEM],
        out_specs=[VMEM] * chips,
        compiler_params=small,
        name="add_core",
    )(keep, swap(send, n))
    arrived = [lax.ppermute(x, "blk", xor_pairs(n, 2 * key)) for key, x in zip(keys, sends)]
    return pl.pallas_call(
        add_chips_kernel,
        out_shape=jax.ShapeDtypeStruct((rows, WC), jnp.float32),
        in_specs=[VMEM] * chips,
        out_specs=VMEM,
        compiler_params=small,
        name="add_chips",
    )(own, *arrived)


def gather_body(grad_out, activations, basis_out, basis_in, eigenvalues, tile_order, block_map):
    n_blocks = lax.axis_size("blk")
    tile_width = basis_out.shape[1]
    tok_rows = grad_out.shape[0]
    full_in = eigenvalues.shape[1]
    tokens = n_blocks * tok_rows
    dot = functools.partial(jnp.dot, preferred_element_type=jnp.float32)
    in_rows = lax.all_gather(basis_in[:WC], "blk", axis=1, tiled=True)
    acts = lax.all_gather(activations, "blk", axis=0, tiled=True)
    in_tile = dot(acts, basis_in).astype(jnp.bfloat16)
    rotated_in = lax.all_gather(in_tile, "blk", axis=1, tiled=True)
    grads = lax.all_gather(grad_out, "blk", axis=0, tiled=True)
    rotated_out = dot(grads, basis_out).astype(jnp.bfloat16)
    aligned = jnp.take(
        rotated_out.reshape(n_blocks, tok_rows, tile_width), block_map, axis=0
    ).reshape(tokens, tile_width)
    grad_tile = dot(aligned.T, rotated_in) / tokens
    damped = jnp.take(
        eigenvalues.reshape(tile_width, full_in // LANES, LANES), tile_order, axis=1
    ).reshape(tile_width, full_in)
    scaled = (grad_tile / damped).astype(jnp.bfloat16)
    projected = dot(scaled, in_rows.T).astype(jnp.bfloat16)
    return lax.psum_scatter(
        dot(basis_out[:WR], projected), "blk", scatter_dimension=0, tiled=True
    )


def solution(mesh):
    n = mesh.shape["blk"]

    def body(*args):
        wide = args[3].shape[1] % LANES == 0 and args[2].shape[1] % LANES == 0
        doubles = n & (n - 1) == 0 and args[0].shape[0] & (args[0].shape[0] - 1) == 0
        if wide and doubles and WR % (16 * n) == 0:
            return ring_body(n, *args)
        return gather_body(*args)

    placed = (
        P(("grp", "blk"), None),
        P(("grp", "blk"), None),
        P(None, "blk"),
        P(None, "blk"),
        P("blk", None),
        P(),
        P(),
    )
    return jax.shard_map(
        body, mesh=mesh, in_specs=placed, out_specs=P(("grp", "blk"), None), check_vma=False
    )
```

```python
import functools

import jax
import jax.numpy as jnp
from jax import lax
from jax.experimental import pallas as pl
from jax.experimental.pallas import tpu as pltpu
from jax.sharding import PartitionSpec as P

WR = 768
WC = 512
LANES = 128
MIB = 1 << 20


def ring_of(n):
    chips = n // 2
    return [*range(0, chips, 2), *range(chips - 1, 0, -2)]


def shift_pairs(n, by):
    ring = ring_of(n)
    return [
        (2 * ring[p] + c, 2 * ring[(p + by) % len(ring)] + c)
        for p in range(len(ring))
        for c in range(2)
    ]


def ring_source(me, steps, other, chips):
    chip, core = me // 2, lax.rem(me, 2)
    place = jnp.where(lax.rem(chip, 2) == 0, chip // 2, chips - 1 - chip // 2)
    place = lax.rem(place + chips - steps, chips)
    chip = jnp.where(place < chips // 2, 2 * place, 2 * (chips - 1 - place) + 1)
    return 2 * chip + (core ^ other)


def xor_pairs(n, key):
    return [(b, b ^ key) for b in range(n)]


def exchange(x, n, stride):
    groups = [list(range(first, n, stride)) for first in range(stride)]
    return lax.all_to_all(x, "blk", 0, 0, axis_index_groups=groups, tiled=True)


def swap(x, n):
    return lax.ppermute(x, "blk", xor_pairs(n, 1))


def bits_of(size):
    return size.bit_length() - 1


def held_tokens(me, tokens, tok_rows):
    row = lax.broadcasted_iota(jnp.int32, (tokens, tokens), 1)
    pairs = tokens // tok_rows // 4
    place = row >> bits_of(tok_rows)
    chip = 2 * (place & (pairs - 1)) + ((place >> bits_of(pairs)) & 1)
    other = row >> bits_of(tokens // 2)
    device = me ^ (2 * chip + other)
    return (device << bits_of(tok_rows)) + (row & (tok_rows - 1))


def reorder(wanted, held, rotated):
    order = jnp.where(wanted == held, 1.0, 0.0).astype(jnp.bfloat16)
    return jnp.dot(order, rotated.astype(jnp.bfloat16), preferred_element_type=jnp.float32)


def part_kernel(*refs):
    grads_ref, acts_ref = refs[-2:]
    first = grads_ref.shape[2]
    for at, ref in enumerate(refs[:-2]):
        grads_ref[at] = ref[0, :, :first]
        acts_ref[at] = ref[0, :, first:]


def rotate_in_kernel(tok_rows, near_ref, far_ref, basis_ref, out_ref):
    tokens = out_ref.shape[1]
    depth = near_ref.shape[2]
    acts = jnp.concatenate([ref[...].reshape(-1, depth) for ref in (near_ref, far_ref)], axis=0)
    rotated = jnp.dot(acts, basis_ref[...], preferred_element_type=jnp.float32)
    wanted = lax.broadcasted_iota(jnp.int32, (tokens, tokens), 0)
    held = held_tokens(lax.axis_index("blk"), tokens, tok_rows)
    ordered = reorder(wanted, held, rotated).astype(jnp.bfloat16)
    for copy in range(out_ref.shape[0]):
        out_ref[copy] = ordered


def keep_kernel(basis_ref, kept_ref):
    kept_ref[...] = basis_ref[...]


def rotate_part(first, near_ref, far_ref, basis_ref, basis, total, sem):
    steps, depth = basis.shape[:2]

    def copy_of(step):
        rows = pl.ds(pl.multiple_of((first + step) * depth, depth), depth)
        return pltpu.make_async_copy(basis_ref.at[rows], basis.at[step], sem.at[step])

    @pl.loop(0, steps)
    def _(step):
        copy_of(step).start()

    @pl.loop(0, steps)
    def _(step):
        columns = pl.ds(pl.multiple_of((first + step) * depth, depth), depth)
        rows = [ref[:, :, columns].reshape(-1, depth) for ref in (near_ref, far_ref)]
        grads = jnp.concatenate(rows, axis=0)
        copy_of(step).wait()
        total[...] += jnp.dot(grads, basis[step], preferred_element_type=jnp.float32)


def rotate_first_kernel(near_ref, far_ref, basis_ref, out_ref, basis, sem):
    out_ref[...] = jnp.zeros_like(out_ref)
    rotate_part(0, near_ref, far_ref, basis_ref, basis, out_ref, sem)


def rotate_last_kernel(
    tok_rows,
    first,
    near_ref,
    far_ref,
    basis_ref,
    map_ref,
    start_ref,
    out_ref,
    basis,
    total,
    stored_map,
    sem,
):
    tokens = total.shape[0]
    map_copy = pltpu.make_async_copy(map_ref, stored_map, sem.at[basis.shape[0]])
    map_copy.start()
    total[...] = start_ref[...]
    rotate_part(first, near_ref, far_ref, basis_ref, basis, total, sem)
    map_copy.wait()
    row = lax.broadcasted_iota(jnp.int32, (tokens, tokens), 0)
    block = row >> bits_of(tok_rows)
    wanted = jnp.zeros_like(row)
    for stored in range(tokens // tok_rows):
        wanted = jnp.where(block == stored, stored_map[stored] * tok_rows, wanted)
    wanted += row & (tok_rows - 1)
    held = held_tokens(lax.axis_index("blk"), tokens, tok_rows)
    out_ref[...] = reorder(wanted, held, total[...]).T.astype(jnp.bfloat16)


def scale_kernel(
    begun,
    aligned_ref,
    near_ref,
    far_ref,
    tiles_ref,
    eigen_ref,
    out_ref,
    damped,
    tiles,
    lanes,
    rotated,
    sem,
):
    blocks, depth = damped.shape[:2]
    chips, _, width = near_ref.shape
    per_piece = width // LANES

    def copy_of(block):
        rows = pl.ds(pl.multiple_of(block * depth, depth), depth)
        return pltpu.make_async_copy(eigen_ref.at[rows], damped.at[block], sem.at[block])

    tiles_copy = pltpu.make_async_copy(tiles_ref, tiles, sem.at[blocks])
    tiles_copy.start()

    @pl.loop(0, blocks)
    def _(block):
        copy_of(block).start()

    tiles_copy.wait()
    me = lax.axis_index("blk")
    for at, steps in enumerate(begun):
        for other, rotated_ref in enumerate((near_ref, far_ref)):
            source = ring_source(me, steps, other, chips)
            piece = 2 * at + other
            rotated[piece] = rotated_ref[source // 2]
            for part in range(per_piece):
                lanes[piece * per_piece + part] = tiles[source * per_piece + part] * LANES

    @pl.loop(0, blocks)
    def _(block):
        rows = pl.ds(pl.multiple_of(block * depth, depth), depth)
        aligned = aligned_ref[rows, :]
        copy_of(block).wait()
        for piece in range(2 * chips):
            grad = jnp.dot(aligned, rotated[piece], preferred_element_type=jnp.float32)
            for part in range(per_piece):
                tile = piece * per_piece + part
                eigen = damped[block, :, pl.ds(pl.multiple_of(lanes[tile], LANES), LANES)]
                inverse = pl.reciprocal(eigen, approx=True)
                inverse = inverse * (2.0 - eigen * inverse)
                scaled = grad[:, part * LANES : (part + 1) * LANES] * inverse
                out_ref[rows, tile * LANES : (tile + 1) * LANES] = scaled.astype(jnp.bfloat16)


def project_kernel(cuts, scaled_ref, basis_out_ref, *refs):
    pieces = refs[:-4]
    out_ref, window_ref, basis, sem = refs[-4:]
    width = pieces[0].shape[0]
    copies = [
        pltpu.make_async_copy(piece, basis.at[pl.ds(at * width, width)], sem.at[at])
        for at, piece in enumerate(pieces)
    ]
    window_copy = pltpu.make_async_copy(
        basis_out_ref.at[pl.ds(0, window_ref.shape[0])], window_ref, sem.at[len(pieces)]
    )
    window_copy.start()
    for copy in copies:
        copy.start()
    for first, last in zip(cuts[:-1], cuts[1:]):
        for copy in copies[first:last]:
            copy.wait()
        deep = slice(first * width, last * width)
        part = jnp.dot(scaled_ref[:, deep], basis[deep, :], preferred_element_type=jnp.float32)
        out_ref[...] = part if first == 0 else out_ref[...] + part

    window_copy.wait()


def window_kernel(scale, window_ref, scaled_ref, projected_ref, *refs):
    pieces = refs[:-3]
    send_ref, keep_ref, result = refs[-3:]
    chips, rows, _ = keep_ref.shape
    width = pieces[0].shape[0]
    total = projected_ref[...]
    first = scaled_ref.shape[1] - width * len(pieces)
    basis = jnp.concatenate([piece[...] for piece in pieces], axis=0)
    total += jnp.dot(scaled_ref[:, first:], basis, preferred_element_type=jnp.float32)
    result[...] = scale * jnp.dot(
        window_ref[...], total.astype(jnp.bfloat16), preferred_element_type=jnp.float32
    )
    core = lax.rem(lax.axis_index("blk"), 2)
    for k in range(chips):
        mine = pl.ds(pl.multiple_of((2 * k + core) * rows, rows), rows)
        keep_ref[k] = result[mine, :]
        other = pl.ds(pl.multiple_of((2 * k + 1 - core) * rows, rows), rows)
        send_ref[k] = result[other, :].astype(jnp.bfloat16)


def add_core_kernel(keys, keep_ref, got_ref, own_ref, *send_refs):
    chip = lax.axis_index("blk") // 2
    for key, ref in zip((0, *keys), (own_ref, *send_refs)):
        at = chip ^ key
        ref[...] = (keep_ref[at] + got_ref[at].astype(jnp.float32)).astype(ref.dtype)


def add_chips_kernel(own_ref, *refs):
    total = own_ref[...]
    for ref in refs[:-1]:
        total += ref[...].astype(jnp.float32)
    refs[-1][...] = total


VMEM = pl.BlockSpec(memory_space=pltpu.VMEM)
SMEM = pl.BlockSpec(memory_space=pltpu.SMEM)
ANY = pl.BlockSpec(memory_space=pl.ANY)
CHEAP = pl.CostEstimate(flops=1, bytes_accessed=1, transcendentals=0)


def after(first, *others):
    return lax.optimization_barrier((first, *others))


def ring_body(n, grad_out, activations, basis_out, basis_in, eigenvalues, tile_order, block_map):
    tok_rows, full_out = grad_out.shape
    tile_width = basis_out.shape[1]
    full_in, in_width = basis_in.shape
    tokens = n * tok_rows
    chips = n // 2
    to_right = lambda x: lax.ppermute(x, "blk", shift_pairs(n, 1))
    to_left = lambda x: lax.ppermute(x, "blk", shift_pairs(n, -1))
    steps = chips // 2

    own = basis_in[:WC].T

    pairs = chips // 2
    both = jnp.concatenate([grad_out, activations], axis=1)[None]
    got = [lax.ppermute(both, "blk", xor_pairs(n, 4 * key)) for key in range(1, pairs)]
    kept = pl.pallas_call(
        keep_kernel,
        out_shape=jax.ShapeDtypeStruct(basis_in.shape, jnp.bfloat16),
        in_specs=[VMEM],
        out_specs=VMEM,
        compiler_params=pltpu.CompilerParams(vmem_limit_bytes=8 * MIB),
        cost_estimate=CHEAP,
        name="keep",
    )(basis_in)
    both, own, kept, *got = after(both, own, kept, *got)
    depth, later = 1024, 9
    grads, acts = pl.pallas_call(
        part_kernel,
        out_shape=(
            jax.ShapeDtypeStruct((pairs, tok_rows, full_out), jnp.bfloat16),
            jax.ShapeDtypeStruct((pairs, tok_rows, full_in), jnp.bfloat16),
        ),
        in_specs=[VMEM] * pairs,
        out_specs=(VMEM, VMEM),
        compiler_params=pltpu.CompilerParams(vmem_limit_bytes=8 * MIB),
        name="part",
    )(both, *got)
    acts, grads, own = after(acts, grads, own)
    acts_got = lax.ppermute(acts, "blk", xor_pairs(n, 2))
    grads_got = lax.ppermute(grads, "blk", xor_pairs(n, 2))
    acts = jnp.concatenate([acts, acts_got], axis=0)
    rotated = pl.pallas_call(
        functools.partial(rotate_in_kernel, tok_rows),
        out_shape=jax.ShapeDtypeStruct((chips, tokens, in_width), jnp.bfloat16),
        in_specs=[VMEM, VMEM, VMEM],
        out_specs=VMEM,
        compiler_params=pltpu.CompilerParams(vmem_limit_bytes=8 * MIB),
        cost_estimate=CHEAP,
        name="rotate_in",
    )(acts, swap(acts, n), kept)

    grads_got, own, _ = after(grads_got, own, rotated)
    rotated = exchange(rotated, n, 2)
    right, left = [own, to_right(own)], [own, to_left(own)]
    grads = jnp.concatenate([grads, grads_got], axis=0)
    grads_far = swap(grads, n)
    far = [swap(own, n)]

    rotate = lambda kernel, count, scratch, shape, dtype, *operands: pl.pallas_call(
        kernel,
        out_shape=jax.ShapeDtypeStruct(shape, dtype),
        in_specs=[ANY if x is basis_out or x is block_map else VMEM for x in operands],
        out_specs=VMEM,
        scratch_shapes=[pltpu.VMEM((count, depth, tile_width), jnp.bfloat16)]
        + scratch
        + [pltpu.SemaphoreType.DMA((count + 1,))],
        compiler_params=pltpu.CompilerParams(vmem_limit_bytes=40 * MIB),
        cost_estimate=CHEAP,
        name=kernel.func.__name__[:-7],
    )(*operands)
    start = rotate(
        functools.partial(rotate_first_kernel),
        full_out // depth - later,
        [],
        (tokens, tile_width),
        jnp.float32,
        grads,
        grads_far,
        basis_out,
    )
    start, right[-1], left[-1], *far = after(start, right[-1], left[-1], *far)
    far += [swap(right[-1], n), swap(left[-1], n)]
    right.append(to_right(right[-1]))
    left.append(to_left(left[-1]))
    start, grads, rotated = after(start, grads, rotated)
    rotated_far = swap(rotated, n)
    aligned = rotate(
        functools.partial(rotate_last_kernel, tok_rows, full_out // depth - later),
        later,
        [
            pltpu.VMEM((tokens, tile_width), jnp.float32),
            pltpu.SMEM(block_map.shape, jnp.int32),
        ],
        (tile_width, tokens),
        jnp.bfloat16,
        grads,
        grads_far,
        basis_out,
        block_map,
        start,
    )

    aligned, right[-1], left[-1], rotated_far, *far = after(
        aligned, right[-1], left[-1], rotated_far, *far
    )
    far += [swap(right[-1], n), swap(left[-1], n)]
    right.append(to_right(right[-1]))
    left.append(to_left(left[-1]))
    begun = [0] + [at for step in range(1, steps) for at in (step, chips - step)] + [steps]
    blocks = 8
    scaled = pl.pallas_call(
        functools.partial(scale_kernel, begun),
        out_shape=jax.ShapeDtypeStruct((tile_width, full_in), jnp.bfloat16),
        in_specs=[VMEM] * 3 + [ANY] * 2,
        out_specs=VMEM,
        scratch_shapes=[
            pltpu.VMEM((blocks, tile_width // blocks, full_in), jnp.float32),
            pltpu.SMEM(tile_order.shape, jnp.int32),
            pltpu.SMEM(tile_order.shape, jnp.int32),
            pltpu.VMEM((n, tokens, in_width), jnp.bfloat16),
            pltpu.SemaphoreType.DMA((blocks + 1,)),
        ],
        compiler_params=pltpu.CompilerParams(vmem_limit_bytes=40 * MIB),
        cost_estimate=CHEAP,
        name="scale",
    )(aligned, rotated, rotated_far, tile_order, eigenvalues)

    scaled, right[-1], left[-1], *far = after(scaled, right[-1], left[-1], *far)
    cut = in_width // 2
    last = [to_right(right[-1][:cut]), to_left(left[-1][cut:])]
    near = [right[at] if at < steps else left[chips - at] for at in begun[:-1]]
    far += [swap(piece, n) for piece in near[len(far) :]]
    pieces = [piece for pair in zip(near, far) for piece in pair]
    projected, window = pl.pallas_call(
        functools.partial(project_kernel, (0, 6, len(pieces))),
        out_shape=(
            jax.ShapeDtypeStruct((tile_width, WC), jnp.float32),
            jax.ShapeDtypeStruct((WR, tile_width), jnp.bfloat16),
        ),
        in_specs=[VMEM] + [ANY] * (len(pieces) + 1),
        out_specs=(VMEM, VMEM),
        scratch_shapes=[
            pltpu.VMEM((len(pieces) * in_width, WC), jnp.bfloat16),
            pltpu.SemaphoreType.DMA((len(pieces) + 1,)),
        ],
        compiler_params=pltpu.CompilerParams(vmem_limit_bytes=24 * MIB),
        cost_estimate=CHEAP,
        name="project",
    )(scaled, basis_out, *pieces)

    projected, *last = after(projected, *last)
    last += [swap(piece, n) for piece in last]
    rows = WR // n
    send, keep = pl.pallas_call(
        functools.partial(window_kernel, 1.0 / tokens),
        out_shape=(
            jax.ShapeDtypeStruct((chips, rows, WC), jnp.bfloat16),
            jax.ShapeDtypeStruct((chips, rows, WC), jnp.float32),
        ),
        in_specs=[VMEM] * 7,
        out_specs=(VMEM, VMEM),
        scratch_shapes=[pltpu.VMEM((WR, WC), jnp.float32)],
        compiler_params=pltpu.CompilerParams(vmem_limit_bytes=24 * MIB),
        cost_estimate=CHEAP,
        name="window",
    )(window, scaled, projected, *last)

    keys = [*range(chips - 2, 0, -2), *range(chips - 1, 0, -2)]
    small = pltpu.CompilerParams(vmem_limit_bytes=8 * MIB)
    own, *sends = pl.pallas_call(
        functools.partial(add_core_kernel, keys),
        out_shape=[jax.ShapeDtypeStruct((rows, WC), jnp.float32)]
        + [jax.ShapeDtypeStruct((rows, WC), jnp.bfloat16)] * len(keys),
        in_specs=[VMEM, VMEM],
        out_specs=[VMEM] * chips,
        compiler_params=small,
        name="add_core",
    )(keep, swap(send, n))
    arrived = [lax.ppermute(x, "blk", xor_pairs(n, 2 * key)) for key, x in zip(keys, sends)]
    return pl.pallas_call(
        add_chips_kernel,
        out_shape=jax.ShapeDtypeStruct((rows, WC), jnp.float32),
        in_specs=[VMEM] * chips,
        out_specs=VMEM,
        compiler_params=small,
        name="add_chips",
    )(own, *arrived)


def gather_body(grad_out, activations, basis_out, basis_in, eigenvalues, tile_order, block_map):
    n_blocks = lax.axis_size("blk")
    tile_width = basis_out.shape[1]
    tok_rows = grad_out.shape[0]
    full_in = eigenvalues.shape[1]
    tokens = n_blocks * tok_rows
    dot = functools.partial(jnp.dot, preferred_element_type=jnp.float32)
    in_rows = lax.all_gather(basis_in[:WC], "blk", axis=1, tiled=True)
    acts = lax.all_gather(activations, "blk", axis=0, tiled=True)
    in_tile = dot(acts, basis_in).astype(jnp.bfloat16)
    rotated_in = lax.all_gather(in_tile, "blk", axis=1, tiled=True)
    grads = lax.all_gather(grad_out, "blk", axis=0, tiled=True)
    rotated_out = dot(grads, basis_out).astype(jnp.bfloat16)
    aligned = jnp.take(
        rotated_out.reshape(n_blocks, tok_rows, tile_width), block_map, axis=0
    ).reshape(tokens, tile_width)
    grad_tile = dot(aligned.T, rotated_in) / tokens
    damped = jnp.take(
        eigenvalues.reshape(tile_width, full_in // LANES, LANES), tile_order, axis=1
    ).reshape(tile_width, full_in)
    scaled = (grad_tile / damped).astype(jnp.bfloat16)
    projected = dot(scaled, in_rows.T).astype(jnp.bfloat16)
    return lax.psum_scatter(
        dot(basis_out[:WR], projected), "blk", scatter_dimension=0, tiled=True
    )


def solution(mesh):
    n = mesh.shape["blk"]

    def body(*args):
        wide = args[3].shape[1] % LANES == 0 and args[2].shape[1] % LANES == 0
        doubles = n & (n - 1) == 0 and args[0].shape[0] & (args[0].shape[0] - 1) == 0
        if wide and doubles and WR % (16 * n) == 0:
            return ring_body(n, *args)
        return gather_body(*args)

    placed = (
        P(("grp", "blk"), None),
        P(("grp", "blk"), None),
        P(None, "blk"),
        P(None, "blk"),
        P("blk", None),
        P(),
        P(),
    )
    return jax.shard_map(
        body, mesh=mesh, in_specs=placed, out_specs=P(("grp", "blk"), None), check_vma=False
    )
```

```python
import functools

import jax
import jax.numpy as jnp
from jax import lax
from jax.experimental import pallas as pl
from jax.experimental.pallas import tpu as pltpu
from jax.sharding import PartitionSpec as P

WR = 768
WC = 512
LANES = 128
MIB = 1 << 20


def ring_of(n):
    chips = n // 2
    return [*range(0, chips, 2), *range(chips - 1, 0, -2)]


def shift_pairs(n, by):
    ring = ring_of(n)
    return [
        (2 * ring[p] + c, 2 * ring[(p + by) % len(ring)] + c)
        for p in range(len(ring))
        for c in range(2)
    ]


def ring_source(me, steps, other, chips):
    chip, core = me // 2, lax.rem(me, 2)
    place = jnp.where(lax.rem(chip, 2) == 0, chip // 2, chips - 1 - chip // 2)
    place = lax.rem(place + chips - steps, chips)
    chip = jnp.where(place < chips // 2, 2 * place, 2 * (chips - 1 - place) + 1)
    return 2 * chip + (core ^ other)


def xor_pairs(n, key):
    return [(b, b ^ key) for b in range(n)]


def exchange(x, n, stride):
    groups = [list(range(first, n, stride)) for first in range(stride)]
    return lax.all_to_all(x, "blk", 0, 0, axis_index_groups=groups, tiled=True)


def swap(x, n):
    return lax.ppermute(x, "blk", xor_pairs(n, 1))


def swap_both(first, last, n):
    both = pl.pallas_call(
        lay_kernel,
        out_shape=jax.ShapeDtypeStruct((2, *first.shape), first.dtype),
        in_specs=[VMEM, VMEM],
        out_specs=VMEM,
        compiler_params=pltpu.CompilerParams(vmem_limit_bytes=8 * MIB),
        cost_estimate=CHEAP,
        name="lay",
    )(first, last)
    return swap(both, n)


def bits_of(size):
    return size.bit_length() - 1


def held_tokens(me, tokens, tok_rows):
    row = lax.broadcasted_iota(jnp.int32, (tokens, tokens), 1)
    pairs = tokens // tok_rows // 4
    place = row >> bits_of(tok_rows)
    chip = 2 * (place & (pairs - 1)) + ((place >> bits_of(pairs)) & 1)
    other = row >> bits_of(tokens // 2)
    device = me ^ (2 * chip + other)
    return (device << bits_of(tok_rows)) + (row & (tok_rows - 1))


def reorder(wanted, held, rotated):
    order = jnp.where(wanted == held, 1.0, 0.0).astype(jnp.bfloat16)
    return jnp.dot(order, rotated.astype(jnp.bfloat16), preferred_element_type=jnp.float32)


def lay_kernel(first_ref, last_ref, out_ref):
    out_ref[0] = first_ref[...]
    out_ref[1] = last_ref[...]


def part_kernel(*refs):
    grads_ref, acts_ref = refs[-2:]
    first = grads_ref.shape[2]
    for at, ref in enumerate(refs[:-2]):
        grads_ref[at] = ref[0, :, :first]
        acts_ref[at] = ref[0, :, first:]


def rotate_in_kernel(tok_rows, near_ref, far_ref, basis_ref, out_ref):
    tokens = out_ref.shape[1]
    depth = near_ref.shape[2]
    acts = jnp.concatenate([ref[...].reshape(-1, depth) for ref in (near_ref, far_ref)], axis=0)
    rotated = jnp.dot(acts, basis_ref[...], preferred_element_type=jnp.float32)
    wanted = lax.broadcasted_iota(jnp.int32, (tokens, tokens), 0)
    held = held_tokens(lax.axis_index("blk"), tokens, tok_rows)
    ordered = reorder(wanted, held, rotated).astype(jnp.bfloat16)
    for copy in range(out_ref.shape[0]):
        out_ref[copy] = ordered


def keep_kernel(basis_ref, kept_ref):
    kept_ref[...] = basis_ref[...]


def rotate_part(first, near_ref, far_ref, basis_ref, basis, total, sem):
    steps, depth = basis.shape[:2]

    def copy_of(step):
        rows = pl.ds(pl.multiple_of((first + step) * depth, depth), depth)
        return pltpu.make_async_copy(basis_ref.at[rows], basis.at[step], sem.at[step])

    @pl.loop(0, steps)
    def _(step):
        copy_of(step).start()

    @pl.loop(0, steps)
    def _(step):
        columns = pl.ds(pl.multiple_of((first + step) * depth, depth), depth)
        rows = [ref[:, :, columns].reshape(-1, depth) for ref in (near_ref, far_ref)]
        grads = jnp.concatenate(rows, axis=0)
        copy_of(step).wait()
        total[...] += jnp.dot(grads, basis[step], preferred_element_type=jnp.float32)


def rotate_first_kernel(near_ref, far_ref, basis_ref, out_ref, basis, sem):
    out_ref[...] = jnp.zeros_like(out_ref)
    rotate_part(0, near_ref, far_ref, basis_ref, basis, out_ref, sem)


def rotate_last_kernel(
    tok_rows,
    first,
    near_ref,
    far_ref,
    basis_ref,
    map_ref,
    start_ref,
    out_ref,
    basis,
    total,
    stored_map,
    sem,
):
    tokens = total.shape[0]
    map_copy = pltpu.make_async_copy(map_ref, stored_map, sem.at[basis.shape[0]])
    map_copy.start()
    total[...] = start_ref[...]
    rotate_part(first, near_ref, far_ref, basis_ref, basis, total, sem)
    map_copy.wait()
    row = lax.broadcasted_iota(jnp.int32, (tokens, tokens), 0)
    block = row >> bits_of(tok_rows)
    wanted = jnp.zeros_like(row)
    for stored in range(tokens // tok_rows):
        wanted = jnp.where(block == stored, stored_map[stored] * tok_rows, wanted)
    wanted += row & (tok_rows - 1)
    held = held_tokens(lax.axis_index("blk"), tokens, tok_rows)
    out_ref[...] = reorder(wanted, held, total[...]).T.astype(jnp.bfloat16)


def scale_kernel(
    begun,
    aligned_ref,
    near_ref,
    far_ref,
    tiles_ref,
    eigen_ref,
    out_ref,
    damped,
    tiles,
    lanes,
    rotated,
    sem,
):
    blocks, depth = damped.shape[:2]
    chips, _, width = near_ref.shape
    per_piece = width // LANES

    def copy_of(block):
        rows = pl.ds(pl.multiple_of(block * depth, depth), depth)
        return pltpu.make_async_copy(eigen_ref.at[rows], damped.at[block], sem.at[block])

    tiles_copy = pltpu.make_async_copy(tiles_ref, tiles, sem.at[blocks])
    tiles_copy.start()

    @pl.loop(0, blocks)
    def _(block):
        copy_of(block).start()

    tiles_copy.wait()
    me = lax.axis_index("blk")
    for at, steps in enumerate(begun):
        for other, rotated_ref in enumerate((near_ref, far_ref)):
            source = ring_source(me, steps, other, chips)
            piece = 2 * at + other
            rotated[piece] = rotated_ref[source // 2]
            for part in range(per_piece):
                lanes[piece * per_piece + part] = tiles[source * per_piece + part] * LANES

    @pl.loop(0, blocks)
    def _(block):
        rows = pl.ds(pl.multiple_of(block * depth, depth), depth)
        aligned = aligned_ref[rows, :]
        copy_of(block).wait()
        for piece in range(2 * chips):
            grad = jnp.dot(aligned, rotated[piece], preferred_element_type=jnp.float32)
            for part in range(per_piece):
                tile = piece * per_piece + part
                eigen = damped[block, :, pl.ds(pl.multiple_of(lanes[tile], LANES), LANES)]
                inverse = pl.reciprocal(eigen, approx=True)
                inverse = inverse * (2.0 - eigen * inverse)
                scaled = grad[:, part * LANES : (part + 1) * LANES] * inverse
                out_ref[rows, tile * LANES : (tile + 1) * LANES] = scaled.astype(jnp.bfloat16)


def project_kernel(cuts, scaled_ref, basis_out_ref, *refs):
    out_ref, window_ref, basis, sem = refs[-4:]
    near = refs[: cuts[-1] // 2]
    own_far, *pairs = refs[len(near) : -4]
    far = [own_far] + [pair.at[at] for pair in pairs for at in range(2)]
    pieces = [piece for pair in zip(near, far) for piece in pair]
    width = pieces[0].shape[0]
    copies = [
        pltpu.make_async_copy(piece, basis.at[pl.ds(at * width, width)], sem.at[at])
        for at, piece in enumerate(pieces)
    ]
    window_copy = pltpu.make_async_copy(
        basis_out_ref.at[pl.ds(0, window_ref.shape[0])], window_ref, sem.at[len(pieces)]
    )
    window_copy.start()
    for copy in copies:
        copy.start()
    for first, last in zip(cuts[:-1], cuts[1:]):
        for copy in copies[first:last]:
            copy.wait()
        deep = slice(first * width, last * width)
        part = jnp.dot(scaled_ref[:, deep], basis[deep, :], preferred_element_type=jnp.float32)
        out_ref[...] = part if first == 0 else out_ref[...] + part

    window_copy.wait()


def window_kernel(
    scale,
    window_ref,
    scaled_ref,
    projected_ref,
    first_ref,
    last_ref,
    far_ref,
    send_ref,
    keep_ref,
    result,
):
    chips, rows, _ = keep_ref.shape
    basis = jnp.concatenate([first_ref[...], last_ref[...], far_ref[0], far_ref[1]], axis=0)
    columns = slice(scaled_ref.shape[1] - basis.shape[0], None)
    total = projected_ref[...] + jnp.dot(
        scaled_ref[:, columns], basis, preferred_element_type=jnp.float32
    )
    result[...] = scale * jnp.dot(
        window_ref[...], total.astype(jnp.bfloat16), preferred_element_type=jnp.float32
    )
    core = lax.rem(lax.axis_index("blk"), 2)
    for k in range(chips):
        mine = pl.ds(pl.multiple_of((2 * k + core) * rows, rows), rows)
        keep_ref[k] = result[mine, :]
        other = pl.ds(pl.multiple_of((2 * k + 1 - core) * rows, rows), rows)
        send_ref[k] = result[other, :].astype(jnp.bfloat16)


def add_core_kernel(keys, keep_ref, got_ref, own_ref, *send_refs):
    chip = lax.axis_index("blk") // 2
    for key, ref in zip((0, *keys), (own_ref, *send_refs)):
        at = chip ^ key
        ref[...] = (keep_ref[at] + got_ref[at].astype(jnp.float32)).astype(ref.dtype)


def add_chips_kernel(own_ref, *refs):
    total = own_ref[...]
    for ref in refs[:-1]:
        total += ref[...].astype(jnp.float32)
    refs[-1][...] = total


VMEM = pl.BlockSpec(memory_space=pltpu.VMEM)
SMEM = pl.BlockSpec(memory_space=pltpu.SMEM)
ANY = pl.BlockSpec(memory_space=pl.ANY)
CHEAP = pl.CostEstimate(flops=1, bytes_accessed=1, transcendentals=0)


def after(first, *others):
    return lax.optimization_barrier((first, *others))


def ring_body(n, grad_out, activations, basis_out, basis_in, eigenvalues, tile_order, block_map):
    tok_rows, full_out = grad_out.shape
    tile_width = basis_out.shape[1]
    full_in, in_width = basis_in.shape
    tokens = n * tok_rows
    chips = n // 2
    to_right = lambda x: lax.ppermute(x, "blk", shift_pairs(n, 1))
    to_left = lambda x: lax.ppermute(x, "blk", shift_pairs(n, -1))
    steps = chips // 2

    own = basis_in[:WC].T

    pairs = chips // 2
    both = jnp.concatenate([grad_out, activations], axis=1)[None]
    got = [lax.ppermute(both, "blk", xor_pairs(n, 4 * key)) for key in range(1, pairs)]
    kept = pl.pallas_call(
        keep_kernel,
        out_shape=jax.ShapeDtypeStruct(basis_in.shape, jnp.bfloat16),
        in_specs=[VMEM],
        out_specs=VMEM,
        compiler_params=pltpu.CompilerParams(vmem_limit_bytes=8 * MIB),
        cost_estimate=CHEAP,
        name="keep",
    )(basis_in)
    both, own, kept, *got = after(both, own, kept, *got)
    depth, later = 1024, 9
    grads, acts = pl.pallas_call(
        part_kernel,
        out_shape=(
            jax.ShapeDtypeStruct((pairs, tok_rows, full_out), jnp.bfloat16),
            jax.ShapeDtypeStruct((pairs, tok_rows, full_in), jnp.bfloat16),
        ),
        in_specs=[VMEM] * pairs,
        out_specs=(VMEM, VMEM),
        compiler_params=pltpu.CompilerParams(vmem_limit_bytes=8 * MIB),
        name="part",
    )(both, *got)
    acts, grads, own = after(acts, grads, own)
    acts_got = lax.ppermute(acts, "blk", xor_pairs(n, 2))
    grads_got = lax.ppermute(grads, "blk", xor_pairs(n, 2))
    acts = jnp.concatenate([acts, acts_got], axis=0)
    rotated = pl.pallas_call(
        functools.partial(rotate_in_kernel, tok_rows),
        out_shape=jax.ShapeDtypeStruct((chips, tokens, in_width), jnp.bfloat16),
        in_specs=[VMEM, VMEM, VMEM],
        out_specs=VMEM,
        compiler_params=pltpu.CompilerParams(vmem_limit_bytes=8 * MIB),
        cost_estimate=CHEAP,
        name="rotate_in",
    )(acts, swap(acts, n), kept)

    grads_got, own, _ = after(grads_got, own, rotated)
    rotated = exchange(rotated, n, 2)
    right, left = [own, to_right(own)], [own, to_left(own)]
    grads = jnp.concatenate([grads, grads_got], axis=0)
    grads_far = swap(grads, n)
    far = [swap(own, n)]

    rotate = lambda kernel, count, scratch, shape, dtype, *operands: pl.pallas_call(
        kernel,
        out_shape=jax.ShapeDtypeStruct(shape, dtype),
        in_specs=[ANY if x is basis_out or x is block_map else VMEM for x in operands],
        out_specs=VMEM,
        scratch_shapes=[pltpu.VMEM((count, depth, tile_width), jnp.bfloat16)]
        + scratch
        + [pltpu.SemaphoreType.DMA((count + 1,))],
        compiler_params=pltpu.CompilerParams(vmem_limit_bytes=40 * MIB),
        cost_estimate=CHEAP,
        name=kernel.func.__name__[:-7],
    )(*operands)
    start = rotate(
        functools.partial(rotate_first_kernel),
        full_out // depth - later,
        [],
        (tokens, tile_width),
        jnp.float32,
        grads,
        grads_far,
        basis_out,
    )
    start, right[-1], left[-1], *far = after(start, right[-1], left[-1], *far)
    far += [swap_both(right[-1], left[-1], n)]
    right.append(to_right(right[-1]))
    left.append(to_left(left[-1]))
    start, grads, rotated = after(start, grads, rotated)
    rotated_far = swap(rotated, n)
    aligned = rotate(
        functools.partial(rotate_last_kernel, tok_rows, full_out // depth - later),
        later,
        [
            pltpu.VMEM((tokens, tile_width), jnp.float32),
            pltpu.SMEM(block_map.shape, jnp.int32),
        ],
        (tile_width, tokens),
        jnp.bfloat16,
        grads,
        grads_far,
        basis_out,
        block_map,
        start,
    )

    aligned, right[-1], left[-1], rotated_far, *far = after(
        aligned, right[-1], left[-1], rotated_far, *far
    )
    far += [swap_both(right[-1], left[-1], n)]
    right.append(to_right(right[-1]))
    left.append(to_left(left[-1]))
    begun = [0] + [at for step in range(1, steps) for at in (step, chips - step)] + [steps]
    blocks = 8
    scaled = pl.pallas_call(
        functools.partial(scale_kernel, begun),
        out_shape=jax.ShapeDtypeStruct((tile_width, full_in), jnp.bfloat16),
        in_specs=[VMEM] * 3 + [ANY] * 2,
        out_specs=VMEM,
        scratch_shapes=[
            pltpu.VMEM((blocks, tile_width // blocks, full_in), jnp.float32),
            pltpu.SMEM(tile_order.shape, jnp.int32),
            pltpu.SMEM(tile_order.shape, jnp.int32),
            pltpu.VMEM((n, tokens, in_width), jnp.bfloat16),
            pltpu.SemaphoreType.DMA((blocks + 1,)),
        ],
        compiler_params=pltpu.CompilerParams(vmem_limit_bytes=40 * MIB),
        cost_estimate=CHEAP,
        name="scale",
    )(aligned, rotated, rotated_far, tile_order, eigenvalues)

    scaled, right[-1], left[-1], *far = after(scaled, right[-1], left[-1], *far)
    cut = in_width // 2
    last = [to_right(right[-1][:cut]), to_left(left[-1][cut:])]
    near = [right[at] if at < steps else left[chips - at] for at in begun[:-1]]
    far += [swap_both(right[-1], left[-1], n)]
    count = 2 * len(near)
    projected, window = pl.pallas_call(
        functools.partial(project_kernel, (0, 6, count)),
        out_shape=(
            jax.ShapeDtypeStruct((tile_width, WC), jnp.float32),
            jax.ShapeDtypeStruct((WR, tile_width), jnp.bfloat16),
        ),
        in_specs=[VMEM] + [ANY] * (1 + len(near) + len(far)),
        out_specs=(VMEM, VMEM),
        scratch_shapes=[
            pltpu.VMEM((count * in_width, WC), jnp.bfloat16),
            pltpu.SemaphoreType.DMA((count + 1,)),
        ],
        compiler_params=pltpu.CompilerParams(vmem_limit_bytes=24 * MIB),
        cost_estimate=CHEAP,
        name="project",
    )(scaled, basis_out, *near, *far)

    projected, *last = after(projected, *last)
    last.append(swap_both(*last, n))
    rows = WR // n
    send, keep = pl.pallas_call(
        functools.partial(window_kernel, 1.0 / tokens),
        out_shape=(
            jax.ShapeDtypeStruct((chips, rows, WC), jnp.bfloat16),
            jax.ShapeDtypeStruct((chips, rows, WC), jnp.float32),
        ),
        in_specs=[VMEM] * 6,
        out_specs=(VMEM, VMEM),
        scratch_shapes=[pltpu.VMEM((WR, WC), jnp.float32)],
        compiler_params=pltpu.CompilerParams(vmem_limit_bytes=24 * MIB),
        cost_estimate=CHEAP,
        name="window",
    )(window, scaled, projected, *last)

    keys = [*range(chips - 2, 0, -2), *range(chips - 1, 0, -2)]
    small = pltpu.CompilerParams(vmem_limit_bytes=8 * MIB)
    own, *sends = pl.pallas_call(
        functools.partial(add_core_kernel, keys),
        out_shape=[jax.ShapeDtypeStruct((rows, WC), jnp.float32)]
        + [jax.ShapeDtypeStruct((rows, WC), jnp.bfloat16)] * len(keys),
        in_specs=[VMEM, VMEM],
        out_specs=[VMEM] * chips,
        compiler_params=small,
        name="add_core",
    )(keep, swap(send, n))
    arrived = [lax.ppermute(x, "blk", xor_pairs(n, 2 * key)) for key, x in zip(keys, sends)]
    return pl.pallas_call(
        add_chips_kernel,
        out_shape=jax.ShapeDtypeStruct((rows, WC), jnp.float32),
        in_specs=[VMEM] * chips,
        out_specs=VMEM,
        compiler_params=small,
        name="add_chips",
    )(own, *arrived)


def gather_body(grad_out, activations, basis_out, basis_in, eigenvalues, tile_order, block_map):
    n_blocks = lax.axis_size("blk")
    tile_width = basis_out.shape[1]
    tok_rows = grad_out.shape[0]
    full_in = eigenvalues.shape[1]
    tokens = n_blocks * tok_rows
    dot = functools.partial(jnp.dot, preferred_element_type=jnp.float32)
    in_rows = lax.all_gather(basis_in[:WC], "blk", axis=1, tiled=True)
    acts = lax.all_gather(activations, "blk", axis=0, tiled=True)
    in_tile = dot(acts, basis_in).astype(jnp.bfloat16)
    rotated_in = lax.all_gather(in_tile, "blk", axis=1, tiled=True)
    grads = lax.all_gather(grad_out, "blk", axis=0, tiled=True)
    rotated_out = dot(grads, basis_out).astype(jnp.bfloat16)
    aligned = jnp.take(
        rotated_out.reshape(n_blocks, tok_rows, tile_width), block_map, axis=0
    ).reshape(tokens, tile_width)
    grad_tile = dot(aligned.T, rotated_in) / tokens
    damped = jnp.take(
        eigenvalues.reshape(tile_width, full_in // LANES, LANES), tile_order, axis=1
    ).reshape(tile_width, full_in)
    scaled = (grad_tile / damped).astype(jnp.bfloat16)
    projected = dot(scaled, in_rows.T).astype(jnp.bfloat16)
    return lax.psum_scatter(
        dot(basis_out[:WR], projected), "blk", scatter_dimension=0, tiled=True
    )


def solution(mesh):
    n = mesh.shape["blk"]

    def body(*args):
        wide = args[3].shape[1] % LANES == 0 and args[2].shape[1] % LANES == 0
        doubles = n & (n - 1) == 0 and args[0].shape[0] & (args[0].shape[0] - 1) == 0
        if wide and doubles and WR % (16 * n) == 0:
            return ring_body(n, *args)
        return gather_body(*args)

    placed = (
        P(("grp", "blk"), None),
        P(("grp", "blk"), None),
        P(None, "blk"),
        P(None, "blk"),
        P("blk", None),
        P(),
        P(),
    )
    return jax.shard_map(
        body, mesh=mesh, in_specs=placed, out_specs=P(("grp", "blk"), None), check_vma=False
    )
```

```python
import functools

import jax
import jax.numpy as jnp
from jax import lax
from jax.experimental import pallas as pl
from jax.experimental.pallas import tpu as pltpu
from jax.sharding import PartitionSpec as P

WR = 768
WC = 512
LANES = 128
MIB = 1 << 20


def ring_of(n):
    chips = n // 2
    return [*range(0, chips, 2), *range(chips - 1, 0, -2)]


def shift_pairs(n, by):
    ring = ring_of(n)
    return [
        (2 * ring[p] + c, 2 * ring[(p + by) % len(ring)] + c)
        for p in range(len(ring))
        for c in range(2)
    ]


def ring_source(me, steps, other, chips):
    chip, core = me // 2, lax.rem(me, 2)
    place = jnp.where(lax.rem(chip, 2) == 0, chip // 2, chips - 1 - chip // 2)
    place = lax.rem(place + chips - steps, chips)
    chip = jnp.where(place < chips // 2, 2 * place, 2 * (chips - 1 - place) + 1)
    return 2 * chip + (core ^ other)


def xor_pairs(n, key):
    return [(b, b ^ key) for b in range(n)]


def exchange(x, n, stride):
    groups = [list(range(first, n, stride)) for first in range(stride)]
    return lax.all_to_all(x, "blk", 0, 0, axis_index_groups=groups, tiled=True)


def swap(x, n):
    return lax.ppermute(x, "blk", xor_pairs(n, 1))


def bits_of(size):
    return size.bit_length() - 1


def held_tokens(me, tokens, tok_rows):
    row = lax.broadcasted_iota(jnp.int32, (tokens, tokens), 1)
    pairs = tokens // tok_rows // 4
    place = row >> bits_of(tok_rows)
    chip = 2 * (place & (pairs - 1)) + ((place >> bits_of(pairs)) & 1)
    other = row >> bits_of(tokens // 2)
    device = me ^ (2 * chip + other)
    return (device << bits_of(tok_rows)) + (row & (tok_rows - 1))


def reorder(wanted, held, rotated):
    order = jnp.where(wanted == held, 1.0, 0.0).astype(jnp.bfloat16)
    return jnp.dot(order, rotated.astype(jnp.bfloat16), preferred_element_type=jnp.float32)


def part_kernel(*refs):
    grads_ref, acts_ref = refs[-2:]
    first = grads_ref.shape[2]
    for at, ref in enumerate(refs[:-2]):
        grads_ref[at] = ref[0, :, :first]
        acts_ref[at] = ref[0, :, first:]


def rotate_in_kernel(tok_rows, near_ref, far_ref, basis_ref, out_ref):
    tokens = out_ref.shape[1]
    depth = near_ref.shape[2]
    acts = jnp.concatenate([ref[...].reshape(-1, depth) for ref in (near_ref, far_ref)], axis=0)
    rotated = jnp.dot(acts, basis_ref[...], preferred_element_type=jnp.float32)
    wanted = lax.broadcasted_iota(jnp.int32, (tokens, tokens), 0)
    held = held_tokens(lax.axis_index("blk"), tokens, tok_rows)
    ordered = reorder(wanted, held, rotated).astype(jnp.bfloat16)
    for copy in range(out_ref.shape[0]):
        out_ref[copy] = ordered


def keep_kernel(basis_ref, kept_ref):
    kept_ref[...] = basis_ref[...]


def rotate_part(first, near_ref, far_ref, basis_ref, basis, total, sem):
    steps, depth = basis.shape[:2]

    def copy_of(step):
        rows = pl.ds(pl.multiple_of((first + step) * depth, depth), depth)
        return pltpu.make_async_copy(basis_ref.at[rows], basis.at[step], sem.at[step])

    @pl.loop(0, steps)
    def _(step):
        copy_of(step).start()

    @pl.loop(0, steps)
    def _(step):
        columns = pl.ds(pl.multiple_of((first + step) * depth, depth), depth)
        rows = [ref[:, :, columns].reshape(-1, depth) for ref in (near_ref, far_ref)]
        grads = jnp.concatenate(rows, axis=0)
        copy_of(step).wait()
        total[...] += jnp.dot(grads, basis[step], preferred_element_type=jnp.float32)


def rotate_first_kernel(near_ref, far_ref, basis_ref, out_ref, basis, sem):
    out_ref[...] = jnp.zeros_like(out_ref)
    rotate_part(0, near_ref, far_ref, basis_ref, basis, out_ref, sem)


def rotate_last_kernel(
    tok_rows,
    first,
    near_ref,
    far_ref,
    basis_ref,
    map_ref,
    start_ref,
    out_ref,
    basis,
    total,
    stored_map,
    sem,
):
    tokens = total.shape[0]
    map_copy = pltpu.make_async_copy(map_ref, stored_map, sem.at[basis.shape[0]])
    map_copy.start()
    total[...] = start_ref[...]
    rotate_part(first, near_ref, far_ref, basis_ref, basis, total, sem)
    map_copy.wait()
    row = lax.broadcasted_iota(jnp.int32, (tokens, tokens), 0)
    block = row >> bits_of(tok_rows)
    wanted = jnp.zeros_like(row)
    for stored in range(tokens // tok_rows):
        wanted = jnp.where(block == stored, stored_map[stored] * tok_rows, wanted)
    wanted += row & (tok_rows - 1)
    held = held_tokens(lax.axis_index("blk"), tokens, tok_rows)
    out_ref[...] = reorder(wanted, held, total[...]).T.astype(jnp.bfloat16)


def scale_kernel(
    begun,
    aligned_ref,
    near_ref,
    far_ref,
    tiles_ref,
    eigen_ref,
    out_ref,
    damped,
    tiles,
    lanes,
    rotated,
    sem,
):
    blocks, depth = damped.shape[:2]
    chips, _, width = near_ref.shape
    per_piece = width // LANES

    def copy_of(block):
        rows = pl.ds(pl.multiple_of(block * depth, depth), depth)
        return pltpu.make_async_copy(eigen_ref.at[rows], damped.at[block], sem.at[block])

    tiles_copy = pltpu.make_async_copy(tiles_ref, tiles, sem.at[blocks])
    tiles_copy.start()

    @pl.loop(0, blocks)
    def _(block):
        copy_of(block).start()

    tiles_copy.wait()
    me = lax.axis_index("blk")
    for at, steps in enumerate(begun):
        for other, rotated_ref in enumerate((near_ref, far_ref)):
            source = ring_source(me, steps, other, chips)
            piece = 2 * at + other
            rotated[piece] = rotated_ref[source // 2]
            for part in range(per_piece):
                lanes[piece * per_piece + part] = tiles[source * per_piece + part] * LANES

    @pl.loop(0, blocks)
    def _(block):
        rows = pl.ds(pl.multiple_of(block * depth, depth), depth)
        aligned = aligned_ref[rows, :]
        copy_of(block).wait()
        for piece in range(2 * chips):
            grad = jnp.dot(aligned, rotated[piece], preferred_element_type=jnp.float32)
            for part in range(per_piece):
                tile = piece * per_piece + part
                eigen = damped[block, :, pl.ds(pl.multiple_of(lanes[tile], LANES), LANES)]
                inverse = pl.reciprocal(eigen, approx=True)
                inverse = inverse * (2.0 - eigen * inverse)
                scaled = grad[:, part * LANES : (part + 1) * LANES] * inverse
                out_ref[rows, tile * LANES : (tile + 1) * LANES] = scaled.astype(jnp.bfloat16)


def project_kernel(cuts, scaled_ref, basis_out_ref, *refs):
    pieces = refs[:-4]
    out_ref, window_ref, basis, sem = refs[-4:]
    width = pieces[0].shape[0]
    copies = [
        pltpu.make_async_copy(piece, basis.at[pl.ds(at * width, width)], sem.at[at])
        for at, piece in enumerate(pieces)
    ]
    window_copy = pltpu.make_async_copy(
        basis_out_ref.at[pl.ds(0, window_ref.shape[0])], window_ref, sem.at[len(pieces)]
    )
    window_copy.start()
    for copy in copies:
        copy.start()
    for first, last in zip(cuts[:-1], cuts[1:]):
        for copy in copies[first:last]:
            copy.wait()
        deep = slice(first * width, last * width)
        part = jnp.dot(scaled_ref[:, deep], basis[deep, :], preferred_element_type=jnp.float32)
        out_ref[...] = part if first == 0 else out_ref[...] + part

    window_copy.wait()


def window_kernel(scale, window_ref, scaled_ref, projected_ref, *refs):
    pieces = refs[:-3]
    send_ref, keep_ref, result = refs[-3:]
    chips, rows, _ = keep_ref.shape
    width = pieces[0].shape[0]
    total = projected_ref[...]
    first = scaled_ref.shape[1] - width * len(pieces)
    basis = jnp.concatenate([piece[...] for piece in pieces], axis=0)
    total += jnp.dot(scaled_ref[:, first:], basis, preferred_element_type=jnp.float32)
    result[...] = scale * jnp.dot(
        window_ref[...], total.astype(jnp.bfloat16), preferred_element_type=jnp.float32
    )
    core = lax.rem(lax.axis_index("blk"), 2)
    for k in range(chips):
        mine = pl.ds(pl.multiple_of((2 * k + core) * rows, rows), rows)
        keep_ref[k] = result[mine, :]
        other = pl.ds(pl.multiple_of((2 * k + 1 - core) * rows, rows), rows)
        send_ref[k] = result[other, :].astype(jnp.bfloat16)


def add_core_kernel(keys, keep_ref, got_ref, own_ref, *send_refs):
    chip = lax.axis_index("blk") // 2
    for key, ref in zip((0, *keys), (own_ref, *send_refs)):
        at = chip ^ key
        ref[...] = (keep_ref[at] + got_ref[at].astype(jnp.float32)).astype(ref.dtype)


def add_chips_kernel(own_ref, *refs):
    total = own_ref[...]
    for ref in refs[:-1]:
        total += ref[...].astype(jnp.float32)
    refs[-1][...] = total


VMEM = pl.BlockSpec(memory_space=pltpu.VMEM)
SMEM = pl.BlockSpec(memory_space=pltpu.SMEM)
ANY = pl.BlockSpec(memory_space=pl.ANY)
CHEAP = pl.CostEstimate(flops=1, bytes_accessed=1, transcendentals=0)


def after(first, *others):
    return lax.optimization_barrier((first, *others))


def ring_body(n, grad_out, activations, basis_out, basis_in, eigenvalues, tile_order, block_map):
    tok_rows, full_out = grad_out.shape
    tile_width = basis_out.shape[1]
    full_in, in_width = basis_in.shape
    tokens = n * tok_rows
    chips = n // 2
    to_right = lambda x: lax.ppermute(x, "blk", shift_pairs(n, 1))
    to_left = lambda x: lax.ppermute(x, "blk", shift_pairs(n, -1))
    steps = chips // 2

    own = basis_in[:WC].T

    pairs = chips // 2
    both = jnp.concatenate([grad_out, activations], axis=1)[None]
    got = [lax.ppermute(both, "blk", xor_pairs(n, 4 * key)) for key in range(pairs - 1, 0, -1)]
    got.reverse()
    kept = pl.pallas_call(
        keep_kernel,
        out_shape=jax.ShapeDtypeStruct(basis_in.shape, jnp.bfloat16),
        in_specs=[VMEM],
        out_specs=VMEM,
        compiler_params=pltpu.CompilerParams(vmem_limit_bytes=8 * MIB),
        cost_estimate=CHEAP,
        name="keep",
    )(basis_in)
    both, own, kept, *got = after(both, own, kept, *got)
    depth, later = 1024, 9
    grads, acts = pl.pallas_call(
        part_kernel,
        out_shape=(
            jax.ShapeDtypeStruct((pairs, tok_rows, full_out), jnp.bfloat16),
            jax.ShapeDtypeStruct((pairs, tok_rows, full_in), jnp.bfloat16),
        ),
        in_specs=[VMEM] * pairs,
        out_specs=(VMEM, VMEM),
        compiler_params=pltpu.CompilerParams(vmem_limit_bytes=8 * MIB),
        name="part",
    )(both, *got)
    acts, grads, own = after(acts, grads, own)
    acts_got = lax.ppermute(acts, "blk", xor_pairs(n, 2))
    grads_got = lax.ppermute(grads, "blk", xor_pairs(n, 2))
    acts = jnp.concatenate([acts, acts_got], axis=0)
    rotated = pl.pallas_call(
        functools.partial(rotate_in_kernel, tok_rows),
        out_shape=jax.ShapeDtypeStruct((chips, tokens, in_width), jnp.bfloat16),
        in_specs=[VMEM, VMEM, VMEM],
        out_specs=VMEM,
        compiler_params=pltpu.CompilerParams(vmem_limit_bytes=8 * MIB),
        cost_estimate=CHEAP,
        name="rotate_in",
    )(acts, swap(acts, n), kept)

    grads_got, own, _ = after(grads_got, own, rotated)
    rotated = exchange(rotated, n, 2)
    right, left = [own, to_right(own)], [own, to_left(own)]
    grads = jnp.concatenate([grads, grads_got], axis=0)
    grads_far = swap(grads, n)
    far = [swap(own, n)]

    rotate = lambda kernel, count, scratch, shape, dtype, *operands: pl.pallas_call(
        kernel,
        out_shape=jax.ShapeDtypeStruct(shape, dtype),
        in_specs=[ANY if x is basis_out or x is block_map else VMEM for x in operands],
        out_specs=VMEM,
        scratch_shapes=[pltpu.VMEM((count, depth, tile_width), jnp.bfloat16)]
        + scratch
        + [pltpu.SemaphoreType.DMA((count + 1,))],
        compiler_params=pltpu.CompilerParams(vmem_limit_bytes=40 * MIB),
        cost_estimate=CHEAP,
        name=kernel.func.__name__[:-7],
    )(*operands)
    start = rotate(
        functools.partial(rotate_first_kernel),
        full_out // depth - later,
        [],
        (tokens, tile_width),
        jnp.float32,
        grads,
        grads_far,
        basis_out,
    )
    start, right[-1], left[-1], *far = after(start, right[-1], left[-1], *far)
    far += [swap(right[-1], n), swap(left[-1], n)]
    right.append(to_right(right[-1]))
    left.append(to_left(left[-1]))
    start, grads, rotated = after(start, grads, rotated)
    rotated_far = swap(rotated, n)
    aligned = rotate(
        functools.partial(rotate_last_kernel, tok_rows, full_out // depth - later),
        later,
        [
            pltpu.VMEM((tokens, tile_width), jnp.float32),
            pltpu.SMEM(block_map.shape, jnp.int32),
        ],
        (tile_width, tokens),
        jnp.bfloat16,
        grads,
        grads_far,
        basis_out,
        block_map,
        start,
    )

    aligned, right[-1], left[-1], rotated_far, *far = after(
        aligned, right[-1], left[-1], rotated_far, *far
    )
    far += [swap(right[-1], n), swap(left[-1], n)]
    right.append(to_right(right[-1]))
    left.append(to_left(left[-1]))
    begun = [0] + [at for step in range(1, steps) for at in (step, chips - step)] + [steps]
    blocks = 8
    scaled = pl.pallas_call(
        functools.partial(scale_kernel, begun),
        out_shape=jax.ShapeDtypeStruct((tile_width, full_in), jnp.bfloat16),
        in_specs=[VMEM] * 3 + [ANY] * 2,
        out_specs=VMEM,
        scratch_shapes=[
            pltpu.VMEM((blocks, tile_width // blocks, full_in), jnp.float32),
            pltpu.SMEM(tile_order.shape, jnp.int32),
            pltpu.SMEM(tile_order.shape, jnp.int32),
            pltpu.VMEM((n, tokens, in_width), jnp.bfloat16),
            pltpu.SemaphoreType.DMA((blocks + 1,)),
        ],
        compiler_params=pltpu.CompilerParams(vmem_limit_bytes=40 * MIB),
        cost_estimate=CHEAP,
        name="scale",
    )(aligned, rotated, rotated_far, tile_order, eigenvalues)

    scaled, right[-1], left[-1], *far = after(scaled, right[-1], left[-1], *far)
    cut = in_width // 2
    last = [to_right(right[-1][:cut]), to_left(left[-1][cut:])]
    near = [right[at] if at < steps else left[chips - at] for at in begun[:-1]]
    far += [swap(piece, n) for piece in near[len(far) :]]
    pieces = [piece for pair in zip(near, far) for piece in pair]
    projected, window = pl.pallas_call(
        functools.partial(project_kernel, (0, 6, len(pieces))),
        out_shape=(
            jax.ShapeDtypeStruct((tile_width, WC), jnp.float32),
            jax.ShapeDtypeStruct((WR, tile_width), jnp.bfloat16),
        ),
        in_specs=[VMEM] + [ANY] * (len(pieces) + 1),
        out_specs=(VMEM, VMEM),
        scratch_shapes=[
            pltpu.VMEM((len(pieces) * in_width, WC), jnp.bfloat16),
            pltpu.SemaphoreType.DMA((len(pieces) + 1,)),
        ],
        compiler_params=pltpu.CompilerParams(vmem_limit_bytes=24 * MIB),
        cost_estimate=CHEAP,
        name="project",
    )(scaled, basis_out, *pieces)

    projected, *last = after(projected, *last)
    last += [swap(piece, n) for piece in last]
    rows = WR // n
    send, keep = pl.pallas_call(
        functools.partial(window_kernel, 1.0 / tokens),
        out_shape=(
            jax.ShapeDtypeStruct((chips, rows, WC), jnp.bfloat16),
            jax.ShapeDtypeStruct((chips, rows, WC), jnp.float32),
        ),
        in_specs=[VMEM] * 7,
        out_specs=(VMEM, VMEM),
        scratch_shapes=[pltpu.VMEM((WR, WC), jnp.float32)],
        compiler_params=pltpu.CompilerParams(vmem_limit_bytes=24 * MIB),
        cost_estimate=CHEAP,
        name="window",
    )(window, scaled, projected, *last)

    keys = [*range(2, chips, 2), *range(1, chips, 2)]
    small = pltpu.CompilerParams(vmem_limit_bytes=8 * MIB)
    own, *sends = pl.pallas_call(
        functools.partial(add_core_kernel, keys),
        out_shape=[jax.ShapeDtypeStruct((rows, WC), jnp.float32)]
        + [jax.ShapeDtypeStruct((rows, WC), jnp.bfloat16)] * len(keys),
        in_specs=[VMEM, VMEM],
        out_specs=[VMEM] * chips,
        compiler_params=small,
        name="add_core",
    )(keep, swap(send, n))
    arrived = [lax.ppermute(x, "blk", xor_pairs(n, 2 * key)) for key, x in zip(keys, sends)]
    return pl.pallas_call(
        add_chips_kernel,
        out_shape=jax.ShapeDtypeStruct((rows, WC), jnp.float32),
        in_specs=[VMEM] * chips,
        out_specs=VMEM,
        compiler_params=small,
        name="add_chips",
    )(own, *arrived)


def gather_body(grad_out, activations, basis_out, basis_in, eigenvalues, tile_order, block_map):
    n_blocks = lax.axis_size("blk")
    tile_width = basis_out.shape[1]
    tok_rows = grad_out.shape[0]
    full_in = eigenvalues.shape[1]
    tokens = n_blocks * tok_rows
    dot = functools.partial(jnp.dot, preferred_element_type=jnp.float32)
    in_rows = lax.all_gather(basis_in[:WC], "blk", axis=1, tiled=True)
    acts = lax.all_gather(activations, "blk", axis=0, tiled=True)
    in_tile = dot(acts, basis_in).astype(jnp.bfloat16)
    rotated_in = lax.all_gather(in_tile, "blk", axis=1, tiled=True)
    grads = lax.all_gather(grad_out, "blk", axis=0, tiled=True)
    rotated_out = dot(grads, basis_out).astype(jnp.bfloat16)
    aligned = jnp.take(
        rotated_out.reshape(n_blocks, tok_rows, tile_width), block_map, axis=0
    ).reshape(tokens, tile_width)
    grad_tile = dot(aligned.T, rotated_in) / tokens
    damped = jnp.take(
        eigenvalues.reshape(tile_width, full_in // LANES, LANES), tile_order, axis=1
    ).reshape(tile_width, full_in)
    scaled = (grad_tile / damped).astype(jnp.bfloat16)
    projected = dot(scaled, in_rows.T).astype(jnp.bfloat16)
    return lax.psum_scatter(
        dot(basis_out[:WR], projected), "blk", scatter_dimension=0, tiled=True
    )


def solution(mesh):
    n = mesh.shape["blk"]

    def body(*args):
        wide = args[3].shape[1] % LANES == 0 and args[2].shape[1] % LANES == 0
        doubles = n & (n - 1) == 0 and args[0].shape[0] & (args[0].shape[0] - 1) == 0
        if wide and doubles and WR % (16 * n) == 0:
            return ring_body(n, *args)
        return gather_body(*args)

    placed = (
        P(("grp", "blk"), None),
        P(("grp", "blk"), None),
        P(None, "blk"),
        P(None, "blk"),
        P("blk", None),
        P(),
        P(),
    )
    return jax.shard_map(
        body, mesh=mesh, in_specs=placed, out_specs=P(("grp", "blk"), None), check_vma=False
    )
```

```python
import functools

import jax
import jax.numpy as jnp
from jax import lax
from jax.experimental import pallas as pl
from jax.experimental.pallas import tpu as pltpu
from jax.sharding import PartitionSpec as P

WR = 768
WC = 512
LANES = 128
MIB = 1 << 20


def ring_of(n):
    chips = n // 2
    return [*range(0, chips, 2), *range(chips - 1, 0, -2)]


def shift_pairs(n, by):
    ring = ring_of(n)
    return [
        (2 * ring[p] + c, 2 * ring[(p + by) % len(ring)] + c)
        for p in range(len(ring))
        for c in range(2)
    ]


def ring_source(me, steps, other, chips):
    chip, core = me // 2, lax.rem(me, 2)
    place = jnp.where(lax.rem(chip, 2) == 0, chip // 2, chips - 1 - chip // 2)
    place = lax.rem(place + chips - steps, chips)
    chip = jnp.where(place < chips // 2, 2 * place, 2 * (chips - 1 - place) + 1)
    return 2 * chip + (core ^ other)


def xor_pairs(n, key):
    return [(b, b ^ key) for b in range(n)]


def exchange(x, n, stride):
    groups = [list(range(first, n, stride)) for first in range(stride)]
    return lax.all_to_all(x, "blk", 0, 0, axis_index_groups=groups, tiled=True)


def swap(x, n):
    return lax.ppermute(x, "blk", xor_pairs(n, 1))


def bits_of(size):
    return size.bit_length() - 1


def held_tokens(me, tokens, tok_rows):
    row = lax.broadcasted_iota(jnp.int32, (tokens, tokens), 1)
    pairs = tokens // tok_rows // 4
    place = row >> bits_of(tok_rows)
    chip = 2 * (place & (pairs - 1)) + ((place >> bits_of(pairs)) & 1)
    other = row >> bits_of(tokens // 2)
    device = me ^ (2 * chip + other)
    return (device << bits_of(tok_rows)) + (row & (tok_rows - 1))


def reorder(wanted, held, rotated):
    order = jnp.where(wanted == held, 1.0, 0.0).astype(jnp.bfloat16)
    return jnp.dot(order, rotated.astype(jnp.bfloat16), preferred_element_type=jnp.float32)


def part_kernel(*refs):
    grads_ref, acts_ref = refs[-2:]
    first = grads_ref.shape[2]
    for at, ref in enumerate(refs[:-2]):
        grads_ref[at] = ref[0, :, :first]
        acts_ref[at] = ref[0, :, first:]


def rotate_in_kernel(tok_rows, near_ref, far_ref, basis_ref, out_ref):
    tokens = out_ref.shape[1]
    depth = near_ref.shape[2]
    acts = jnp.concatenate([ref[...].reshape(-1, depth) for ref in (near_ref, far_ref)], axis=0)
    rotated = jnp.dot(acts, basis_ref[...], preferred_element_type=jnp.float32)
    wanted = lax.broadcasted_iota(jnp.int32, (tokens, tokens), 0)
    held = held_tokens(lax.axis_index("blk"), tokens, tok_rows)
    ordered = reorder(wanted, held, rotated).astype(jnp.bfloat16)
    for copy in range(out_ref.shape[0]):
        out_ref[copy] = ordered


def keep_kernel(basis_ref, kept_ref):
    kept_ref[...] = basis_ref[...]


def rotate_part(first, near_ref, far_ref, basis_ref, basis, total, sem):
    steps, depth = basis.shape[:2]

    def copy_of(step):
        rows = pl.ds(pl.multiple_of((first + step) * depth, depth), depth)
        return pltpu.make_async_copy(basis_ref.at[rows], basis.at[step], sem.at[step])

    @pl.loop(0, steps)
    def _(step):
        copy_of(step).start()

    @pl.loop(0, steps)
    def _(step):
        columns = pl.ds(pl.multiple_of((first + step) * depth, depth), depth)
        rows = [ref[:, :, columns].reshape(-1, depth) for ref in (near_ref, far_ref)]
        grads = jnp.concatenate(rows, axis=0)
        copy_of(step).wait()
        total[...] += jnp.dot(grads, basis[step], preferred_element_type=jnp.float32)


def rotate_first_kernel(near_ref, far_ref, basis_ref, out_ref, basis, sem):
    out_ref[...] = jnp.zeros_like(out_ref)
    rotate_part(0, near_ref, far_ref, basis_ref, basis, out_ref, sem)


def rotate_last_kernel(
    tok_rows,
    first,
    near_ref,
    far_ref,
    basis_ref,
    map_ref,
    start_ref,
    out_ref,
    basis,
    total,
    stored_map,
    sem,
):
    tokens = total.shape[0]
    map_copy = pltpu.make_async_copy(map_ref, stored_map, sem.at[basis.shape[0]])
    map_copy.start()
    total[...] = start_ref[...]
    rotate_part(first, near_ref, far_ref, basis_ref, basis, total, sem)
    map_copy.wait()
    row = lax.broadcasted_iota(jnp.int32, (tokens, tokens), 0)
    block = row >> bits_of(tok_rows)
    wanted = jnp.zeros_like(row)
    for stored in range(tokens // tok_rows):
        wanted = jnp.where(block == stored, stored_map[stored] * tok_rows, wanted)
    wanted += row & (tok_rows - 1)
    held = held_tokens(lax.axis_index("blk"), tokens, tok_rows)
    out_ref[...] = reorder(wanted, held, total[...]).T.astype(jnp.bfloat16)


def scale_kernel(
    begun,
    aligned_ref,
    near_ref,
    far_ref,
    tiles_ref,
    eigen_ref,
    out_ref,
    damped,
    tiles,
    lanes,
    rotated,
    sem,
):
    blocks, depth = damped.shape[:2]
    chips, _, width = near_ref.shape
    per_piece = width // LANES

    def copy_of(block):
        rows = pl.ds(pl.multiple_of(block * depth, depth), depth)
        return pltpu.make_async_copy(eigen_ref.at[rows], damped.at[block], sem.at[block])

    tiles_copy = pltpu.make_async_copy(tiles_ref, tiles, sem.at[blocks])
    tiles_copy.start()

    @pl.loop(0, blocks)
    def _(block):
        copy_of(block).start()

    tiles_copy.wait()
    me = lax.axis_index("blk")
    for at, steps in enumerate(begun):
        for other, rotated_ref in enumerate((near_ref, far_ref)):
            source = ring_source(me, steps, other, chips)
            piece = 2 * at + other
            rotated[piece] = rotated_ref[source // 2]
            for part in range(per_piece):
                lanes[piece * per_piece + part] = tiles[source * per_piece + part] * LANES

    @pl.loop(0, blocks)
    def _(block):
        rows = pl.ds(pl.multiple_of(block * depth, depth), depth)
        aligned = aligned_ref[rows, :]
        copy_of(block).wait()
        for piece in range(2 * chips):
            grad = jnp.dot(aligned, rotated[piece], preferred_element_type=jnp.float32)
            for part in range(per_piece):
                tile = piece * per_piece + part
                eigen = damped[block, :, pl.ds(pl.multiple_of(lanes[tile], LANES), LANES)]
                inverse = pl.reciprocal(eigen, approx=True)
                inverse = inverse * (2.0 - eigen * inverse)
                scaled = grad[:, part * LANES : (part + 1) * LANES] * inverse
                out_ref[rows, tile * LANES : (tile + 1) * LANES] = scaled.astype(jnp.bfloat16)


def project_kernel(cuts, scaled_ref, basis_out_ref, *refs):
    pieces = refs[:-4]
    out_ref, window_ref, basis, sem = refs[-4:]
    width = pieces[0].shape[0]
    copies = [
        pltpu.make_async_copy(piece, basis.at[pl.ds(at * width, width)], sem.at[at])
        for at, piece in enumerate(pieces)
    ]
    window_copy = pltpu.make_async_copy(
        basis_out_ref.at[pl.ds(0, window_ref.shape[0])], window_ref, sem.at[len(pieces)]
    )
    window_copy.start()
    for copy in copies:
        copy.start()
    for first, last in zip(cuts[:-1], cuts[1:]):
        for copy in copies[first:last]:
            copy.wait()
        deep = slice(first * width, last * width)
        part = jnp.dot(scaled_ref[:, deep], basis[deep, :], preferred_element_type=jnp.float32)
        out_ref[...] = part if first == 0 else out_ref[...] + part

    window_copy.wait()


def window_kernel(scale, window_ref, scaled_ref, projected_ref, *refs):
    pieces = refs[:-3]
    send_ref, keep_ref, result = refs[-3:]
    chips, rows, _ = keep_ref.shape
    width = pieces[0].shape[0]
    total = projected_ref[...]
    first = scaled_ref.shape[1] - width * len(pieces)
    basis = jnp.concatenate([piece[...] for piece in pieces], axis=0)
    total += jnp.dot(scaled_ref[:, first:], basis, preferred_element_type=jnp.float32)
    result[...] = scale * jnp.dot(
        window_ref[...], total.astype(jnp.bfloat16), preferred_element_type=jnp.float32
    )
    core = lax.rem(lax.axis_index("blk"), 2)
    for k in range(chips):
        mine = pl.ds(pl.multiple_of((2 * k + core) * rows, rows), rows)
        keep_ref[k] = result[mine, :]
        other = pl.ds(pl.multiple_of((2 * k + 1 - core) * rows, rows), rows)
        send_ref[k] = result[other, :].astype(jnp.bfloat16)


def add_core_kernel(keys, keep_ref, got_ref, own_ref, *send_refs):
    chip = lax.axis_index("blk") // 2
    for key, ref in zip((0, *keys), (own_ref, *send_refs)):
        at = chip ^ key
        ref[...] = (keep_ref[at] + got_ref[at].astype(jnp.float32)).astype(ref.dtype)


def add_chips_kernel(own_ref, *refs):
    total = own_ref[...]
    for ref in refs[:-1]:
        total += ref[...].astype(jnp.float32)
    refs[-1][...] = total


VMEM = pl.BlockSpec(memory_space=pltpu.VMEM)
SMEM = pl.BlockSpec(memory_space=pltpu.SMEM)
ANY = pl.BlockSpec(memory_space=pl.ANY)
CHEAP = pl.CostEstimate(flops=1, bytes_accessed=1, transcendentals=0)


def after(first, *others):
    return lax.optimization_barrier((first, *others))


def ring_body(n, grad_out, activations, basis_out, basis_in, eigenvalues, tile_order, block_map):
    tok_rows, full_out = grad_out.shape
    tile_width = basis_out.shape[1]
    full_in, in_width = basis_in.shape
    tokens = n * tok_rows
    chips = n // 2
    to_right = lambda x: lax.ppermute(x, "blk", shift_pairs(n, 1))
    to_left = lambda x: lax.ppermute(x, "blk", shift_pairs(n, -1))
    steps = chips // 2

    own = basis_in[:WC].T

    pairs = chips // 2
    both = jnp.concatenate([grad_out, activations], axis=1)[None]
    got = [lax.ppermute(both, "blk", xor_pairs(n, 4 * key)) for key in range(1, pairs)]
    kept = pl.pallas_call(
        keep_kernel,
        out_shape=jax.ShapeDtypeStruct(basis_in.shape, jnp.bfloat16),
        in_specs=[VMEM],
        out_specs=VMEM,
        compiler_params=pltpu.CompilerParams(vmem_limit_bytes=8 * MIB),
        cost_estimate=CHEAP,
        name="keep",
    )(basis_in)
    both, own, kept, *got = after(both, own, kept, *got)
    depth, later = 1024, 9
    grads, acts = pl.pallas_call(
        part_kernel,
        out_shape=(
            jax.ShapeDtypeStruct((pairs, tok_rows, full_out), jnp.bfloat16),
            jax.ShapeDtypeStruct((pairs, tok_rows, full_in), jnp.bfloat16),
        ),
        in_specs=[VMEM] * pairs,
        out_specs=(VMEM, VMEM),
        compiler_params=pltpu.CompilerParams(vmem_limit_bytes=8 * MIB),
        name="part",
    )(both, *got)
    acts, grads, own = after(acts, grads, own)
    acts_got = lax.ppermute(acts, "blk", xor_pairs(n, 2))
    grads_got = lax.ppermute(grads, "blk", xor_pairs(n, 2))
    acts = jnp.concatenate([acts, acts_got], axis=0)
    rotated = pl.pallas_call(
        functools.partial(rotate_in_kernel, tok_rows),
        out_shape=jax.ShapeDtypeStruct((chips, tokens, in_width), jnp.bfloat16),
        in_specs=[VMEM, VMEM, VMEM],
        out_specs=VMEM,
        compiler_params=pltpu.CompilerParams(vmem_limit_bytes=8 * MIB),
        cost_estimate=CHEAP,
        name="rotate_in",
    )(acts, swap(acts, n), kept)

    grads_got, own, _ = after(grads_got, own, rotated)
    rotated = exchange(rotated, n, 2)
    right, left = [own, to_right(own)], [own, to_left(own)]
    grads = jnp.concatenate([grads, grads_got], axis=0)
    grads_far = swap(grads, n)
    far = [swap(own, n)]

    rotate = lambda kernel, count, scratch, shape, dtype, *operands: pl.pallas_call(
        kernel,
        out_shape=jax.ShapeDtypeStruct(shape, dtype),
        in_specs=[ANY if x is basis_out or x is block_map else VMEM for x in operands],
        out_specs=VMEM,
        scratch_shapes=[pltpu.VMEM((count, depth, tile_width), jnp.bfloat16)]
        + scratch
        + [pltpu.SemaphoreType.DMA((count + 1,))],
        compiler_params=pltpu.CompilerParams(vmem_limit_bytes=40 * MIB),
        cost_estimate=CHEAP,
        name=kernel.func.__name__[:-7],
    )(*operands)
    start = rotate(
        functools.partial(rotate_first_kernel),
        full_out // depth - later,
        [],
        (tokens, tile_width),
        jnp.float32,
        grads,
        grads_far,
        basis_out,
    )
    start, right[-1], left[-1], *far = after(start, right[-1], left[-1], *far)
    far += [swap(right[-1], n), swap(left[-1], n)]
    right.append(to_right(right[-1]))
    left.append(to_left(left[-1]))
    start, grads, rotated = after(start, grads, rotated)
    rotated_far = swap(rotated, n)
    aligned = rotate(
        functools.partial(rotate_last_kernel, tok_rows, full_out // depth - later),
        later,
        [
            pltpu.VMEM((tokens, tile_width), jnp.float32),
            pltpu.SMEM(block_map.shape, jnp.int32),
        ],
        (tile_width, tokens),
        jnp.bfloat16,
        grads,
        grads_far,
        basis_out,
        block_map,
        start,
    )

    aligned, right[-1], left[-1], rotated_far, *far = after(
        aligned, right[-1], left[-1], rotated_far, *far
    )
    far += [swap(right[-1], n), swap(left[-1], n)]
    right.append(to_right(right[-1]))
    left.append(to_left(left[-1]))
    begun = [0] + [at for step in range(1, steps) for at in (step, chips - step)] + [steps]
    blocks = 8
    scaled = pl.pallas_call(
        functools.partial(scale_kernel, begun),
        out_shape=jax.ShapeDtypeStruct((tile_width, full_in), jnp.bfloat16),
        in_specs=[VMEM] * 3 + [ANY] * 2,
        out_specs=VMEM,
        scratch_shapes=[
            pltpu.VMEM((blocks, tile_width // blocks, full_in), jnp.float32),
            pltpu.SMEM(tile_order.shape, jnp.int32),
            pltpu.SMEM(tile_order.shape, jnp.int32),
            pltpu.VMEM((n, tokens, in_width), jnp.bfloat16),
            pltpu.SemaphoreType.DMA((blocks + 1,)),
        ],
        compiler_params=pltpu.CompilerParams(vmem_limit_bytes=40 * MIB),
        cost_estimate=CHEAP,
        name="scale",
    )(aligned, rotated, rotated_far, tile_order, eigenvalues)

    scaled, right[-1], left[-1], *far = after(scaled, right[-1], left[-1], *far)
    cut = in_width // 2
    last = [to_right(right[-1][:cut]), to_left(left[-1][cut:])]
    near = [right[at] if at < steps else left[chips - at] for at in begun[:-1]]
    far += [swap(piece, n) for piece in near[len(far) :]]
    pieces = [piece for pair in zip(near, far) for piece in pair]
    projected, window = pl.pallas_call(
        functools.partial(project_kernel, (0, 6, len(pieces))),
        out_shape=(
            jax.ShapeDtypeStruct((tile_width, WC), jnp.float32),
            jax.ShapeDtypeStruct((WR, tile_width), jnp.bfloat16),
        ),
        in_specs=[VMEM] + [ANY] * (len(pieces) + 1),
        out_specs=(VMEM, VMEM),
        scratch_shapes=[
            pltpu.VMEM((len(pieces) * in_width, WC), jnp.bfloat16),
            pltpu.SemaphoreType.DMA((len(pieces) + 1,)),
        ],
        compiler_params=pltpu.CompilerParams(vmem_limit_bytes=24 * MIB),
        cost_estimate=CHEAP,
        name="project",
    )(scaled, basis_out, *pieces)

    projected, *last = after(projected, *last)
    last += [swap(piece, n) for piece in last]
    rows = WR // n
    send, keep = pl.pallas_call(
        functools.partial(window_kernel, 1.0 / tokens),
        out_shape=(
            jax.ShapeDtypeStruct((chips, rows, WC), jnp.bfloat16),
            jax.ShapeDtypeStruct((chips, rows, WC), jnp.float32),
        ),
        in_specs=[VMEM] * 7,
        out_specs=(VMEM, VMEM),
        scratch_shapes=[pltpu.VMEM((WR, WC), jnp.float32)],
        compiler_params=pltpu.CompilerParams(vmem_limit_bytes=24 * MIB),
        cost_estimate=CHEAP,
        name="window",
    )(window, scaled, projected, *last)

    keys = [*range(chips - 1, 0, -2), *range(chips - 2, 0, -2)]
    small = pltpu.CompilerParams(vmem_limit_bytes=8 * MIB)
    own, *sends = pl.pallas_call(
        functools.partial(add_core_kernel, keys),
        out_shape=[jax.ShapeDtypeStruct((rows, WC), jnp.float32)]
        + [jax.ShapeDtypeStruct((rows, WC), jnp.bfloat16)] * len(keys),
        in_specs=[VMEM, VMEM],
        out_specs=[VMEM] * chips,
        compiler_params=small,
        name="add_core",
    )(keep, swap(send, n))
    arrived = [lax.ppermute(x, "blk", xor_pairs(n, 2 * key)) for key, x in zip(keys, sends)]
    return pl.pallas_call(
        add_chips_kernel,
        out_shape=jax.ShapeDtypeStruct((rows, WC), jnp.float32),
        in_specs=[VMEM] * chips,
        out_specs=VMEM,
        compiler_params=small,
        name="add_chips",
    )(own, *arrived)


def gather_body(grad_out, activations, basis_out, basis_in, eigenvalues, tile_order, block_map):
    n_blocks = lax.axis_size("blk")
    tile_width = basis_out.shape[1]
    tok_rows = grad_out.shape[0]
    full_in = eigenvalues.shape[1]
    tokens = n_blocks * tok_rows
    dot = functools.partial(jnp.dot, preferred_element_type=jnp.float32)
    in_rows = lax.all_gather(basis_in[:WC], "blk", axis=1, tiled=True)
    acts = lax.all_gather(activations, "blk", axis=0, tiled=True)
    in_tile = dot(acts, basis_in).astype(jnp.bfloat16)
    rotated_in = lax.all_gather(in_tile, "blk", axis=1, tiled=True)
    grads = lax.all_gather(grad_out, "blk", axis=0, tiled=True)
    rotated_out = dot(grads, basis_out).astype(jnp.bfloat16)
    aligned = jnp.take(
        rotated_out.reshape(n_blocks, tok_rows, tile_width), block_map, axis=0
    ).reshape(tokens, tile_width)
    grad_tile = dot(aligned.T, rotated_in) / tokens
    damped = jnp.take(
        eigenvalues.reshape(tile_width, full_in // LANES, LANES), tile_order, axis=1
    ).reshape(tile_width, full_in)
    scaled = (grad_tile / damped).astype(jnp.bfloat16)
    projected = dot(scaled, in_rows.T).astype(jnp.bfloat16)
    return lax.psum_scatter(
        dot(basis_out[:WR], projected), "blk", scatter_dimension=0, tiled=True
    )


def solution(mesh):
    n = mesh.shape["blk"]

    def body(*args):
        wide = args[3].shape[1] % LANES == 0 and args[2].shape[1] % LANES == 0
        doubles = n & (n - 1) == 0 and args[0].shape[0] & (args[0].shape[0] - 1) == 0
        if wide and doubles and WR % (16 * n) == 0:
            return ring_body(n, *args)
        return gather_body(*args)

    placed = (
        P(("grp", "blk"), None),
        P(("grp", "blk"), None),
        P(None, "blk"),
        P(None, "blk"),
        P("blk", None),
        P(),
        P(),
    )
    return jax.shard_map(
        body, mesh=mesh, in_specs=placed, out_specs=P(("grp", "blk"), None), check_vma=False
    )
```

```python
import functools

import jax
import jax.numpy as jnp
from jax import lax
from jax.experimental import pallas as pl
from jax.experimental.pallas import tpu as pltpu
from jax.sharding import PartitionSpec as P

WR = 768
WC = 512
LANES = 128
MIB = 1 << 20


def ring_of(n):
    chips = n // 2
    return [*range(0, chips, 2), *range(chips - 1, 0, -2)]


def shift_pairs(n, by):
    ring = ring_of(n)
    return [
        (2 * ring[p] + c, 2 * ring[(p + by) % len(ring)] + c)
        for p in range(len(ring))
        for c in range(2)
    ]


def ring_source(me, steps, other, chips):
    chip, core = me // 2, lax.rem(me, 2)
    place = jnp.where(lax.rem(chip, 2) == 0, chip // 2, chips - 1 - chip // 2)
    place = lax.rem(place + chips - steps, chips)
    chip = jnp.where(place < chips // 2, 2 * place, 2 * (chips - 1 - place) + 1)
    return 2 * chip + (core ^ other)


def xor_pairs(n, key):
    return [(b, b ^ key) for b in range(n)]


def exchange(x, n, stride):
    groups = [list(range(first, n, stride)) for first in range(stride)]
    return lax.all_to_all(x, "blk", 0, 0, axis_index_groups=groups, tiled=True)


def swap(x, n):
    return lax.ppermute(x, "blk", xor_pairs(n, 1))


def bits_of(size):
    return size.bit_length() - 1


def held_tokens(me, tokens, tok_rows):
    row = lax.broadcasted_iota(jnp.int32, (tokens, tokens), 1)
    pairs = tokens // tok_rows // 4
    place = row >> bits_of(tok_rows)
    chip = 2 * (place & (pairs - 1)) + ((place >> bits_of(pairs)) & 1)
    other = row >> bits_of(tokens // 2)
    device = me ^ (2 * chip + other)
    return (device << bits_of(tok_rows)) + (row & (tok_rows - 1))


def reorder(wanted, held, rotated):
    order = jnp.where(wanted == held, 1.0, 0.0).astype(jnp.bfloat16)
    return jnp.dot(order, rotated.astype(jnp.bfloat16), preferred_element_type=jnp.float32)


def part_kernel(*refs):
    grads_ref, acts_ref = refs[-2:]
    first = grads_ref.shape[2]
    for at, ref in enumerate(refs[:-2]):
        grads_ref[at] = ref[0, :, :first]
        acts_ref[at] = ref[0, :, first:]


def rotate_in_kernel(tok_rows, near_ref, far_ref, basis_ref, out_ref):
    tokens = out_ref.shape[1]
    depth = near_ref.shape[2]
    acts = jnp.concatenate([ref[...].reshape(-1, depth) for ref in (near_ref, far_ref)], axis=0)
    rotated = jnp.dot(acts, basis_ref[...], preferred_element_type=jnp.float32)
    wanted = lax.broadcasted_iota(jnp.int32, (tokens, tokens), 0)
    held = held_tokens(lax.axis_index("blk"), tokens, tok_rows)
    ordered = reorder(wanted, held, rotated).astype(jnp.bfloat16)
    for copy in range(out_ref.shape[0]):
        out_ref[copy] = ordered


def keep_kernel(basis_ref, kept_ref):
    kept_ref[...] = basis_ref[...]


def rotate_part(first, near_ref, far_ref, basis_ref, basis, total, sem):
    steps, depth = basis.shape[:2]

    def copy_of(step):
        rows = pl.ds(pl.multiple_of((first + step) * depth, depth), depth)
        return pltpu.make_async_copy(basis_ref.at[rows], basis.at[step], sem.at[step])

    @pl.loop(0, steps)
    def _(step):
        copy_of(step).start()

    @pl.loop(0, steps)
    def _(step):
        columns = pl.ds(pl.multiple_of((first + step) * depth, depth), depth)
        rows = [ref[:, :, columns].reshape(-1, depth) for ref in (near_ref, far_ref)]
        grads = jnp.concatenate(rows, axis=0)
        copy_of(step).wait()
        total[...] += jnp.dot(grads, basis[step], preferred_element_type=jnp.float32)


def rotate_first_kernel(near_ref, far_ref, basis_ref, out_ref, basis, sem):
    out_ref[...] = jnp.zeros_like(out_ref)
    rotate_part(0, near_ref, far_ref, basis_ref, basis, out_ref, sem)


def rotate_last_kernel(
    tok_rows,
    first,
    near_ref,
    far_ref,
    basis_ref,
    map_ref,
    start_ref,
    out_ref,
    basis,
    total,
    stored_map,
    sem,
):
    tokens = total.shape[0]
    map_copy = pltpu.make_async_copy(map_ref, stored_map, sem.at[basis.shape[0]])
    map_copy.start()
    total[...] = start_ref[...]
    rotate_part(first, near_ref, far_ref, basis_ref, basis, total, sem)
    map_copy.wait()
    row = lax.broadcasted_iota(jnp.int32, (tokens, tokens), 0)
    block = row >> bits_of(tok_rows)
    wanted = jnp.zeros_like(row)
    for stored in range(tokens // tok_rows):
        wanted = jnp.where(block == stored, stored_map[stored] * tok_rows, wanted)
    wanted += row & (tok_rows - 1)
    held = held_tokens(lax.axis_index("blk"), tokens, tok_rows)
    out_ref[...] = reorder(wanted, held, total[...]).T.astype(jnp.bfloat16)


def scale_kernel(
    begun,
    aligned_ref,
    near_ref,
    far_ref,
    tiles_ref,
    eigen_ref,
    out_ref,
    damped,
    tiles,
    lanes,
    rotated,
    sem,
):
    blocks, depth = damped.shape[:2]
    chips, _, width = near_ref.shape
    per_piece = width // LANES

    def copy_of(block):
        rows = pl.ds(pl.multiple_of(block * depth, depth), depth)
        return pltpu.make_async_copy(eigen_ref.at[rows], damped.at[block], sem.at[block])

    tiles_copy = pltpu.make_async_copy(tiles_ref, tiles, sem.at[blocks])
    tiles_copy.start()

    @pl.loop(0, blocks)
    def _(block):
        copy_of(block).start()

    tiles_copy.wait()
    me = lax.axis_index("blk")
    for at, steps in enumerate(begun):
        for other, rotated_ref in enumerate((near_ref, far_ref)):
            source = ring_source(me, steps, other, chips)
            piece = 2 * at + other
            rotated[piece] = rotated_ref[source // 2]
            for part in range(per_piece):
                lanes[piece * per_piece + part] = tiles[source * per_piece + part] * LANES

    @pl.loop(0, blocks)
    def _(block):
        rows = pl.ds(pl.multiple_of(block * depth, depth), depth)
        aligned = aligned_ref[rows, :]
        copy_of(block).wait()
        for piece in range(2 * chips):
            grad = jnp.dot(aligned, rotated[piece], preferred_element_type=jnp.float32)
            for part in range(per_piece):
                tile = piece * per_piece + part
                eigen = damped[block, :, pl.ds(pl.multiple_of(lanes[tile], LANES), LANES)]
                inverse = pl.reciprocal(eigen, approx=True)
                inverse = inverse * (2.0 - eigen * inverse)
                scaled = grad[:, part * LANES : (part + 1) * LANES] * inverse
                out_ref[rows, tile * LANES : (tile + 1) * LANES] = scaled.astype(jnp.bfloat16)


def project_kernel(cuts, scaled_ref, basis_out_ref, *refs):
    pieces = refs[:-4]
    out_ref, window_ref, basis, sem = refs[-4:]
    width = pieces[0].shape[0]
    copies = [
        pltpu.make_async_copy(piece, basis.at[pl.ds(at * width, width)], sem.at[at])
        for at, piece in enumerate(pieces)
    ]
    window_copy = pltpu.make_async_copy(
        basis_out_ref.at[pl.ds(0, window_ref.shape[0])], window_ref, sem.at[len(pieces)]
    )
    window_copy.start()
    for copy in copies:
        copy.start()
    for first, last in zip(cuts[:-1], cuts[1:]):
        for copy in copies[first:last]:
            copy.wait()
        deep = slice(first * width, last * width)
        part = jnp.dot(scaled_ref[:, deep], basis[deep, :], preferred_element_type=jnp.float32)
        out_ref[...] = part if first == 0 else out_ref[...] + part

    window_copy.wait()


def mix_kernel(window_ref, scaled_ref, projected_ref, part_ref, mixed_ref):
    part_ref[...] = jnp.dot(
        window_ref[...],
        projected_ref[...].astype(jnp.bfloat16),
        preferred_element_type=jnp.float32,
    )
    columns = slice(scaled_ref.shape[1] - mixed_ref.shape[1], None)
    mixed = jnp.dot(
        window_ref[...], scaled_ref[:, columns], preferred_element_type=jnp.float32
    )
    mixed_ref[...] = mixed.astype(jnp.bfloat16)


def window_kernel(scale, part_ref, mixed_ref, *refs):
    pieces = refs[:-3]
    send_ref, keep_ref, result = refs[-3:]
    chips, rows, _ = keep_ref.shape
    basis = jnp.concatenate([piece[...] for piece in pieces], axis=0)
    result[...] = scale * (
        part_ref[...] + jnp.dot(mixed_ref[...], basis, preferred_element_type=jnp.float32)
    )
    core = lax.rem(lax.axis_index("blk"), 2)
    for k in range(chips):
        mine = pl.ds(pl.multiple_of((2 * k + core) * rows, rows), rows)
        keep_ref[k] = result[mine, :]
        other = pl.ds(pl.multiple_of((2 * k + 1 - core) * rows, rows), rows)
        send_ref[k] = result[other, :].astype(jnp.bfloat16)


def add_core_kernel(keys, keep_ref, got_ref, own_ref, *send_refs):
    chip = lax.axis_index("blk") // 2
    for key, ref in zip((0, *keys), (own_ref, *send_refs)):
        at = chip ^ key
        ref[...] = (keep_ref[at] + got_ref[at].astype(jnp.float32)).astype(ref.dtype)


def add_chips_kernel(own_ref, *refs):
    total = own_ref[...]
    for ref in refs[:-1]:
        total += ref[...].astype(jnp.float32)
    refs[-1][...] = total


VMEM = pl.BlockSpec(memory_space=pltpu.VMEM)
SMEM = pl.BlockSpec(memory_space=pltpu.SMEM)
ANY = pl.BlockSpec(memory_space=pl.ANY)
CHEAP = pl.CostEstimate(flops=1, bytes_accessed=1, transcendentals=0)


def after(first, *others):
    return lax.optimization_barrier((first, *others))


def ring_body(n, grad_out, activations, basis_out, basis_in, eigenvalues, tile_order, block_map):
    tok_rows, full_out = grad_out.shape
    tile_width = basis_out.shape[1]
    full_in, in_width = basis_in.shape
    tokens = n * tok_rows
    chips = n // 2
    to_right = lambda x: lax.ppermute(x, "blk", shift_pairs(n, 1))
    to_left = lambda x: lax.ppermute(x, "blk", shift_pairs(n, -1))
    steps = chips // 2

    own = basis_in[:WC].T

    pairs = chips // 2
    both = jnp.concatenate([grad_out, activations], axis=1)[None]
    got = [lax.ppermute(both, "blk", xor_pairs(n, 4 * key)) for key in range(1, pairs)]
    kept = pl.pallas_call(
        keep_kernel,
        out_shape=jax.ShapeDtypeStruct(basis_in.shape, jnp.bfloat16),
        in_specs=[VMEM],
        out_specs=VMEM,
        compiler_params=pltpu.CompilerParams(vmem_limit_bytes=8 * MIB),
        cost_estimate=CHEAP,
        name="keep",
    )(basis_in)
    both, own, kept, *got = after(both, own, kept, *got)
    depth, later = 1024, 9
    grads, acts = pl.pallas_call(
        part_kernel,
        out_shape=(
            jax.ShapeDtypeStruct((pairs, tok_rows, full_out), jnp.bfloat16),
            jax.ShapeDtypeStruct((pairs, tok_rows, full_in), jnp.bfloat16),
        ),
        in_specs=[VMEM] * pairs,
        out_specs=(VMEM, VMEM),
        compiler_params=pltpu.CompilerParams(vmem_limit_bytes=8 * MIB),
        name="part",
    )(both, *got)
    acts, grads, own = after(acts, grads, own)
    acts_got = lax.ppermute(acts, "blk", xor_pairs(n, 2))
    grads_got = lax.ppermute(grads, "blk", xor_pairs(n, 2))
    acts = jnp.concatenate([acts, acts_got], axis=0)
    rotated = pl.pallas_call(
        functools.partial(rotate_in_kernel, tok_rows),
        out_shape=jax.ShapeDtypeStruct((chips, tokens, in_width), jnp.bfloat16),
        in_specs=[VMEM, VMEM, VMEM],
        out_specs=VMEM,
        compiler_params=pltpu.CompilerParams(vmem_limit_bytes=8 * MIB),
        cost_estimate=CHEAP,
        name="rotate_in",
    )(acts, swap(acts, n), kept)

    grads_got, own, _ = after(grads_got, own, rotated)
    rotated = exchange(rotated, n, 2)
    right, left = [own, to_right(own)], [own, to_left(own)]
    grads = jnp.concatenate([grads, grads_got], axis=0)
    grads_far = swap(grads, n)
    far = [swap(own, n)]

    rotate = lambda kernel, count, scratch, shape, dtype, *operands: pl.pallas_call(
        kernel,
        out_shape=jax.ShapeDtypeStruct(shape, dtype),
        in_specs=[ANY if x is basis_out or x is block_map else VMEM for x in operands],
        out_specs=VMEM,
        scratch_shapes=[pltpu.VMEM((count, depth, tile_width), jnp.bfloat16)]
        + scratch
        + [pltpu.SemaphoreType.DMA((count + 1,))],
        compiler_params=pltpu.CompilerParams(vmem_limit_bytes=40 * MIB),
        cost_estimate=CHEAP,
        name=kernel.func.__name__[:-7],
    )(*operands)
    start = rotate(
        functools.partial(rotate_first_kernel),
        full_out // depth - later,
        [],
        (tokens, tile_width),
        jnp.float32,
        grads,
        grads_far,
        basis_out,
    )
    start, right[-1], left[-1], *far = after(start, right[-1], left[-1], *far)
    far += [swap(right[-1], n), swap(left[-1], n)]
    right.append(to_right(right[-1]))
    left.append(to_left(left[-1]))
    start, grads, rotated = after(start, grads, rotated)
    rotated_far = swap(rotated, n)
    aligned = rotate(
        functools.partial(rotate_last_kernel, tok_rows, full_out // depth - later),
        later,
        [
            pltpu.VMEM((tokens, tile_width), jnp.float32),
            pltpu.SMEM(block_map.shape, jnp.int32),
        ],
        (tile_width, tokens),
        jnp.bfloat16,
        grads,
        grads_far,
        basis_out,
        block_map,
        start,
    )

    aligned, right[-1], left[-1], rotated_far, *far = after(
        aligned, right[-1], left[-1], rotated_far, *far
    )
    far += [swap(right[-1], n), swap(left[-1], n)]
    right.append(to_right(right[-1]))
    left.append(to_left(left[-1]))
    begun = [0] + [at for step in range(1, steps) for at in (step, chips - step)] + [steps]
    blocks = 8
    scaled = pl.pallas_call(
        functools.partial(scale_kernel, begun),
        out_shape=jax.ShapeDtypeStruct((tile_width, full_in), jnp.bfloat16),
        in_specs=[VMEM] * 3 + [ANY] * 2,
        out_specs=VMEM,
        scratch_shapes=[
            pltpu.VMEM((blocks, tile_width // blocks, full_in), jnp.float32),
            pltpu.SMEM(tile_order.shape, jnp.int32),
            pltpu.SMEM(tile_order.shape, jnp.int32),
            pltpu.VMEM((n, tokens, in_width), jnp.bfloat16),
            pltpu.SemaphoreType.DMA((blocks + 1,)),
        ],
        compiler_params=pltpu.CompilerParams(vmem_limit_bytes=40 * MIB),
        cost_estimate=CHEAP,
        name="scale",
    )(aligned, rotated, rotated_far, tile_order, eigenvalues)

    scaled, right[-1], left[-1], *far = after(scaled, right[-1], left[-1], *far)
    cut = in_width // 2
    last = [to_right(right[-1][:cut]), to_left(left[-1][cut:])]
    near = [right[at] if at < steps else left[chips - at] for at in begun[:-1]]
    far += [swap(piece, n) for piece in near[len(far) :]]
    pieces = [piece for pair in zip(near, far) for piece in pair]
    projected, window = pl.pallas_call(
        functools.partial(project_kernel, (0, 6, len(pieces))),
        out_shape=(
            jax.ShapeDtypeStruct((tile_width, WC), jnp.float32),
            jax.ShapeDtypeStruct((WR, tile_width), jnp.bfloat16),
        ),
        in_specs=[VMEM] + [ANY] * (len(pieces) + 1),
        out_specs=(VMEM, VMEM),
        scratch_shapes=[
            pltpu.VMEM((len(pieces) * in_width, WC), jnp.bfloat16),
            pltpu.SemaphoreType.DMA((len(pieces) + 1,)),
        ],
        compiler_params=pltpu.CompilerParams(vmem_limit_bytes=24 * MIB),
        cost_estimate=CHEAP,
        name="project",
    )(scaled, basis_out, *pieces)

    projected, *last = after(projected, *last)
    last += [swap(piece, n) for piece in last]
    rows = WR // n
    part, mixed = pl.pallas_call(
        mix_kernel,
        out_shape=(
            jax.ShapeDtypeStruct((WR, WC), jnp.float32),
            jax.ShapeDtypeStruct((WR, 2 * in_width), jnp.bfloat16),
        ),
        in_specs=[VMEM] * 3,
        out_specs=(VMEM, VMEM),
        compiler_params=pltpu.CompilerParams(vmem_limit_bytes=24 * MIB),
        cost_estimate=CHEAP,
        name="mix",
    )(window, scaled, projected)
    send, keep = pl.pallas_call(
        functools.partial(window_kernel, 1.0 / tokens),
        out_shape=(
            jax.ShapeDtypeStruct((chips, rows, WC), jnp.bfloat16),
            jax.ShapeDtypeStruct((chips, rows, WC), jnp.float32),
        ),
        in_specs=[VMEM] * 6,
        out_specs=(VMEM, VMEM),
        scratch_shapes=[pltpu.VMEM((WR, WC), jnp.float32)],
        compiler_params=pltpu.CompilerParams(vmem_limit_bytes=24 * MIB),
        cost_estimate=CHEAP,
        name="window",
    )(part, mixed, *last)

    keys = [*range(chips - 2, 0, -2), *range(chips - 1, 0, -2)]
    small = pltpu.CompilerParams(vmem_limit_bytes=8 * MIB)
    own, *sends = pl.pallas_call(
        functools.partial(add_core_kernel, keys),
        out_shape=[jax.ShapeDtypeStruct((rows, WC), jnp.float32)]
        + [jax.ShapeDtypeStruct((rows, WC), jnp.bfloat16)] * len(keys),
        in_specs=[VMEM, VMEM],
        out_specs=[VMEM] * chips,
        compiler_params=small,
        name="add_core",
    )(keep, swap(send, n))
    arrived = [lax.ppermute(x, "blk", xor_pairs(n, 2 * key)) for key, x in zip(keys, sends)]
    return pl.pallas_call(
        add_chips_kernel,
        out_shape=jax.ShapeDtypeStruct((rows, WC), jnp.float32),
        in_specs=[VMEM] * chips,
        out_specs=VMEM,
        compiler_params=small,
        name="add_chips",
    )(own, *arrived)


def gather_body(grad_out, activations, basis_out, basis_in, eigenvalues, tile_order, block_map):
    n_blocks = lax.axis_size("blk")
    tile_width = basis_out.shape[1]
    tok_rows = grad_out.shape[0]
    full_in = eigenvalues.shape[1]
    tokens = n_blocks * tok_rows
    dot = functools.partial(jnp.dot, preferred_element_type=jnp.float32)
    in_rows = lax.all_gather(basis_in[:WC], "blk", axis=1, tiled=True)
    acts = lax.all_gather(activations, "blk", axis=0, tiled=True)
    in_tile = dot(acts, basis_in).astype(jnp.bfloat16)
    rotated_in = lax.all_gather(in_tile, "blk", axis=1, tiled=True)
    grads = lax.all_gather(grad_out, "blk", axis=0, tiled=True)
    rotated_out = dot(grads, basis_out).astype(jnp.bfloat16)
    aligned = jnp.take(
        rotated_out.reshape(n_blocks, tok_rows, tile_width), block_map, axis=0
    ).reshape(tokens, tile_width)
    grad_tile = dot(aligned.T, rotated_in) / tokens
    damped = jnp.take(
        eigenvalues.reshape(tile_width, full_in // LANES, LANES), tile_order, axis=1
    ).reshape(tile_width, full_in)
    scaled = (grad_tile / damped).astype(jnp.bfloat16)
    projected = dot(scaled, in_rows.T).astype(jnp.bfloat16)
    return lax.psum_scatter(
        dot(basis_out[:WR], projected), "blk", scatter_dimension=0, tiled=True
    )


def solution(mesh):
    n = mesh.shape["blk"]

    def body(*args):
        wide = args[3].shape[1] % LANES == 0 and args[2].shape[1] % LANES == 0
        doubles = n & (n - 1) == 0 and args[0].shape[0] & (args[0].shape[0] - 1) == 0
        if wide and doubles and WR % (16 * n) == 0:
            return ring_body(n, *args)
        return gather_body(*args)

    placed = (
        P(("grp", "blk"), None),
        P(("grp", "blk"), None),
        P(None, "blk"),
        P(None, "blk"),
        P("blk", None),
        P(),
        P(),
    )
    return jax.shard_map(
        body, mesh=mesh, in_specs=placed, out_specs=P(("grp", "blk"), None), check_vma=False
    )
```

```python
import functools

import jax
import jax.numpy as jnp
from jax import lax
from jax.experimental import pallas as pl
from jax.experimental.pallas import tpu as pltpu
from jax.sharding import PartitionSpec as P

WR = 768
WC = 512
LANES = 128
MIB = 1 << 20


def ring_of(n):
    chips = n // 2
    return [*range(0, chips, 2), *range(chips - 1, 0, -2)]


def shift_pairs(n, by):
    ring = ring_of(n)
    return [
        (2 * ring[p] + c, 2 * ring[(p + by) % len(ring)] + c)
        for p in range(len(ring))
        for c in range(2)
    ]


def ring_source(me, steps, other, chips):
    chip, core = me // 2, lax.rem(me, 2)
    place = jnp.where(lax.rem(chip, 2) == 0, chip // 2, chips - 1 - chip // 2)
    place = lax.rem(place + chips - steps, chips)
    chip = jnp.where(place < chips // 2, 2 * place, 2 * (chips - 1 - place) + 1)
    return 2 * chip + (core ^ other)


def xor_pairs(n, key):
    return [(b, b ^ key) for b in range(n)]


def exchange(x, n, stride):
    groups = [list(range(first, n, stride)) for first in range(stride)]
    return lax.all_to_all(x, "blk", 0, 0, axis_index_groups=groups, tiled=True)


def swap(x, n):
    return lax.ppermute(x, "blk", xor_pairs(n, 1))


def bits_of(size):
    return size.bit_length() - 1


def held_tokens(me, tokens, tok_rows):
    row = lax.broadcasted_iota(jnp.int32, (tokens, tokens), 1)
    pairs = tokens // tok_rows // 4
    place = row >> bits_of(tok_rows)
    chip = 2 * (place & (pairs - 1)) + ((place >> bits_of(pairs)) & 1)
    other = row >> bits_of(tokens // 2)
    device = me ^ (2 * chip + other)
    return (device << bits_of(tok_rows)) + (row & (tok_rows - 1))


def reorder(wanted, held, rotated):
    order = jnp.where(wanted == held, 1.0, 0.0).astype(jnp.bfloat16)
    return jnp.dot(order, rotated.astype(jnp.bfloat16), preferred_element_type=jnp.float32)


def part_kernel(*refs):
    grads_ref, acts_ref = refs[-2:]
    first = grads_ref.shape[2]
    for at, ref in enumerate(refs[:-2]):
        grads_ref[at] = ref[0, :, :first]
        acts_ref[at] = ref[0, :, first:]


def rotate_in_kernel(tok_rows, near_ref, far_ref, basis_ref, out_ref):
    tokens = out_ref.shape[1]
    depth = near_ref.shape[2]
    acts = jnp.concatenate([ref[...].reshape(-1, depth) for ref in (near_ref, far_ref)], axis=0)
    rotated = jnp.dot(acts, basis_ref[...], preferred_element_type=jnp.float32)
    wanted = lax.broadcasted_iota(jnp.int32, (tokens, tokens), 0)
    held = held_tokens(lax.axis_index("blk"), tokens, tok_rows)
    ordered = reorder(wanted, held, rotated).astype(jnp.bfloat16)
    for copy in range(out_ref.shape[0]):
        out_ref[copy] = ordered


def keep_kernel(basis_ref, kept_ref):
    kept_ref[...] = basis_ref[...]


def rotate_part(first, near_ref, far_ref, basis_ref, basis, total, sem):
    steps, depth = basis.shape[:2]

    def copy_of(step):
        rows = pl.ds(pl.multiple_of((first + step) * depth, depth), depth)
        return pltpu.make_async_copy(basis_ref.at[rows], basis.at[step], sem.at[step])

    @pl.loop(0, steps)
    def _(step):
        copy_of(step).start()

    @pl.loop(0, steps)
    def _(step):
        columns = pl.ds(pl.multiple_of((first + step) * depth, depth), depth)
        rows = [ref[:, :, columns].reshape(-1, depth) for ref in (near_ref, far_ref)]
        grads = jnp.concatenate(rows, axis=0)
        copy_of(step).wait()
        total[...] += jnp.dot(grads, basis[step], preferred_element_type=jnp.float32)


def rotate_first_kernel(near_ref, far_ref, basis_ref, out_ref, basis, sem):
    out_ref[...] = jnp.zeros_like(out_ref)
    rotate_part(0, near_ref, far_ref, basis_ref, basis, out_ref, sem)


def rotate_last_kernel(
    tok_rows,
    first,
    near_ref,
    far_ref,
    basis_ref,
    map_ref,
    start_ref,
    out_ref,
    basis,
    total,
    stored_map,
    sem,
):
    tokens = total.shape[0]
    map_copy = pltpu.make_async_copy(map_ref, stored_map, sem.at[basis.shape[0]])
    map_copy.start()
    total[...] = start_ref[...]
    rotate_part(first, near_ref, far_ref, basis_ref, basis, total, sem)
    map_copy.wait()
    row = lax.broadcasted_iota(jnp.int32, (tokens, tokens), 0)
    block = row >> bits_of(tok_rows)
    wanted = jnp.zeros_like(row)
    for stored in range(tokens // tok_rows):
        wanted = jnp.where(block == stored, stored_map[stored] * tok_rows, wanted)
    wanted += row & (tok_rows - 1)
    held = held_tokens(lax.axis_index("blk"), tokens, tok_rows)
    out_ref[...] = reorder(wanted, held, total[...]).T.astype(jnp.bfloat16)


def scale_kernel(
    begun,
    aligned_ref,
    near_ref,
    far_ref,
    tiles_ref,
    eigen_ref,
    out_ref,
    damped,
    tiles,
    lanes,
    rotated,
    sem,
):
    blocks, depth = damped.shape[:2]
    chips, _, width = near_ref.shape
    per_piece = width // LANES

    def copy_of(block):
        rows = pl.ds(pl.multiple_of(block * depth, depth), depth)
        return pltpu.make_async_copy(eigen_ref.at[rows], damped.at[block], sem.at[block])

    tiles_copy = pltpu.make_async_copy(tiles_ref, tiles, sem.at[blocks])
    tiles_copy.start()

    @pl.loop(0, blocks)
    def _(block):
        copy_of(block).start()

    tiles_copy.wait()
    me = lax.axis_index("blk")
    for at, steps in enumerate(begun):
        for other, rotated_ref in enumerate((near_ref, far_ref)):
            source = ring_source(me, steps, other, chips)
            piece = 2 * at + other
            rotated[piece] = rotated_ref[source // 2]
            for part in range(per_piece):
                lanes[piece * per_piece + part] = tiles[source * per_piece + part] * LANES

    @pl.loop(0, blocks)
    def _(block):
        rows = pl.ds(pl.multiple_of(block * depth, depth), depth)
        aligned = aligned_ref[rows, :]
        copy_of(block).wait()
        for piece in range(2 * chips):
            grad = jnp.dot(aligned, rotated[piece], preferred_element_type=jnp.float32)
            for part in range(per_piece):
                tile = piece * per_piece + part
                eigen = damped[block, :, pl.ds(pl.multiple_of(lanes[tile], LANES), LANES)]
                inverse = pl.reciprocal(eigen, approx=True)
                inverse = inverse * (2.0 - eigen * inverse)
                scaled = grad[:, part * LANES : (part + 1) * LANES] * inverse
                out_ref[rows, tile * LANES : (tile + 1) * LANES] = scaled.astype(jnp.bfloat16)


def project_kernel(cuts, scaled_ref, basis_out_ref, *refs):
    pieces = refs[:-4]
    out_ref, window_ref, basis, sem = refs[-4:]
    width = pieces[0].shape[0]
    copies = [
        pltpu.make_async_copy(piece, basis.at[pl.ds(at * width, width)], sem.at[at])
        for at, piece in enumerate(pieces)
    ]
    window_copy = pltpu.make_async_copy(
        basis_out_ref.at[pl.ds(0, window_ref.shape[0])], window_ref, sem.at[len(pieces)]
    )
    window_copy.start()
    for copy in copies:
        copy.start()
    for first, last in zip(cuts[:-1], cuts[1:]):
        for copy in copies[first:last]:
            copy.wait()
        deep = slice(first * width, last * width)
        part = jnp.dot(scaled_ref[:, deep], basis[deep, :], preferred_element_type=jnp.float32)
        out_ref[...] = part if first == 0 else out_ref[...] + part

    window_copy.wait()


def mix_kernel(window_ref, scaled_ref, mixed_ref):
    columns = slice(scaled_ref.shape[1] - mixed_ref.shape[1], None)
    mixed = jnp.dot(
        window_ref[...], scaled_ref[:, columns], preferred_element_type=jnp.float32
    )
    mixed_ref[...] = mixed.astype(jnp.bfloat16)


def most_kernel(window_ref, projected_ref, part_ref):
    part_ref[...] = jnp.dot(
        window_ref[...],
        projected_ref[...].astype(jnp.bfloat16),
        preferred_element_type=jnp.float32,
    )


def window_kernel(scale, part_ref, mixed_ref, *refs):
    pieces = refs[:-3]
    send_ref, keep_ref, result = refs[-3:]
    chips, rows, _ = keep_ref.shape
    basis = jnp.concatenate([piece[...] for piece in pieces], axis=0)
    result[...] = scale * (
        part_ref[...] + jnp.dot(mixed_ref[...], basis, preferred_element_type=jnp.float32)
    )
    core = lax.rem(lax.axis_index("blk"), 2)
    for k in range(chips):
        mine = pl.ds(pl.multiple_of((2 * k + core) * rows, rows), rows)
        keep_ref[k] = result[mine, :]
        other = pl.ds(pl.multiple_of((2 * k + 1 - core) * rows, rows), rows)
        send_ref[k] = result[other, :].astype(jnp.bfloat16)


def add_core_kernel(keys, keep_ref, got_ref, own_ref, *send_refs):
    chip = lax.axis_index("blk") // 2
    for key, ref in zip((0, *keys), (own_ref, *send_refs)):
        at = chip ^ key
        ref[...] = (keep_ref[at] + got_ref[at].astype(jnp.float32)).astype(ref.dtype)


def add_chips_kernel(own_ref, *refs):
    total = own_ref[...]
    for ref in refs[:-1]:
        total += ref[...].astype(jnp.float32)
    refs[-1][...] = total


VMEM = pl.BlockSpec(memory_space=pltpu.VMEM)
SMEM = pl.BlockSpec(memory_space=pltpu.SMEM)
ANY = pl.BlockSpec(memory_space=pl.ANY)
CHEAP = pl.CostEstimate(flops=1, bytes_accessed=1, transcendentals=0)


def after(first, *others):
    return lax.optimization_barrier((first, *others))


def ring_body(n, grad_out, activations, basis_out, basis_in, eigenvalues, tile_order, block_map):
    tok_rows, full_out = grad_out.shape
    tile_width = basis_out.shape[1]
    full_in, in_width = basis_in.shape
    tokens = n * tok_rows
    chips = n // 2
    to_right = lambda x: lax.ppermute(x, "blk", shift_pairs(n, 1))
    to_left = lambda x: lax.ppermute(x, "blk", shift_pairs(n, -1))
    steps = chips // 2

    own = basis_in[:WC].T

    pairs = chips // 2
    both = jnp.concatenate([grad_out, activations], axis=1)[None]
    got = [lax.ppermute(both, "blk", xor_pairs(n, 4 * key)) for key in range(1, pairs)]
    kept = pl.pallas_call(
        keep_kernel,
        out_shape=jax.ShapeDtypeStruct(basis_in.shape, jnp.bfloat16),
        in_specs=[VMEM],
        out_specs=VMEM,
        compiler_params=pltpu.CompilerParams(vmem_limit_bytes=8 * MIB),
        cost_estimate=CHEAP,
        name="keep",
    )(basis_in)
    both, own, kept, *got = after(both, own, kept, *got)
    depth, later = 1024, 9
    grads, acts = pl.pallas_call(
        part_kernel,
        out_shape=(
            jax.ShapeDtypeStruct((pairs, tok_rows, full_out), jnp.bfloat16),
            jax.ShapeDtypeStruct((pairs, tok_rows, full_in), jnp.bfloat16),
        ),
        in_specs=[VMEM] * pairs,
        out_specs=(VMEM, VMEM),
        compiler_params=pltpu.CompilerParams(vmem_limit_bytes=8 * MIB),
        name="part",
    )(both, *got)
    acts, grads, own = after(acts, grads, own)
    acts_got = lax.ppermute(acts, "blk", xor_pairs(n, 2))
    grads_got = lax.ppermute(grads, "blk", xor_pairs(n, 2))
    acts = jnp.concatenate([acts, acts_got], axis=0)
    rotated = pl.pallas_call(
        functools.partial(rotate_in_kernel, tok_rows),
        out_shape=jax.ShapeDtypeStruct((chips, tokens, in_width), jnp.bfloat16),
        in_specs=[VMEM, VMEM, VMEM],
        out_specs=VMEM,
        compiler_params=pltpu.CompilerParams(vmem_limit_bytes=8 * MIB),
        cost_estimate=CHEAP,
        name="rotate_in",
    )(acts, swap(acts, n), kept)

    grads_got, own, _ = after(grads_got, own, rotated)
    rotated = exchange(rotated, n, 2)
    right, left = [own, to_right(own)], [own, to_left(own)]
    grads = jnp.concatenate([grads, grads_got], axis=0)
    grads_far = swap(grads, n)
    far = [swap(own, n)]

    rotate = lambda kernel, count, scratch, shape, dtype, *operands: pl.pallas_call(
        kernel,
        out_shape=jax.ShapeDtypeStruct(shape, dtype),
        in_specs=[ANY if x is basis_out or x is block_map else VMEM for x in operands],
        out_specs=VMEM,
        scratch_shapes=[pltpu.VMEM((count, depth, tile_width), jnp.bfloat16)]
        + scratch
        + [pltpu.SemaphoreType.DMA((count + 1,))],
        compiler_params=pltpu.CompilerParams(vmem_limit_bytes=40 * MIB),
        cost_estimate=CHEAP,
        name=kernel.func.__name__[:-7],
    )(*operands)
    start = rotate(
        functools.partial(rotate_first_kernel),
        full_out // depth - later,
        [],
        (tokens, tile_width),
        jnp.float32,
        grads,
        grads_far,
        basis_out,
    )
    start, right[-1], left[-1], *far = after(start, right[-1], left[-1], *far)
    far += [swap(right[-1], n), swap(left[-1], n)]
    right.append(to_right(right[-1]))
    left.append(to_left(left[-1]))
    start, grads, rotated = after(start, grads, rotated)
    rotated_far = swap(rotated, n)
    aligned = rotate(
        functools.partial(rotate_last_kernel, tok_rows, full_out // depth - later),
        later,
        [
            pltpu.VMEM((tokens, tile_width), jnp.float32),
            pltpu.SMEM(block_map.shape, jnp.int32),
        ],
        (tile_width, tokens),
        jnp.bfloat16,
        grads,
        grads_far,
        basis_out,
        block_map,
        start,
    )

    aligned, right[-1], left[-1], rotated_far, *far = after(
        aligned, right[-1], left[-1], rotated_far, *far
    )
    far += [swap(right[-1], n), swap(left[-1], n)]
    right.append(to_right(right[-1]))
    left.append(to_left(left[-1]))
    begun = [0] + [at for step in range(1, steps) for at in (step, chips - step)] + [steps]
    blocks = 8
    scaled = pl.pallas_call(
        functools.partial(scale_kernel, begun),
        out_shape=jax.ShapeDtypeStruct((tile_width, full_in), jnp.bfloat16),
        in_specs=[VMEM] * 3 + [ANY] * 2,
        out_specs=VMEM,
        scratch_shapes=[
            pltpu.VMEM((blocks, tile_width // blocks, full_in), jnp.float32),
            pltpu.SMEM(tile_order.shape, jnp.int32),
            pltpu.SMEM(tile_order.shape, jnp.int32),
            pltpu.VMEM((n, tokens, in_width), jnp.bfloat16),
            pltpu.SemaphoreType.DMA((blocks + 1,)),
        ],
        compiler_params=pltpu.CompilerParams(vmem_limit_bytes=40 * MIB),
        cost_estimate=CHEAP,
        name="scale",
    )(aligned, rotated, rotated_far, tile_order, eigenvalues)

    scaled, right[-1], left[-1], *far = after(scaled, right[-1], left[-1], *far)
    cut = in_width // 2
    last = [to_right(right[-1][:cut]), to_left(left[-1][cut:])]
    near = [right[at] if at < steps else left[chips - at] for at in begun[:-1]]
    far += [swap(piece, n) for piece in near[len(far) :]]
    pieces = [piece for pair in zip(near, far) for piece in pair]
    projected, window = pl.pallas_call(
        functools.partial(project_kernel, (0, 6, len(pieces))),
        out_shape=(
            jax.ShapeDtypeStruct((tile_width, WC), jnp.float32),
            jax.ShapeDtypeStruct((WR, tile_width), jnp.bfloat16),
        ),
        in_specs=[VMEM] + [ANY] * (len(pieces) + 1),
        out_specs=(VMEM, VMEM),
        scratch_shapes=[
            pltpu.VMEM((len(pieces) * in_width, WC), jnp.bfloat16),
            pltpu.SemaphoreType.DMA((len(pieces) + 1,)),
        ],
        compiler_params=pltpu.CompilerParams(vmem_limit_bytes=24 * MIB),
        cost_estimate=CHEAP,
        name="project",
    )(scaled, basis_out, *pieces)

    def product(kernel, shape, dtype, *operands):
        return pl.pallas_call(
            kernel,
            out_shape=jax.ShapeDtypeStruct(shape, dtype),
            in_specs=[VMEM] * len(operands),
            out_specs=VMEM,
            compiler_params=pltpu.CompilerParams(vmem_limit_bytes=24 * MIB),
            cost_estimate=CHEAP,
            name=kernel.__name__[:-7],
        )(*operands)

    mixed = product(mix_kernel, (WR, 2 * in_width), jnp.bfloat16, window, scaled)
    projected, mixed, *last = after(projected, mixed, *last)
    last += [swap(piece, n) for piece in last]
    part = product(most_kernel, (WR, WC), jnp.float32, window, projected)
    rows = WR // n
    send, keep = pl.pallas_call(
        functools.partial(window_kernel, 1.0 / tokens),
        out_shape=(
            jax.ShapeDtypeStruct((chips, rows, WC), jnp.bfloat16),
            jax.ShapeDtypeStruct((chips, rows, WC), jnp.float32),
        ),
        in_specs=[VMEM] * 6,
        out_specs=(VMEM, VMEM),
        scratch_shapes=[pltpu.VMEM((WR, WC), jnp.float32)],
        compiler_params=pltpu.CompilerParams(vmem_limit_bytes=24 * MIB),
        cost_estimate=CHEAP,
        name="window",
    )(part, mixed, *last)

    keys = [*range(chips - 2, 0, -2), *range(chips - 1, 0, -2)]
    small = pltpu.CompilerParams(vmem_limit_bytes=8 * MIB)
    own, *sends = pl.pallas_call(
        functools.partial(add_core_kernel, keys),
        out_shape=[jax.ShapeDtypeStruct((rows, WC), jnp.float32)]
        + [jax.ShapeDtypeStruct((rows, WC), jnp.bfloat16)] * len(keys),
        in_specs=[VMEM, VMEM],
        out_specs=[VMEM] * chips,
        compiler_params=small,
        name="add_core",
    )(keep, swap(send, n))
    arrived = [lax.ppermute(x, "blk", xor_pairs(n, 2 * key)) for key, x in zip(keys, sends)]
    return pl.pallas_call(
        add_chips_kernel,
        out_shape=jax.ShapeDtypeStruct((rows, WC), jnp.float32),
        in_specs=[VMEM] * chips,
        out_specs=VMEM,
        compiler_params=small,
        name="add_chips",
    )(own, *arrived)


def gather_body(grad_out, activations, basis_out, basis_in, eigenvalues, tile_order, block_map):
    n_blocks = lax.axis_size("blk")
    tile_width = basis_out.shape[1]
    tok_rows = grad_out.shape[0]
    full_in = eigenvalues.shape[1]
    tokens = n_blocks * tok_rows
    dot = functools.partial(jnp.dot, preferred_element_type=jnp.float32)
    in_rows = lax.all_gather(basis_in[:WC], "blk", axis=1, tiled=True)
    acts = lax.all_gather(activations, "blk", axis=0, tiled=True)
    in_tile = dot(acts, basis_in).astype(jnp.bfloat16)
    rotated_in = lax.all_gather(in_tile, "blk", axis=1, tiled=True)
    grads = lax.all_gather(grad_out, "blk", axis=0, tiled=True)
    rotated_out = dot(grads, basis_out).astype(jnp.bfloat16)
    aligned = jnp.take(
        rotated_out.reshape(n_blocks, tok_rows, tile_width), block_map, axis=0
    ).reshape(tokens, tile_width)
    grad_tile = dot(aligned.T, rotated_in) / tokens
    damped = jnp.take(
        eigenvalues.reshape(tile_width, full_in // LANES, LANES), tile_order, axis=1
    ).reshape(tile_width, full_in)
    scaled = (grad_tile / damped).astype(jnp.bfloat16)
    projected = dot(scaled, in_rows.T).astype(jnp.bfloat16)
    return lax.psum_scatter(
        dot(basis_out[:WR], projected), "blk", scatter_dimension=0, tiled=True
    )


def solution(mesh):
    n = mesh.shape["blk"]

    def body(*args):
        wide = args[3].shape[1] % LANES == 0 and args[2].shape[1] % LANES == 0
        doubles = n & (n - 1) == 0 and args[0].shape[0] & (args[0].shape[0] - 1) == 0
        if wide and doubles and WR % (16 * n) == 0:
            return ring_body(n, *args)
        return gather_body(*args)

    placed = (
        P(("grp", "blk"), None),
        P(("grp", "blk"), None),
        P(None, "blk"),
        P(None, "blk"),
        P("blk", None),
        P(),
        P(),
    )
    return jax.shard_map(
        body, mesh=mesh, in_specs=placed, out_specs=P(("grp", "blk"), None), check_vma=False
    )
```

```python
import functools

import jax
import jax.numpy as jnp
from jax import lax
from jax.experimental import pallas as pl
from jax.experimental.pallas import tpu as pltpu
from jax.sharding import PartitionSpec as P

WR = 768
WC = 512
LANES = 128
MIB = 1 << 20


def ring_of(n):
    chips = n // 2
    return [*range(0, chips, 2), *range(chips - 1, 0, -2)]


def shift_pairs(n, by):
    ring = ring_of(n)
    return [
        (2 * ring[p] + c, 2 * ring[(p + by) % len(ring)] + c)
        for p in range(len(ring))
        for c in range(2)
    ]


def ring_source(me, steps, other, chips):
    chip, core = me // 2, lax.rem(me, 2)
    place = jnp.where(lax.rem(chip, 2) == 0, chip // 2, chips - 1 - chip // 2)
    place = lax.rem(place + chips - steps, chips)
    chip = jnp.where(place < chips // 2, 2 * place, 2 * (chips - 1 - place) + 1)
    return 2 * chip + (core ^ other)


def xor_pairs(n, key):
    return [(b, b ^ key) for b in range(n)]


def exchange(x, n, stride):
    groups = [list(range(first, n, stride)) for first in range(stride)]
    return lax.all_to_all(x, "blk", 0, 0, axis_index_groups=groups, tiled=True)


def swap(x, n):
    return lax.ppermute(x, "blk", xor_pairs(n, 1))


def bits_of(size):
    return size.bit_length() - 1


def held_tokens(me, tokens, tok_rows):
    row = lax.broadcasted_iota(jnp.int32, (tokens, tokens), 1)
    pairs = tokens // tok_rows // 4
    place = row >> bits_of(tok_rows)
    chip = 2 * (place & (pairs - 1)) + ((place >> bits_of(pairs)) & 1)
    other = row >> bits_of(tokens // 2)
    device = me ^ (2 * chip + other)
    return (device << bits_of(tok_rows)) + (row & (tok_rows - 1))


def reorder(wanted, held, rotated):
    order = jnp.where(wanted == held, 1.0, 0.0).astype(jnp.bfloat16)
    return jnp.dot(order, rotated.astype(jnp.bfloat16), preferred_element_type=jnp.float32)


def part_kernel(*refs):
    grads_ref, acts_ref = refs[-2:]
    first = grads_ref.shape[2]
    for at, ref in enumerate(refs[:-2]):
        grads_ref[at] = ref[0, :, :first]
        acts_ref[at] = ref[0, :, first:]


def rotate_in_kernel(tok_rows, near_ref, far_ref, basis_ref, out_ref):
    tokens = out_ref.shape[1]
    depth = near_ref.shape[2]
    acts = jnp.concatenate([ref[...].reshape(-1, depth) for ref in (near_ref, far_ref)], axis=0)
    rotated = jnp.dot(acts, basis_ref[...], preferred_element_type=jnp.float32)
    wanted = lax.broadcasted_iota(jnp.int32, (tokens, tokens), 0)
    held = held_tokens(lax.axis_index("blk"), tokens, tok_rows)
    ordered = reorder(wanted, held, rotated).astype(jnp.bfloat16)
    for copy in range(out_ref.shape[0]):
        out_ref[copy] = ordered


def keep_kernel(basis_ref, kept_ref):
    kept_ref[...] = basis_ref[...]


def rotate_part(first, near_ref, far_ref, basis_ref, basis, total, sem):
    steps, depth = basis.shape[:2]

    def copy_of(step):
        rows = pl.ds(pl.multiple_of((first + step) * depth, depth), depth)
        return pltpu.make_async_copy(basis_ref.at[rows], basis.at[step], sem.at[step])

    @pl.loop(0, steps)
    def _(step):
        copy_of(step).start()

    @pl.loop(0, steps)
    def _(step):
        columns = pl.ds(pl.multiple_of((first + step) * depth, depth), depth)
        rows = [ref[:, :, columns].reshape(-1, depth) for ref in (near_ref, far_ref)]
        grads = jnp.concatenate(rows, axis=0)
        copy_of(step).wait()
        total[...] += jnp.dot(grads, basis[step], preferred_element_type=jnp.float32)


def rotate_first_kernel(near_ref, far_ref, basis_ref, out_ref, basis, sem):
    out_ref[...] = jnp.zeros_like(out_ref)
    rotate_part(0, near_ref, far_ref, basis_ref, basis, out_ref, sem)


def rotate_last_kernel(
    tok_rows,
    first,
    near_ref,
    far_ref,
    basis_ref,
    map_ref,
    start_ref,
    out_ref,
    basis,
    total,
    stored_map,
    sem,
):
    tokens = total.shape[0]
    map_copy = pltpu.make_async_copy(map_ref, stored_map, sem.at[basis.shape[0]])
    map_copy.start()
    total[...] = start_ref[...]
    rotate_part(first, near_ref, far_ref, basis_ref, basis, total, sem)
    map_copy.wait()
    row = lax.broadcasted_iota(jnp.int32, (tokens, tokens), 0)
    block = row >> bits_of(tok_rows)
    wanted = jnp.zeros_like(row)
    for stored in range(tokens // tok_rows):
        wanted = jnp.where(block == stored, stored_map[stored] * tok_rows, wanted)
    wanted += row & (tok_rows - 1)
    held = held_tokens(lax.axis_index("blk"), tokens, tok_rows)
    out_ref[...] = reorder(wanted, held, total[...]).T.astype(jnp.bfloat16)


def scale_kernel(
    begun,
    aligned_ref,
    near_ref,
    far_ref,
    tiles_ref,
    eigen_ref,
    out_ref,
    damped,
    tiles,
    lanes,
    rotated,
    sem,
):
    blocks, depth = damped.shape[:2]
    chips, _, width = near_ref.shape
    per_piece = width // LANES

    def copy_of(block):
        rows = pl.ds(pl.multiple_of(block * depth, depth), depth)
        return pltpu.make_async_copy(eigen_ref.at[rows], damped.at[block], sem.at[block])

    tiles_copy = pltpu.make_async_copy(tiles_ref, tiles, sem.at[blocks])
    tiles_copy.start()

    @pl.loop(0, blocks)
    def _(block):
        copy_of(block).start()

    tiles_copy.wait()
    me = lax.axis_index("blk")
    for at, steps in enumerate(begun):
        for other, rotated_ref in enumerate((near_ref, far_ref)):
            source = ring_source(me, steps, other, chips)
            piece = 2 * at + other
            rotated[piece] = rotated_ref[source // 2]
            for part in range(per_piece):
                lanes[piece * per_piece + part] = tiles[source * per_piece + part] * LANES

    @pl.loop(0, blocks)
    def _(block):
        rows = pl.ds(pl.multiple_of(block * depth, depth), depth)
        aligned = aligned_ref[rows, :]
        copy_of(block).wait()
        for piece in range(2 * chips):
            grad = jnp.dot(aligned, rotated[piece], preferred_element_type=jnp.float32)
            for part in range(per_piece):
                tile = piece * per_piece + part
                eigen = damped[block, :, pl.ds(pl.multiple_of(lanes[tile], LANES), LANES)]
                inverse = pl.reciprocal(eigen, approx=True)
                inverse = inverse * (2.0 - eigen * inverse)
                scaled = grad[:, part * LANES : (part + 1) * LANES] * inverse
                out_ref[rows, tile * LANES : (tile + 1) * LANES] = scaled.astype(jnp.bfloat16)


def project_kernel(cuts, scaled_ref, *refs):
    pieces = refs[:-3]
    out_ref, basis, sem = refs[-3:]
    width = pieces[0].shape[0]
    copies = [
        pltpu.make_async_copy(piece, basis.at[pl.ds(at * width, width)], sem.at[at])
        for at, piece in enumerate(pieces)
    ]
    for copy in copies:
        copy.start()
    for first, last in zip(cuts[:-1], cuts[1:]):
        for copy in copies[first:last]:
            copy.wait()
        deep = slice(first * width, last * width)
        part = jnp.dot(scaled_ref[:, deep], basis[deep, :], preferred_element_type=jnp.float32)
        out_ref[...] = part if first == 0 else out_ref[...] + part


def mix_kernel(basis_out_ref, scaled_ref, window_ref, near_ref, far_ref, sem):
    copy = pltpu.make_async_copy(
        basis_out_ref.at[pl.ds(0, window_ref.shape[0])], window_ref, sem.at[0]
    )
    copy.start()
    copy.wait()
    width = near_ref.shape[1]
    first = scaled_ref.shape[1] - 2 * width
    mixed = jnp.dot(window_ref[...], scaled_ref[:, first:], preferred_element_type=jnp.float32)
    near_ref[...] = mixed[:, :width].astype(jnp.bfloat16)
    far_ref[...] = mixed[:, width:].astype(jnp.bfloat16)


def window_kernel(scale, window_ref, projected_ref, near_ref, got_ref, *refs):
    pieces = refs[:-3]
    send_ref, keep_ref, result = refs[-3:]
    chips, rows, _ = keep_ref.shape
    basis = jnp.concatenate([piece[...] for piece in pieces], axis=0)
    mixed = near_ref[...].astype(jnp.float32) + got_ref[...].astype(jnp.float32)
    total = jnp.dot(
        window_ref[...],
        projected_ref[...].astype(jnp.bfloat16),
        preferred_element_type=jnp.float32,
    )
    total += jnp.dot(mixed.astype(jnp.bfloat16), basis, preferred_element_type=jnp.float32)
    result[...] = scale * total
    core = lax.rem(lax.axis_index("blk"), 2)
    for k in range(chips):
        mine = pl.ds(pl.multiple_of((2 * k + core) * rows, rows), rows)
        keep_ref[k] = result[mine, :]
        other = pl.ds(pl.multiple_of((2 * k + 1 - core) * rows, rows), rows)
        send_ref[k] = result[other, :].astype(jnp.bfloat16)


def add_core_kernel(keys, keep_ref, got_ref, own_ref, *send_refs):
    chip = lax.axis_index("blk") // 2
    for key, ref in zip((0, *keys), (own_ref, *send_refs)):
        at = chip ^ key
        ref[...] = (keep_ref[at] + got_ref[at].astype(jnp.float32)).astype(ref.dtype)


def add_chips_kernel(own_ref, *refs):
    total = own_ref[...]
    for ref in refs[:-1]:
        total += ref[...].astype(jnp.float32)
    refs[-1][...] = total


VMEM = pl.BlockSpec(memory_space=pltpu.VMEM)
SMEM = pl.BlockSpec(memory_space=pltpu.SMEM)
ANY = pl.BlockSpec(memory_space=pl.ANY)
CHEAP = pl.CostEstimate(flops=1, bytes_accessed=1, transcendentals=0)


def after(first, *others):
    return lax.optimization_barrier((first, *others))


def ring_body(n, grad_out, activations, basis_out, basis_in, eigenvalues, tile_order, block_map):
    tok_rows, full_out = grad_out.shape
    tile_width = basis_out.shape[1]
    full_in, in_width = basis_in.shape
    tokens = n * tok_rows
    chips = n // 2
    to_right = lambda x: lax.ppermute(x, "blk", shift_pairs(n, 1))
    to_left = lambda x: lax.ppermute(x, "blk", shift_pairs(n, -1))
    steps = chips // 2

    own = basis_in[:WC].T

    pairs = chips // 2
    both = jnp.concatenate([grad_out, activations], axis=1)[None]
    got = [lax.ppermute(both, "blk", xor_pairs(n, 4 * key)) for key in range(1, pairs)]
    kept = pl.pallas_call(
        keep_kernel,
        out_shape=jax.ShapeDtypeStruct(basis_in.shape, jnp.bfloat16),
        in_specs=[VMEM],
        out_specs=VMEM,
        compiler_params=pltpu.CompilerParams(vmem_limit_bytes=8 * MIB),
        cost_estimate=CHEAP,
        name="keep",
    )(basis_in)
    both, own, kept, *got = after(both, own, kept, *got)
    depth, later = 1024, 9
    grads, acts = pl.pallas_call(
        part_kernel,
        out_shape=(
            jax.ShapeDtypeStruct((pairs, tok_rows, full_out), jnp.bfloat16),
            jax.ShapeDtypeStruct((pairs, tok_rows, full_in), jnp.bfloat16),
        ),
        in_specs=[VMEM] * pairs,
        out_specs=(VMEM, VMEM),
        compiler_params=pltpu.CompilerParams(vmem_limit_bytes=8 * MIB),
        name="part",
    )(both, *got)
    acts, grads, own = after(acts, grads, own)
    acts_got = lax.ppermute(acts, "blk", xor_pairs(n, 2))
    grads_got = lax.ppermute(grads, "blk", xor_pairs(n, 2))
    acts = jnp.concatenate([acts, acts_got], axis=0)
    rotated = pl.pallas_call(
        functools.partial(rotate_in_kernel, tok_rows),
        out_shape=jax.ShapeDtypeStruct((chips, tokens, in_width), jnp.bfloat16),
        in_specs=[VMEM, VMEM, VMEM],
        out_specs=VMEM,
        compiler_params=pltpu.CompilerParams(vmem_limit_bytes=8 * MIB),
        cost_estimate=CHEAP,
        name="rotate_in",
    )(acts, swap(acts, n), kept)

    grads_got, own, _ = after(grads_got, own, rotated)
    rotated = exchange(rotated, n, 2)
    right, left = [own, to_right(own)], [own, to_left(own)]
    grads = jnp.concatenate([grads, grads_got], axis=0)
    grads_far = swap(grads, n)
    far = [swap(own, n)]

    rotate = lambda kernel, count, scratch, shape, dtype, *operands: pl.pallas_call(
        kernel,
        out_shape=jax.ShapeDtypeStruct(shape, dtype),
        in_specs=[ANY if x is basis_out or x is block_map else VMEM for x in operands],
        out_specs=VMEM,
        scratch_shapes=[pltpu.VMEM((count, depth, tile_width), jnp.bfloat16)]
        + scratch
        + [pltpu.SemaphoreType.DMA((count + 1,))],
        compiler_params=pltpu.CompilerParams(vmem_limit_bytes=40 * MIB),
        cost_estimate=CHEAP,
        name=kernel.func.__name__[:-7],
    )(*operands)
    start = rotate(
        functools.partial(rotate_first_kernel),
        full_out // depth - later,
        [],
        (tokens, tile_width),
        jnp.float32,
        grads,
        grads_far,
        basis_out,
    )
    start, right[-1], left[-1], *far = after(start, right[-1], left[-1], *far)
    far += [swap(right[-1], n), swap(left[-1], n)]
    right.append(to_right(right[-1]))
    left.append(to_left(left[-1]))
    start, grads, rotated = after(start, grads, rotated)
    rotated_far = swap(rotated, n)
    aligned = rotate(
        functools.partial(rotate_last_kernel, tok_rows, full_out // depth - later),
        later,
        [
            pltpu.VMEM((tokens, tile_width), jnp.float32),
            pltpu.SMEM(block_map.shape, jnp.int32),
        ],
        (tile_width, tokens),
        jnp.bfloat16,
        grads,
        grads_far,
        basis_out,
        block_map,
        start,
    )

    aligned, right[-1], left[-1], rotated_far, *far = after(
        aligned, right[-1], left[-1], rotated_far, *far
    )
    far += [swap(right[-1], n), swap(left[-1], n)]
    right.append(to_right(right[-1]))
    left.append(to_left(left[-1]))
    begun = [0] + [at for step in range(1, steps) for at in (step, chips - step)] + [steps]
    blocks = 8
    scaled = pl.pallas_call(
        functools.partial(scale_kernel, begun),
        out_shape=jax.ShapeDtypeStruct((tile_width, full_in), jnp.bfloat16),
        in_specs=[VMEM] * 3 + [ANY] * 2,
        out_specs=VMEM,
        scratch_shapes=[
            pltpu.VMEM((blocks, tile_width // blocks, full_in), jnp.float32),
            pltpu.SMEM(tile_order.shape, jnp.int32),
            pltpu.SMEM(tile_order.shape, jnp.int32),
            pltpu.VMEM((n, tokens, in_width), jnp.bfloat16),
            pltpu.SemaphoreType.DMA((blocks + 1,)),
        ],
        compiler_params=pltpu.CompilerParams(vmem_limit_bytes=40 * MIB),
        cost_estimate=CHEAP,
        name="scale",
    )(aligned, rotated, rotated_far, tile_order, eigenvalues)

    mix = (WR, in_width)
    window, mixed, mixed_far = pl.pallas_call(
        mix_kernel,
        out_shape=tuple(
            jax.ShapeDtypeStruct(shape, jnp.bfloat16) for shape in ((WR, tile_width), mix, mix)
        ),
        in_specs=[ANY, VMEM],
        out_specs=(VMEM,) * 3,
        scratch_shapes=[pltpu.SemaphoreType.DMA((1,))],
        compiler_params=pltpu.CompilerParams(vmem_limit_bytes=40 * MIB),
        cost_estimate=CHEAP,
        name="mix",
    )(basis_out, scaled)
    scaled, mixed, mixed_far, right[-1], left[-1], *far = after(
        scaled, mixed, mixed_far, right[-1], left[-1], *far
    )
    mixed_got = swap(mixed_far, n)
    cut = in_width // 2
    last = [to_right(right[-1][:cut]), to_left(left[-1][cut:])]
    near = [right[at] if at < steps else left[chips - at] for at in begun[:-1]]
    far += [swap(piece, n) for piece in near[len(far) :]]
    pieces = [piece for pair in zip(near, far) for piece in pair]
    projected = pl.pallas_call(
        functools.partial(project_kernel, (0, 6, len(pieces))),
        out_shape=jax.ShapeDtypeStruct((tile_width, WC), jnp.float32),
        in_specs=[VMEM] + [ANY] * len(pieces),
        out_specs=VMEM,
        scratch_shapes=[
            pltpu.VMEM((len(pieces) * in_width, WC), jnp.bfloat16),
            pltpu.SemaphoreType.DMA((len(pieces),)),
        ],
        compiler_params=pltpu.CompilerParams(vmem_limit_bytes=24 * MIB),
        cost_estimate=CHEAP,
        name="project",
    )(scaled, *pieces)

    rows = WR // n
    send, keep = pl.pallas_call(
        functools.partial(window_kernel, 1.0 / tokens),
        out_shape=(
            jax.ShapeDtypeStruct((chips, rows, WC), jnp.bfloat16),
            jax.ShapeDtypeStruct((chips, rows, WC), jnp.float32),
        ),
        in_specs=[VMEM] * 6,
        out_specs=(VMEM, VMEM),
        scratch_shapes=[pltpu.VMEM((WR, WC), jnp.float32)],
        compiler_params=pltpu.CompilerParams(vmem_limit_bytes=24 * MIB),
        cost_estimate=CHEAP,
        name="window",
    )(window, projected, mixed, mixed_got, *last)

    keys = [*range(chips - 2, 0, -2), *range(chips - 1, 0, -2)]
    small = pltpu.CompilerParams(vmem_limit_bytes=8 * MIB)
    own, *sends = pl.pallas_call(
        functools.partial(add_core_kernel, keys),
        out_shape=[jax.ShapeDtypeStruct((rows, WC), jnp.float32)]
        + [jax.ShapeDtypeStruct((rows, WC), jnp.bfloat16)] * len(keys),
        in_specs=[VMEM, VMEM],
        out_specs=[VMEM] * chips,
        compiler_params=small,
        name="add_core",
    )(keep, swap(send, n))
    arrived = [lax.ppermute(x, "blk", xor_pairs(n, 2 * key)) for key, x in zip(keys, sends)]
    return pl.pallas_call(
        add_chips_kernel,
        out_shape=jax.ShapeDtypeStruct((rows, WC), jnp.float32),
        in_specs=[VMEM] * chips,
        out_specs=VMEM,
        compiler_params=small,
        name="add_chips",
    )(own, *arrived)


def gather_body(grad_out, activations, basis_out, basis_in, eigenvalues, tile_order, block_map):
    n_blocks = lax.axis_size("blk")
    tile_width = basis_out.shape[1]
    tok_rows = grad_out.shape[0]
    full_in = eigenvalues.shape[1]
    tokens = n_blocks * tok_rows
    dot = functools.partial(jnp.dot, preferred_element_type=jnp.float32)
    in_rows = lax.all_gather(basis_in[:WC], "blk", axis=1, tiled=True)
    acts = lax.all_gather(activations, "blk", axis=0, tiled=True)
    in_tile = dot(acts, basis_in).astype(jnp.bfloat16)
    rotated_in = lax.all_gather(in_tile, "blk", axis=1, tiled=True)
    grads = lax.all_gather(grad_out, "blk", axis=0, tiled=True)
    rotated_out = dot(grads, basis_out).astype(jnp.bfloat16)
    aligned = jnp.take(
        rotated_out.reshape(n_blocks, tok_rows, tile_width), block_map, axis=0
    ).reshape(tokens, tile_width)
    grad_tile = dot(aligned.T, rotated_in) / tokens
    damped = jnp.take(
        eigenvalues.reshape(tile_width, full_in // LANES, LANES), tile_order, axis=1
    ).reshape(tile_width, full_in)
    scaled = (grad_tile / damped).astype(jnp.bfloat16)
    projected = dot(scaled, in_rows.T).astype(jnp.bfloat16)
    return lax.psum_scatter(
        dot(basis_out[:WR], projected), "blk", scatter_dimension=0, tiled=True
    )


def solution(mesh):
    n = mesh.shape["blk"]

    def body(*args):
        wide = args[3].shape[1] % LANES == 0 and args[2].shape[1] % LANES == 0
        doubles = n & (n - 1) == 0 and args[0].shape[0] & (args[0].shape[0] - 1) == 0
        if wide and doubles and WR % (16 * n) == 0:
            return ring_body(n, *args)
        return gather_body(*args)

    placed = (
        P(("grp", "blk"), None),
        P(("grp", "blk"), None),
        P(None, "blk"),
        P(None, "blk"),
        P("blk", None),
        P(),
        P(),
    )
    return jax.shard_map(
        body, mesh=mesh, in_specs=placed, out_specs=P(("grp", "blk"), None), check_vma=False
    )
```

```python
import functools

import jax
import jax.numpy as jnp
from jax import lax
from jax.experimental import pallas as pl
from jax.experimental.pallas import tpu as pltpu
from jax.sharding import PartitionSpec as P

WR = 768
WC = 512
LANES = 128
MIB = 1 << 20


def ring_of(n):
    chips = n // 2
    return [*range(0, chips, 2), *range(chips - 1, 0, -2)]


def shift_pairs(n, by):
    ring = ring_of(n)
    return [
        (2 * ring[p] + c, 2 * ring[(p + by) % len(ring)] + c)
        for p in range(len(ring))
        for c in range(2)
    ]


def ring_source(me, steps, other, chips):
    chip, core = me // 2, lax.rem(me, 2)
    place = jnp.where(lax.rem(chip, 2) == 0, chip // 2, chips - 1 - chip // 2)
    place = lax.rem(place + chips - steps, chips)
    chip = jnp.where(place < chips // 2, 2 * place, 2 * (chips - 1 - place) + 1)
    return 2 * chip + (core ^ other)


def xor_pairs(n, key):
    return [(b, b ^ key) for b in range(n)]


def exchange(x, n, stride):
    groups = [list(range(first, n, stride)) for first in range(stride)]
    return lax.all_to_all(x, "blk", 0, 0, axis_index_groups=groups, tiled=True)


def swap(x, n):
    return lax.ppermute(x, "blk", xor_pairs(n, 1))


def bits_of(size):
    return size.bit_length() - 1


def held_tokens(me, tokens, tok_rows):
    row = lax.broadcasted_iota(jnp.int32, (tokens, tokens), 1)
    pairs = tokens // tok_rows // 4
    place = row >> bits_of(tok_rows)
    chip = 2 * (place & (pairs - 1)) + ((place >> bits_of(pairs)) & 1)
    other = row >> bits_of(tokens // 2)
    device = me ^ (2 * chip + other)
    return (device << bits_of(tok_rows)) + (row & (tok_rows - 1))


def reorder(wanted, held, rotated):
    order = jnp.where(wanted == held, 1.0, 0.0).astype(jnp.bfloat16)
    return jnp.dot(order, rotated.astype(jnp.bfloat16), preferred_element_type=jnp.float32)


def part_kernel(*refs):
    grads_ref, acts_ref = refs[-2:]
    first = grads_ref.shape[2]
    for at, ref in enumerate(refs[:-2]):
        grads_ref[at] = ref[0, :, :first]
        acts_ref[at] = ref[0, :, first:]


def rotate_in_kernel(tok_rows, near_ref, far_ref, basis_ref, out_ref):
    tokens = out_ref.shape[1]
    depth = near_ref.shape[2]
    acts = jnp.concatenate([ref[...].reshape(-1, depth) for ref in (near_ref, far_ref)], axis=0)
    rotated = jnp.dot(acts, basis_ref[...], preferred_element_type=jnp.float32)
    wanted = lax.broadcasted_iota(jnp.int32, (tokens, tokens), 0)
    held = held_tokens(lax.axis_index("blk"), tokens, tok_rows)
    ordered = reorder(wanted, held, rotated).astype(jnp.bfloat16)
    for copy in range(out_ref.shape[0]):
        out_ref[copy] = ordered


def keep_kernel(basis_ref, kept_ref):
    kept_ref[...] = basis_ref[...]


def rotate_part(first, near_ref, far_ref, basis_ref, basis, total, sem):
    steps, depth = basis.shape[:2]

    def copy_of(step):
        rows = pl.ds(pl.multiple_of((first + step) * depth, depth), depth)
        return pltpu.make_async_copy(basis_ref.at[rows], basis.at[step], sem.at[step])

    @pl.loop(0, steps)
    def _(step):
        copy_of(step).start()

    @pl.loop(0, steps)
    def _(step):
        columns = pl.ds(pl.multiple_of((first + step) * depth, depth), depth)
        rows = [ref[:, :, columns].reshape(-1, depth) for ref in (near_ref, far_ref)]
        grads = jnp.concatenate(rows, axis=0)
        copy_of(step).wait()
        total[...] += jnp.dot(grads, basis[step], preferred_element_type=jnp.float32)


def rotate_first_kernel(near_ref, far_ref, basis_ref, out_ref, basis, sem):
    out_ref[...] = jnp.zeros_like(out_ref)
    rotate_part(0, near_ref, far_ref, basis_ref, basis, out_ref, sem)


def rotate_last_kernel(
    tok_rows,
    first,
    near_ref,
    far_ref,
    basis_ref,
    map_ref,
    start_ref,
    out_ref,
    basis,
    total,
    stored_map,
    sem,
):
    tokens = total.shape[0]
    map_copy = pltpu.make_async_copy(map_ref, stored_map, sem.at[basis.shape[0]])
    map_copy.start()
    total[...] = start_ref[...]
    rotate_part(first, near_ref, far_ref, basis_ref, basis, total, sem)
    map_copy.wait()
    row = lax.broadcasted_iota(jnp.int32, (tokens, tokens), 0)
    block = row >> bits_of(tok_rows)
    wanted = jnp.zeros_like(row)
    for stored in range(tokens // tok_rows):
        wanted = jnp.where(block == stored, stored_map[stored] * tok_rows, wanted)
    wanted += row & (tok_rows - 1)
    held = held_tokens(lax.axis_index("blk"), tokens, tok_rows)
    out_ref[...] = reorder(wanted, held, total[...]).T.astype(jnp.bfloat16)


def scale_kernel(
    begun,
    aligned_ref,
    near_ref,
    far_ref,
    tiles_ref,
    eigen_ref,
    basis_out_ref,
    out_ref,
    window_ref,
    damped,
    tiles,
    lanes,
    rotated,
    sem,
):
    blocks, depth = damped.shape[:2]
    chips, _, width = near_ref.shape
    per_piece = width // LANES

    def copy_of(block):
        rows = pl.ds(pl.multiple_of(block * depth, depth), depth)
        return pltpu.make_async_copy(eigen_ref.at[rows], damped.at[block], sem.at[block])

    tiles_copy = pltpu.make_async_copy(tiles_ref, tiles, sem.at[blocks])
    tiles_copy.start()

    @pl.loop(0, blocks)
    def _(block):
        copy_of(block).start()

    window_copy = pltpu.make_async_copy(
        basis_out_ref.at[pl.ds(0, window_ref.shape[0])], window_ref, sem.at[blocks + 1]
    )
    window_copy.start()
    tiles_copy.wait()
    me = lax.axis_index("blk")
    for at, steps in enumerate(begun):
        for other, rotated_ref in enumerate((near_ref, far_ref)):
            source = ring_source(me, steps, other, chips)
            piece = 2 * at + other
            rotated[piece] = rotated_ref[source // 2]
            for part in range(per_piece):
                lanes[piece * per_piece + part] = tiles[source * per_piece + part] * LANES

    @pl.loop(0, blocks)
    def _(block):
        rows = pl.ds(pl.multiple_of(block * depth, depth), depth)
        aligned = aligned_ref[rows, :]
        copy_of(block).wait()
        for piece in range(2 * chips):
            grad = jnp.dot(aligned, rotated[piece], preferred_element_type=jnp.float32)
            for part in range(per_piece):
                tile = piece * per_piece + part
                eigen = damped[block, :, pl.ds(pl.multiple_of(lanes[tile], LANES), LANES)]
                inverse = pl.reciprocal(eigen, approx=True)
                inverse = inverse * (2.0 - eigen * inverse)
                scaled = grad[:, part * LANES : (part + 1) * LANES] * inverse
                out_ref[rows, tile * LANES : (tile + 1) * LANES] = scaled.astype(jnp.bfloat16)

    window_copy.wait()


def project_kernel(cuts, scaled_ref, *refs):
    pieces = refs[:-3]
    out_ref, basis, sem = refs[-3:]
    width = pieces[0].shape[0]
    copies = [
        pltpu.make_async_copy(piece, basis.at[pl.ds(at * width, width)], sem.at[at])
        for at, piece in enumerate(pieces)
    ]
    for copy in copies:
        copy.start()
    for first, last in zip(cuts[:-1], cuts[1:]):
        for copy in copies[first:last]:
            copy.wait()
        deep = slice(first * width, last * width)
        part = jnp.dot(scaled_ref[:, deep], basis[deep, :], preferred_element_type=jnp.float32)
        out_ref[...] = part if first == 0 else out_ref[...] + part


def mix_kernel(window_ref, scaled_ref, near_ref, far_ref):
    width = near_ref.shape[1]
    first = scaled_ref.shape[1] - 2 * width
    mixed = jnp.dot(window_ref[...], scaled_ref[:, first:], preferred_element_type=jnp.float32)
    near_ref[...] = mixed[:, :width].astype(jnp.bfloat16)
    far_ref[...] = mixed[:, width:].astype(jnp.bfloat16)


def window_kernel(scale, window_ref, projected_ref, near_ref, got_ref, *refs):
    pieces = refs[:-3]
    send_ref, keep_ref, result = refs[-3:]
    chips, rows, _ = keep_ref.shape
    basis = jnp.concatenate([piece[...] for piece in pieces], axis=0)
    mixed = near_ref[...].astype(jnp.float32) + got_ref[...].astype(jnp.float32)
    total = jnp.dot(
        window_ref[...],
        projected_ref[...].astype(jnp.bfloat16),
        preferred_element_type=jnp.float32,
    )
    total += jnp.dot(mixed.astype(jnp.bfloat16), basis, preferred_element_type=jnp.float32)
    result[...] = scale * total
    core = lax.rem(lax.axis_index("blk"), 2)
    for k in range(chips):
        mine = pl.ds(pl.multiple_of((2 * k + core) * rows, rows), rows)
        keep_ref[k] = result[mine, :]
        other = pl.ds(pl.multiple_of((2 * k + 1 - core) * rows, rows), rows)
        send_ref[k] = result[other, :].astype(jnp.bfloat16)


def add_core_kernel(keys, keep_ref, got_ref, own_ref, *send_refs):
    chip = lax.axis_index("blk") // 2
    for key, ref in zip((0, *keys), (own_ref, *send_refs)):
        at = chip ^ key
        ref[...] = (keep_ref[at] + got_ref[at].astype(jnp.float32)).astype(ref.dtype)


def add_chips_kernel(own_ref, *refs):
    total = own_ref[...]
    for ref in refs[:-1]:
        total += ref[...].astype(jnp.float32)
    refs[-1][...] = total


VMEM = pl.BlockSpec(memory_space=pltpu.VMEM)
SMEM = pl.BlockSpec(memory_space=pltpu.SMEM)
ANY = pl.BlockSpec(memory_space=pl.ANY)
CHEAP = pl.CostEstimate(flops=1, bytes_accessed=1, transcendentals=0)


def after(first, *others):
    return lax.optimization_barrier((first, *others))


def ring_body(n, grad_out, activations, basis_out, basis_in, eigenvalues, tile_order, block_map):
    tok_rows, full_out = grad_out.shape
    tile_width = basis_out.shape[1]
    full_in, in_width = basis_in.shape
    tokens = n * tok_rows
    chips = n // 2
    to_right = lambda x: lax.ppermute(x, "blk", shift_pairs(n, 1))
    to_left = lambda x: lax.ppermute(x, "blk", shift_pairs(n, -1))
    steps = chips // 2

    own = basis_in[:WC].T

    pairs = chips // 2
    both = jnp.concatenate([grad_out, activations], axis=1)[None]
    got = [lax.ppermute(both, "blk", xor_pairs(n, 4 * key)) for key in range(1, pairs)]
    kept = pl.pallas_call(
        keep_kernel,
        out_shape=jax.ShapeDtypeStruct(basis_in.shape, jnp.bfloat16),
        in_specs=[VMEM],
        out_specs=VMEM,
        compiler_params=pltpu.CompilerParams(vmem_limit_bytes=8 * MIB),
        cost_estimate=CHEAP,
        name="keep",
    )(basis_in)
    both, own, kept, *got = after(both, own, kept, *got)
    depth, later = 1024, 9
    grads, acts = pl.pallas_call(
        part_kernel,
        out_shape=(
            jax.ShapeDtypeStruct((pairs, tok_rows, full_out), jnp.bfloat16),
            jax.ShapeDtypeStruct((pairs, tok_rows, full_in), jnp.bfloat16),
        ),
        in_specs=[VMEM] * pairs,
        out_specs=(VMEM, VMEM),
        compiler_params=pltpu.CompilerParams(vmem_limit_bytes=8 * MIB),
        name="part",
    )(both, *got)
    acts, grads, own = after(acts, grads, own)
    acts_got = lax.ppermute(acts, "blk", xor_pairs(n, 2))
    grads_got = lax.ppermute(grads, "blk", xor_pairs(n, 2))
    acts = jnp.concatenate([acts, acts_got], axis=0)
    rotated = pl.pallas_call(
        functools.partial(rotate_in_kernel, tok_rows),
        out_shape=jax.ShapeDtypeStruct((chips, tokens, in_width), jnp.bfloat16),
        in_specs=[VMEM, VMEM, VMEM],
        out_specs=VMEM,
        compiler_params=pltpu.CompilerParams(vmem_limit_bytes=8 * MIB),
        cost_estimate=CHEAP,
        name="rotate_in",
    )(acts, swap(acts, n), kept)

    grads_got, own, _ = after(grads_got, own, rotated)
    rotated = exchange(rotated, n, 2)
    right, left = [own, to_right(own)], [own, to_left(own)]
    grads = jnp.concatenate([grads, grads_got], axis=0)
    grads_far = swap(grads, n)
    far = [swap(own, n)]

    rotate = lambda kernel, count, scratch, shape, dtype, *operands: pl.pallas_call(
        kernel,
        out_shape=jax.ShapeDtypeStruct(shape, dtype),
        in_specs=[ANY if x is basis_out or x is block_map else VMEM for x in operands],
        out_specs=VMEM,
        scratch_shapes=[pltpu.VMEM((count, depth, tile_width), jnp.bfloat16)]
        + scratch
        + [pltpu.SemaphoreType.DMA((count + 1,))],
        compiler_params=pltpu.CompilerParams(vmem_limit_bytes=40 * MIB),
        cost_estimate=CHEAP,
        name=kernel.func.__name__[:-7],
    )(*operands)
    start = rotate(
        functools.partial(rotate_first_kernel),
        full_out // depth - later,
        [],
        (tokens, tile_width),
        jnp.float32,
        grads,
        grads_far,
        basis_out,
    )
    start, right[-1], left[-1], *far = after(start, right[-1], left[-1], *far)
    far += [swap(right[-1], n), swap(left[-1], n)]
    right.append(to_right(right[-1]))
    left.append(to_left(left[-1]))
    start, grads, rotated = after(start, grads, rotated)
    rotated_far = swap(rotated, n)
    aligned = rotate(
        functools.partial(rotate_last_kernel, tok_rows, full_out // depth - later),
        later,
        [
            pltpu.VMEM((tokens, tile_width), jnp.float32),
            pltpu.SMEM(block_map.shape, jnp.int32),
        ],
        (tile_width, tokens),
        jnp.bfloat16,
        grads,
        grads_far,
        basis_out,
        block_map,
        start,
    )

    aligned, right[-1], left[-1], rotated_far, *far = after(
        aligned, right[-1], left[-1], rotated_far, *far
    )
    far += [swap(right[-1], n), swap(left[-1], n)]
    right.append(to_right(right[-1]))
    left.append(to_left(left[-1]))
    begun = [0] + [at for step in range(1, steps) for at in (step, chips - step)] + [steps]
    blocks = 8
    scaled, window = pl.pallas_call(
        functools.partial(scale_kernel, begun),
        out_shape=(
            jax.ShapeDtypeStruct((tile_width, full_in), jnp.bfloat16),
            jax.ShapeDtypeStruct((WR, tile_width), jnp.bfloat16),
        ),
        in_specs=[VMEM] * 3 + [ANY] * 3,
        out_specs=(VMEM, VMEM),
        scratch_shapes=[
            pltpu.VMEM((blocks, tile_width // blocks, full_in), jnp.float32),
            pltpu.SMEM(tile_order.shape, jnp.int32),
            pltpu.SMEM(tile_order.shape, jnp.int32),
            pltpu.VMEM((n, tokens, in_width), jnp.bfloat16),
            pltpu.SemaphoreType.DMA((blocks + 2,)),
        ],
        compiler_params=pltpu.CompilerParams(vmem_limit_bytes=40 * MIB),
        cost_estimate=CHEAP,
        name="scale",
    )(aligned, rotated, rotated_far, tile_order, eigenvalues, basis_out)

    mix = (WR, in_width)
    mixed, mixed_far = pl.pallas_call(
        mix_kernel,
        out_shape=(jax.ShapeDtypeStruct(mix, jnp.bfloat16),) * 2,
        in_specs=[VMEM, VMEM],
        out_specs=(VMEM, VMEM),
        compiler_params=pltpu.CompilerParams(vmem_limit_bytes=40 * MIB),
        cost_estimate=CHEAP,
        name="mix",
    )(window, scaled)
    scaled, mixed, mixed_far, right[-1], left[-1], *far = after(
        scaled, mixed, mixed_far, right[-1], left[-1], *far
    )
    mixed_got = swap(mixed_far, n)
    cut = in_width // 2
    last = [to_right(right[-1][:cut]), to_left(left[-1][cut:])]
    near = [right[at] if at < steps else left[chips - at] for at in begun[:-1]]
    far += [swap(piece, n) for piece in near[len(far) :]]
    pieces = [piece for pair in zip(near, far) for piece in pair]
    projected = pl.pallas_call(
        functools.partial(project_kernel, (0, 6, len(pieces))),
        out_shape=jax.ShapeDtypeStruct((tile_width, WC), jnp.float32),
        in_specs=[VMEM] + [ANY] * len(pieces),
        out_specs=VMEM,
        scratch_shapes=[
            pltpu.VMEM((len(pieces) * in_width, WC), jnp.bfloat16),
            pltpu.SemaphoreType.DMA((len(pieces),)),
        ],
        compiler_params=pltpu.CompilerParams(vmem_limit_bytes=24 * MIB),
        cost_estimate=CHEAP,
        name="project",
    )(scaled, *pieces)

    rows = WR // n
    send, keep = pl.pallas_call(
        functools.partial(window_kernel, 1.0 / tokens),
        out_shape=(
            jax.ShapeDtypeStruct((chips, rows, WC), jnp.bfloat16),
            jax.ShapeDtypeStruct((chips, rows, WC), jnp.float32),
        ),
        in_specs=[VMEM] * 6,
        out_specs=(VMEM, VMEM),
        scratch_shapes=[pltpu.VMEM((WR, WC), jnp.float32)],
        compiler_params=pltpu.CompilerParams(vmem_limit_bytes=24 * MIB),
        cost_estimate=CHEAP,
        name="window",
    )(window, projected, mixed, mixed_got, *last)

    keys = [*range(chips - 2, 0, -2), *range(chips - 1, 0, -2)]
    small = pltpu.CompilerParams(vmem_limit_bytes=8 * MIB)
    own, *sends = pl.pallas_call(
        functools.partial(add_core_kernel, keys),
        out_shape=[jax.ShapeDtypeStruct((rows, WC), jnp.float32)]
        + [jax.ShapeDtypeStruct((rows, WC), jnp.bfloat16)] * len(keys),
        in_specs=[VMEM, VMEM],
        out_specs=[VMEM] * chips,
        compiler_params=small,
        name="add_core",
    )(keep, swap(send, n))
    arrived = [lax.ppermute(x, "blk", xor_pairs(n, 2 * key)) for key, x in zip(keys, sends)]
    return pl.pallas_call(
        add_chips_kernel,
        out_shape=jax.ShapeDtypeStruct((rows, WC), jnp.float32),
        in_specs=[VMEM] * chips,
        out_specs=VMEM,
        compiler_params=small,
        name="add_chips",
    )(own, *arrived)


def gather_body(grad_out, activations, basis_out, basis_in, eigenvalues, tile_order, block_map):
    n_blocks = lax.axis_size("blk")
    tile_width = basis_out.shape[1]
    tok_rows = grad_out.shape[0]
    full_in = eigenvalues.shape[1]
    tokens = n_blocks * tok_rows
    dot = functools.partial(jnp.dot, preferred_element_type=jnp.float32)
    in_rows = lax.all_gather(basis_in[:WC], "blk", axis=1, tiled=True)
    acts = lax.all_gather(activations, "blk", axis=0, tiled=True)
    in_tile = dot(acts, basis_in).astype(jnp.bfloat16)
    rotated_in = lax.all_gather(in_tile, "blk", axis=1, tiled=True)
    grads = lax.all_gather(grad_out, "blk", axis=0, tiled=True)
    rotated_out = dot(grads, basis_out).astype(jnp.bfloat16)
    aligned = jnp.take(
        rotated_out.reshape(n_blocks, tok_rows, tile_width), block_map, axis=0
    ).reshape(tokens, tile_width)
    grad_tile = dot(aligned.T, rotated_in) / tokens
    damped = jnp.take(
        eigenvalues.reshape(tile_width, full_in // LANES, LANES), tile_order, axis=1
    ).reshape(tile_width, full_in)
    scaled = (grad_tile / damped).astype(jnp.bfloat16)
    projected = dot(scaled, in_rows.T).astype(jnp.bfloat16)
    return lax.psum_scatter(
        dot(basis_out[:WR], projected), "blk", scatter_dimension=0, tiled=True
    )


def solution(mesh):
    n = mesh.shape["blk"]

    def body(*args):
        wide = args[3].shape[1] % LANES == 0 and args[2].shape[1] % LANES == 0
        doubles = n & (n - 1) == 0 and args[0].shape[0] & (args[0].shape[0] - 1) == 0
        if wide and doubles and WR % (16 * n) == 0:
            return ring_body(n, *args)
        return gather_body(*args)

    placed = (
        P(("grp", "blk"), None),
        P(("grp", "blk"), None),
        P(None, "blk"),
        P(None, "blk"),
        P("blk", None),
        P(),
        P(),
    )
    return jax.shard_map(
        body, mesh=mesh, in_specs=placed, out_specs=P(("grp", "blk"), None), check_vma=False
    )
```
